32 devices in a mesh: fsdp: 8 (over y, x, core), seq: 4 (over z).
Axes of the slice: x: 2, y: 2, z: 4, core: 2. Of those that a mesh axis runs over, the one named last changes fastest.
Arguments:
- tokens: bfloat16 [8, 2048, 1024], P('fsdp', 'seq'), may hold values from -6 to 6
- cotangent: bfloat16 [8, 2048, 1024], P('fsdp', 'seq'), may hold values from -6 to 6
- segment_ids: int32 [8, 2048], P('fsdp', 'seq'), may hold values from 0 to 8, as said below
- norm_gain: float32 [1024], replicated, may hold values from 0.5 to 1.5
- ffn_gain: float32 [1024], replicated, may hold values from 0.5 to 1.5
- mixer_gain: float32 [1536], replicated, may hold values from 0.5 to 1.5
- conv_weight: float32 [4, 1792], replicated, may hold values from -3 to 3
- conv_bias: float32 [1792], replicated, may hold values from -3 to 3
- decay_log: float32 [24], replicated, may hold values from -7.6 to -0.7
- step_bias: float32 [24], replicated, may hold values from -1 to 1
- skip_gain: float32 [24], replicated, may hold values from 0.5 to 1.5
- in_proj: float32 [1024, 3352], P('fsdp'), may hold values from -0.1875 to 0.1875
- mixer_out: float32 [1536, 1024], P('fsdp'), may hold values from -0.15625 to 0.15625
- qkv_proj: float32 [1024, 768], P('fsdp'), may hold values from -0.1875 to 0.1875
- attn_proj: float32 [512, 1024], P('fsdp'), may hold values from -1 to 1
- gate_up: float32 [1024, 4096], P('fsdp'), may hold values from -0.1875 to 0.1875
- down_proj: float32 [2048, 1024], P('fsdp'), may hold values from -0.125 to 0.125
Outputs:
- layer_out: bfloat16 [8, 2048, 1024], P('fsdp', 'seq')
- input_grad: float32 [8, 2048, 1024], P('fsdp', 'seq')
- norm_gain_grad: float32 [1024], replicated
- ffn_gain_grad: float32 [1024], replicated
- mixer_gain_grad: float32 [1536], replicated
- conv_weight_grad: float32 [4, 1792], replicated
- conv_bias_grad: float32 [1792], replicated
- decay_log_grad: float32 [24], replicated
- step_bias_grad: float32 [24], replicated
- skip_gain_grad: float32 [24], replicated
- in_proj_grad: float32 [1024, 3352], P('fsdp')
- mixer_out_grad: float32 [1536, 1024], P('fsdp')
- qkv_proj_grad: float32 [1024, 768], P('fsdp')
- attn_proj_grad: float32 [512, 1024], P('fsdp')
- gate_up_grad: float32 [1024, 4096], P('fsdp')
- down_proj_grad: float32 [2048, 1024], P('fsdp')
The draws below stay inside these ranges and needn't reach their ends.
Inputs may be any that keep to these rules, and one draw needn't show every extreme that they name: `segment_ids`: in each sequence the numbers never fall, each document is a run of equal numbers, and one document starts within the first 512 tokens and ends within the last 512.
All inputs are finite; a program needn't handle non-finite values.
Results may differ from the reference program's by a relative error of at most 0.019.
The reference program's roundings to bfloat16 on the way count: a program that leaves them out, or rounds other values in their place, can miss the bound.
Values may be sent and summed in bfloat16 or wider, within the bound.
A program may use at most 320 MiB of HBM per device.

```python
import jax
import jax.numpy as jnp
from jax import lax

D = 1024
FF = 2048
QUERY_HEADS = 8
KEY_VALUE_HEADS = 2
HEAD_WIDTH = 64
MH = 24
MP = 64
NS = 128
KC = 4
SUB = 128
KEYS_PER_BLOCK = 512
TOK = 512
SEQS = 8
LENGTH = 2048
DI = 1536
CW = 1792
ZW = 3352
QW = 768


def draw_segment_ids(key, part):
    key = jax.random.fold_in(key, 7)
    subkeys = jax.random.split(key, 4)
    first_cut = jax.random.randint(subkeys[0], (SEQS, 1), 1, TOK)
    last_cut = jax.random.randint(subkeys[1], (SEQS, 1), LENGTH - TOK + 1, LENGTH)
    early_raw = jax.random.randint(subkeys[2], (SEQS, 3), 0, TOK)
    late_raw = jax.random.randint(subkeys[3], (SEQS, 3), 0, TOK)
    early_cuts = 1 + early_raw * (first_cut - 1) // TOK
    late_cuts = last_cut + late_raw * (LENGTH - last_cut) // TOK
    cuts = jnp.concatenate([early_cuts, first_cut, last_cut, late_cuts], axis=1)
    token_positions = jnp.arange(LENGTH, dtype=jnp.int32)
    return jnp.sum((token_positions[None, :, None] >= cuts[:, None, :]).astype(jnp.int32), axis=-1)


def levels(own_key, shape, shards, low, largest):
    factor_of, own = 1.0, jax.random.fold_in(own_key, 6)
    for dim, parts in shards:
        heights = jnp.exp(jax.random.uniform(jax.random.fold_in(own, dim), (parts,), jnp.float32, low / len(shards), largest / len(shards)))
        factor_of = factor_of * jnp.repeat(heights, shape[dim] // parts).reshape([-1 if axis == dim else 1 for axis in range(len(shape))])
    return factor_of


def scatter_about(key, extent, width, limit, cuts=(), kind=jnp.bfloat16):
    values = width * jax.random.normal(key, extent, jnp.float32)
    if cuts:
        values = values * levels(key, extent, cuts, -0.22, 0.18)
    return jnp.clip(values, -limit, limit).astype(kind)


def setup_inputs(seed: int = 0) -> dict:
    arg_keys = jax.random.split(jax.random.key(seed), 18)
    return {
        "tokens": scatter_about(arg_keys[0], (SEQS, LENGTH, D), 1.0, 6.0, ((0, 8), (1, 4))),
        "cotangent": scatter_about(arg_keys[1], (SEQS, LENGTH, D), 1.0, 6.0, ((0, 8), (1, 4))),
        "segment_ids": draw_segment_ids(jax.random.fold_in(arg_keys[17], 71), 0),
        "norm_gain": jnp.clip(1.0 + 0.1 * jax.random.normal(arg_keys[3], (D,), jnp.float32), 0.5, 1.5),
        "ffn_gain": jnp.clip(1.0 + 0.1 * jax.random.normal(arg_keys[4], (D,), jnp.float32), 0.5, 1.5),
        "mixer_gain": jnp.clip(1.0 + 0.1 * jax.random.normal(arg_keys[5], (DI,), jnp.float32), 0.5, 1.5),
        "conv_weight": scatter_about(arg_keys[6], (KC, CW), 0.5, 3.0, (), jnp.float32),
        "conv_bias": scatter_about(arg_keys[7], (CW,), 0.5, 3.0, (), jnp.float32),
        "decay_log": jnp.clip(jax.random.uniform(arg_keys[8], (MH,), jnp.float32, -7.6, -0.7), -7.6, -0.7),
        "step_bias": jnp.clip(jax.random.uniform(arg_keys[9], (MH,), jnp.float32, -1.0, 1.0), -1.0, 1.0),
        "skip_gain": jnp.clip(jax.random.uniform(arg_keys[10], (MH,), jnp.float32, 0.5, 1.5), 0.5, 1.5),
        "in_proj": scatter_about(arg_keys[11], (D, ZW), D ** -0.5, 0.1875, ((0, 8),), jnp.float32),
        "mixer_out": scatter_about(arg_keys[12], (DI, D), DI ** -0.5, 0.15625, ((0, 8),), jnp.float32),
        "qkv_proj": scatter_about(arg_keys[13], (D, QW), D ** -0.5, 0.1875, ((0, 8),), jnp.float32),
        "attn_proj": scatter_about(arg_keys[14], (QUERY_HEADS * HEAD_WIDTH, D), (QUERY_HEADS * HEAD_WIDTH // 16) ** -0.5, 1.0, ((0, 8),), jnp.float32),
        "gate_up": scatter_about(arg_keys[15], (D, 2 * FF), D ** -0.5, 0.1875, ((0, 8),), jnp.float32),
        "down_proj": scatter_about(arg_keys[16], (FF, D), FF ** -0.5, 0.125, ((0, 8),), jnp.float32),
    }


epsilon = 1e-05
rope_base = 100000000000.0
highest = lax.Precision.HIGHEST

@jax.custom_vjp
def lower_bound(v):
    return lax.optimization_barrier(v.astype(jnp.bfloat16)).astype(jnp.float32)

@jax.custom_vjp
def low_back(v):
    return v

def low_keep(v):
    return (lower_bound(v), None)

def low_pass(kept, grad):
    return (grad,)

def back_keep(v):
    return (v, None)

def back_low(kept, grad):
    return (lower_bound(grad),)
lower_bound.defvjp(low_keep, low_pass)
low_back.defvjp(back_keep, back_low)

def matmul(left, right):
    return jnp.dot(left, right, precision=highest, preferred_element_type=jnp.float32)

def rms_scale(values, gain_vec):
    return values * lax.rsqrt(lax.optimization_barrier(jnp.mean(values * values, axis=-1, keepdims=True)) + epsilon) * gain_vec

def apply_rotation(values, token_positions):
    half_width = values.shape[-1] // 2
    exponent = jnp.arange(half_width, dtype=jnp.float32) * (2.0 / values.shape[-1])
    frequencies = jnp.power(rope_base, -exponent)
    angles = token_positions.astype(jnp.float32)[:, None] * frequencies[None, :]
    cosine = jnp.cos(angles)[:, None, :]
    sine_part = jnp.sin(angles)[:, None, :]
    first_half = values[..., :half_width]
    second = values[..., half_width:]
    return jnp.concatenate([first_half * cosine - second * sine_part, second * cosine + first_half * sine_part], axis=-1)

def conv_apply(rows_in, edge_in, weight, bias_vec, segment_labels, edge_segments):
    tap_count = weight.shape[0]
    count_of_rows = rows_in.shape[0]
    padded = jnp.concatenate([edge_in, rows_in], axis=0)
    padded_seg = jnp.concatenate([edge_segments, segment_labels], axis=0)
    running = jnp.zeros_like(rows_in) + bias_vec[None, :]
    for offset in range(tap_count):
        same_doc = (padded_seg[offset:offset + count_of_rows] == segment_labels).astype(jnp.float32)
        running = running + weight[offset][None, :] * padded[offset:offset + count_of_rows] * same_doc[:, None]
    return jax.nn.silu(running)

def ssd_block(carried, inputs):
    values_in, key_mat, read_mat, step_size, log_decay, segment_labels, before = inputs
    cum_decay = jnp.cumsum(log_decay, axis=0)
    indices = jnp.arange(segment_labels.shape[0])
    allowed = (indices[:, None] >= indices[None, :]) & (segment_labels[:, None] == segment_labels[None, :])
    mask_cube = allowed[:, :, None]
    log_gap = cum_decay[:, None, :] - cum_decay[None, :, :]
    decays = jnp.where(mask_cube, jnp.exp(jnp.where(mask_cube, log_gap, 0.0)), 0.0)
    affinity = jnp.dot(read_mat, key_mat.T, precision=highest)
    mixing = decays * affinity[:, :, None] * step_size[None, :, :]
    within = jnp.einsum('tsh,shp->thp', mixing, values_in, precision=highest)
    entry_decay = jnp.exp(cum_decay) * (segment_labels == before).astype(jnp.float32)[:, None]
    from_state = jnp.einsum('tn,hpn->thp', read_mat, carried, precision=highest) * entry_decay[:, :, None]
    keep_mask = (segment_labels == segment_labels[-1]).astype(jnp.float32)
    tail_weight = jnp.exp(cum_decay[-1][None, :] - cum_decay) * keep_mask[:, None] * step_size
    fresh_state = jnp.einsum('sh,shp,sn->hpn', tail_weight, values_in, key_mat, precision=highest)
    passing = jnp.exp(cum_decay[-1]) * (segment_labels[-1] == before).astype(jnp.float32)
    return (passing[:, None, None] * carried + fresh_state, within + from_state)

def attention_fn(query_matrix, gathered_keys, gathered_values, segment_labels):
    sequence_length = segment_labels.shape[0]
    block_count = sequence_length // KEYS_PER_BLOCK
    score_scale = HEAD_WIDTH ** (-0.5)
    key_positions = jnp.arange(sequence_length, dtype=jnp.int32)

    def one_block(packed):
        query_rows, beginning_row = packed
        query_seg = lax.dynamic_slice_in_dim(segment_labels, beginning_row, KEYS_PER_BLOCK, 0)
        query_pos = beginning_row + jnp.arange(KEYS_PER_BLOCK, dtype=jnp.int32)
        scores = low_back(jnp.einsum('ikgd,jkd->kgij', query_rows, gathered_keys, precision=highest) * score_scale)
        allowed = (key_positions[None, :] <= query_pos[:, None]) & (query_seg[:, None] == segment_labels[None, :])
        masked = jnp.where(allowed, scores, -1e+30)
        row_top = lax.optimization_barrier(jnp.max(masked, axis=-1, keepdims=True))
        row_total = lax.optimization_barrier(jnp.sum(jnp.where(allowed, jnp.exp(masked - row_top), 0.0), axis=-1, keepdims=True))
        log_total = row_top + jnp.log(row_total)
        attn_weights = lower_bound(jnp.where(allowed, jnp.exp(masked - log_total), 0.0))
        return jnp.einsum('kgij,jkd->ikgd', attn_weights, gathered_values, precision=highest)
    shaped = query_matrix.reshape((block_count, KEYS_PER_BLOCK) + query_matrix.shape[1:])
    starts = jnp.arange(block_count, dtype=jnp.int32) * KEYS_PER_BLOCK
    outputs = lax.map(jax.checkpoint(one_block), (shaped, starts))
    return outputs.reshape(query_matrix.shape)

def layer(token_rows, segment_labels, params):
    norm_gain, ffn_gain, mixer_gain, conv_weight, conv_bias, decay_log, step_bias, skip_gain, in_proj, mixer_out, qkv_proj, attn_proj, gate_up, down_proj = params
    sequence_length = token_rows.shape[0]
    normed = lower_bound(rms_scale(token_rows, norm_gain))
    mixed = low_back(matmul(normed, lower_bound(in_proj)))
    gate_z = mixed[:, :DI]
    conv_rows = lower_bound(mixed[:, DI:DI + CW])
    step_raw = mixed[:, DI + CW:]
    edge_segments = jnp.full((KC - 1,), -1, jnp.int32)
    activated = lower_bound(conv_apply(conv_rows, jnp.zeros((KC - 1, CW), jnp.float32), conv_weight, conv_bias, segment_labels, edge_segments))
    values_in = activated[:, :DI].reshape(sequence_length, MH, MP)
    key_mat = activated[:, DI:DI + NS]
    read_mat = activated[:, DI + NS:]
    step_size = jax.nn.softplus(step_raw + step_bias)
    log_decay = -step_size * jnp.exp(decay_log)
    block_count = sequence_length // SUB
    befores = jnp.concatenate([jnp.full((1,), -1, jnp.int32), segment_labels[:-1]])[::SUB]
    start_state = jnp.zeros((MH, MP, NS), jnp.float32)
    ignored, outputs = lax.scan(jax.checkpoint(ssd_block), start_state, (values_in.reshape(block_count, SUB, MH, MP), key_mat.reshape(block_count, SUB, NS), read_mat.reshape(block_count, SUB, NS), step_size.reshape(block_count, SUB, MH), log_decay.reshape(block_count, SUB, MH), segment_labels.reshape(block_count, SUB), befores))
    mixer_y = outputs.reshape(sequence_length, MH, MP) + skip_gain[None, :, None] * values_in
    gated = lower_bound(low_back(rms_scale(mixer_y.reshape(sequence_length, DI) * jax.nn.silu(gate_z), mixer_gain)))
    mamba_out = matmul(gated, lower_bound(mixer_out))
    query_key_value = low_back(matmul(normed, lower_bound(qkv_proj)))
    token_positions = jnp.arange(sequence_length, dtype=jnp.int32)
    query_matrix = lower_bound(apply_rotation(query_key_value[:, :QUERY_HEADS * HEAD_WIDTH].reshape(sequence_length, QUERY_HEADS, HEAD_WIDTH), token_positions))
    gathered_keys = lower_bound(apply_rotation(query_key_value[:, QUERY_HEADS * HEAD_WIDTH:(QUERY_HEADS + KEY_VALUE_HEADS) * HEAD_WIDTH].reshape(sequence_length, KEY_VALUE_HEADS, HEAD_WIDTH), token_positions))
    gathered_values = lower_bound(query_key_value[:, (QUERY_HEADS + KEY_VALUE_HEADS) * HEAD_WIDTH:].reshape(sequence_length, KEY_VALUE_HEADS, HEAD_WIDTH))
    attended_rows = attention_fn(query_matrix.reshape(sequence_length, KEY_VALUE_HEADS, QUERY_HEADS // KEY_VALUE_HEADS, HEAD_WIDTH), gathered_keys, gathered_values, segment_labels)
    attended_rows = lower_bound(low_back(attended_rows.reshape(sequence_length, QUERY_HEADS * HEAD_WIDTH)))
    attn_out = matmul(attended_rows, lower_bound(attn_proj))
    hidden = token_rows + low_back(attn_out + mamba_out)
    ffn_in = lower_bound(rms_scale(hidden, ffn_gain))
    gates = low_back(matmul(ffn_in, lower_bound(gate_up)))
    act = lower_bound(jax.nn.silu(gates[:, :FF]) * gates[:, FF:])
    return hidden + matmul(act, lower_bound(down_proj))

def reference(tokens, cotangent, segment_ids, norm_gain, ffn_gain, mixer_gain, conv_weight, conv_bias, decay_log, step_bias, skip_gain, in_proj, mixer_out, qkv_proj, attn_proj, gate_up, down_proj):
    params = (norm_gain, ffn_gain, mixer_gain, conv_weight, conv_bias, decay_log, step_bias, skip_gain, in_proj, mixer_out, qkv_proj, attn_proj, gate_up, down_proj)

    def one_sequence(totals, inputs):
        token_rows, back_rows, segment_labels = inputs

        def forward(values, weights):
            return layer(values, segment_labels, weights)
        result, pullback = jax.vjp(forward, token_rows.astype(jnp.float32), params)
        row_grad, weight_grads = pullback(back_rows.astype(jnp.float32))
        totals = jax.tree.map(lambda first_sum, second_sum: first_sum + second_sum, totals, weight_grads)
        return (totals, (result.astype(jnp.bfloat16), row_grad))
    zero_filled = jax.tree.map(jnp.zeros_like, params)
    totals, (outputs, grads) = lax.scan(one_sequence, zero_filled, (tokens, cotangent, segment_ids))
    return (outputs, grads, totals[0], totals[1], totals[2], totals[3], totals[4], totals[5], totals[6], totals[7], totals[8], totals[9], totals[10], totals[11], totals[12], totals[13])
```

```python
import jax
import jax.numpy as jnp
from jax import lax
from jax.experimental import pallas as pl
from jax.experimental.pallas import tpu as pltpu
from jax.sharding import PartitionSpec as P

FF = 2048
QUERY_HEADS = 8
KEY_VALUE_HEADS = 2
HEAD_WIDTH = 64
MH = 24
MP = 64
NS = 128
KC = 4
SUB = 128
DI = 1536
CW = 1792
EDGE = 8

epsilon = 1e-05
rope_base = 100000000000.0
highest = lax.Precision.HIGHEST
f32 = jnp.float32
bf16 = jnp.bfloat16


def dot_nn(left, right):
    return jnp.dot(left, right, preferred_element_type=jnp.float32)


def dot_nt(left, right):
    return lax.dot_general(
        left, right, (((1,), (1,)), ((), ())), preferred_element_type=jnp.float32
    )


def dot_tn(left, right):
    return lax.dot_general(
        left, right, (((0,), (0,)), ((), ())), preferred_element_type=jnp.float32
    )


def exact(left, right):
    return jnp.dot(left, right, precision=highest, preferred_element_type=jnp.float32)


def low(values):
    return values.astype(jnp.bfloat16)


def split(values):
    top = low(values)
    return top, low(values - top.astype(jnp.float32))


def iota(shape, axis):
    return lax.broadcasted_iota(jnp.int32, shape, axis)


def spreader():
    return low(jnp.where(iota((128, DI), 1) // MP == iota((128, DI), 0), 1.0, 0.0))


def widen(values, spread):
    top, rest = split(values)
    return dot_nn(top, spread) + dot_nn(rest, spread)


def widen_row(row, spread):
    return widen(jnp.broadcast_to(row, (8, 128)), spread)[0:1]


def head_sums(values, spread):
    top, rest = split(values)
    return dot_nt(top, spread) + dot_nt(rest, spread)


def softplus(values):
    return jnp.maximum(values, 0.0) + jnp.log1p(jnp.exp(-jnp.abs(values)))


def sigmoid(values):
    return 1.0 / (1.0 + jnp.exp(-values))


def lane_halves(rows):
    lane = iota((rows, 128), 1)
    return lane < MP


def rounded_to(values):
    return low(values).astype(jnp.float32)


def front_kernel(conv_ref, seg_ref, raw_ref, bias_ref, rate_ref, weight_ref, cbias_ref,
                 act_ref, dt_ref, cum_ref, end_ref, pass_ref):
    chunks = raw_ref.shape[0] // SUB

    def tile(j, carry):
        col = pl.ds(pl.multiple_of(j * 128, 128), 128)
        for c in range(chunks):
            r0 = c * SUB
            seg = seg_ref[pl.ds(r0 + 8, SUB), :]
            total = jnp.broadcast_to(cbias_ref[0:1, col], (SUB, 128))
            for k in range(KC):
                x = rounded_to(conv_ref[pl.ds(r0 + 9 - KC + k, SUB), col])
                if k < KC - 1:
                    x = jnp.where(seg_ref[pl.ds(r0 + 9 - KC + k, SUB), :] == seg, x, 0.0)
                total = total + weight_ref[k : k + 1, col] * x
            act_ref[pl.ds(r0, SUB), col] = low(total * sigmoid(total))
        return carry

    lax.fori_loop(0, CW // 128, tile, 0)
    spread = spreader()
    lower = jnp.where(iota((SUB, SUB), 0) >= iota((SUB, SUB), 1), 1.0, 0.0)
    end_ref[...] = jnp.zeros_like(end_ref)
    gain = jnp.ones((1, 128), jnp.float32)
    for c in range(chunks):
        rows = pl.ds(c * SUB, SUB)
        dt = softplus(raw_ref[rows, :] + bias_ref[...])
        cum = exact(lower, -dt * jnp.exp(rate_ref[...]))
        dt_ref[rows, :] = dt
        cum_ref[rows, :] = cum
        seg = seg_ref[pl.ds(c * SUB + 8, SUB), :]
        before = seg_ref[pl.ds(c * SUB + 7, 1), :]
        last = seg[SUB - 1 :, :]
        end = cum[SUB - 1 :, :]
        weight = jnp.where(seg == last, jnp.exp(end - cum), 0.0) * dt
        passing = jnp.where(last == before, jnp.exp(end), 0.0)
        gain = gain * passing
        values = act_ref[rows, 0:DI].astype(jnp.float32)
        fresh = dot_tn(act_ref[rows, DI : DI + NS], low(widen(weight, spread) * values))
        end_ref[...] = widen_row(passing, spread) * end_ref[...] + fresh
    pass_ref[...] = widen_row(gain, spread)


def mid_kernel(act_ref, dt_ref, cum_ref, seg_ref, segrow_ref, state_ref, z_ref, gain_ref, skip_ref,
               y_ref, gated_ref, kept_ref, carry_ref):
    chunks = act_ref.shape[0] // SUB
    spread = spreader()
    carry_ref[...] = state_ref[...]
    half = lane_halves(SUB)

    def chunk(c, nothing):
        r0 = pl.multiple_of(c * SUB, SUB)
        rows = pl.ds(r0, SUB)
        dt, cum = dt_ref[rows, :], cum_ref[rows, :]
        cum_t = cum.T
        seg = seg_ref[pl.ds(pl.multiple_of(r0 + 8, 8), SUB), :]
        before = seg_ref[pl.ds(pl.multiple_of(r0, 8), 8), :][7:8]
        last, end = seg[SUB - 1 :, :], cum[SUB - 1 :, :]
        keys, reads = act_ref[rows, DI : DI + NS], act_ref[rows, DI + NS : CW]
        affinity = dot_nt(reads, keys)
        allowed = (iota((SUB, SUB), 0) >= iota((SUB, SUB), 1)) & (seg == segrow_ref[0:1, rows])
        state = low(carry_ref[...])
        kept_ref[pl.ds(c, 1)] = state[None]
        entry = widen(jnp.where(seg == before, jnp.exp(cum), 0.0), spread)
        y_ref[rows, :] = dot_nn(reads, state) * entry
        values = act_ref[rows, 0:DI].astype(jnp.float32)
        scaled = values * widen(dt, spread)
        weight = jnp.where(seg == last, jnp.exp(end - cum), 0.0)
        passing = jnp.where(last == before, jnp.exp(end), 0.0)
        fresh = dot_tn(keys, low(widen(weight, spread) * scaled))
        carry_ref[...] = widen_row(passing, spread) * carry_ref[...] + fresh
        for pair in range(MH // 2):
            cols = slice(pair * 128, pair * 128 + 128)
            parts = []
            for h in (2 * pair, 2 * pair + 1):
                gap = jnp.where(allowed, cum[:, h : h + 1] - cum_t[h : h + 1, :], -1e30)
                parts.append(low(jnp.exp(gap) * affinity))
            v = scaled[:, cols]
            right = jnp.concatenate([low(jnp.where(half, v, 0.0)), low(jnp.where(half, 0.0, v))], 0)
            y_ref[rows, cols] = y_ref[rows, cols] + dot_nn(jnp.concatenate(parts, 1), right)
        z = z_ref[rows, :]
        g = (y_ref[rows, :] + skip_ref[...] * values) * (z * sigmoid(z))
        scale = lax.rsqrt(jnp.mean(g * g, axis=1, keepdims=True) + epsilon)
        gated_ref[rows, :] = low(g * scale * gain_ref[...])
        return nothing

    lax.fori_loop(0, chunks, chunk, 0)


def gate_back_kernel(grad_ref, y_ref, act_ref, z_ref, dt_ref, cum_ref, seg_ref, gain_ref, skip_ref,
                     ygrad_ref, zgrad_ref, gain_grad_ref, state_grad_ref):
    chunks = act_ref.shape[0] // SUB
    spread = spreader()
    gain_grad_ref[...] = jnp.zeros_like(gain_grad_ref)
    state_grad_ref[...] = jnp.zeros_like(state_grad_ref)

    def chunk(i, nothing):
        c = chunks - 1 - i
        r0 = pl.multiple_of(c * SUB, SUB)
        rows = pl.ds(r0, SUB)
        values = act_ref[rows, 0:DI].astype(jnp.float32)
        z = z_ref[rows, :]
        sig = sigmoid(z)
        silu = z * sig
        u = y_ref[rows, :] + skip_ref[...] * values
        g = u * silu
        grad = grad_ref[rows, :].astype(jnp.float32)
        scale = lax.rsqrt(jnp.mean(g * g, axis=1, keepdims=True) + epsilon)
        unit = g * scale
        gain_grad_ref[...] += jnp.sum(grad * unit, axis=0, keepdims=True)
        h = grad * gain_ref[...]
        dg = scale * (h - unit * jnp.mean(h * unit, axis=1, keepdims=True))
        dy = dg * silu
        ygrad_ref[rows, :] = dy
        zgrad_ref[rows, :] = low(dg * u * (sig * (1.0 + z * (1.0 - sig))))
        cum = cum_ref[rows, :]
        seg = seg_ref[pl.ds(pl.multiple_of(r0 + 8, 8), SUB), :]
        before = seg_ref[pl.ds(pl.multiple_of(r0, 8), 8), :][7:8]
        last, end = seg[SUB - 1 :, :], cum[SUB - 1 :, :]
        entry = widen(jnp.where(seg == before, jnp.exp(cum), 0.0), spread)
        passing = jnp.where(last == before, jnp.exp(end), 0.0)
        fresh = dot_tn(act_ref[rows, DI + NS : CW], low(entry * dy))
        state_grad_ref[...] = widen_row(passing, spread) * state_grad_ref[...] + fresh
        return nothing

    lax.fori_loop(0, chunks, chunk, 0)


def back_kernel(act_ref, dt_ref, cum_ref, seg_ref, segrow_ref, raw_ref, bias_ref, rate_ref, kept_ref,
                y_ref, ygrad_ref, later_ref, conv_ref, weight_ref, cbias_ref, skip_ref,
                raw_grad_ref, conv_grad_ref, weight_grad_ref, cbias_grad_ref, rate_grad_ref,
                bias_grad_ref, skip_grad_ref, act_grad_ref, carry_ref, pre_ref):
    rows_total = act_ref.shape[0]
    chunks = rows_total // SUB
    spread = spreader()
    half = lane_halves(SUB)
    upper = jnp.where(iota((SUB, SUB), 1) >= iota((SUB, SUB), 0), 1.0, 0.0)
    rate = jnp.exp(rate_ref[...])
    carry_ref[...] = later_ref[...]
    rate_grad_ref[...] = jnp.zeros_like(rate_grad_ref)
    bias_grad_ref[...] = jnp.zeros_like(bias_grad_ref)
    skip_grad_ref[...] = jnp.zeros_like(skip_grad_ref)

    def chunk(i, nothing):
        c = chunks - 1 - i
        r0 = pl.multiple_of(c * SUB, SUB)
        rows = pl.ds(r0, SUB)
        dt, cum = dt_ref[rows, :], cum_ref[rows, :]
        cum_t = cum.T
        seg = seg_ref[pl.ds(pl.multiple_of(r0 + 8, 8), SUB), :]
        before = seg_ref[pl.ds(pl.multiple_of(r0, 8), 8), :][7:8]
        last, end = seg[SUB - 1 :, :], cum[SUB - 1 :, :]
        keys, reads = act_ref[rows, DI : DI + NS], act_ref[rows, DI + NS : CW]
        affinity = dot_nt(keys, reads)
        allowed = (iota((SUB, SUB), 1) >= iota((SUB, SUB), 0)) & (seg == segrow_ref[0:1, rows])
        values = act_ref[rows, 0:DI].astype(jnp.float32)
        wide_dt = widen(dt, spread)
        scaled = values * wide_dt
        scaled_low = low(scaled)
        dy = ygrad_ref[rows, :]
        dy_low = low(dy)
        state, carry = kept_ref[pl.ds(c, 1)][0], carry_ref[...]
        carry_low = low(carry)
        wide_weight = widen(jnp.where(seg == last, jnp.exp(end - cum), 0.0), spread)
        wide_entry = widen(jnp.where(seg == before, jnp.exp(cum), 0.0), spread)
        wide_pass = widen_row(jnp.where(last == before, jnp.exp(end), 0.0), spread)
        from_state = dot_nn(keys, carry_low) * wide_weight
        mixed_grad = jnp.zeros((SUB, SUB), jnp.float32)
        for pair in range(MH // 2):
            cols = slice(pair * 128, pair * 128 + 128)
            v, d = scaled[:, cols], dy[:, cols]
            left = jnp.concatenate([low(jnp.where(half, v, 0.0)), low(jnp.where(half, 0.0, v))], 0)
            right = jnp.concatenate([low(jnp.where(half, d, 0.0)), low(jnp.where(half, 0.0, d))], 0)
            weight_grad = dot_nt(left, dy_low[:, cols])
            parts = []
            for n, h in enumerate((2 * pair, 2 * pair + 1)):
                gap = jnp.where(allowed, cum_t[h : h + 1, :] - cum[:, h : h + 1], -1e30)
                decay = jnp.exp(gap)
                parts.append(low(decay * affinity))
                mixed_grad = mixed_grad + decay * weight_grad[n * SUB : (n + 1) * SUB]
            act_grad_ref[rows, cols] = dot_nn(jnp.concatenate(parts, 1), right)
        x = act_grad_ref[rows, 0:DI] + from_state
        act_grad_ref[rows, 0:DI] = wide_dt * x + skip_ref[...] * dy
        mixed_low = low(mixed_grad)
        act_grad_ref[rows, DI : DI + NS] = dot_nn(mixed_low, reads) + dot_nt(
            low(wide_weight * scaled), carry_low
        )
        entered = low(wide_entry * dy)
        act_grad_ref[rows, DI + NS : CW] = dot_tn(mixed_low, keys) + dot_nt(entered, state)
        scaled_exact = scaled_low.astype(jnp.float32)
        direct = head_sums(values * x, spread)
        given = head_sums(scaled_exact * x, spread)
        taken = head_sums(dy_low.astype(jnp.float32) * y_ref[rows, :], spread)
        tail = jnp.sum(scaled_exact * from_state, axis=0, keepdims=True) + jnp.sum(
            wide_pass * carry * state.astype(jnp.float32), axis=0, keepdims=True
        )
        tail = head_sums(jnp.broadcast_to(tail, (8, DI)), spread)[0:1]
        decay_grad = exact(upper, taken - given) + tail
        rate_grad_ref[...] += jnp.sum(decay_grad * (-dt * rate), axis=0, keepdims=True)
        dt_grad = direct - decay_grad * rate
        raw_grad = dt_grad * sigmoid(raw_ref[rows, :] + bias_ref[...])
        raw_grad_ref[rows, :] = raw_grad
        bias_grad_ref[...] += jnp.sum(raw_grad, axis=0, keepdims=True)
        skip_sum = jnp.sum(dy * values, axis=0, keepdims=True)
        skip_grad_ref[...] += head_sums(jnp.broadcast_to(skip_sum, (8, DI)), spread)[0:1]
        carry_ref[...] = wide_pass * carry + dot_tn(reads, entered)
        return nothing

    lax.fori_loop(0, chunks, chunk, 0)
    weight_grad_ref[...] = jnp.zeros_like(weight_grad_ref)
    pre_ref[0:8, :] = jnp.zeros((8, 128), jnp.float32)
    pre_ref[rows_total + 8 : rows_total + 16, :] = jnp.zeros((8, 128), jnp.float32)

    def tile(j, carry):
        col = pl.ds(pl.multiple_of(j * 128, 128), 128)
        sums = [jnp.zeros((1, 128), jnp.float32) for _ in range(KC + 1)]
        for c in range(chunks):
            r0 = c * SUB
            seg = seg_ref[pl.ds(r0 + 8, SUB), :]
            total = jnp.broadcast_to(cbias_ref[0:1, col], (SUB, 128))
            taps = []
            for k in range(KC):
                x = rounded_to(conv_ref[pl.ds(r0 + 9 - KC + k, SUB), col])
                if k < KC - 1:
                    x = jnp.where(seg_ref[pl.ds(r0 + 9 - KC + k, SUB), :] == seg, x, 0.0)
                taps.append(x)
                total = total + weight_ref[k : k + 1, col] * x
            sig = sigmoid(total)
            pre = act_grad_ref[pl.ds(r0, SUB), col] * (sig * (1.0 + total * (1.0 - sig)))
            pre_ref[pl.ds(r0 + 8, SUB), :] = pre
            for k in range(KC):
                sums[k] = sums[k] + jnp.sum(pre * taps[k], axis=0, keepdims=True)
            sums[KC] = sums[KC] + jnp.sum(pre, axis=0, keepdims=True)
        for k in range(KC):
            weight_grad_ref[k : k + 1, col] = sums[k]
        cbias_grad_ref[0:1, col] = sums[KC]
        for c in range(chunks + 1):
            r0 = c * SUB
            size = SUB if c < chunks else 8
            seg = seg_ref[pl.ds(r0, size), :]
            total = jnp.zeros((size, 128), jnp.float32)
            for back in range(KC):
                x = pre_ref[pl.ds(r0 + back, size), :]
                if back:
                    x = jnp.where(seg_ref[pl.ds(r0 + back, size), :] == seg, x, 0.0)
                total = total + weight_ref[KC - 1 - back : KC - back, col] * x
            conv_grad_ref[pl.ds(r0, size), col] = total
        return carry

    lax.fori_loop(0, CW // 128, tile, 0)


def partner(values):
    lane = iota(values.shape, 1)
    half = HEAD_WIDTH // 2
    return jnp.where(
        lane % HEAD_WIDTH < half, pltpu.roll(values, 128 - half, 1), pltpu.roll(values, half, 1)
    )


def rotate_kernel(qkv_ref, cos_ref, sin_ref, query_ref, kv_ref):
    cos, sin = cos_ref[...], sin_ref[...]
    for g in range(5):
        x = qkv_ref[:, g * 128 : g * 128 + 128]
        x = low(x * cos + partner(x) * sin)
        if g < 4:
            query_ref[:, g * 128 : g * 128 + 128] = x * jnp.bfloat16(HEAD_WIDTH**-0.5)
        else:
            kv_ref[:, 0:128] = x
    kv_ref[:, 128:256] = low(qkv_ref[:, 640:768])


def lane_variants(block, out_ref):
    other = pltpu.roll(block, 64, 1)
    half = iota(block.shape, 1) < HEAD_WIDTH
    out_ref[0] = low(jnp.where(half, block, 0.0))
    out_ref[1] = low(jnp.where(half, 0.0, other))
    out_ref[2] = low(jnp.where(half, other, 0.0))
    out_ref[3] = low(jnp.where(half, 0.0, block))


def attend_bias(b, own, rows, segcol_ref, segrow_ref, bias_ref):
    seg = segcol_ref[pl.ds(pl.multiple_of(b * rows, rows), rows), :]
    seg = jnp.concatenate([seg] * (rows // 128), 1)
    causal = (iota((rows, rows), 0) - iota((rows, rows), 1)) <= jnp.where(b < own, rows, 0)
    bias_ref[...] = jnp.where(causal & (seg == segrow_ref[...]), 0.0, -1e30)


def attend_kernel(own_ref, query_ref, kv_ref, segcol_ref, segrow_ref, out_ref, out_t_ref, total_ref,
                  bias_ref, keys_ref, top_ref, sum_ref):
    rows = query_ref.shape[0]
    own = own_ref[0]
    top_ref[...] = jnp.full_like(top_ref, -1e30)
    sum_ref[...] = jnp.zeros_like(sum_ref)
    out_t_ref[...] = jnp.zeros_like(out_t_ref)

    def block(i, nothing):
        b = own - i
        at = pl.ds(pl.multiple_of(b * rows, rows), rows)
        attend_bias(b, own, rows, segcol_ref, segrow_ref, bias_ref)
        lane_variants(kv_ref[at, 0:128].astype(jnp.float32), keys_ref)
        values_t = low(kv_ref[at, 128:256].astype(jnp.float32).T)
        for h in range(QUERY_HEADS):
            g, kv = h // 2, h // 4
            scores = dot_nt(keys_ref[kv * 2 + h % 2], query_ref[:, g * 128 : g * 128 + 128])
            scores = scores + bias_ref[...]
            old = top_ref[h : h + 1, :]
            top = jnp.maximum(old, jnp.max(scores, axis=0, keepdims=True))
            p = jnp.exp(scores - top)
            fade = jnp.exp(old - top)
            top_ref[h : h + 1, :] = top
            sum_ref[h : h + 1, :] = sum_ref[h : h + 1, :] * fade + jnp.sum(p, 0, keepdims=True)
            at_h = slice(h * 64, h * 64 + 64)
            out_t_ref[at_h, :] = out_t_ref[at_h, :] * fade + dot_nn(
                values_t[kv * 64 : kv * 64 + 64, :], low(p)
            )
        return nothing

    lax.fori_loop(0, own + 1, block, 0)
    total_ref[...] = top_ref[...] + jnp.log(sum_ref[...])
    for h in range(QUERY_HEADS):
        at_h = slice(h * 64, h * 64 + 64)
        out_t_ref[at_h, :] = out_t_ref[at_h, :] / sum_ref[h : h + 1, :]
    out_ref[...] = low(out_t_ref[...].T)


def attend_back_kernel(own_ref, query_ref, kv_ref, segcol_ref, segrow_ref, grad_ref, out_t_ref,
                       total_ref, cos_ref, sin_ref, query_grad_ref, kv_grad_ref,
                       bias_ref, keys_ref, values_ref, dkeys_ref, dvalues_ref, spread_ref, dq_ref,
                       query_half_ref, grad_half_ref):
    rows = query_ref.shape[0]
    own = own_ref[0]
    kv_grad_ref[...] = jnp.zeros_like(kv_grad_ref)
    dq_ref[...] = jnp.zeros_like(dq_ref)
    grad_t = grad_ref[...].astype(jnp.float32).T
    product = grad_t * out_t_ref[...]
    for h in range(QUERY_HEADS):
        spread_ref[h : h + 1, :] = jnp.sum(product[h * 64 : h * 64 + 64, :], 0, keepdims=True)
        g = h // 2
        half = (iota((rows, 128), 1) < HEAD_WIDTH) == (h % 2 == 0)
        for src, dst in ((query_ref, query_half_ref), (grad_ref, grad_half_ref)):
            dst[h] = low(jnp.where(half, src[:, g * 128 : g * 128 + 128].astype(jnp.float32), 0.0))

    def block(b, nothing):
        at = pl.ds(pl.multiple_of(b * rows, rows), rows)
        attend_bias(b, own, rows, segcol_ref, segrow_ref, bias_ref)
        keys = kv_ref[at, 0:128].astype(jnp.float32)
        lane_variants(keys, keys_ref)
        lane_variants(kv_ref[at, 128:256].astype(jnp.float32), values_ref)
        keys_t = low(keys.T)
        dkeys_ref[...] = jnp.zeros_like(dkeys_ref)
        dvalues_ref[...] = jnp.zeros_like(dvalues_ref)
        for h in range(QUERY_HEADS):
            g, kv = h // 2, h // 4
            lanes = slice(g * 128, g * 128 + 128)
            scores = dot_nt(keys_ref[kv * 2 + h % 2], query_ref[:, lanes]) + bias_ref[...]
            p = jnp.exp(scores - total_ref[h : h + 1, :])
            dp = dot_nt(values_ref[kv * 2 + h % 2], grad_ref[:, lanes])
            ds = low(p * (dp - spread_ref[h : h + 1, :]))
            dkeys_ref[kv] += dot_nn(ds, query_half_ref[h])
            dvalues_ref[kv] += dot_nn(low(p), grad_half_ref[h])
            dq_ref[h * 64 : h * 64 + 64, :] += dot_nn(keys_t[kv * 64 : kv * 64 + 64, :], ds)
        half = iota((rows, 128), 1) < HEAD_WIDTH
        for src, lanes in ((dkeys_ref, slice(0, 128)), (dvalues_ref, slice(128, 256))):
            first, second = src[0], src[1]
            kv_grad_ref[at, lanes] = low(
                jnp.where(half, first + pltpu.roll(first, 64, 1), second + pltpu.roll(second, 64, 1))
            )
        return nothing

    lax.fori_loop(0, own + 1, block, 0)
    dq = dq_ref[...].T * (HEAD_WIDTH**-0.5)
    cos, sin = cos_ref[...], sin_ref[...]
    for g in range(4):
        x = dq[:, g * 128 : g * 128 + 128]
        query_grad_ref[:, g * 128 : g * 128 + 128] = low(x * cos + partner(x * sin))


vmem = pl.BlockSpec(memory_space=pltpu.VMEM)
smem = pl.BlockSpec(memory_space=pltpu.SMEM)


def call(kernel, outs, args, scratch=(), first=vmem, flops=10**9):
    return pl.pallas_call(
        kernel,
        out_shape=[jax.ShapeDtypeStruct(shape, kind) for shape, kind in outs],
        in_specs=[first] + [vmem] * (len(args) - 1),
        out_specs=[vmem] * len(outs),
        scratch_shapes=[pltpu.VMEM(shape, kind) for shape, kind in scratch],
        compiler_params=pltpu.CompilerParams(vmem_limit_bytes=56 * 2**20),
        cost_estimate=pl.CostEstimate(flops=flops, bytes_accessed=10**7, transcendentals=10**6),
    )(*args)


def shifted(array, axis, by):
    devices = lax.axis_size(axis)
    pairs = [(i, i + by) for i in range(devices) if 0 <= i + by < devices]
    return lax.ppermute(array, axis, pairs)


def contract(left, right):
    return dot_tn(left, right)


def rms_scale(values, gain_vec):
    return (
        values * lax.rsqrt(jnp.mean(values * values, axis=-1, keepdims=True) + epsilon) * gain_vec
    )


def gathered(shard):
    return lax.all_gather(low(shard), "fsdp", axis=0, tiled=True)


def reduced(gradient):
    piece = lax.psum_scatter(low(gradient), "fsdp", scatter_dimension=0, tiled=True)
    return piece


def padded(vector):
    return jnp.pad(vector, (0, 128 - vector.shape[0]))[None]


def on_device(
    tokens,
    cotangent,
    segment_ids,
    norm_gain,
    ffn_gain,
    mixer_gain,
    conv_weight,
    conv_bias,
    decay_log,
    step_bias,
    skip_gain,
    in_proj,
    mixer_out,
    qkv_proj,
    attn_proj,
    gate_up,
    down_proj,
):
    place, devices = lax.axis_index("seq"), lax.axis_size("seq")
    count = tokens.shape[1]
    seg_all = lax.all_gather(segment_ids[0], "seq", axis=0, tiled=True).astype(f32)
    edge_tokens = shifted(tokens[0, count - EDGE :], "seq", 1)
    qkv_full = gathered(qkv_proj)
    in_full = gathered(in_proj)
    mix_full = gathered(mixer_out)
    attn_full = gathered(attn_proj)
    gate_full = gathered(gate_up)
    down_full = gathered(down_proj)

    seg_padded = jnp.pad(seg_all, (EDGE, EDGE), constant_values=-1.0)
    seg_ext = lax.dynamic_slice_in_dim(seg_padded, place * count, count + 2 * EDGE, 0)
    seg_wide = jnp.broadcast_to(seg_ext[:, None], (count + 2 * EDGE, 128))
    seg_row = segment_ids.astype(f32)
    seg_col = jnp.broadcast_to(seg_all[:, None], (seg_all.shape[0], 128))
    own = place.astype(jnp.int32)[None]

    position = place * count + jnp.arange(count, dtype=jnp.int32)
    half = HEAD_WIDTH // 2
    lane = jnp.arange(128, dtype=jnp.int32)
    exponent = (lane % half).astype(f32) * (2.0 / HEAD_WIDTH)
    frequencies = jnp.power(rope_base, -exponent)
    angles = position.astype(f32)[:, None] * frequencies[None, :]
    cosine = jnp.cos(angles)
    signed = jnp.sin(angles) * jnp.where(lane % HEAD_WIDTH < half, -1.0, 1.0)[None]

    token_rows = tokens[0].astype(f32)
    normed32, norm_pull = jax.vjp(rms_scale, token_rows, norm_gain)
    normed = low(normed32)
    normed_edge = low(rms_scale(edge_tokens.astype(f32), norm_gain))
    normed_ext = jnp.concatenate([normed_edge, normed], axis=0)

    qkv = dot_nn(normed, qkv_full)
    query, kv = call(
        rotate_kernel,
        [((count, 512), bf16), ((count, 256), bf16)],
        (qkv, cosine, signed),
    )
    kv_all = lax.all_gather(kv, "seq", axis=0, tiled=True)
    length = kv_all.shape[0]

    step_weights = jnp.pad(in_full[:, DI + CW :], ((0, 0), (0, 128 - MH)))
    conv_ext = dot_nn(normed_ext, in_full[:, DI : DI + CW])
    step_raw = dot_nn(normed, step_weights)
    gate_z = dot_nn(normed, in_full[:, :DI])
    bias_row, rate_row = padded(step_bias), padded(decay_log)
    act, dt, cum, end_state, passing = call(
        front_kernel,
        [
            ((count, CW), bf16),
            ((count, 128), f32),
            ((count, 128), f32),
            ((NS, DI), f32),
            ((1, DI), f32),
        ],
        (conv_ext, seg_wide, step_raw, bias_row, rate_row, conv_weight, conv_bias[None]),
    )
    pass_top, pass_rest = split(passing)
    states = lax.all_gather(
        jnp.concatenate([low(end_state), pass_top, pass_rest, jnp.zeros((14, DI), bf16)], 0), "seq"
    ).astype(f32)
    passings = states[:, NS : NS + 1] + states[:, NS + 1 : NS + 2]
    state_in = jnp.zeros((NS, DI), f32)
    for k in range(devices):
        state_in = jnp.where(k < place, passings[k] * state_in + states[k, :NS], state_in)

    attended, attended_t, log_total = call(
        attend_kernel,
        [((count, 512), bf16), ((512, count), f32), ((QUERY_HEADS, count), f32)],
        (own, query, kv_all, seg_col, seg_row),
        (
            ((count, count), f32),
            ((4, count, 128), bf16),
            ((QUERY_HEADS, count), f32),
            ((QUERY_HEADS, count), f32),
        ),
        smem,
    )
    skip_row = jnp.repeat(skip_gain, MP)[None]
    mixer_y, gated, kept = call(
        mid_kernel,
        [((count, DI), f32), ((count, DI), bf16), ((count // SUB, NS, DI), bf16)],
        (act, dt, cum, seg_wide, seg_row, state_in, gate_z, mixer_gain[None], skip_row),
        (((NS, DI), f32),),
    )
    hidden = token_rows + (dot_nn(attended, attn_full) + dot_nn(gated, mix_full))
    ffn_in32, ffn_pull = jax.vjp(rms_scale, hidden, ffn_gain)
    ffn_in = low(ffn_in32)
    gates = dot_nn(ffn_in, gate_full)

    def swiglu(values):
        return jax.nn.silu(values[:, :FF]) * values[:, FF:]

    act32, act_pull = jax.vjp(swiglu, gates)
    inner = low(act32)
    result = hidden + dot_nn(inner, down_full)
    back_rows = cotangent[0]
    down_piece = reduced(contract(inner, back_rows))
    (gates_grad,) = act_pull(dot_nt(back_rows, down_full))
    gates_grad = low(gates_grad)
    gate_piece = reduced(contract(ffn_in, gates_grad))
    hidden_extra, ffn_gain_grad = ffn_pull(dot_nt(gates_grad, gate_full))
    hidden_grad = back_rows.astype(f32) + hidden_extra
    branch = low(hidden_grad)
    attn_piece = reduced(contract(attended, branch))
    attended_grad = low(dot_nt(branch, attn_full))
    mixer_piece = reduced(contract(gated, branch))
    gated_grad = low(dot_nt(branch, mix_full))

    y_grad, gate_z_grad, mixer_gain_grad, state_grad = call(
        gate_back_kernel,
        [((count, DI), f32), ((count, DI), bf16), ((1, DI), f32), ((NS, DI), f32)],
        (gated_grad, mixer_y, act, gate_z, dt, cum, seg_wide, mixer_gain[None], skip_row),
    )
    grads = lax.all_gather(low(state_grad), "seq").astype(f32)
    later = jnp.zeros((NS, DI), f32)
    for k in reversed(range(devices)):
        later = jnp.where(k > place, passings[k] * later + grads[k], later)

    query_grad, kv_grad = call(
        attend_back_kernel,
        [((count, 512), bf16), ((length, 256), bf16)],
        (own, query, kv_all, seg_col, seg_row, attended_grad, attended_t, log_total, cosine, signed),
        (
            ((count, count), f32),
            ((4, count, 128), bf16),
            ((4, count, 128), bf16),
            ((2, count, 128), f32),
            ((2, count, 128), f32),
            ((QUERY_HEADS, count), f32),
            ((512, count), f32),
            ((QUERY_HEADS, count, 128), bf16),
            ((QUERY_HEADS, count, 128), bf16),
        ),
        smem,
    )
    kv_own = lax.psum_scatter(kv_grad, "seq", scatter_dimension=0, tiled=True).astype(f32)

    def swap(values):
        shaped = values.reshape(count, 2, 2, half)
        return shaped[:, :, ::-1].reshape(count, 128)

    key_grad = kv_own[:, :128]
    key_grad = key_grad * cosine + swap(key_grad * signed)
    qkv_grad = jnp.concatenate([query_grad, low(key_grad), low(kv_own[:, 128:])], axis=1)
    qkv_piece = reduced(contract(normed, qkv_grad))
    normed_grad = dot_nt(qkv_grad, qkv_full)

    raw_grad, conv_grad, conv_weight_grad, conv_bias_grad, rate_grad, bias_grad, skip_grad = call(
        back_kernel,
        [
            ((count, 128), f32),
            ((count + EDGE, CW), f32),
            ((KC, CW), f32),
            ((1, CW), f32),
            ((1, 128), f32),
            ((1, 128), f32),
            ((1, 128), f32),
        ],
        (
            act, dt, cum, seg_wide, seg_row, step_raw, bias_row, rate_row, kept,
            mixer_y, y_grad, later, conv_ext, conv_weight, conv_bias[None], skip_row,
        ),
        (((count, CW), f32), ((NS, DI), f32), ((count + 2 * EDGE, 128), f32)),
    )
    edge_back = shifted(conv_grad[:EDGE], "seq", -1)
    conv_grad = conv_grad[EDGE:] + jnp.pad(edge_back, ((count - EDGE, 0), (0, 0)))
    mixed_grad = jnp.concatenate([gate_z_grad, low(conv_grad), low(raw_grad[:, :MH])], axis=1)
    in_piece = reduced(contract(normed, mixed_grad))
    normed_grad = normed_grad + dot_nt(mixed_grad, in_full)
    rows_extra, norm_gain_grad = norm_pull(normed_grad)
    input_grad = hidden_grad + rows_extra
    pieces = (in_piece, mixer_piece, qkv_piece, attn_piece, gate_piece, down_piece)
    shards = [lax.psum(piece, "seq").astype(f32) for piece in pieces]
    small = lax.psum(
        (
            norm_gain_grad,
            ffn_gain_grad,
            mixer_gain_grad[0],
            conv_weight_grad,
            conv_bias_grad[0],
            rate_grad[0, :MH],
            bias_grad[0, :MH],
            skip_grad[0, :MH],
        ),
        ("fsdp", "seq"),
    )
    return (low(result)[None], input_grad[None], *small, *shards)


def solution(mesh):
    rows, whole, split_rows = P("fsdp", "seq", None), P(), P("fsdp", None)
    return jax.shard_map(
        on_device,
        mesh=mesh,
        in_specs=(rows, rows, P("fsdp", "seq"), *[whole] * 8, *[split_rows] * 6),
        out_specs=(rows, rows, *[whole] * 8, *[split_rows] * 6),
        check_vma=False,
    )
```

```python
import jax
import jax.numpy as jnp
from jax import lax
from jax.experimental import pallas as pl
from jax.experimental.pallas import tpu as pltpu
from jax.sharding import PartitionSpec as P

FF = 2048
QUERY_HEADS = 8
KEY_VALUE_HEADS = 2
HEAD_WIDTH = 64
MH = 24
MP = 64
NS = 128
KC = 4
SUB = 128
DI = 1536
CW = 1792
EDGE = 8

epsilon = 1e-05
rope_base = 100000000000.0
highest = lax.Precision.HIGHEST
f32 = jnp.float32
bf16 = jnp.bfloat16


def dot_nn(left, right):
    return jnp.dot(left, right, preferred_element_type=jnp.float32)


def dot_nt(left, right):
    return lax.dot_general(
        left, right, (((1,), (1,)), ((), ())), preferred_element_type=jnp.float32
    )


def dot_tn(left, right):
    return lax.dot_general(
        left, right, (((0,), (0,)), ((), ())), preferred_element_type=jnp.float32
    )


def exact(left, right):
    return jnp.dot(left, right, precision=highest, preferred_element_type=jnp.float32)


def low(values):
    return values.astype(jnp.bfloat16)


def split(values):
    top = low(values)
    return top, low(values - top.astype(jnp.float32))


def iota(shape, axis):
    return lax.broadcasted_iota(jnp.int32, shape, axis)


def spreader():
    return low(jnp.where(iota((128, DI), 1) // MP == iota((128, DI), 0), 1.0, 0.0))


def widen(values, spread):
    top, rest = split(values)
    return dot_nn(top, spread) + dot_nn(rest, spread)


def widen_row(row, spread):
    return widen(jnp.broadcast_to(row, (8, 128)), spread)[0:1]


def head_sums(values, spread):
    top, rest = split(values)
    return dot_nt(top, spread) + dot_nt(rest, spread)


def softplus(values):
    return jnp.maximum(values, 0.0) + jnp.log1p(jnp.exp(-jnp.abs(values)))


def sigmoid(values):
    return 1.0 / (1.0 + jnp.exp(-values))


def lane_halves(rows):
    lane = iota((rows, 128), 1)
    return lane < MP


def rounded_to(values):
    return low(values).astype(jnp.float32)


def front_conv(conv_ref, seg_ref, weight_ref, cbias_ref, act_ref):
    chunks = act_ref.shape[0] // SUB

    def tile(j, carry):
        col = pl.ds(pl.multiple_of(j * 128, 128), 128)
        for c in range(chunks):
            r0 = c * SUB
            seg = seg_ref[pl.ds(r0 + 8, SUB), :]
            total = jnp.broadcast_to(cbias_ref[0:1, col], (SUB, 128))
            for k in range(KC):
                x = rounded_to(conv_ref[pl.ds(r0 + 9 - KC + k, SUB), col])
                if k < KC - 1:
                    x = jnp.where(seg_ref[pl.ds(r0 + 9 - KC + k, SUB), :] == seg, x, 0.0)
                total = total + weight_ref[k : k + 1, col] * x
            act_ref[pl.ds(r0, SUB), col] = low(total * sigmoid(total))
        return carry

    lax.fori_loop(0, CW // 128, tile, 0)


def front_state(seg_ref, raw_ref, bias_ref, rate_ref, act_ref, dt_ref, cum_ref, end_ref, pass_ref):
    chunks = raw_ref.shape[0] // SUB
    spread = spreader()
    lower = jnp.where(iota((SUB, SUB), 0) >= iota((SUB, SUB), 1), 1.0, 0.0)
    end_ref[...] = jnp.zeros_like(end_ref)
    gain = jnp.ones((1, 128), jnp.float32)
    for c in range(chunks):
        rows = pl.ds(c * SUB, SUB)
        dt = softplus(raw_ref[rows, :] + bias_ref[...])
        cum = exact(lower, -dt * jnp.exp(rate_ref[...]))
        dt_ref[rows, :] = dt
        cum_ref[rows, :] = cum
        seg = seg_ref[pl.ds(c * SUB + 8, SUB), :]
        before = seg_ref[pl.ds(c * SUB + 7, 1), :]
        last = seg[SUB - 1 :, :]
        end = cum[SUB - 1 :, :]
        weight = jnp.where(seg == last, jnp.exp(end - cum), 0.0) * dt
        passing = jnp.where(last == before, jnp.exp(end), 0.0)
        gain = gain * passing
        values = act_ref[rows, 0:DI].astype(jnp.float32)
        fresh = dot_tn(act_ref[rows, DI : DI + NS], low(widen(weight, spread) * values))
        end_ref[...] = widen_row(passing, spread) * end_ref[...] + fresh
    pass_ref[...] = widen_row(gain, spread)


def mid_kernel(act_ref, dt_ref, cum_ref, seg_ref, segrow_ref, state_ref, z_ref, gain_ref, skip_ref,
               y_ref, gated_ref, kept_ref, carry_ref, first, until):
    spread = spreader()
    if first == 0:
        carry_ref[...] = state_ref[...]
    half = lane_halves(SUB)

    def chunk(c, nothing):
        r0 = pl.multiple_of(c * SUB, SUB)
        rows = pl.ds(r0, SUB)
        dt, cum = dt_ref[rows, :], cum_ref[rows, :]
        cum_t = cum.T
        seg = seg_ref[pl.ds(pl.multiple_of(r0 + 8, 8), SUB), :]
        before = seg_ref[pl.ds(pl.multiple_of(r0, 8), 8), :][7:8]
        last, end = seg[SUB - 1 :, :], cum[SUB - 1 :, :]
        keys, reads = act_ref[rows, DI : DI + NS], act_ref[rows, DI + NS : CW]
        affinity = dot_nt(reads, keys)
        allowed = (iota((SUB, SUB), 0) >= iota((SUB, SUB), 1)) & (seg == segrow_ref[0:1, rows])
        state = low(carry_ref[...])
        kept_ref[pl.ds(c, 1)] = state[None]
        entry = widen(jnp.where(seg == before, jnp.exp(cum), 0.0), spread)
        y_ref[rows, :] = dot_nn(reads, state) * entry
        values = act_ref[rows, 0:DI].astype(jnp.float32)
        scaled = values * widen(dt, spread)
        weight = jnp.where(seg == last, jnp.exp(end - cum), 0.0)
        passing = jnp.where(last == before, jnp.exp(end), 0.0)
        fresh = dot_tn(keys, low(widen(weight, spread) * scaled))
        carry_ref[...] = widen_row(passing, spread) * carry_ref[...] + fresh
        for pair in range(MH // 2):
            cols = slice(pair * 128, pair * 128 + 128)
            parts = []
            for h in (2 * pair, 2 * pair + 1):
                gap = jnp.where(allowed, cum[:, h : h + 1] - cum_t[h : h + 1, :], -1e30)
                parts.append(low(jnp.exp(gap) * affinity))
            v = scaled[:, cols]
            right = jnp.concatenate([low(jnp.where(half, v, 0.0)), low(jnp.where(half, 0.0, v))], 0)
            y_ref[rows, cols] = y_ref[rows, cols] + dot_nn(jnp.concatenate(parts, 1), right)
        z = z_ref[rows, :]
        g = (y_ref[rows, :] + skip_ref[...] * values) * (z * sigmoid(z))
        scale = lax.rsqrt(jnp.mean(g * g, axis=1, keepdims=True) + epsilon)
        gated_ref[rows, :] = low(g * scale * gain_ref[...])
        return nothing

    lax.fori_loop(first, until, chunk, 0)


def gate_back_kernel(grad_ref, y_ref, act_ref, z_ref, dt_ref, cum_ref, seg_ref, gain_ref, skip_ref,
                     ygrad_ref, zgrad_ref, gain_grad_ref, state_grad_ref):
    chunks = act_ref.shape[0] // SUB
    spread = spreader()
    gain_grad_ref[...] = jnp.zeros_like(gain_grad_ref)
    state_grad_ref[...] = jnp.zeros_like(state_grad_ref)

    def chunk(i, nothing):
        c = chunks - 1 - i
        r0 = pl.multiple_of(c * SUB, SUB)
        rows = pl.ds(r0, SUB)
        values = act_ref[rows, 0:DI].astype(jnp.float32)
        z = z_ref[rows, :]
        sig = sigmoid(z)
        silu = z * sig
        u = y_ref[rows, :] + skip_ref[...] * values
        g = u * silu
        grad = grad_ref[rows, :].astype(jnp.float32)
        scale = lax.rsqrt(jnp.mean(g * g, axis=1, keepdims=True) + epsilon)
        unit = g * scale
        gain_grad_ref[...] += jnp.sum(grad * unit, axis=0, keepdims=True)
        h = grad * gain_ref[...]
        dg = scale * (h - unit * jnp.mean(h * unit, axis=1, keepdims=True))
        dy = dg * silu
        ygrad_ref[rows, :] = dy
        zgrad_ref[rows, :] = low(dg * u * (sig * (1.0 + z * (1.0 - sig))))
        cum = cum_ref[rows, :]
        seg = seg_ref[pl.ds(pl.multiple_of(r0 + 8, 8), SUB), :]
        before = seg_ref[pl.ds(pl.multiple_of(r0, 8), 8), :][7:8]
        last, end = seg[SUB - 1 :, :], cum[SUB - 1 :, :]
        entry = widen(jnp.where(seg == before, jnp.exp(cum), 0.0), spread)
        passing = jnp.where(last == before, jnp.exp(end), 0.0)
        fresh = dot_tn(act_ref[rows, DI + NS : CW], low(entry * dy))
        state_grad_ref[...] = widen_row(passing, spread) * state_grad_ref[...] + fresh
        return nothing

    lax.fori_loop(0, chunks, chunk, 0)


def back_kernel(act_ref, dt_ref, cum_ref, seg_ref, segrow_ref, raw_ref, bias_ref, rate_ref, kept_ref,
                y_ref, ygrad_ref, later_ref, conv_ref, weight_ref, cbias_ref, skip_ref,
                raw_grad_ref, conv_grad_ref, weight_grad_ref, cbias_grad_ref, rate_grad_ref,
                bias_grad_ref, skip_grad_ref, act_grad_ref, carry_ref, pre_ref):
    rows_total = act_ref.shape[0]
    chunks = rows_total // SUB
    spread = spreader()
    half = lane_halves(SUB)
    upper = jnp.where(iota((SUB, SUB), 1) >= iota((SUB, SUB), 0), 1.0, 0.0)
    rate = jnp.exp(rate_ref[...])
    carry_ref[...] = later_ref[...]
    rate_grad_ref[...] = jnp.zeros_like(rate_grad_ref)
    bias_grad_ref[...] = jnp.zeros_like(bias_grad_ref)
    skip_grad_ref[...] = jnp.zeros_like(skip_grad_ref)

    def chunk(i, nothing):
        c = chunks - 1 - i
        r0 = pl.multiple_of(c * SUB, SUB)
        rows = pl.ds(r0, SUB)
        dt, cum = dt_ref[rows, :], cum_ref[rows, :]
        cum_t = cum.T
        seg = seg_ref[pl.ds(pl.multiple_of(r0 + 8, 8), SUB), :]
        before = seg_ref[pl.ds(pl.multiple_of(r0, 8), 8), :][7:8]
        last, end = seg[SUB - 1 :, :], cum[SUB - 1 :, :]
        keys, reads = act_ref[rows, DI : DI + NS], act_ref[rows, DI + NS : CW]
        affinity = dot_nt(keys, reads)
        allowed = (iota((SUB, SUB), 1) >= iota((SUB, SUB), 0)) & (seg == segrow_ref[0:1, rows])
        values = act_ref[rows, 0:DI].astype(jnp.float32)
        wide_dt = widen(dt, spread)
        scaled = values * wide_dt
        scaled_low = low(scaled)
        dy = ygrad_ref[rows, :]
        dy_low = low(dy)
        state, carry = kept_ref[pl.ds(c, 1)][0], carry_ref[...]
        carry_low = low(carry)
        wide_weight = widen(jnp.where(seg == last, jnp.exp(end - cum), 0.0), spread)
        wide_entry = widen(jnp.where(seg == before, jnp.exp(cum), 0.0), spread)
        wide_pass = widen_row(jnp.where(last == before, jnp.exp(end), 0.0), spread)
        from_state = dot_nn(keys, carry_low) * wide_weight
        mixed_grad = jnp.zeros((SUB, SUB), jnp.float32)
        for pair in range(MH // 2):
            cols = slice(pair * 128, pair * 128 + 128)
            v, d = scaled[:, cols], dy[:, cols]
            left = jnp.concatenate([low(jnp.where(half, v, 0.0)), low(jnp.where(half, 0.0, v))], 0)
            right = jnp.concatenate([low(jnp.where(half, d, 0.0)), low(jnp.where(half, 0.0, d))], 0)
            weight_grad = dot_nt(left, dy_low[:, cols])
            parts = []
            for n, h in enumerate((2 * pair, 2 * pair + 1)):
                gap = jnp.where(allowed, cum_t[h : h + 1, :] - cum[:, h : h + 1], -1e30)
                decay = jnp.exp(gap)
                parts.append(low(decay * affinity))
                mixed_grad = mixed_grad + decay * weight_grad[n * SUB : (n + 1) * SUB]
            act_grad_ref[rows, cols] = dot_nn(jnp.concatenate(parts, 1), right)
        x = act_grad_ref[rows, 0:DI] + from_state
        act_grad_ref[rows, 0:DI] = wide_dt * x + skip_ref[...] * dy
        mixed_low = low(mixed_grad)
        act_grad_ref[rows, DI : DI + NS] = dot_nn(mixed_low, reads) + dot_nt(
            low(wide_weight * scaled), carry_low
        )
        entered = low(wide_entry * dy)
        act_grad_ref[rows, DI + NS : CW] = dot_tn(mixed_low, keys) + dot_nt(entered, state)
        scaled_exact = scaled_low.astype(jnp.float32)
        direct = head_sums(values * x, spread)
        given = head_sums(scaled_exact * x, spread)
        taken = head_sums(dy_low.astype(jnp.float32) * y_ref[rows, :], spread)
        tail = jnp.sum(scaled_exact * from_state, axis=0, keepdims=True) + jnp.sum(
            wide_pass * carry * state.astype(jnp.float32), axis=0, keepdims=True
        )
        tail = head_sums(jnp.broadcast_to(tail, (8, DI)), spread)[0:1]
        decay_grad = exact(upper, taken - given) + tail
        rate_grad_ref[...] += jnp.sum(decay_grad * (-dt * rate), axis=0, keepdims=True)
        dt_grad = direct - decay_grad * rate
        raw_grad = dt_grad * sigmoid(raw_ref[rows, :] + bias_ref[...])
        raw_grad_ref[rows, :] = raw_grad
        bias_grad_ref[...] += jnp.sum(raw_grad, axis=0, keepdims=True)
        skip_sum = jnp.sum(dy * values, axis=0, keepdims=True)
        skip_grad_ref[...] += head_sums(jnp.broadcast_to(skip_sum, (8, DI)), spread)[0:1]
        carry_ref[...] = wide_pass * carry + dot_tn(reads, entered)
        return nothing

    lax.fori_loop(0, chunks, chunk, 0)
    weight_grad_ref[...] = jnp.zeros_like(weight_grad_ref)
    pre_ref[0:8, :] = jnp.zeros((8, 128), jnp.float32)
    pre_ref[rows_total + 8 : rows_total + 16, :] = jnp.zeros((8, 128), jnp.float32)

    def tile(j, carry):
        col = pl.ds(pl.multiple_of(j * 128, 128), 128)
        sums = [jnp.zeros((1, 128), jnp.float32) for _ in range(KC + 1)]
        for c in range(chunks):
            r0 = c * SUB
            seg = seg_ref[pl.ds(r0 + 8, SUB), :]
            total = jnp.broadcast_to(cbias_ref[0:1, col], (SUB, 128))
            taps = []
            for k in range(KC):
                x = rounded_to(conv_ref[pl.ds(r0 + 9 - KC + k, SUB), col])
                if k < KC - 1:
                    x = jnp.where(seg_ref[pl.ds(r0 + 9 - KC + k, SUB), :] == seg, x, 0.0)
                taps.append(x)
                total = total + weight_ref[k : k + 1, col] * x
            sig = sigmoid(total)
            pre = act_grad_ref[pl.ds(r0, SUB), col] * (sig * (1.0 + total * (1.0 - sig)))
            pre_ref[pl.ds(r0 + 8, SUB), :] = pre
            for k in range(KC):
                sums[k] = sums[k] + jnp.sum(pre * taps[k], axis=0, keepdims=True)
            sums[KC] = sums[KC] + jnp.sum(pre, axis=0, keepdims=True)
        for k in range(KC):
            weight_grad_ref[k : k + 1, col] = sums[k]
        cbias_grad_ref[0:1, col] = sums[KC]
        for c in range(chunks + 1):
            r0 = c * SUB
            size = SUB if c < chunks else 8
            seg = seg_ref[pl.ds(r0, size), :]
            total = jnp.zeros((size, 128), jnp.float32)
            for back in range(KC):
                x = pre_ref[pl.ds(r0 + back, size), :]
                if back:
                    x = jnp.where(seg_ref[pl.ds(r0 + back, size), :] == seg, x, 0.0)
                total = total + weight_ref[KC - 1 - back : KC - back, col] * x
            conv_grad_ref[pl.ds(r0, size), col] = total
        return carry

    lax.fori_loop(0, CW // 128, tile, 0)


def partner(values):
    lane = iota(values.shape, 1)
    half = HEAD_WIDTH // 2
    return jnp.where(
        lane % HEAD_WIDTH < half, pltpu.roll(values, 128 - half, 1), pltpu.roll(values, half, 1)
    )


def rotate_kernel(qkv_ref, cos_ref, sin_ref, query_ref, kv_ref):
    cos, sin = cos_ref[...], sin_ref[...]
    for g in range(5):
        x = qkv_ref[:, g * 128 : g * 128 + 128]
        x = low(x * cos + partner(x) * sin)
        if g < 4:
            query_ref[:, g * 128 : g * 128 + 128] = x * jnp.bfloat16(HEAD_WIDTH**-0.5)
        else:
            kv_ref[:, 0:128] = x
    kv_ref[:, 128:256] = low(qkv_ref[:, 640:768])


def lane_variants(block, out_ref):
    other = pltpu.roll(block, 64, 1)
    half = iota(block.shape, 1) < HEAD_WIDTH
    out_ref[0] = low(jnp.where(half, block, 0.0))
    out_ref[1] = low(jnp.where(half, 0.0, other))
    out_ref[2] = low(jnp.where(half, other, 0.0))
    out_ref[3] = low(jnp.where(half, 0.0, block))


def attend_bias(b, own, rows, segcol_ref, segrow_ref, bias_ref):
    seg = segcol_ref[pl.ds(pl.multiple_of(b * rows, rows), rows), :]
    seg = jnp.concatenate([seg] * (rows // 128), 1)
    causal = (iota((rows, rows), 0) - iota((rows, rows), 1)) <= jnp.where(b < own, rows, 0)
    bias_ref[...] = jnp.where(causal & (seg == segrow_ref[...]), 0.0, -1e30)


def attend_start(top_ref, sum_ref, out_t_ref):
    top_ref[...] = jnp.full_like(top_ref, -1e30)
    sum_ref[...] = jnp.zeros_like(sum_ref)
    out_t_ref[...] = jnp.zeros_like(out_t_ref)


def attend_block(b, own, query_ref, kv_ref, segcol_ref, segrow_ref, out_t_ref, bias_ref, keys_ref,
                 values_t_ref, top_ref, sum_ref):
    rows = query_ref.shape[0]
    at = pl.ds(pl.multiple_of(b * rows, rows), rows)
    attend_bias(b, own, rows, segcol_ref, segrow_ref, bias_ref)
    lane_variants(kv_ref[at, 0:128].astype(jnp.float32), keys_ref)
    values_t_ref[...] = low(kv_ref[at, 128:256].astype(jnp.float32).T)

    def pair(g, nothing):
        kv = g // 2
        query = query_ref[:, pl.ds(pl.multiple_of(g * 128, 128), 128)]
        for side in range(2):
            h = g * 2 + side
            row = pl.ds(pl.multiple_of(h * 8, 8), 8)
            scores = dot_nt(keys_ref[kv * 2 + side], query)
            scores = scores + bias_ref[...]
            old = top_ref[row, :][0:1]
            top = jnp.maximum(old, jnp.max(scores, axis=0, keepdims=True))
            p = jnp.exp(scores - top)
            fade = jnp.exp(old - top)
            total = sum_ref[row, :][0:1] * fade + jnp.sum(p, 0, keepdims=True)
            top_ref[row, :] = jnp.broadcast_to(top, (8, rows))
            sum_ref[row, :] = jnp.broadcast_to(total, (8, rows))
            at_h = pl.ds(pl.multiple_of(h * 64, 64), 64)
            values_t = values_t_ref[pl.ds(pl.multiple_of(kv * 64, 64), 64), :]
            out_t_ref[at_h, :] = out_t_ref[at_h, :] * fade + dot_nn(values_t, low(p))
        return nothing

    lax.fori_loop(0, QUERY_HEADS // 2, pair, 0)


def attend_finish(out_ref, out_t_ref, total_ref, top_ref, sum_ref):
    for h in range(QUERY_HEADS):
        at_h = slice(h * 64, h * 64 + 64)
        total_ref[h : h + 1, :] = top_ref[h * 8 : h * 8 + 1, :] + jnp.log(sum_ref[h * 8 : h * 8 + 1, :])
        out_t_ref[at_h, :] = out_t_ref[at_h, :] / sum_ref[h * 8 : h * 8 + 1, :]
    out_ref[...] = low(out_t_ref[...].T)


def attend_back_kernel(own_ref, query_ref, kv_ref, segcol_ref, segrow_ref, grad_ref, out_t_ref,
                       total_ref, cos_ref, sin_ref, query_grad_ref, kv_grad_ref,
                       bias_ref, keys_ref, values_ref, dkeys_ref, dvalues_ref, spread_ref, dq_ref,
                       query_half_ref, grad_half_ref):
    rows = query_ref.shape[0]
    own = own_ref[0]
    kv_grad_ref[...] = jnp.zeros_like(kv_grad_ref)
    dq_ref[...] = jnp.zeros_like(dq_ref)
    grad_t = grad_ref[...].astype(jnp.float32).T
    product = grad_t * out_t_ref[...]
    for h in range(QUERY_HEADS):
        spread_ref[h : h + 1, :] = jnp.sum(product[h * 64 : h * 64 + 64, :], 0, keepdims=True)
        g = h // 2
        half = (iota((rows, 128), 1) < HEAD_WIDTH) == (h % 2 == 0)
        for src, dst in ((query_ref, query_half_ref), (grad_ref, grad_half_ref)):
            dst[h] = low(jnp.where(half, src[:, g * 128 : g * 128 + 128].astype(jnp.float32), 0.0))

    def block(b, nothing):
        at = pl.ds(pl.multiple_of(b * rows, rows), rows)
        attend_bias(b, own, rows, segcol_ref, segrow_ref, bias_ref)
        keys = kv_ref[at, 0:128].astype(jnp.float32)
        lane_variants(keys, keys_ref)
        lane_variants(kv_ref[at, 128:256].astype(jnp.float32), values_ref)
        keys_t = low(keys.T)
        dkeys_ref[...] = jnp.zeros_like(dkeys_ref)
        dvalues_ref[...] = jnp.zeros_like(dvalues_ref)
        for h in range(QUERY_HEADS):
            g, kv = h // 2, h // 4
            lanes = slice(g * 128, g * 128 + 128)
            scores = dot_nt(keys_ref[kv * 2 + h % 2], query_ref[:, lanes]) + bias_ref[...]
            p = jnp.exp(scores - total_ref[h : h + 1, :])
            dp = dot_nt(values_ref[kv * 2 + h % 2], grad_ref[:, lanes])
            ds = low(p * (dp - spread_ref[h : h + 1, :]))
            dkeys_ref[kv] += dot_nn(ds, query_half_ref[h])
            dvalues_ref[kv] += dot_nn(low(p), grad_half_ref[h])
            dq_ref[h * 64 : h * 64 + 64, :] += dot_nn(keys_t[kv * 64 : kv * 64 + 64, :], ds)
        half = iota((rows, 128), 1) < HEAD_WIDTH
        for src, lanes in ((dkeys_ref, slice(0, 128)), (dvalues_ref, slice(128, 256))):
            first, second = src[0], src[1]
            kv_grad_ref[at, lanes] = low(
                jnp.where(half, first + pltpu.roll(first, 64, 1), second + pltpu.roll(second, 64, 1))
            )
        return nothing

    lax.fori_loop(0, own + 1, block, 0)
    dq = dq_ref[...].T * (HEAD_WIDTH**-0.5)
    cos, sin = cos_ref[...], sin_ref[...]
    for g in range(4):
        x = dq[:, g * 128 : g * 128 + 128]
        query_grad_ref[:, g * 128 : g * 128 + 128] = low(x * cos + partner(x * sin))


vmem = pl.BlockSpec(memory_space=pltpu.VMEM)
smem = pl.BlockSpec(memory_space=pltpu.SMEM)


def call(kernel, outs, args, scratch=(), first=vmem, flops=10**9):
    return pl.pallas_call(
        kernel,
        out_shape=[jax.ShapeDtypeStruct(shape, kind) for shape, kind in outs],
        in_specs=[first] + [vmem] * (len(args) - 1),
        out_specs=[vmem] * len(outs),
        scratch_shapes=[pltpu.VMEM(shape, kind) for shape, kind in scratch],
        compiler_params=pltpu.CompilerParams(vmem_limit_bytes=56 * 2**20),
        cost_estimate=pl.CostEstimate(flops=flops, bytes_accessed=10**7, transcendentals=10**6),
    )(*args)


MESH = pl.DeviceIdType.MESH


def position_bits(count):
    index = lax.axis_index("fsdp")
    return [(index // (1 << b)) % 2 for b in reversed(range(count))]


def across(bits, axis):
    count = len(bits)
    index = lax.axis_index("fsdp")
    step = 1 << (count - 1 - axis)
    return (index + step * (1 - 2 * bits[axis]), lax.axis_index("seq"))


def along(by):
    return (lax.axis_index("fsdp"), lax.axis_index("seq") + by)


class Item:
    def __init__(self, number, weight, start, size, order):
        self.number, self.weight, self.start, self.size, self.order = number, weight, start, size, order


def plan_items(shapes, parts, bit_count):
    items = []
    for w, ((rows, _), count) in enumerate(zip(shapes, parts)):
        for p in range(count):
            turn = p % max(bit_count - 1, 1)
            ici = list(range(bit_count - 1))
            order = [bit_count - 1] + ici[turn:] + ici[:turn]
            items.append(Item(len(items), w, p * (rows // count), rows // count, order))
    return items


class Reducer:
    def __init__(self, bit_count, depth, items, whole, own, landed, zin, zmid, total, out, send, recv, own_sem):
        self.bit_count, self.depth, self.items = bit_count, depth, items
        self.whole, self.own, self.landed = whole, own, landed
        self.zin, self.zmid, self.total, self.out = zin, zmid, total, out
        self.send, self.recv, self.own_sem = send, recv, own_sem
        self.bits = position_bits(bit_count)
        self.place = lax.axis_index("seq")

    def rows(self, item):
        return pl.ds(item.start, item.size)

    def left(self, item, stage):
        return sorted(item.order[stage:])

    def pick(self, item, stage, mine):
        axis = item.order[stage]
        at = self.left(item, stage).index(axis)
        bit = self.bits[axis] if mine else 1 - self.bits[axis]
        lead = [slice(None)] * (self.bit_count - stage)
        lead[at] = bit
        return (*lead, self.rows(item))

    def source(self, item, stage):
        if stage == 0:
            return self.whole[item.weight]
        return self.own[item.weight] if stage == 1 else self.landed[stage - 1][item.weight]

    def copy(self, item, stage):
        lead = (slice(None),) * (self.bit_count - stage - 1)
        return pltpu.make_async_remote_copy(
            self.source(item, stage).at[self.pick(item, stage, False)],
            self.landed[stage][item.weight].at[(*lead, self.rows(item))],
            self.send.at[item.number, stage],
            self.recv.at[item.number, stage],
            device_id=across(self.bits, item.order[stage]),
            device_id_type=MESH,
        )

    def own_copy(self, item):
        lead = (slice(None),) * (self.bit_count - 1)
        return pltpu.make_async_copy(
            self.whole[item.weight].at[self.pick(item, 0, True)],
            self.own[item.weight].at[(*lead, self.rows(item))],
            self.own_sem.at[item.number],
        )

    def begin(self, item):
        self.copy(item, 0).start()
        self.own_copy(item).start()

    def add(self, dst, dst_lead, other, other_lead, item):
        group = 16

        def step(i, nothing):
            at = pl.ds(pl.multiple_of(item.start + i * group, group), group)
            dst[(*dst_lead, at)] = low(
                dst[(*dst_lead, at)].astype(f32) + other[(*other_lead, at)].astype(f32)
            )
            return nothing

        lax.fori_loop(0, item.size // group, step, 0)

    def advance(self, item, stage):
        self.copy(item, stage).wait_recv()
        landed = self.landed[stage][item.weight]
        kept = self.bit_count - stage - 1
        places = [[(i >> (kept - 1 - b)) & 1 for b in range(kept)] for i in range(1 << kept)]
        if stage == 0:
            self.own_copy(item).wait()
            for lead in places:
                self.add(self.own[item.weight], lead, landed, lead, item)
        else:
            source = self.source(item, stage)
            axis = item.order[stage]
            at = self.left(item, stage).index(axis)
            for lead in places:
                from_lead = [*lead[:at], self.bits[axis], *lead[at:]]
                self.add(landed, lead, source, from_lead, item)
        if stage + 1 < self.bit_count:
            self.copy(item, stage + 1).start()

    def z_copy(self, item, kind, by):
        w, rows = item.weight, self.rows(item)
        last = self.landed[self.bit_count - 1][w]
        src, dst = {
            "in": (last, self.zin[w]),
            "mid": (last, self.zmid[w]),
            "out": (self.total[w], self.total[w]),
        }[kind]
        slot = self.bit_count + {"in": 0, "mid": 1, "out": 2}[kind]
        return pltpu.make_async_remote_copy(
            src.at[rows],
            dst.at[rows],
            self.send.at[item.number, slot],
            self.recv.at[item.number, slot],
            device_id=along(by),
            device_id_type=MESH,
        )

    def sides(self):
        half = self.depth // 2
        outermost = (self.place == 0) | (self.place == self.depth - 1)
        middle = (self.place == half - 1) | (self.place == half)
        inward = 1 - 2 * (self.place // half)
        return outermost, middle, inward

    def z_first(self, item):
        outermost, middle, inward = self.sides()

        @pl.when(outermost & jnp.logical_not(middle))
        def _():
            self.z_copy(item, "in", inward).start()

    def z_second(self, item):
        outermost, middle, inward = self.sides()

        @pl.when(jnp.logical_not(outermost))
        def _():
            self.z_copy(item, "in", -inward).wait_recv()
            self.add(self.landed[self.bit_count - 1][item.weight], (), self.zin[item.weight], (), item)

            @pl.when(jnp.logical_not(middle))
            def _():
                self.z_copy(item, "in", inward).start()

        @pl.when(middle)
        def _():
            self.z_copy(item, "mid", inward).start()

    def z_third(self, item):
        outermost, middle, inward = self.sides()

        @pl.when(middle)
        def _():
            self.z_copy(item, "mid", inward).wait_recv()
            group = 16
            last, other = self.landed[self.bit_count - 1][item.weight], self.zmid[item.weight]

            def step(i, nothing):
                at = pl.ds(pl.multiple_of(item.start + i * group, group), group)
                self.total[item.weight][at] = low(last[at].astype(f32) + other[at].astype(f32))
                return nothing

            lax.fori_loop(0, item.size // group, step, 0)

            @pl.when(jnp.logical_not(outermost))
            def _():
                self.z_copy(item, "out", -inward).start()

    def z_fourth(self, item):
        outermost, middle, inward = self.sides()

        @pl.when(jnp.logical_not(middle))
        def _():
            self.z_copy(item, "out", inward).wait_recv()

            @pl.when(jnp.logical_not(outermost))
            def _():
                self.z_copy(item, "out", -inward).start()

        group = 16

        def step(i, nothing):
            at = pl.ds(pl.multiple_of(item.start + i * group, group), group)
            self.out[item.weight][at] = self.total[item.weight][at]
            return nothing

        lax.fori_loop(0, item.size // group, step, 0)

    def finish(self, item):
        outermost, middle, inward = self.sides()
        for stage in range(self.bit_count):
            self.copy(item, stage).wait_send()

        @pl.when(jnp.logical_not(middle))
        def _():
            self.z_copy(item, "in", inward).wait_send()

        @pl.when(middle)
        def _():
            self.z_copy(item, "mid", inward).wait_send()

        @pl.when(jnp.logical_not(outermost))
        def _():
            self.z_copy(item, "out", -inward).wait_send()

    def actions(self, lag, z_lag):
        steps = []
        for i, item in enumerate(self.items):
            for stage in range(self.bit_count):
                steps.append((i + lag * stage, stage, lambda item=item, s=stage: self.advance(item, s)))
            t = i + lag * (self.bit_count - 1)
            for n, run in enumerate((self.z_first, self.z_second, self.z_third, self.z_fourth)):
                steps.append((t + n * z_lag, self.bit_count + n, lambda item=item, run=run: run(item)))
        return [action for _, _, action in sorted(steps, key=lambda s: s[:2])]


def enter(bit_count, depth):
    bits = position_bits(bit_count)
    place = lax.axis_index("seq")
    barrier = pltpu.get_barrier_semaphore()
    for axis in range(bit_count):
        pl.semaphore_signal(barrier, inc=1, device_id=across(bits, axis), device_id_type=MESH)

    @pl.when(place > 0)
    def _():
        pl.semaphore_signal(barrier, inc=1, device_id=along(-1), device_id_type=MESH)

    @pl.when(place < depth - 1)
    def _():
        pl.semaphore_signal(barrier, inc=1, device_id=along(1), device_id_type=MESH)

    ends = jnp.where(place == 0, 1, 0) + jnp.where(place == depth - 1, 1, 0)
    pl.semaphore_wait(barrier, bit_count + 2 - ends)


def small_sum(bit_count, depth, src, buf, out, send, recv):
    bits = position_bits(bit_count)
    place = lax.axis_index("seq")
    half = depth // 2
    outermost = (place == 0) | (place == depth - 1)
    middle = (place == half - 1) | (place == half)
    inward = 1 - 2 * (place // half)

    def flip(stage):
        return pltpu.make_async_remote_copy(
            (src if stage == 0 else out.at[stage - 1]),
            buf.at[stage],
            send.at[stage],
            recv.at[stage],
            device_id=across(bits, bit_count - 1 - stage),
            device_id_type=MESH,
        )

    def z_copy(kind, by):
        n = bit_count + kind
        return pltpu.make_async_remote_copy(
            out.at[(bit_count - 1, bit_count, bit_count + 1)[kind]],
            (buf.at[bit_count], buf.at[bit_count + 1], out.at[bit_count + 1])[kind],
            send.at[n],
            recv.at[n],
            device_id=along(by),
            device_id_type=MESH,
        )

    def flip_done(stage):
        flip(stage).wait_recv()
        mine = src[...] if stage == 0 else out[stage - 1]
        out[stage] = mine + buf[stage]
        if stage + 1 < bit_count:
            flip(stage + 1).start()

    def z_in():
        @pl.when(jnp.logical_not(middle))
        def _():
            @pl.when(jnp.logical_not(outermost))
            def _():
                z_copy(0, -inward).wait_recv()
                out[bit_count - 1] = out[bit_count - 1] + buf[bit_count]

            z_copy(0, inward).start()

        @pl.when(middle)
        def _():
            out[bit_count] = out[bit_count - 1]

            @pl.when(jnp.logical_not(outermost))
            def _():
                z_copy(0, -inward).wait_recv()
                out[bit_count] = out[bit_count] + buf[bit_count]

            z_copy(1, inward).start()

    def z_mid():
        @pl.when(middle)
        def _():
            z_copy(1, inward).wait_recv()
            out[bit_count + 1] = out[bit_count] + buf[bit_count + 1]

    def z_out():
        @pl.when(jnp.logical_not(middle))
        def _():
            z_copy(2, inward).wait_recv()

        @pl.when(jnp.logical_not(outermost))
        def _():
            z_copy(2, -inward).start()

    def finish():
        for stage in range(bit_count):
            flip(stage).wait_send()

        @pl.when(jnp.logical_not(middle))
        def _():
            z_copy(0, inward).wait_send()

        @pl.when(middle)
        def _():
            z_copy(1, inward).wait_send()

        @pl.when(jnp.logical_not(outermost))
        def _():
            z_copy(2, -inward).wait_send()

    begin = lambda: flip(0).start()
    steps = [lambda s=s: flip_done(s) for s in range(bit_count)] + [z_in, z_mid, z_out]
    return begin, steps, finish


def bit_length(count):
    return count.bit_length() - 1


def reduce_all(gradients, small, parts):
    fsdp, depth = lax.axis_size("fsdp"), lax.axis_size("seq")
    bit_count = bit_length(fsdp)
    shapes = [(g.shape[0] // fsdp, g.shape[1]) for g in gradients]
    items = plan_items(shapes, parts, bit_count)
    count = len(shapes)

    def kernel(*refs):
        at = 0

        def take(n):
            nonlocal at
            at += n
            return refs[at - n : at]

        whole, (small_ref,) = take(count), take(1)
        out, (small_out,) = take(count), take(1)
        own = take(count)
        landed = [take(count) for _ in range(bit_count)]
        zin, zmid, total = take(count), take(count), take(count)
        (small_buf, small_work) = take(2)
        send, recv, own_sem, small_send, small_recv = take(5)
        enter(bit_count, depth)
        work = Reducer(bit_count, depth, items, whole, own, landed, zin, zmid, total, out, send, recv, own_sem)
        begin, steps, finish = small_sum(
            bit_count, depth, small_ref, small_buf, small_work, small_send, small_recv
        )
        begin()
        for item in items:
            work.begin(item)
        for n, action in enumerate(work.actions(2, 3)):
            action()
            if n % 2 == 1 and steps:
                steps.pop(0)()
        for step in steps:
            step()
        small_out[...] = small_work[bit_count + 1]
        for item in items:
            work.finish(item)
        finish()

    two = (2,) * bit_count
    stacks = [[pltpu.VMEM((*two[: bit_count - 1 - s], *shape), bf16) for shape in shapes] for s in range(bit_count)]
    flat = [pltpu.VMEM(shape, bf16) for shape in shapes]
    scratch = [*stacks[0], *[b for stage in stacks for b in stage], *flat, *flat, *flat]
    scratch += [pltpu.VMEM((bit_count + 2, *small.shape), f32)] * 2
    scratch += [
        pltpu.SemaphoreType.DMA((len(items), bit_count + 3)),
        pltpu.SemaphoreType.DMA((len(items), bit_count + 3)),
        pltpu.SemaphoreType.DMA((len(items),)),
        pltpu.SemaphoreType.DMA((bit_count + 3,)),
        pltpu.SemaphoreType.DMA((bit_count + 3,)),
    ]
    return pl.pallas_call(
        kernel,
        out_shape=[jax.ShapeDtypeStruct(shape, bf16) for shape in shapes]
        + [jax.ShapeDtypeStruct(small.shape, f32)],
        in_specs=[pl.BlockSpec(memory_space=pl.ANY)] * count + [vmem],
        out_specs=[vmem] * (count + 1),
        scratch_shapes=scratch,
        compiler_params=pltpu.CompilerParams(
            collective_id=0, has_side_effects=True, vmem_limit_bytes=60 * 2**20
        ),
    )(*[g.reshape(*two, *shape) for g, shape in zip(gradients, shapes)], small)


class Gatherer:
    def __init__(self, bit_count, items, shards, whole, loads, load_sem, cast_to, own_sem, send, recv):
        self.bit_count, self.items = bit_count, items
        self.shards, self.whole, self.loads, self.load_sem = shards, whole, loads, load_sem
        self.cast_to, self.own_sem, self.send, self.recv = cast_to, own_sem, send, recv
        self.bits = position_bits(bit_count)
        self.index = lax.axis_index("fsdp")
        self.ready = set()
        self.todo = []
        self.done = set()

    def block(self, axes):
        at = self.index
        for axis in axes:
            at = at + (1 << (self.bit_count - 1 - axis)) * (1 - 2 * self.bits[axis])
        return at

    def subsets(self, order):
        sets = [()]
        for axis in order:
            sets = sets + [(*s, axis) for s in sets]
        return sets

    def rows(self, item, axes):
        shard_rows = self.cast_to[item.weight].shape[0]
        return pl.ds(pl.multiple_of(self.block(axes) * shard_rows + item.start, 16), item.size)

    def copy(self, item, stage, number, axes):
        whole = self.whole[item.weight]
        at = self.rows(item, axes)
        src = self.cast_to[item.weight].at[pl.ds(item.start, item.size)] if not axes else whole.at[at]
        slot = (1 << stage) - 1 + number
        return pltpu.make_async_remote_copy(
            src,
            whole.at[at],
            self.send.at[item.number, slot],
            self.recv.at[item.number, slot],
            device_id=across(self.bits, item.order[stage]),
            device_id_type=MESH,
        )

    def landed(self, item, stage, number, axes):
        whole = self.whole[item.weight]
        at = self.rows(item, (*axes, item.order[stage]))
        slot = (1 << stage) - 1 + number
        return pltpu.make_async_remote_copy(
            whole.at[at],
            whole.at[at],
            self.send.at[item.number, slot],
            self.recv.at[item.number, slot],
            device_id=across(self.bits, item.order[stage]),
            device_id_type=MESH,
        )

    def load(self, weight):
        return pltpu.make_async_copy(self.shards[weight], self.loads[weight], self.load_sem.at[weight])

    def own(self, weight):
        rows = self.cast_to[weight].shape[0]
        return pltpu.make_async_copy(
            self.cast_to[weight],
            self.whole[weight].at[pl.ds(pl.multiple_of(self.index * rows, 16), rows)],
            self.own_sem.at[weight],
        )

    def begin(self, item):
        w = item.weight
        if w not in self.ready:
            self.ready.add(w)
            self.load(w).wait()
            group = 16

            def step(i, nothing):
                at = pl.ds(pl.multiple_of(i * group, group), group)
                self.cast_to[w][at] = low(self.loads[w][at])
                return nothing

            lax.fori_loop(0, self.cast_to[w].shape[0] // group, step, 0)
            self.own(w).start()
        for stage in range(self.bit_count):
            self.copy(item, stage, 0, ()).start()

    def advance(self, item, stage):
        before = self.subsets(item.order[:stage])
        for number, axes in enumerate(before):
            self.landed(item, stage, number, axes).wait_recv()
        for later in range(stage + 1, self.bit_count):
            sets = self.subsets(item.order[:later])
            for number, axes in enumerate(before):
                mine = (*axes, item.order[stage])
                self.copy(item, later, sets.index(mine), mine).start()
        if stage == self.bit_count - 1:
            self.done.add(item.number)

    def plan(self, lag):
        steps = []
        for i, item in enumerate(self.items):
            steps.append((i, 0, lambda item=item: self.begin(item)))
            for stage in range(self.bit_count):
                steps.append((i + lag * (stage + 1), stage + 1, lambda item=item, s=stage: self.advance(item, s)))
        self.todo = [action for _, _, action in sorted(steps, key=lambda s: s[:2])]

    def pump(self, count):
        for _ in range(min(count, len(self.todo))):
            self.todo.pop(0)()

    def until(self, weight):
        numbers = {item.number for item in self.items if item.weight == weight}
        while not numbers <= self.done:
            self.todo.pop(0)()
        self.own(weight).wait()

    def finish(self):
        for item in self.items:
            for stage in range(self.bit_count):
                for number, axes in enumerate(self.subsets(item.order[:stage])):
                    self.copy(item, stage, number, axes).wait_send()


def multiply(out_ref, out_rows, left, right_ref, first, width, tile):
    def step(j, nothing):
        at = pl.ds(pl.multiple_of(j * tile, tile), tile)
        from_at = pl.ds(pl.multiple_of(first + j * tile, 128), tile)
        out_ref[out_rows, at] = dot_nn(left[...], right_ref[:, from_at])
        return nothing

    lax.fori_loop(0, width // tile, step, 0)


def forward_part(tokens, seg_rows, norm_gain, cosine, signed, bias_row, rate_row, conv_weight,
                 conv_bias, mixer_gain, skip_row, shards, parts):
    fsdp, depth = lax.axis_size("fsdp"), lax.axis_size("seq")
    bit_count = bit_length(fsdp)
    shapes = [s.shape for s in shards]
    items = plan_items(shapes, parts, bit_count)
    count = tokens.shape[0]
    weights = len(shards)
    pieces = 2
    kept_shape = (count // SUB, NS, DI)
    results = dict(
        normed=((count, 1024), bf16),
        conv=((count + EDGE, CW), f32),
        raw=((count, 128), f32),
        z=((count, DI), f32),
        act=((count, CW), bf16),
        dt=((count, 128), f32),
        cum=((count, 128), f32),
        passing=((1, DI), f32),
        query=((count, 512), bf16),
        kv=((depth * count, 256), bf16),
        attended=((count, 512), bf16),
        attended_t=((512, count), f32),
        log_total=((QUERY_HEADS, count), f32),
        y=((count, DI), f32),
        gated=((count, DI), bf16),
        kept=(kept_shape, bf16),
        seg_wide=((count + 2 * EDGE, 128), f32),
        seg_col=((depth * count, 128), f32),
    )
    names = list(results)
    local = dict(
        normed_edge=((16, 1024), bf16),
        edge=((16, 1024), bf16),
        seg_all=((depth * 8, count), f32),
        qkv=((count, 768), f32),
        end=((NS, DI), f32),
        state=((NS, DI), f32),
        carry=((NS, DI), f32),
        state_send=((NS, DI), bf16),
        state_recv=((NS, DI), bf16),
        bias=((count, count), f32),
        keys=((4, count, 128), bf16),
        values_t=((128, count), bf16),
        top=((QUERY_HEADS * 8, count), f32),
        total=((QUERY_HEADS * 8, count), f32),
    )
    in_vmem = (0, 1)

    def kernel(*refs):
        at = 0

        def take(n):
            nonlocal at
            at += n
            return refs[at - n : at]

        (tokens_ref, segrow_ref, gain_ref, cos_ref, sin_ref, bias_ref, rate_ref, weight_ref, cbias_ref,
         mixer_gain_ref, skip_ref) = take(11)
        shard_refs = take(weights)
        out = dict(zip(names, take(len(names))))
        whole_out = take(weights)
        v = dict(zip(names, take(len(names))))
        v.update(zip(local, take(len(local))))
        loads, cast_to = take(weights), take(weights)
        whole_vmem = take(len(in_vmem))
        send, recv, load_sem, own_sem, save_sem, z_send, z_recv = take(7)
        place = lax.axis_index("seq")
        whole = [whole_vmem[in_vmem.index(w)] if w in in_vmem else whole_out[w] for w in range(weights)]
        gather = Gatherer(bit_count, items, shard_refs, whole, loads, load_sem, cast_to, own_sem, send, recv)
        for w in range(weights):
            gather.load(w).start()
        enter(bit_count, depth)
        gather.plan(2)
        saved = []

        def save(src, dst):
            copy = pltpu.make_async_copy(src, dst, save_sem.at[len(saved)])
            copy.start()
            saved.append(copy)

        def keep(*which):
            for name in which:
                save(v[name], out[name])

        def to_next(src, dst, slot):
            return pltpu.make_async_remote_copy(
                src, dst, z_send.at[slot], z_recv.at[slot], device_id=along(1), device_id_type=MESH
            )

        started = []

        def send_on(condition, src, dst, slot):
            @pl.when(condition)
            def _():
                to_next(src, dst, slot).start()

            started.append((condition, src, dst, slot))

        def ring(ref, rows, hop, slot):
            b = place - hop + 1
            part = ref.at[pl.ds(pl.multiple_of(jnp.maximum(b, 0) * rows, 8), rows)]
            send_on((b >= 0) & (place < depth - 1), part, part, slot)

        def ring_wait(ref, rows, hop, slot):
            b = place - hop
            part = ref.at[pl.ds(pl.multiple_of(jnp.maximum(b, 0) * rows, 8), rows)]

            @pl.when(b >= 0)
            def _():
                to_next(part, part, slot).wait_recv()

        tail = tokens_ref.at[pl.ds(count - 16, 16)]
        gather.pump(2)
        send_on(place < depth - 1, tail, v["edge"], 0)
        v["seg_all"][pl.ds(pl.multiple_of(place * 8, 8), 8)] = jnp.broadcast_to(segrow_ref[...], (8, count))
        ring(v["seg_all"], 8, 1, 1)

        def normalise(src, dst, rows, group):
            def step(i, nothing):
                at = pl.ds(pl.multiple_of(i * group, group), group)
                x = src[at].astype(f32)
                scale = lax.rsqrt(jnp.mean(x * x, axis=1, keepdims=True) + epsilon)
                dst[at] = low(x * scale * gain_ref[...])
                return nothing

            lax.fori_loop(0, rows // group, step, 0)

        normalise(tokens_ref, v["normed"], count, 64)
        gather.pump(1)

        @pl.when(place == 0)
        def _():
            v["edge"][...] = jnp.zeros((16, 1024), bf16)

        @pl.when(place > 0)
        def _():
            to_next(tail, v["edge"], 0).wait_recv()

        normalise(v["edge"], v["normed_edge"], 16, 16)
        gather.pump(1)
        for hop in range(1, depth):
            ring_wait(v["seg_all"], 8, hop, hop)
            if hop < depth - 1:
                ring(v["seg_all"], 8, hop + 1, hop + 1)

        def column(row):
            return jnp.broadcast_to(row, (128, count)).T

        for b in range(depth):

            @pl.when(b <= place)
            def _(b=b):
                v["seg_col"][b * count : (b + 1) * count, :] = column(v["seg_all"][b * 8 : b * 8 + 1, :])

            @pl.when(b > place)
            def _(b=b):
                v["seg_col"][b * count : (b + 1) * count, :] = jnp.full((count, 128), -2.0, f32)

        own_rows = pl.ds(pl.multiple_of(place * count, 8), count)
        v["seg_wide"][EDGE : EDGE + count, :] = v["seg_col"][own_rows, :]
        v["seg_wide"][EDGE + count :, :] = jnp.full((EDGE, 128), -2.0, f32)
        before = pl.ds(pl.multiple_of(jnp.maximum(place * count - EDGE, 0), 8), EDGE)
        v["seg_wide"][0:EDGE, :] = jnp.where(place == 0, -1.0, v["seg_col"][before, :])
        v["raw"][...] = jnp.zeros((count, 128), f32)
        gather.until(0)
        save(whole[0], whole_out[0])
        multiply(v["conv"], pl.ds(EDGE, count), v["normed"], whole[0], DI, CW, 256)
        v["conv"][0:EDGE, :] = dot_nn(v["normed_edge"][...], whole[0][:, DI : DI + CW])[EDGE:]
        v["raw"][:, 0:MH] = dot_nn(v["normed"][...], whole[0][:, DI + CW : DI + CW + MH])
        gather.pump(4)
        front_conv(v["conv"], v["seg_wide"], weight_ref, cbias_ref, v["act"])
        gather.pump(4)
        front_state(v["seg_wide"], v["raw"], bias_ref, rate_ref, v["act"], v["dt"], v["cum"], v["end"], v["passing"])
        keep("normed", "conv", "raw", "act", "dt", "cum", "passing", "seg_wide", "seg_col")
        width = DI // pieces
        state_slot, kv_slot = depth, depth + pieces

        def chain(j):
            for p in range(pieces):
                cols = pl.ds(p * width, width)

                @pl.when(place == j)
                def _():
                    if j == 0:
                        v["state"][:, cols] = jnp.zeros((NS, width), f32)
                    else:
                        to_next(
                            v["state_send"].at[:, cols], v["state_recv"].at[:, cols], state_slot + p
                        ).wait_recv()
                        v["state"][:, cols] = v["state_recv"][:, cols].astype(f32)
                    if j < depth - 1:
                        v["state_send"][:, cols] = low(
                            v["passing"][:, cols] * v["state"][:, cols] + v["end"][:, cols]
                        )
                        to_next(
                            v["state_send"].at[:, cols], v["state_recv"].at[:, cols], state_slot + p
                        ).start()

        chain(0)
        gather.until(1)
        save(whole[1], whole_out[1])
        multiply(v["qkv"], slice(None), v["normed"], whole[1], 0, 768, 256)
        rotate_kernel(v["qkv"], cos_ref, sin_ref, v["query"], v["kv"].at[own_rows])
        ring(v["kv"], count, 1, kv_slot + 1)
        keep("query")
        gather.pump(4)
        multiply(v["z"], slice(None), v["normed"], whole[0], 0, DI, 256)
        keep("z")
        gather.pump(4)
        chain(1)
        attend_start(v["top"], v["total"], v["attended_t"])

        def attend(b):
            attend_block(b, place, v["query"], v["kv"], v["seg_col"], segrow_ref, v["attended_t"], v["bias"],
                         v["keys"], v["values_t"], v["top"], v["total"])

        attend(place)
        gather.pump(4)
        for hop in range(1, depth):
            ring_wait(v["kv"], count, hop, kv_slot + hop)
            if hop < depth - 1:
                ring(v["kv"], count, hop + 1, kv_slot + hop + 1)

            @pl.when(place >= hop)
            def _(hop=hop):
                attend(place - hop)

            gather.pump(4)
            if hop < depth - 1:
                chain(hop + 1)

        attend_finish(v["attended"], v["attended_t"], v["log_total"], v["top"], v["total"])
        keep("attended", "attended_t", "log_total", "kv")
        for first in range(0, count // SUB, 2):
            gather.pump(4)
            mid_kernel(v["act"], v["dt"], v["cum"], v["seg_wide"], segrow_ref, v["state"], v["z"], mixer_gain_ref,
                       skip_ref, v["y"], v["gated"], v["kept"], v["carry"], first, first + 2)
        keep("y", "gated", "kept")
        for w in range(2, weights):
            gather.until(w)
        gather.finish()
        for condition, src, dst, slot in started:

            @pl.when(condition)
            def _(src=src, dst=dst, slot=slot):
                to_next(src, dst, slot).wait_send()

        @pl.when(place < depth - 1)
        def _():
            for p in range(pieces):
                cols = pl.ds(p * width, width)
                to_next(v["state_send"].at[:, cols], v["state_recv"].at[:, cols], state_slot + p).wait_send()

        for copy in saved:
            copy.wait()

    wholes = [((fsdp * rows, cols), bf16) for rows, cols in shapes]
    scratch = [pltpu.VMEM(*results[n]) for n in names] + [pltpu.VMEM(*a) for a in local.values()]
    scratch += [pltpu.VMEM(shape, f32) for shape in shapes] + [pltpu.VMEM(shape, bf16) for shape in shapes]
    scratch += [pltpu.VMEM(*wholes[w]) for w in in_vmem]
    slots = (1 << bit_count) - 1
    z_slots = depth + pieces + depth
    scratch += [
        pltpu.SemaphoreType.DMA((len(items), slots)),
        pltpu.SemaphoreType.DMA((len(items), slots)),
        pltpu.SemaphoreType.DMA((weights,)),
        pltpu.SemaphoreType.DMA((weights,)),
        pltpu.SemaphoreType.DMA((len(names) + 2,)),
        pltpu.SemaphoreType.DMA((z_slots,)),
        pltpu.SemaphoreType.DMA((z_slots,)),
    ]
    hbm = pl.BlockSpec(memory_space=pl.ANY)
    made = pl.pallas_call(
        kernel,
        out_shape=[jax.ShapeDtypeStruct(*a) for a in list(results.values()) + wholes],
        in_specs=[vmem] * 11 + [hbm] * weights,
        out_specs=[hbm] * (len(names) + weights),
        scratch_shapes=scratch,
        compiler_params=pltpu.CompilerParams(
            collective_id=1, has_side_effects=True, vmem_limit_bytes=62 * 2**20
        ),
    )(tokens, seg_rows, norm_gain, cosine, signed, bias_row, rate_row, conv_weight, conv_bias, mixer_gain,
      skip_row, *shards)
    return dict(zip(names, made)), made[len(names) :]


def shifted(array, axis, by):
    devices = lax.axis_size(axis)
    pairs = [(i, i + by) for i in range(devices) if 0 <= i + by < devices]
    return lax.ppermute(array, axis, pairs)


def contract(left, right):
    return dot_tn(left, right)


def rms_scale(values, gain_vec):
    return (
        values * lax.rsqrt(jnp.mean(values * values, axis=-1, keepdims=True) + epsilon) * gain_vec
    )


def reduced(gradient):
    return low(gradient)


def padded(vector):
    return jnp.pad(vector, (0, 128 - vector.shape[0]))[None]


def on_device(
    tokens,
    cotangent,
    segment_ids,
    norm_gain,
    ffn_gain,
    mixer_gain,
    conv_weight,
    conv_bias,
    decay_log,
    step_bias,
    skip_gain,
    in_proj,
    mixer_out,
    qkv_proj,
    attn_proj,
    gate_up,
    down_proj,
):
    place, devices = lax.axis_index("seq"), lax.axis_size("seq")
    count = tokens.shape[1]
    position = place * count + jnp.arange(count, dtype=jnp.int32)
    half = HEAD_WIDTH // 2
    lane = jnp.arange(128, dtype=jnp.int32)
    exponent = (lane % half).astype(f32) * (2.0 / HEAD_WIDTH)
    frequencies = jnp.power(rope_base, -exponent)
    angles = position.astype(f32)[:, None] * frequencies[None, :]
    cosine = jnp.cos(angles)
    signed = jnp.sin(angles) * jnp.where(lane % HEAD_WIDTH < half, -1.0, 1.0)[None]
    seg_row = segment_ids.astype(f32)
    bias_row, rate_row = padded(step_bias), padded(decay_log)
    skip_row = jnp.repeat(skip_gain, MP)[None]
    own = place.astype(jnp.int32)[None]
    v, (in_full, qkv_full, mix_full, attn_full, gate_full, down_full) = forward_part(
        tokens[0], seg_row, norm_gain[None], cosine, signed, bias_row, rate_row, conv_weight, conv_bias[None],
        mixer_gain[None], skip_row, (in_proj, qkv_proj, mixer_out, attn_proj, gate_up, down_proj),
        (4, 2, 2, 2, 4, 4),
    )
    normed, attended, gated, mixer_y, act, dt, cum = (
        v[n] for n in ("normed", "attended", "gated", "y", "act", "dt", "cum")
    )
    gate_z, seg_wide, seg_col, kept, kv_all, query = (
        v[n] for n in ("z", "seg_wide", "seg_col", "kept", "kv", "query")
    )
    attended_t, log_total, conv_ext, step_raw = (v[n] for n in ("attended_t", "log_total", "conv", "raw"))
    length = kv_all.shape[0]
    token_rows = tokens[0].astype(f32)
    _, norm_pull = jax.vjp(rms_scale, token_rows, norm_gain)
    hidden = token_rows + (dot_nn(attended, attn_full) + dot_nn(gated, mix_full))
    ffn_in32, ffn_pull = jax.vjp(rms_scale, hidden, ffn_gain)
    ffn_in = low(ffn_in32)
    gates = dot_nn(ffn_in, gate_full)

    def swiglu(values):
        return jax.nn.silu(values[:, :FF]) * values[:, FF:]

    act32, act_pull = jax.vjp(swiglu, gates)
    inner = low(act32)
    result = hidden + dot_nn(inner, down_full)
    back_rows = cotangent[0]
    down_piece = reduced(contract(inner, back_rows))
    (gates_grad,) = act_pull(dot_nt(back_rows, down_full))
    gates_grad = low(gates_grad)
    gate_piece = reduced(contract(ffn_in, gates_grad))
    hidden_extra, ffn_gain_grad = ffn_pull(dot_nt(gates_grad, gate_full))
    hidden_grad = back_rows.astype(f32) + hidden_extra
    branch = low(hidden_grad)
    attn_piece = reduced(contract(attended, branch))
    attended_grad = low(dot_nt(branch, attn_full))
    mixer_piece = reduced(contract(gated, branch))
    gated_grad = low(dot_nt(branch, mix_full))

    y_grad, gate_z_grad, mixer_gain_grad, state_grad = call(
        gate_back_kernel,
        [((count, DI), f32), ((count, DI), bf16), ((1, DI), f32), ((NS, DI), f32)],
        (gated_grad, mixer_y, act, gate_z, dt, cum, seg_wide, mixer_gain[None], skip_row),
    )
    grads = lax.all_gather(low(state_grad), "seq").astype(f32)
    passings = lax.all_gather(v["passing"], "seq")
    later = jnp.zeros((NS, DI), f32)
    for k in reversed(range(devices)):
        later = jnp.where(k > place, passings[k] * later + grads[k], later)

    query_grad, kv_grad = call(
        attend_back_kernel,
        [((count, 512), bf16), ((length, 256), bf16)],
        (own, query, kv_all, seg_col, seg_row, attended_grad, attended_t, log_total, cosine, signed),
        (
            ((count, count), f32),
            ((4, count, 128), bf16),
            ((4, count, 128), bf16),
            ((2, count, 128), f32),
            ((2, count, 128), f32),
            ((QUERY_HEADS, count), f32),
            ((512, count), f32),
            ((QUERY_HEADS, count, 128), bf16),
            ((QUERY_HEADS, count, 128), bf16),
        ),
        smem,
    )
    kv_own = lax.psum_scatter(kv_grad, "seq", scatter_dimension=0, tiled=True).astype(f32)

    def swap(values):
        shaped = values.reshape(count, 2, 2, half)
        return shaped[:, :, ::-1].reshape(count, 128)

    key_grad = kv_own[:, :128]
    key_grad = key_grad * cosine + swap(key_grad * signed)
    qkv_grad = jnp.concatenate([query_grad, low(key_grad), low(kv_own[:, 128:])], axis=1)
    qkv_piece = reduced(contract(normed, qkv_grad))
    normed_grad = dot_nt(qkv_grad, qkv_full)

    raw_grad, conv_grad, conv_weight_grad, conv_bias_grad, rate_grad, bias_grad, skip_grad = call(
        back_kernel,
        [
            ((count, 128), f32),
            ((count + EDGE, CW), f32),
            ((KC, CW), f32),
            ((1, CW), f32),
            ((1, 128), f32),
            ((1, 128), f32),
            ((1, 128), f32),
        ],
        (
            act, dt, cum, seg_wide, seg_row, step_raw, bias_row, rate_row, kept,
            mixer_y, y_grad, later, conv_ext, conv_weight, conv_bias[None], skip_row,
        ),
        (((count, CW), f32), ((NS, DI), f32), ((count + 2 * EDGE, 128), f32)),
    )
    edge_back = shifted(conv_grad[:EDGE], "seq", -1)
    conv_grad = conv_grad[EDGE:] + jnp.pad(edge_back, ((count - EDGE, 0), (0, 0)))
    mixed_grad = jnp.concatenate([gate_z_grad, low(conv_grad), low(raw_grad[:, :MH])], axis=1)
    in_piece = reduced(contract(normed, mixed_grad))
    normed_grad = normed_grad + dot_nt(mixed_grad, in_full)
    rows_extra, norm_gain_grad = norm_pull(normed_grad)
    input_grad = hidden_grad + rows_extra
    pieces = (in_piece, mixer_piece, qkv_piece, attn_piece, gate_piece, down_piece)
    rows = (
        norm_gain_grad,
        ffn_gain_grad,
        mixer_gain_grad,
        conv_weight_grad,
        conv_bias_grad,
        rate_grad,
        bias_grad,
        skip_grad,
    )
    flat = jnp.concatenate([row.reshape(-1) for row in rows])
    flat = jnp.pad(flat, (0, 16384 - flat.shape[0])).reshape(16, 1024)
    *shards, flat = reduce_all(pieces, flat, (4, 2, 2, 2, 4, 4))
    shards = [shard.astype(f32) for shard in shards]
    flat, small, at = flat.reshape(-1), [], 0
    for row, keep in zip(rows, (None, None, None, None, None, MH, MH, MH)):
        part = flat[at : at + row.size].reshape(row.shape)
        at += row.size
        part = part[:, :keep] if keep else part
        small.append(part if part.shape[0] == KC else part.reshape(-1))
    return (low(result)[None], input_grad[None], *small, *shards)


def solution(mesh):
    rows, whole, split_rows = P("fsdp", "seq", None), P(), P("fsdp", None)
    return jax.shard_map(
        on_device,
        mesh=mesh,
        in_specs=(rows, rows, P("fsdp", "seq"), *[whole] * 8, *[split_rows] * 6),
        out_specs=(rows, rows, *[whole] * 8, *[split_rows] * 6),
        check_vma=False,
    )
```

```python
import jax
import jax.numpy as jnp
from jax import lax
from jax.experimental import pallas as pl
from jax.experimental.pallas import tpu as pltpu
from jax.sharding import PartitionSpec as P

FF = 2048
QUERY_HEADS = 8
KEY_VALUE_HEADS = 2
HEAD_WIDTH = 64
MH = 24
MP = 64
NS = 128
KC = 4
SUB = 128
DI = 1536
CW = 1792
EDGE = 8

epsilon = 1e-05
rope_base = 100000000000.0
highest = lax.Precision.HIGHEST
f32 = jnp.float32
bf16 = jnp.bfloat16


def dot_nn(left, right):
    return jnp.dot(left, right, preferred_element_type=jnp.float32)


def dot_nt(left, right):
    return lax.dot_general(
        left, right, (((1,), (1,)), ((), ())), preferred_element_type=jnp.float32
    )


def dot_tn(left, right):
    return lax.dot_general(
        left, right, (((0,), (0,)), ((), ())), preferred_element_type=jnp.float32
    )


def exact(left, right):
    return jnp.dot(left, right, precision=highest, preferred_element_type=jnp.float32)


def low(values):
    return values.astype(jnp.bfloat16)


def split(values):
    top = low(values)
    return top, low(values - top.astype(jnp.float32))


def iota(shape, axis):
    return lax.broadcasted_iota(jnp.int32, shape, axis)


def spreader():
    return low(jnp.where(iota((128, DI), 1) // MP == iota((128, DI), 0), 1.0, 0.0))


def widen(values, spread):
    top, rest = split(values)
    return dot_nn(top, spread) + dot_nn(rest, spread)


def widen_row(row, spread):
    return widen(jnp.broadcast_to(row, (8, 128)), spread)[0:1]


def head_sums(values, spread):
    top, rest = split(values)
    return dot_nt(top, spread) + dot_nt(rest, spread)


def softplus(values):
    return jnp.maximum(values, 0.0) + jnp.log1p(jnp.exp(-jnp.abs(values)))


def sigmoid(values):
    return 1.0 / (1.0 + jnp.exp(-values))


def lane_halves(rows):
    lane = iota((rows, 128), 1)
    return lane < MP


def rounded_to(values):
    return low(values).astype(jnp.float32)


def front_conv(conv_ref, seg_ref, weight_ref, cbias_ref, act_ref):
    chunks = act_ref.shape[0] // SUB

    def tile(j, carry):
        col = pl.ds(pl.multiple_of(j * 128, 128), 128)
        for c in range(chunks):
            r0 = c * SUB
            seg = seg_ref[pl.ds(r0 + 8, SUB), :]
            total = jnp.broadcast_to(cbias_ref[0:1, col], (SUB, 128))
            for k in range(KC):
                x = rounded_to(conv_ref[pl.ds(r0 + 9 - KC + k, SUB), col])
                if k < KC - 1:
                    x = jnp.where(seg_ref[pl.ds(r0 + 9 - KC + k, SUB), :] == seg, x, 0.0)
                total = total + weight_ref[k : k + 1, col] * x
            act_ref[pl.ds(r0, SUB), col] = low(total * sigmoid(total))
        return carry

    lax.fori_loop(0, CW // 128, tile, 0)


def front_state(seg_ref, raw_ref, bias_ref, rate_ref, act_ref, dt_ref, cum_ref, end_ref, pass_ref):
    chunks = raw_ref.shape[0] // SUB
    spread = spreader()
    lower = jnp.where(iota((SUB, SUB), 0) >= iota((SUB, SUB), 1), 1.0, 0.0)
    end_ref[...] = jnp.zeros_like(end_ref)
    gain = jnp.ones((1, 128), jnp.float32)
    for c in range(chunks):
        rows = pl.ds(c * SUB, SUB)
        dt = softplus(raw_ref[rows, :] + bias_ref[...])
        cum = exact(lower, -dt * jnp.exp(rate_ref[...]))
        dt_ref[rows, :] = dt
        cum_ref[rows, :] = cum
        seg = seg_ref[pl.ds(c * SUB + 8, SUB), :]
        before = seg_ref[pl.ds(c * SUB + 7, 1), :]
        last = seg[SUB - 1 :, :]
        end = cum[SUB - 1 :, :]
        weight = jnp.where(seg == last, jnp.exp(end - cum), 0.0) * dt
        passing = jnp.where(last == before, jnp.exp(end), 0.0)
        gain = gain * passing
        values = act_ref[rows, 0:DI].astype(jnp.float32)
        fresh = dot_tn(act_ref[rows, DI : DI + NS], low(widen(weight, spread) * values))
        end_ref[...] = widen_row(passing, spread) * end_ref[...] + fresh
    pass_ref[...] = widen_row(gain, spread)


def mid_kernel(act_ref, dt_ref, cum_ref, seg_ref, segrow_ref, state_ref, z_ref, gain_ref, skip_ref,
               y_ref, gated_ref, kept_ref, carry_ref, first, until):
    spread = spreader()
    if first == 0:
        carry_ref[...] = state_ref[...]
    half = lane_halves(SUB)

    def chunk(c, nothing):
        r0 = pl.multiple_of(c * SUB, SUB)
        rows = pl.ds(r0, SUB)
        dt, cum = dt_ref[rows, :], cum_ref[rows, :]
        cum_t = cum.T
        seg = seg_ref[pl.ds(pl.multiple_of(r0 + 8, 8), SUB), :]
        before = seg_ref[pl.ds(pl.multiple_of(r0, 8), 8), :][7:8]
        last, end = seg[SUB - 1 :, :], cum[SUB - 1 :, :]
        keys, reads = act_ref[rows, DI : DI + NS], act_ref[rows, DI + NS : CW]
        affinity = dot_nt(reads, keys)
        allowed = (iota((SUB, SUB), 0) >= iota((SUB, SUB), 1)) & (seg == segrow_ref[0:1, rows])
        state = low(carry_ref[...])
        kept_ref[pl.ds(c, 1)] = state[None]
        entry = widen(jnp.where(seg == before, jnp.exp(cum), 0.0), spread)
        y_ref[rows, :] = dot_nn(reads, state) * entry
        values = act_ref[rows, 0:DI].astype(jnp.float32)
        scaled = values * widen(dt, spread)
        weight = jnp.where(seg == last, jnp.exp(end - cum), 0.0)
        passing = jnp.where(last == before, jnp.exp(end), 0.0)
        fresh = dot_tn(keys, low(widen(weight, spread) * scaled))
        carry_ref[...] = widen_row(passing, spread) * carry_ref[...] + fresh
        for pair in range(MH // 2):
            cols = slice(pair * 128, pair * 128 + 128)
            parts = []
            for h in (2 * pair, 2 * pair + 1):
                gap = jnp.where(allowed, cum[:, h : h + 1] - cum_t[h : h + 1, :], -1e30)
                parts.append(low(jnp.exp(gap) * affinity))
            v = scaled[:, cols]
            right = jnp.concatenate([low(jnp.where(half, v, 0.0)), low(jnp.where(half, 0.0, v))], 0)
            y_ref[rows, cols] = y_ref[rows, cols] + dot_nn(jnp.concatenate(parts, 1), right)
        z = z_ref[rows, :]
        g = (y_ref[rows, :] + skip_ref[...] * values) * (z * sigmoid(z))
        scale = lax.rsqrt(jnp.mean(g * g, axis=1, keepdims=True) + epsilon)
        gated_ref[rows, :] = low(g * scale * gain_ref[...])
        return nothing

    lax.fori_loop(first, until, chunk, 0)


def gate_back_kernel(grad_ref, y_ref, act_ref, z_ref, dt_ref, cum_ref, seg_ref, gain_ref, skip_ref,
                     ygrad_ref, zgrad_ref, gain_grad_ref, state_grad_ref):
    chunks = act_ref.shape[0] // SUB
    spread = spreader()
    gain_grad_ref[...] = jnp.zeros_like(gain_grad_ref)
    state_grad_ref[...] = jnp.zeros_like(state_grad_ref)

    def chunk(i, nothing):
        c = chunks - 1 - i
        r0 = pl.multiple_of(c * SUB, SUB)
        rows = pl.ds(r0, SUB)
        values = act_ref[rows, 0:DI].astype(jnp.float32)
        z = z_ref[rows, :]
        sig = sigmoid(z)
        silu = z * sig
        u = y_ref[rows, :] + skip_ref[...] * values
        g = u * silu
        grad = grad_ref[rows, :].astype(jnp.float32)
        scale = lax.rsqrt(jnp.mean(g * g, axis=1, keepdims=True) + epsilon)
        unit = g * scale
        gain_grad_ref[...] += jnp.sum(grad * unit, axis=0, keepdims=True)
        h = grad * gain_ref[...]
        dg = scale * (h - unit * jnp.mean(h * unit, axis=1, keepdims=True))
        dy = dg * silu
        ygrad_ref[rows, :] = dy
        zgrad_ref[rows, :] = low(dg * u * (sig * (1.0 + z * (1.0 - sig))))
        cum = cum_ref[rows, :]
        seg = seg_ref[pl.ds(pl.multiple_of(r0 + 8, 8), SUB), :]
        before = seg_ref[pl.ds(pl.multiple_of(r0, 8), 8), :][7:8]
        last, end = seg[SUB - 1 :, :], cum[SUB - 1 :, :]
        entry = widen(jnp.where(seg == before, jnp.exp(cum), 0.0), spread)
        passing = jnp.where(last == before, jnp.exp(end), 0.0)
        fresh = dot_tn(act_ref[rows, DI + NS : CW], low(entry * dy))
        state_grad_ref[...] = widen_row(passing, spread) * state_grad_ref[...] + fresh
        return nothing

    lax.fori_loop(0, chunks, chunk, 0)


def back_kernel(act_ref, dt_ref, cum_ref, seg_ref, segrow_ref, raw_ref, bias_ref, rate_ref, kept_ref,
                y_ref, ygrad_ref, later_ref, conv_ref, weight_ref, cbias_ref, skip_ref,
                raw_grad_ref, conv_grad_ref, weight_grad_ref, cbias_grad_ref, rate_grad_ref,
                bias_grad_ref, skip_grad_ref, act_grad_ref, carry_ref, pre_ref):
    rows_total = act_ref.shape[0]
    chunks = rows_total // SUB
    spread = spreader()
    half = lane_halves(SUB)
    upper = jnp.where(iota((SUB, SUB), 1) >= iota((SUB, SUB), 0), 1.0, 0.0)
    rate = jnp.exp(rate_ref[...])
    carry_ref[...] = later_ref[...]
    rate_grad_ref[...] = jnp.zeros_like(rate_grad_ref)
    bias_grad_ref[...] = jnp.zeros_like(bias_grad_ref)
    skip_grad_ref[...] = jnp.zeros_like(skip_grad_ref)

    def chunk(i, nothing):
        c = chunks - 1 - i
        r0 = pl.multiple_of(c * SUB, SUB)
        rows = pl.ds(r0, SUB)
        dt, cum = dt_ref[rows, :], cum_ref[rows, :]
        cum_t = cum.T
        seg = seg_ref[pl.ds(pl.multiple_of(r0 + 8, 8), SUB), :]
        before = seg_ref[pl.ds(pl.multiple_of(r0, 8), 8), :][7:8]
        last, end = seg[SUB - 1 :, :], cum[SUB - 1 :, :]
        keys, reads = act_ref[rows, DI : DI + NS], act_ref[rows, DI + NS : CW]
        affinity = dot_nt(keys, reads)
        allowed = (iota((SUB, SUB), 1) >= iota((SUB, SUB), 0)) & (seg == segrow_ref[0:1, rows])
        values = act_ref[rows, 0:DI].astype(jnp.float32)
        wide_dt = widen(dt, spread)
        scaled = values * wide_dt
        scaled_low = low(scaled)
        dy = ygrad_ref[rows, :]
        dy_low = low(dy)
        state, carry = kept_ref[pl.ds(c, 1)][0], carry_ref[...]
        carry_low = low(carry)
        wide_weight = widen(jnp.where(seg == last, jnp.exp(end - cum), 0.0), spread)
        wide_entry = widen(jnp.where(seg == before, jnp.exp(cum), 0.0), spread)
        wide_pass = widen_row(jnp.where(last == before, jnp.exp(end), 0.0), spread)
        from_state = dot_nn(keys, carry_low) * wide_weight
        mixed_grad = jnp.zeros((SUB, SUB), jnp.float32)
        for pair in range(MH // 2):
            cols = slice(pair * 128, pair * 128 + 128)
            v, d = scaled[:, cols], dy[:, cols]
            left = jnp.concatenate([low(jnp.where(half, v, 0.0)), low(jnp.where(half, 0.0, v))], 0)
            right = jnp.concatenate([low(jnp.where(half, d, 0.0)), low(jnp.where(half, 0.0, d))], 0)
            weight_grad = dot_nt(left, dy_low[:, cols])
            parts = []
            for n, h in enumerate((2 * pair, 2 * pair + 1)):
                gap = jnp.where(allowed, cum_t[h : h + 1, :] - cum[:, h : h + 1], -1e30)
                decay = jnp.exp(gap)
                parts.append(low(decay * affinity))
                mixed_grad = mixed_grad + decay * weight_grad[n * SUB : (n + 1) * SUB]
            act_grad_ref[rows, cols] = dot_nn(jnp.concatenate(parts, 1), right)
        x = act_grad_ref[rows, 0:DI] + from_state
        act_grad_ref[rows, 0:DI] = wide_dt * x + skip_ref[...] * dy
        mixed_low = low(mixed_grad)
        act_grad_ref[rows, DI : DI + NS] = dot_nn(mixed_low, reads) + dot_nt(
            low(wide_weight * scaled), carry_low
        )
        entered = low(wide_entry * dy)
        act_grad_ref[rows, DI + NS : CW] = dot_tn(mixed_low, keys) + dot_nt(entered, state)
        scaled_exact = scaled_low.astype(jnp.float32)
        direct = head_sums(values * x, spread)
        given = head_sums(scaled_exact * x, spread)
        taken = head_sums(dy_low.astype(jnp.float32) * y_ref[rows, :], spread)
        tail = jnp.sum(scaled_exact * from_state, axis=0, keepdims=True) + jnp.sum(
            wide_pass * carry * state.astype(jnp.float32), axis=0, keepdims=True
        )
        tail = head_sums(jnp.broadcast_to(tail, (8, DI)), spread)[0:1]
        decay_grad = exact(upper, taken - given) + tail
        rate_grad_ref[...] += jnp.sum(decay_grad * (-dt * rate), axis=0, keepdims=True)
        dt_grad = direct - decay_grad * rate
        raw_grad = dt_grad * sigmoid(raw_ref[rows, :] + bias_ref[...])
        raw_grad_ref[rows, :] = raw_grad
        bias_grad_ref[...] += jnp.sum(raw_grad, axis=0, keepdims=True)
        skip_sum = jnp.sum(dy * values, axis=0, keepdims=True)
        skip_grad_ref[...] += head_sums(jnp.broadcast_to(skip_sum, (8, DI)), spread)[0:1]
        carry_ref[...] = wide_pass * carry + dot_tn(reads, entered)
        return nothing

    lax.fori_loop(0, chunks, chunk, 0)
    weight_grad_ref[...] = jnp.zeros_like(weight_grad_ref)
    pre_ref[0:8, :] = jnp.zeros((8, 128), jnp.float32)
    pre_ref[rows_total + 8 : rows_total + 16, :] = jnp.zeros((8, 128), jnp.float32)

    def tile(j, carry):
        col = pl.ds(pl.multiple_of(j * 128, 128), 128)
        sums = [jnp.zeros((1, 128), jnp.float32) for _ in range(KC + 1)]
        for c in range(chunks):
            r0 = c * SUB
            seg = seg_ref[pl.ds(r0 + 8, SUB), :]
            total = jnp.broadcast_to(cbias_ref[0:1, col], (SUB, 128))
            taps = []
            for k in range(KC):
                x = rounded_to(conv_ref[pl.ds(r0 + 9 - KC + k, SUB), col])
                if k < KC - 1:
                    x = jnp.where(seg_ref[pl.ds(r0 + 9 - KC + k, SUB), :] == seg, x, 0.0)
                taps.append(x)
                total = total + weight_ref[k : k + 1, col] * x
            sig = sigmoid(total)
            pre = act_grad_ref[pl.ds(r0, SUB), col] * (sig * (1.0 + total * (1.0 - sig)))
            pre_ref[pl.ds(r0 + 8, SUB), :] = pre
            for k in range(KC):
                sums[k] = sums[k] + jnp.sum(pre * taps[k], axis=0, keepdims=True)
            sums[KC] = sums[KC] + jnp.sum(pre, axis=0, keepdims=True)
        for k in range(KC):
            weight_grad_ref[k : k + 1, col] = sums[k]
        cbias_grad_ref[0:1, col] = sums[KC]
        for c in range(chunks + 1):
            r0 = c * SUB
            size = SUB if c < chunks else 8
            seg = seg_ref[pl.ds(r0, size), :]
            total = jnp.zeros((size, 128), jnp.float32)
            for back in range(KC):
                x = pre_ref[pl.ds(r0 + back, size), :]
                if back:
                    x = jnp.where(seg_ref[pl.ds(r0 + back, size), :] == seg, x, 0.0)
                total = total + weight_ref[KC - 1 - back : KC - back, col] * x
            conv_grad_ref[pl.ds(r0, size), col] = total
        return carry

    lax.fori_loop(0, CW // 128, tile, 0)


def partner(values):
    lane = iota(values.shape, 1)
    half = HEAD_WIDTH // 2
    return jnp.where(
        lane % HEAD_WIDTH < half, pltpu.roll(values, 128 - half, 1), pltpu.roll(values, half, 1)
    )


def rotate_kernel(qkv_ref, cos_ref, sin_ref, query_ref, kv_ref):
    cos, sin = cos_ref[...], sin_ref[...]
    for g in range(5):
        x = qkv_ref[:, g * 128 : g * 128 + 128]
        x = low(x * cos + partner(x) * sin)
        if g < 4:
            query_ref[:, g * 128 : g * 128 + 128] = x * jnp.bfloat16(HEAD_WIDTH**-0.5)
        else:
            kv_ref[:, 0:128] = x
    kv_ref[:, 128:256] = low(qkv_ref[:, 640:768])


def lane_variants(block, out_ref):
    other = pltpu.roll(block, 64, 1)
    half = iota(block.shape, 1) < HEAD_WIDTH
    out_ref[0] = low(jnp.where(half, block, 0.0))
    out_ref[1] = low(jnp.where(half, 0.0, other))
    out_ref[2] = low(jnp.where(half, other, 0.0))
    out_ref[3] = low(jnp.where(half, 0.0, block))


def attend_bias(b, own, rows, segcol_ref, segrow_ref, bias_ref):
    seg = segcol_ref[pl.ds(pl.multiple_of(b * rows, rows), rows), :]
    seg = jnp.concatenate([seg] * (rows // 128), 1)
    causal = (iota((rows, rows), 0) - iota((rows, rows), 1)) <= jnp.where(b < own, rows, 0)
    bias_ref[...] = jnp.where(causal & (seg == segrow_ref[...]), 0.0, -1e30)


def attend_start(top_ref, sum_ref, out_t_ref):
    top_ref[...] = jnp.full_like(top_ref, -1e30)
    sum_ref[...] = jnp.zeros_like(sum_ref)
    out_t_ref[...] = jnp.zeros_like(out_t_ref)


def attend_block(b, own, query_ref, kv_ref, segcol_ref, segrow_ref, out_t_ref, bias_ref, keys_ref,
                 values_t_ref, top_ref, sum_ref):
    rows = query_ref.shape[0]
    at = pl.ds(pl.multiple_of(b * rows, rows), rows)
    attend_bias(b, own, rows, segcol_ref, segrow_ref, bias_ref)
    lane_variants(kv_ref[at, 0:128].astype(jnp.float32), keys_ref)
    values_t_ref[...] = low(kv_ref[at, 128:256].astype(jnp.float32).T)

    def pair(g, nothing):
        kv = g // 2
        query = query_ref[:, pl.ds(pl.multiple_of(g * 128, 128), 128)]
        for side in range(2):
            h = g * 2 + side
            row = pl.ds(pl.multiple_of(h * 8, 8), 8)
            scores = dot_nt(keys_ref[kv * 2 + side], query)
            scores = scores + bias_ref[...]
            old = top_ref[row, :][0:1]
            top = jnp.maximum(old, jnp.max(scores, axis=0, keepdims=True))
            p = jnp.exp(scores - top)
            fade = jnp.exp(old - top)
            total = sum_ref[row, :][0:1] * fade + jnp.sum(p, 0, keepdims=True)
            top_ref[row, :] = jnp.broadcast_to(top, (8, rows))
            sum_ref[row, :] = jnp.broadcast_to(total, (8, rows))
            at_h = pl.ds(pl.multiple_of(h * 64, 64), 64)
            values_t = values_t_ref[pl.ds(pl.multiple_of(kv * 64, 64), 64), :]
            out_t_ref[at_h, :] = out_t_ref[at_h, :] * fade + dot_nn(values_t, low(p))
        return nothing

    lax.fori_loop(0, QUERY_HEADS // 2, pair, 0)


def attend_finish(out_ref, out_t_ref, total_ref, top_ref, sum_ref):
    for h in range(QUERY_HEADS):
        at_h = slice(h * 64, h * 64 + 64)
        total_ref[h : h + 1, :] = top_ref[h * 8 : h * 8 + 1, :] + jnp.log(sum_ref[h * 8 : h * 8 + 1, :])
        out_t_ref[at_h, :] = out_t_ref[at_h, :] / sum_ref[h * 8 : h * 8 + 1, :]
    out_ref[...] = low(out_t_ref[...].T)


def attend_back_kernel(own_ref, query_ref, kv_ref, segcol_ref, segrow_ref, grad_ref, out_t_ref,
                       total_ref, cos_ref, sin_ref, query_grad_ref, kv_grad_ref,
                       bias_ref, keys_ref, values_ref, dkeys_ref, dvalues_ref, spread_ref, dq_ref,
                       query_half_ref, grad_half_ref):
    rows = query_ref.shape[0]
    own = own_ref[0]
    kv_grad_ref[...] = jnp.zeros_like(kv_grad_ref)
    dq_ref[...] = jnp.zeros_like(dq_ref)
    grad_t = grad_ref[...].astype(jnp.float32).T
    product = grad_t * out_t_ref[...]
    for h in range(QUERY_HEADS):
        spread_ref[h : h + 1, :] = jnp.sum(product[h * 64 : h * 64 + 64, :], 0, keepdims=True)
        g = h // 2
        half = (iota((rows, 128), 1) < HEAD_WIDTH) == (h % 2 == 0)
        for src, dst in ((query_ref, query_half_ref), (grad_ref, grad_half_ref)):
            dst[h] = low(jnp.where(half, src[:, g * 128 : g * 128 + 128].astype(jnp.float32), 0.0))

    def block(b, nothing):
        at = pl.ds(pl.multiple_of(b * rows, rows), rows)
        attend_bias(b, own, rows, segcol_ref, segrow_ref, bias_ref)
        keys = kv_ref[at, 0:128].astype(jnp.float32)
        lane_variants(keys, keys_ref)
        lane_variants(kv_ref[at, 128:256].astype(jnp.float32), values_ref)
        keys_t = low(keys.T)
        dkeys_ref[...] = jnp.zeros_like(dkeys_ref)
        dvalues_ref[...] = jnp.zeros_like(dvalues_ref)
        for h in range(QUERY_HEADS):
            g, kv = h // 2, h // 4
            lanes = slice(g * 128, g * 128 + 128)
            scores = dot_nt(keys_ref[kv * 2 + h % 2], query_ref[:, lanes]) + bias_ref[...]
            p = jnp.exp(scores - total_ref[h : h + 1, :])
            dp = dot_nt(values_ref[kv * 2 + h % 2], grad_ref[:, lanes])
            ds = low(p * (dp - spread_ref[h : h + 1, :]))
            dkeys_ref[kv] += dot_nn(ds, query_half_ref[h])
            dvalues_ref[kv] += dot_nn(low(p), grad_half_ref[h])
            dq_ref[h * 64 : h * 64 + 64, :] += dot_nn(keys_t[kv * 64 : kv * 64 + 64, :], ds)
        half = iota((rows, 128), 1) < HEAD_WIDTH
        for src, lanes in ((dkeys_ref, slice(0, 128)), (dvalues_ref, slice(128, 256))):
            first, second = src[0], src[1]
            kv_grad_ref[at, lanes] = low(
                jnp.where(half, first + pltpu.roll(first, 64, 1), second + pltpu.roll(second, 64, 1))
            )
        return nothing

    lax.fori_loop(0, own + 1, block, 0)
    dq = dq_ref[...].T * (HEAD_WIDTH**-0.5)
    cos, sin = cos_ref[...], sin_ref[...]
    for g in range(4):
        x = dq[:, g * 128 : g * 128 + 128]
        query_grad_ref[:, g * 128 : g * 128 + 128] = low(x * cos + partner(x * sin))


vmem = pl.BlockSpec(memory_space=pltpu.VMEM)
smem = pl.BlockSpec(memory_space=pltpu.SMEM)


def call(kernel, outs, args, scratch=(), first=vmem, flops=10**9):
    return pl.pallas_call(
        kernel,
        out_shape=[jax.ShapeDtypeStruct(shape, kind) for shape, kind in outs],
        in_specs=[first] + [vmem] * (len(args) - 1),
        out_specs=[vmem] * len(outs),
        scratch_shapes=[pltpu.VMEM(shape, kind) for shape, kind in scratch],
        compiler_params=pltpu.CompilerParams(vmem_limit_bytes=56 * 2**20),
        cost_estimate=pl.CostEstimate(flops=flops, bytes_accessed=10**7, transcendentals=10**6),
    )(*args)


MESH = pl.DeviceIdType.MESH


def position_bits(count):
    index = lax.axis_index("fsdp")
    return [(index // (1 << b)) % 2 for b in reversed(range(count))]


def across(bits, axis):
    count = len(bits)
    index = lax.axis_index("fsdp")
    step = 1 << (count - 1 - axis)
    return (index + step * (1 - 2 * bits[axis]), lax.axis_index("seq"))


def along(by):
    return (lax.axis_index("fsdp"), lax.axis_index("seq") + by)


class Item:
    def __init__(self, number, weight, start, size, order):
        self.number, self.weight, self.start, self.size, self.order = number, weight, start, size, order


def plan_items(shapes, parts, bit_count):
    items = []
    for w, ((rows, _), count) in enumerate(zip(shapes, parts)):
        for p in range(count):
            turn = p % max(bit_count - 1, 1)
            ici = list(range(bit_count - 1))
            order = [bit_count - 1] + ici[turn:] + ici[:turn]
            items.append(Item(len(items), w, p * (rows // count), rows // count, order))
    return items


class Reducer:
    def __init__(self, bit_count, depth, items, whole, own, landed, zin, zmid, total, out, send, recv, own_sem):
        self.bit_count, self.depth, self.items = bit_count, depth, items
        self.whole, self.own, self.landed = whole, own, landed
        self.zin, self.zmid, self.total, self.out = zin, zmid, total, out
        self.send, self.recv, self.own_sem = send, recv, own_sem
        self.bits = position_bits(bit_count)
        self.place = lax.axis_index("seq")

    def rows(self, item):
        return pl.ds(item.start, item.size)

    def left(self, item, stage):
        return sorted(item.order[stage:])

    def pick(self, item, stage, mine):
        axis = item.order[stage]
        at = self.left(item, stage).index(axis)
        bit = self.bits[axis] if mine else 1 - self.bits[axis]
        lead = [slice(None)] * (self.bit_count - stage)
        lead[at] = bit
        return (*lead, self.rows(item))

    def source(self, item, stage):
        if stage == 0:
            return self.whole[item.weight]
        return self.own[item.weight] if stage == 1 else self.landed[stage - 1][item.weight]

    def copy(self, item, stage):
        lead = (slice(None),) * (self.bit_count - stage - 1)
        return pltpu.make_async_remote_copy(
            self.source(item, stage).at[self.pick(item, stage, False)],
            self.landed[stage][item.weight].at[(*lead, self.rows(item))],
            self.send.at[item.number, stage],
            self.recv.at[item.number, stage],
            device_id=across(self.bits, item.order[stage]),
            device_id_type=MESH,
        )

    def own_copy(self, item):
        lead = (slice(None),) * (self.bit_count - 1)
        return pltpu.make_async_copy(
            self.whole[item.weight].at[self.pick(item, 0, True)],
            self.own[item.weight].at[(*lead, self.rows(item))],
            self.own_sem.at[item.number],
        )

    def begin(self, item):
        self.copy(item, 0).start()
        self.own_copy(item).start()

    def add(self, dst, dst_lead, other, other_lead, item):
        group = 16

        def step(i, nothing):
            at = pl.ds(pl.multiple_of(item.start + i * group, group), group)
            dst[(*dst_lead, at)] = low(
                dst[(*dst_lead, at)].astype(f32) + other[(*other_lead, at)].astype(f32)
            )
            return nothing

        lax.fori_loop(0, item.size // group, step, 0)

    def advance(self, item, stage):
        self.copy(item, stage).wait_recv()
        landed = self.landed[stage][item.weight]
        kept = self.bit_count - stage - 1
        places = [[(i >> (kept - 1 - b)) & 1 for b in range(kept)] for i in range(1 << kept)]
        if stage == 0:
            self.own_copy(item).wait()
            for lead in places:
                self.add(self.own[item.weight], lead, landed, lead, item)
        else:
            source = self.source(item, stage)
            axis = item.order[stage]
            at = self.left(item, stage).index(axis)
            for lead in places:
                from_lead = [*lead[:at], self.bits[axis], *lead[at:]]
                self.add(landed, lead, source, from_lead, item)
        if stage + 1 < self.bit_count:
            self.copy(item, stage + 1).start()

    def z_copy(self, item, kind, by):
        w, rows = item.weight, self.rows(item)
        last = self.landed[self.bit_count - 1][w]
        src, dst = {
            "in": (last, self.zin[w]),
            "mid": (last, self.zmid[w]),
            "out": (self.total[w], self.total[w]),
        }[kind]
        slot = self.bit_count + {"in": 0, "mid": 1, "out": 2}[kind]
        return pltpu.make_async_remote_copy(
            src.at[rows],
            dst.at[rows],
            self.send.at[item.number, slot],
            self.recv.at[item.number, slot],
            device_id=along(by),
            device_id_type=MESH,
        )

    def sides(self):
        half = self.depth // 2
        outermost = (self.place == 0) | (self.place == self.depth - 1)
        middle = (self.place == half - 1) | (self.place == half)
        inward = 1 - 2 * (self.place // half)
        return outermost, middle, inward

    def z_first(self, item):
        outermost, middle, inward = self.sides()

        @pl.when(outermost & jnp.logical_not(middle))
        def _():
            self.z_copy(item, "in", inward).start()

    def z_second(self, item):
        outermost, middle, inward = self.sides()

        @pl.when(jnp.logical_not(outermost))
        def _():
            self.z_copy(item, "in", -inward).wait_recv()
            self.add(self.landed[self.bit_count - 1][item.weight], (), self.zin[item.weight], (), item)

            @pl.when(jnp.logical_not(middle))
            def _():
                self.z_copy(item, "in", inward).start()

        @pl.when(middle)
        def _():
            self.z_copy(item, "mid", inward).start()

    def z_third(self, item):
        outermost, middle, inward = self.sides()

        @pl.when(middle)
        def _():
            self.z_copy(item, "mid", inward).wait_recv()
            group = 16
            last, other = self.landed[self.bit_count - 1][item.weight], self.zmid[item.weight]

            def step(i, nothing):
                at = pl.ds(pl.multiple_of(item.start + i * group, group), group)
                self.total[item.weight][at] = low(last[at].astype(f32) + other[at].astype(f32))
                return nothing

            lax.fori_loop(0, item.size // group, step, 0)

            @pl.when(jnp.logical_not(outermost))
            def _():
                self.z_copy(item, "out", -inward).start()

    def z_fourth(self, item):
        outermost, middle, inward = self.sides()

        @pl.when(jnp.logical_not(middle))
        def _():
            self.z_copy(item, "out", inward).wait_recv()

            @pl.when(jnp.logical_not(outermost))
            def _():
                self.z_copy(item, "out", -inward).start()

        group = 16

        def step(i, nothing):
            at = pl.ds(pl.multiple_of(item.start + i * group, group), group)
            self.out[item.weight][at] = self.total[item.weight][at]
            return nothing

        lax.fori_loop(0, item.size // group, step, 0)

    def finish(self, item):
        outermost, middle, inward = self.sides()
        for stage in range(self.bit_count):
            self.copy(item, stage).wait_send()

        @pl.when(jnp.logical_not(middle))
        def _():
            self.z_copy(item, "in", inward).wait_send()

        @pl.when(middle)
        def _():
            self.z_copy(item, "mid", inward).wait_send()

        @pl.when(jnp.logical_not(outermost))
        def _():
            self.z_copy(item, "out", -inward).wait_send()

    def actions(self, lag, z_lag):
        steps = []
        for i, item in enumerate(self.items):
            for stage in range(self.bit_count):
                steps.append((i + lag * stage, stage, lambda item=item, s=stage: self.advance(item, s)))
            t = i + lag * (self.bit_count - 1)
            for n, run in enumerate((self.z_first, self.z_second, self.z_third, self.z_fourth)):
                steps.append((t + n * z_lag, self.bit_count + n, lambda item=item, run=run: run(item)))
        return [action for _, _, action in sorted(steps, key=lambda s: s[:2])]


def enter(bit_count, depth):
    bits = position_bits(bit_count)
    place = lax.axis_index("seq")
    barrier = pltpu.get_barrier_semaphore()
    for axis in range(bit_count):
        pl.semaphore_signal(barrier, inc=1, device_id=across(bits, axis), device_id_type=MESH)

    @pl.when(place > 0)
    def _():
        pl.semaphore_signal(barrier, inc=1, device_id=along(-1), device_id_type=MESH)

    @pl.when(place < depth - 1)
    def _():
        pl.semaphore_signal(barrier, inc=1, device_id=along(1), device_id_type=MESH)

    ends = jnp.where(place == 0, 1, 0) + jnp.where(place == depth - 1, 1, 0)
    pl.semaphore_wait(barrier, bit_count + 2 - ends)


def small_sum(bit_count, depth, src, buf, out, send, recv):
    bits = position_bits(bit_count)
    place = lax.axis_index("seq")
    half = depth // 2
    outermost = (place == 0) | (place == depth - 1)
    middle = (place == half - 1) | (place == half)
    inward = 1 - 2 * (place // half)

    def flip(stage):
        return pltpu.make_async_remote_copy(
            (src if stage == 0 else out.at[stage - 1]),
            buf.at[stage],
            send.at[stage],
            recv.at[stage],
            device_id=across(bits, bit_count - 1 - stage),
            device_id_type=MESH,
        )

    def z_copy(kind, by):
        n = bit_count + kind
        return pltpu.make_async_remote_copy(
            out.at[(bit_count - 1, bit_count, bit_count + 1)[kind]],
            (buf.at[bit_count], buf.at[bit_count + 1], out.at[bit_count + 1])[kind],
            send.at[n],
            recv.at[n],
            device_id=along(by),
            device_id_type=MESH,
        )

    def flip_done(stage):
        flip(stage).wait_recv()
        mine = src[...] if stage == 0 else out[stage - 1]
        out[stage] = mine + buf[stage]
        if stage + 1 < bit_count:
            flip(stage + 1).start()

    def z_in():
        @pl.when(jnp.logical_not(middle))
        def _():
            @pl.when(jnp.logical_not(outermost))
            def _():
                z_copy(0, -inward).wait_recv()
                out[bit_count - 1] = out[bit_count - 1] + buf[bit_count]

            z_copy(0, inward).start()

        @pl.when(middle)
        def _():
            out[bit_count] = out[bit_count - 1]

            @pl.when(jnp.logical_not(outermost))
            def _():
                z_copy(0, -inward).wait_recv()
                out[bit_count] = out[bit_count] + buf[bit_count]

            z_copy(1, inward).start()

    def z_mid():
        @pl.when(middle)
        def _():
            z_copy(1, inward).wait_recv()
            out[bit_count + 1] = out[bit_count] + buf[bit_count + 1]

    def z_out():
        @pl.when(jnp.logical_not(middle))
        def _():
            z_copy(2, inward).wait_recv()

        @pl.when(jnp.logical_not(outermost))
        def _():
            z_copy(2, -inward).start()

    def finish():
        for stage in range(bit_count):
            flip(stage).wait_send()

        @pl.when(jnp.logical_not(middle))
        def _():
            z_copy(0, inward).wait_send()

        @pl.when(middle)
        def _():
            z_copy(1, inward).wait_send()

        @pl.when(jnp.logical_not(outermost))
        def _():
            z_copy(2, -inward).wait_send()

    begin = lambda: flip(0).start()
    steps = [lambda s=s: flip_done(s) for s in range(bit_count)] + [z_in, z_mid, z_out]
    return begin, steps, finish


def bit_length(count):
    return count.bit_length() - 1


def reduce_all(gradients, small, parts):
    fsdp, depth = lax.axis_size("fsdp"), lax.axis_size("seq")
    bit_count = bit_length(fsdp)
    shapes = [(g.shape[0] // fsdp, g.shape[1]) for g in gradients]
    items = plan_items(shapes, parts, bit_count)
    count = len(shapes)

    def kernel(*refs):
        at = 0

        def take(n):
            nonlocal at
            at += n
            return refs[at - n : at]

        whole, (small_ref,) = take(count), take(1)
        out, (small_out,) = take(count), take(1)
        own = take(count)
        landed = [take(count) for _ in range(bit_count)]
        zin, zmid, total = take(count), take(count), take(count)
        (small_buf, small_work) = take(2)
        send, recv, own_sem, small_send, small_recv = take(5)
        enter(bit_count, depth)
        work = Reducer(bit_count, depth, items, whole, own, landed, zin, zmid, total, out, send, recv, own_sem)
        begin, steps, finish = small_sum(
            bit_count, depth, small_ref, small_buf, small_work, small_send, small_recv
        )
        begin()
        for item in items:
            work.begin(item)
        for n, action in enumerate(work.actions(2, 3)):
            action()
            if n % 2 == 1 and steps:
                steps.pop(0)()
        for step in steps:
            step()
        small_out[...] = small_work[bit_count + 1]
        for item in items:
            work.finish(item)
        finish()

    two = (2,) * bit_count
    stacks = [[pltpu.VMEM((*two[: bit_count - 1 - s], *shape), bf16) for shape in shapes] for s in range(bit_count)]
    flat = [pltpu.VMEM(shape, bf16) for shape in shapes]
    scratch = [*stacks[0], *[b for stage in stacks for b in stage], *flat, *flat, *flat]
    scratch += [pltpu.VMEM((bit_count + 2, *small.shape), f32)] * 2
    scratch += [
        pltpu.SemaphoreType.DMA((len(items), bit_count + 3)),
        pltpu.SemaphoreType.DMA((len(items), bit_count + 3)),
        pltpu.SemaphoreType.DMA((len(items),)),
        pltpu.SemaphoreType.DMA((bit_count + 3,)),
        pltpu.SemaphoreType.DMA((bit_count + 3,)),
    ]
    return pl.pallas_call(
        kernel,
        out_shape=[jax.ShapeDtypeStruct(shape, bf16) for shape in shapes]
        + [jax.ShapeDtypeStruct(small.shape, f32)],
        in_specs=[pl.BlockSpec(memory_space=pl.ANY)] * count + [vmem],
        out_specs=[vmem] * (count + 1),
        scratch_shapes=scratch,
        compiler_params=pltpu.CompilerParams(
            collective_id=0, has_side_effects=True, vmem_limit_bytes=60 * 2**20
        ),
    )(*[g.reshape(*two, *shape) for g, shape in zip(gradients, shapes)], small)


class Gatherer:
    def __init__(self, bit_count, items, shards, whole, loads, load_sem, cast_to, own_sem, send, recv):
        self.bit_count, self.items = bit_count, items
        self.shards, self.whole, self.loads, self.load_sem = shards, whole, loads, load_sem
        self.cast_to, self.own_sem, self.send, self.recv = cast_to, own_sem, send, recv
        self.bits = position_bits(bit_count)
        self.index = lax.axis_index("fsdp")
        self.ready = set()
        self.todo = []
        self.done = set()

    def block(self, axes):
        at = self.index
        for axis in axes:
            at = at + (1 << (self.bit_count - 1 - axis)) * (1 - 2 * self.bits[axis])
        return at

    def subsets(self, order):
        sets = [()]
        for axis in order:
            sets = sets + [(*s, axis) for s in sets]
        return sets

    def rows(self, item, axes):
        shard_rows = self.cast_to[item.weight].shape[0]
        return pl.ds(pl.multiple_of(self.block(axes) * shard_rows + item.start, 16), item.size)

    def copy(self, item, stage, number, axes):
        whole = self.whole[item.weight]
        at = self.rows(item, axes)
        src = self.cast_to[item.weight].at[pl.ds(item.start, item.size)] if not axes else whole.at[at]
        slot = (1 << stage) - 1 + number
        return pltpu.make_async_remote_copy(
            src,
            whole.at[at],
            self.send.at[item.number, slot],
            self.recv.at[item.number, slot],
            device_id=across(self.bits, item.order[stage]),
            device_id_type=MESH,
        )

    def landed(self, item, stage, number, axes):
        whole = self.whole[item.weight]
        at = self.rows(item, (*axes, item.order[stage]))
        slot = (1 << stage) - 1 + number
        return pltpu.make_async_remote_copy(
            whole.at[at],
            whole.at[at],
            self.send.at[item.number, slot],
            self.recv.at[item.number, slot],
            device_id=across(self.bits, item.order[stage]),
            device_id_type=MESH,
        )

    def load(self, weight):
        return pltpu.make_async_copy(self.shards[weight], self.loads[weight], self.load_sem.at[weight])

    def own(self, weight):
        rows = self.cast_to[weight].shape[0]
        return pltpu.make_async_copy(
            self.cast_to[weight],
            self.whole[weight].at[pl.ds(pl.multiple_of(self.index * rows, 16), rows)],
            self.own_sem.at[weight],
        )

    def begin(self, item):
        w = item.weight
        if w not in self.ready:
            self.ready.add(w)
            self.load(w).wait()
            group = 16

            def step(i, nothing):
                at = pl.ds(pl.multiple_of(i * group, group), group)
                self.cast_to[w][at] = low(self.loads[w][at])
                return nothing

            lax.fori_loop(0, self.cast_to[w].shape[0] // group, step, 0)
            self.own(w).start()
        for stage in range(self.bit_count):
            self.copy(item, stage, 0, ()).start()

    def advance(self, item, stage):
        before = self.subsets(item.order[:stage])
        for number, axes in enumerate(before):
            self.landed(item, stage, number, axes).wait_recv()
        for later in range(stage + 1, self.bit_count):
            sets = self.subsets(item.order[:later])
            for number, axes in enumerate(before):
                mine = (*axes, item.order[stage])
                self.copy(item, later, sets.index(mine), mine).start()
        if stage == self.bit_count - 1:
            self.done.add(item.number)

    def plan(self, lag):
        steps = []
        for i, item in enumerate(self.items):
            steps.append((i, 0, lambda item=item: self.begin(item)))
            for stage in range(self.bit_count):
                steps.append((i + lag * (stage + 1), stage + 1, lambda item=item, s=stage: self.advance(item, s)))
        self.todo = [action for _, _, action in sorted(steps, key=lambda s: s[:2])]

    def pump(self, count):
        for _ in range(min(count, len(self.todo))):
            self.todo.pop(0)()

    def until(self, weight):
        numbers = {item.number for item in self.items if item.weight == weight}
        while not numbers <= self.done:
            self.todo.pop(0)()
        self.own(weight).wait()

    def finish(self):
        for item in self.items:
            for stage in range(self.bit_count):
                for number, axes in enumerate(self.subsets(item.order[:stage])):
                    self.copy(item, stage, number, axes).wait_send()


def multiply(out_ref, out_rows, left, right_ref, first, width, tile):
    def step(j, nothing):
        at = pl.ds(pl.multiple_of(j * tile, tile), tile)
        from_at = pl.ds(pl.multiple_of(first + j * tile, 128), tile)
        out_ref[out_rows, at] = dot_nn(left[...], right_ref[:, from_at])
        return nothing

    lax.fori_loop(0, width // tile, step, 0)


def forward_part(tokens, seg_rows, norm_gain, cosine, signed, bias_row, rate_row, conv_weight,
                 conv_bias, mixer_gain, skip_row, shards, parts):
    fsdp, depth = lax.axis_size("fsdp"), lax.axis_size("seq")
    bit_count = bit_length(fsdp)
    shapes = [s.shape for s in shards]
    items = plan_items(shapes, parts, bit_count)
    for item in items:
        item.order = item.order[1:] + item.order[:1]
    count = tokens.shape[0]
    weights = len(shards)
    pieces = 2
    kept_shape = (count // SUB, NS, DI)
    results = dict(
        normed=((count, 1024), bf16),
        conv=((count + EDGE, CW), f32),
        raw=((count, 128), f32),
        z=((count, DI), f32),
        act=((count, CW), bf16),
        dt=((count, 128), f32),
        cum=((count, 128), f32),
        passing=((1, DI), f32),
        query=((count, 512), bf16),
        kv=((depth * count, 256), bf16),
        attended=((count, 512), bf16),
        attended_t=((512, count), f32),
        log_total=((QUERY_HEADS, count), f32),
        y=((count, DI), f32),
        gated=((count, DI), bf16),
        kept=(kept_shape, bf16),
        seg_wide=((count + 2 * EDGE, 128), f32),
        seg_col=((depth * count, 128), f32),
    )
    names = list(results)
    local = dict(
        normed_edge=((16, 1024), bf16),
        edge=((16, 1024), bf16),
        seg_all=((depth * 8, count), f32),
        qkv=((count, 768), f32),
        end=((NS, DI), f32),
        state=((NS, DI), f32),
        carry=((NS, DI), f32),
        state_send=((NS, DI), bf16),
        state_recv=((NS, DI), bf16),
        bias=((count, count), f32),
        keys=((4, count, 128), bf16),
        values_t=((128, count), bf16),
        top=((QUERY_HEADS * 8, count), f32),
        total=((QUERY_HEADS * 8, count), f32),
    )
    in_vmem = (0, 1)

    def kernel(*refs):
        at = 0

        def take(n):
            nonlocal at
            at += n
            return refs[at - n : at]

        (tokens_ref, segrow_ref, gain_ref, cos_ref, sin_ref, bias_ref, rate_ref, weight_ref, cbias_ref,
         mixer_gain_ref, skip_ref) = take(11)
        shard_refs = take(weights)
        out = dict(zip(names, take(len(names))))
        whole_out = take(weights)
        v = dict(zip(names, take(len(names))))
        v.update(zip(local, take(len(local))))
        loads, cast_to = take(weights), take(weights)
        whole_vmem = take(len(in_vmem))
        send, recv, load_sem, own_sem, save_sem, z_send, z_recv = take(7)
        place = lax.axis_index("seq")
        whole = [whole_vmem[in_vmem.index(w)] if w in in_vmem else whole_out[w] for w in range(weights)]
        gather = Gatherer(bit_count, items, shard_refs, whole, loads, load_sem, cast_to, own_sem, send, recv)
        for w in range(weights):
            gather.load(w).start()
        enter(bit_count, depth)
        gather.plan(2)
        saved = []

        def save(src, dst):
            copy = pltpu.make_async_copy(src, dst, save_sem.at[len(saved)])
            copy.start()
            saved.append(copy)

        def keep(*which):
            for name in which:
                save(v[name], out[name])

        def to_next(src, dst, slot):
            return pltpu.make_async_remote_copy(
                src, dst, z_send.at[slot], z_recv.at[slot], device_id=along(1), device_id_type=MESH
            )

        started = []

        def send_on(condition, src, dst, slot):
            @pl.when(condition)
            def _():
                to_next(src, dst, slot).start()

            started.append((condition, src, dst, slot))

        def ring(ref, rows, hop, slot):
            b = place - hop + 1
            part = ref.at[pl.ds(pl.multiple_of(jnp.maximum(b, 0) * rows, 8), rows)]
            send_on((b >= 0) & (place < depth - 1), part, part, slot)

        def ring_wait(ref, rows, hop, slot):
            b = place - hop
            part = ref.at[pl.ds(pl.multiple_of(jnp.maximum(b, 0) * rows, 8), rows)]

            @pl.when(b >= 0)
            def _():
                to_next(part, part, slot).wait_recv()

        tail = tokens_ref.at[pl.ds(count - 16, 16)]
        gather.pump(2)
        send_on(place < depth - 1, tail, v["edge"], 0)
        v["seg_all"][pl.ds(pl.multiple_of(place * 8, 8), 8)] = jnp.broadcast_to(segrow_ref[...], (8, count))
        ring(v["seg_all"], 8, 1, 1)

        def normalise(src, dst, rows, group):
            def step(i, nothing):
                at = pl.ds(pl.multiple_of(i * group, group), group)
                x = src[at].astype(f32)
                scale = lax.rsqrt(jnp.mean(x * x, axis=1, keepdims=True) + epsilon)
                dst[at] = low(x * scale * gain_ref[...])
                return nothing

            lax.fori_loop(0, rows // group, step, 0)

        normalise(tokens_ref, v["normed"], count, 64)
        gather.pump(1)

        @pl.when(place == 0)
        def _():
            v["edge"][...] = jnp.zeros((16, 1024), bf16)

        @pl.when(place > 0)
        def _():
            to_next(tail, v["edge"], 0).wait_recv()

        normalise(v["edge"], v["normed_edge"], 16, 16)
        gather.pump(1)
        for hop in range(1, depth):
            ring_wait(v["seg_all"], 8, hop, hop)
            if hop < depth - 1:
                ring(v["seg_all"], 8, hop + 1, hop + 1)

        def column(row):
            return jnp.broadcast_to(row, (128, count)).T

        for b in range(depth):

            @pl.when(b <= place)
            def _(b=b):
                v["seg_col"][b * count : (b + 1) * count, :] = column(v["seg_all"][b * 8 : b * 8 + 1, :])

            @pl.when(b > place)
            def _(b=b):
                v["seg_col"][b * count : (b + 1) * count, :] = jnp.full((count, 128), -2.0, f32)

        own_rows = pl.ds(pl.multiple_of(place * count, 8), count)
        v["seg_wide"][EDGE : EDGE + count, :] = v["seg_col"][own_rows, :]
        v["seg_wide"][EDGE + count :, :] = jnp.full((EDGE, 128), -2.0, f32)
        before = pl.ds(pl.multiple_of(jnp.maximum(place * count - EDGE, 0), 8), EDGE)
        v["seg_wide"][0:EDGE, :] = jnp.where(place == 0, -1.0, v["seg_col"][before, :])
        v["raw"][...] = jnp.zeros((count, 128), f32)
        gather.until(0)
        save(whole[0], whole_out[0])
        multiply(v["conv"], pl.ds(EDGE, count), v["normed"], whole[0], DI, CW, 256)
        v["conv"][0:EDGE, :] = dot_nn(v["normed_edge"][...], whole[0][:, DI : DI + CW])[EDGE:]
        v["raw"][:, 0:MH] = dot_nn(v["normed"][...], whole[0][:, DI + CW : DI + CW + MH])
        gather.pump(4)
        front_conv(v["conv"], v["seg_wide"], weight_ref, cbias_ref, v["act"])
        gather.pump(4)
        front_state(v["seg_wide"], v["raw"], bias_ref, rate_ref, v["act"], v["dt"], v["cum"], v["end"], v["passing"])
        keep("normed", "conv", "raw", "act", "dt", "cum", "passing", "seg_wide", "seg_col")
        width = DI // pieces
        state_slot, kv_slot = depth, depth + pieces

        def chain(j):
            for p in range(pieces):
                cols = pl.ds(p * width, width)

                @pl.when(place == j)
                def _():
                    if j == 0:
                        v["state"][:, cols] = jnp.zeros((NS, width), f32)
                    else:
                        to_next(
                            v["state_send"].at[:, cols], v["state_recv"].at[:, cols], state_slot + p
                        ).wait_recv()
                        v["state"][:, cols] = v["state_recv"][:, cols].astype(f32)
                    if j < depth - 1:
                        v["state_send"][:, cols] = low(
                            v["passing"][:, cols] * v["state"][:, cols] + v["end"][:, cols]
                        )
                        to_next(
                            v["state_send"].at[:, cols], v["state_recv"].at[:, cols], state_slot + p
                        ).start()

        chain(0)
        gather.until(1)
        save(whole[1], whole_out[1])
        multiply(v["qkv"], slice(None), v["normed"], whole[1], 0, 768, 256)
        rotate_kernel(v["qkv"], cos_ref, sin_ref, v["query"], v["kv"].at[own_rows])
        ring(v["kv"], count, 1, kv_slot + 1)
        keep("query")
        gather.pump(4)
        multiply(v["z"], slice(None), v["normed"], whole[0], 0, DI, 256)
        keep("z")
        gather.pump(4)
        chain(1)
        attend_start(v["top"], v["total"], v["attended_t"])

        def attend(b):
            attend_block(b, place, v["query"], v["kv"], v["seg_col"], segrow_ref, v["attended_t"], v["bias"],
                         v["keys"], v["values_t"], v["top"], v["total"])

        attend(place)
        gather.pump(4)
        for hop in range(1, depth):
            ring_wait(v["kv"], count, hop, kv_slot + hop)
            if hop < depth - 1:
                ring(v["kv"], count, hop + 1, kv_slot + hop + 1)

            @pl.when(place >= hop)
            def _(hop=hop):
                attend(place - hop)

            gather.pump(4)
            if hop < depth - 1:
                chain(hop + 1)

        attend_finish(v["attended"], v["attended_t"], v["log_total"], v["top"], v["total"])
        keep("attended", "attended_t", "log_total", "kv")
        for first in range(0, count // SUB, 2):
            gather.pump(4)
            mid_kernel(v["act"], v["dt"], v["cum"], v["seg_wide"], segrow_ref, v["state"], v["z"], mixer_gain_ref,
                       skip_ref, v["y"], v["gated"], v["kept"], v["carry"], first, first + 2)
        keep("y", "gated", "kept")
        for w in range(2, weights):
            gather.until(w)
        gather.finish()
        for condition, src, dst, slot in started:

            @pl.when(condition)
            def _(src=src, dst=dst, slot=slot):
                to_next(src, dst, slot).wait_send()

        @pl.when(place < depth - 1)
        def _():
            for p in range(pieces):
                cols = pl.ds(p * width, width)
                to_next(v["state_send"].at[:, cols], v["state_recv"].at[:, cols], state_slot + p).wait_send()

        for copy in saved:
            copy.wait()

    wholes = [((fsdp * rows, cols), bf16) for rows, cols in shapes]
    scratch = [pltpu.VMEM(*results[n]) for n in names] + [pltpu.VMEM(*a) for a in local.values()]
    scratch += [pltpu.VMEM(shape, f32) for shape in shapes] + [pltpu.VMEM(shape, bf16) for shape in shapes]
    scratch += [pltpu.VMEM(*wholes[w]) for w in in_vmem]
    slots = (1 << bit_count) - 1
    z_slots = depth + pieces + depth
    scratch += [
        pltpu.SemaphoreType.DMA((len(items), slots)),
        pltpu.SemaphoreType.DMA((len(items), slots)),
        pltpu.SemaphoreType.DMA((weights,)),
        pltpu.SemaphoreType.DMA((weights,)),
        pltpu.SemaphoreType.DMA((len(names) + 2,)),
        pltpu.SemaphoreType.DMA((z_slots,)),
        pltpu.SemaphoreType.DMA((z_slots,)),
    ]
    hbm = pl.BlockSpec(memory_space=pl.ANY)
    made = pl.pallas_call(
        kernel,
        out_shape=[jax.ShapeDtypeStruct(*a) for a in list(results.values()) + wholes],
        in_specs=[vmem] * 11 + [hbm] * weights,
        out_specs=[hbm] * (len(names) + weights),
        scratch_shapes=scratch,
        compiler_params=pltpu.CompilerParams(
            collective_id=1, has_side_effects=True, vmem_limit_bytes=62 * 2**20
        ),
    )(tokens, seg_rows, norm_gain, cosine, signed, bias_row, rate_row, conv_weight, conv_bias, mixer_gain,
      skip_row, *shards)
    return dict(zip(names, made)), made[len(names) :]


def shifted(array, axis, by):
    devices = lax.axis_size(axis)
    pairs = [(i, i + by) for i in range(devices) if 0 <= i + by < devices]
    return lax.ppermute(array, axis, pairs)


def contract(left, right):
    return dot_tn(left, right)


def rms_scale(values, gain_vec):
    return (
        values * lax.rsqrt(jnp.mean(values * values, axis=-1, keepdims=True) + epsilon) * gain_vec
    )


def reduced(gradient):
    return low(gradient)


def padded(vector):
    return jnp.pad(vector, (0, 128 - vector.shape[0]))[None]


def on_device(
    tokens,
    cotangent,
    segment_ids,
    norm_gain,
    ffn_gain,
    mixer_gain,
    conv_weight,
    conv_bias,
    decay_log,
    step_bias,
    skip_gain,
    in_proj,
    mixer_out,
    qkv_proj,
    attn_proj,
    gate_up,
    down_proj,
):
    place, devices = lax.axis_index("seq"), lax.axis_size("seq")
    count = tokens.shape[1]
    position = place * count + jnp.arange(count, dtype=jnp.int32)
    half = HEAD_WIDTH // 2
    lane = jnp.arange(128, dtype=jnp.int32)
    exponent = (lane % half).astype(f32) * (2.0 / HEAD_WIDTH)
    frequencies = jnp.power(rope_base, -exponent)
    angles = position.astype(f32)[:, None] * frequencies[None, :]
    cosine = jnp.cos(angles)
    signed = jnp.sin(angles) * jnp.where(lane % HEAD_WIDTH < half, -1.0, 1.0)[None]
    seg_row = segment_ids.astype(f32)
    bias_row, rate_row = padded(step_bias), padded(decay_log)
    skip_row = jnp.repeat(skip_gain, MP)[None]
    own = place.astype(jnp.int32)[None]
    v, (in_full, qkv_full, mix_full, attn_full, gate_full, down_full) = forward_part(
        tokens[0], seg_row, norm_gain[None], cosine, signed, bias_row, rate_row, conv_weight, conv_bias[None],
        mixer_gain[None], skip_row, (in_proj, qkv_proj, mixer_out, attn_proj, gate_up, down_proj),
        (4, 2, 2, 2, 4, 4),
    )
    normed, attended, gated, mixer_y, act, dt, cum = (
        v[n] for n in ("normed", "attended", "gated", "y", "act", "dt", "cum")
    )
    gate_z, seg_wide, seg_col, kept, kv_all, query = (
        v[n] for n in ("z", "seg_wide", "seg_col", "kept", "kv", "query")
    )
    attended_t, log_total, conv_ext, step_raw = (v[n] for n in ("attended_t", "log_total", "conv", "raw"))
    length = kv_all.shape[0]
    token_rows = tokens[0].astype(f32)
    _, norm_pull = jax.vjp(rms_scale, token_rows, norm_gain)
    hidden = token_rows + (dot_nn(attended, attn_full) + dot_nn(gated, mix_full))
    ffn_in32, ffn_pull = jax.vjp(rms_scale, hidden, ffn_gain)
    ffn_in = low(ffn_in32)
    gates = dot_nn(ffn_in, gate_full)

    def swiglu(values):
        return jax.nn.silu(values[:, :FF]) * values[:, FF:]

    act32, act_pull = jax.vjp(swiglu, gates)
    inner = low(act32)
    result = hidden + dot_nn(inner, down_full)
    back_rows = cotangent[0]
    down_piece = reduced(contract(inner, back_rows))
    (gates_grad,) = act_pull(dot_nt(back_rows, down_full))
    gates_grad = low(gates_grad)
    gate_piece = reduced(contract(ffn_in, gates_grad))
    hidden_extra, ffn_gain_grad = ffn_pull(dot_nt(gates_grad, gate_full))
    hidden_grad = back_rows.astype(f32) + hidden_extra
    branch = low(hidden_grad)
    attn_piece = reduced(contract(attended, branch))
    attended_grad = low(dot_nt(branch, attn_full))
    mixer_piece = reduced(contract(gated, branch))
    gated_grad = low(dot_nt(branch, mix_full))

    y_grad, gate_z_grad, mixer_gain_grad, state_grad = call(
        gate_back_kernel,
        [((count, DI), f32), ((count, DI), bf16), ((1, DI), f32), ((NS, DI), f32)],
        (gated_grad, mixer_y, act, gate_z, dt, cum, seg_wide, mixer_gain[None], skip_row),
    )
    grads = lax.all_gather(low(state_grad), "seq").astype(f32)
    passings = lax.all_gather(v["passing"], "seq")
    later = jnp.zeros((NS, DI), f32)
    for k in reversed(range(devices)):
        later = jnp.where(k > place, passings[k] * later + grads[k], later)

    query_grad, kv_grad = call(
        attend_back_kernel,
        [((count, 512), bf16), ((length, 256), bf16)],
        (own, query, kv_all, seg_col, seg_row, attended_grad, attended_t, log_total, cosine, signed),
        (
            ((count, count), f32),
            ((4, count, 128), bf16),
            ((4, count, 128), bf16),
            ((2, count, 128), f32),
            ((2, count, 128), f32),
            ((QUERY_HEADS, count), f32),
            ((512, count), f32),
            ((QUERY_HEADS, count, 128), bf16),
            ((QUERY_HEADS, count, 128), bf16),
        ),
        smem,
    )
    kv_own = lax.psum_scatter(kv_grad, "seq", scatter_dimension=0, tiled=True).astype(f32)

    def swap(values):
        shaped = values.reshape(count, 2, 2, half)
        return shaped[:, :, ::-1].reshape(count, 128)

    key_grad = kv_own[:, :128]
    key_grad = key_grad * cosine + swap(key_grad * signed)
    qkv_grad = jnp.concatenate([query_grad, low(key_grad), low(kv_own[:, 128:])], axis=1)
    qkv_piece = reduced(contract(normed, qkv_grad))
    normed_grad = dot_nt(qkv_grad, qkv_full)

    raw_grad, conv_grad, conv_weight_grad, conv_bias_grad, rate_grad, bias_grad, skip_grad = call(
        back_kernel,
        [
            ((count, 128), f32),
            ((count + EDGE, CW), f32),
            ((KC, CW), f32),
            ((1, CW), f32),
            ((1, 128), f32),
            ((1, 128), f32),
            ((1, 128), f32),
        ],
        (
            act, dt, cum, seg_wide, seg_row, step_raw, bias_row, rate_row, kept,
            mixer_y, y_grad, later, conv_ext, conv_weight, conv_bias[None], skip_row,
        ),
        (((count, CW), f32), ((NS, DI), f32), ((count + 2 * EDGE, 128), f32)),
    )
    edge_back = shifted(conv_grad[:EDGE], "seq", -1)
    conv_grad = conv_grad[EDGE:] + jnp.pad(edge_back, ((count - EDGE, 0), (0, 0)))
    mixed_grad = jnp.concatenate([gate_z_grad, low(conv_grad), low(raw_grad[:, :MH])], axis=1)
    in_piece = reduced(contract(normed, mixed_grad))
    normed_grad = normed_grad + dot_nt(mixed_grad, in_full)
    rows_extra, norm_gain_grad = norm_pull(normed_grad)
    input_grad = hidden_grad + rows_extra
    pieces = (in_piece, mixer_piece, qkv_piece, attn_piece, gate_piece, down_piece)
    rows = (
        norm_gain_grad,
        ffn_gain_grad,
        mixer_gain_grad,
        conv_weight_grad,
        conv_bias_grad,
        rate_grad,
        bias_grad,
        skip_grad,
    )
    flat = jnp.concatenate([row.reshape(-1) for row in rows])
    flat = jnp.pad(flat, (0, 16384 - flat.shape[0])).reshape(16, 1024)
    *shards, flat = reduce_all(pieces, flat, (4, 2, 2, 2, 4, 4))
    shards = [shard.astype(f32) for shard in shards]
    flat, small, at = flat.reshape(-1), [], 0
    for row, keep in zip(rows, (None, None, None, None, None, MH, MH, MH)):
        part = flat[at : at + row.size].reshape(row.shape)
        at += row.size
        part = part[:, :keep] if keep else part
        small.append(part if part.shape[0] == KC else part.reshape(-1))
    return (low(result)[None], input_grad[None], *small, *shards)


def solution(mesh):
    rows, whole, split_rows = P("fsdp", "seq", None), P(), P("fsdp", None)
    return jax.shard_map(
        on_device,
        mesh=mesh,
        in_specs=(rows, rows, P("fsdp", "seq"), *[whole] * 8, *[split_rows] * 6),
        out_specs=(rows, rows, *[whole] * 8, *[split_rows] * 6),
        check_vma=False,
    )
```

```python
import jax
import jax.numpy as jnp
from jax import lax
from jax.experimental import pallas as pl
from jax.experimental.pallas import tpu as pltpu
from jax.sharding import PartitionSpec as P

FF = 2048
QUERY_HEADS = 8
KEY_VALUE_HEADS = 2
HEAD_WIDTH = 64
MH = 24
MP = 64
NS = 128
KC = 4
SUB = 128
DI = 1536
CW = 1792
EDGE = 8

epsilon = 1e-05
rope_base = 100000000000.0
highest = lax.Precision.HIGHEST
f32 = jnp.float32
bf16 = jnp.bfloat16


def dot_nn(left, right):
    return jnp.dot(left, right, preferred_element_type=jnp.float32)


def dot_nt(left, right):
    return lax.dot_general(
        left, right, (((1,), (1,)), ((), ())), preferred_element_type=jnp.float32
    )


def dot_tn(left, right):
    return lax.dot_general(
        left, right, (((0,), (0,)), ((), ())), preferred_element_type=jnp.float32
    )


def exact(left, right):
    return jnp.dot(left, right, precision=highest, preferred_element_type=jnp.float32)


def low(values):
    return values.astype(jnp.bfloat16)


def split(values):
    top = low(values)
    return top, low(values - top.astype(jnp.float32))


def iota(shape, axis):
    return lax.broadcasted_iota(jnp.int32, shape, axis)


def spreader():
    return low(jnp.where(iota((128, DI), 1) // MP == iota((128, DI), 0), 1.0, 0.0))


def widen(values, spread):
    top, rest = split(values)
    return dot_nn(top, spread) + dot_nn(rest, spread)


def widen_row(row, spread):
    return widen(jnp.broadcast_to(row, (8, 128)), spread)[0:1]


def head_sums(values, spread):
    top, rest = split(values)
    return dot_nt(top, spread) + dot_nt(rest, spread)


def softplus(values):
    return jnp.maximum(values, 0.0) + jnp.log1p(jnp.exp(-jnp.abs(values)))


def sigmoid(values):
    return 1.0 / (1.0 + jnp.exp(-values))


def lane_halves(rows):
    lane = iota((rows, 128), 1)
    return lane < MP


def rounded_to(values):
    return low(values).astype(jnp.float32)


def front_conv(conv_ref, seg_ref, weight_ref, cbias_ref, act_ref):
    chunks = act_ref.shape[0] // SUB

    def tile(j, carry):
        col = pl.ds(pl.multiple_of(j * 128, 128), 128)
        for c in range(chunks):
            r0 = c * SUB
            seg = seg_ref[pl.ds(r0 + 8, SUB), :]
            total = jnp.broadcast_to(cbias_ref[0:1, col], (SUB, 128))
            for k in range(KC):
                x = rounded_to(conv_ref[pl.ds(r0 + 9 - KC + k, SUB), col])
                if k < KC - 1:
                    x = jnp.where(seg_ref[pl.ds(r0 + 9 - KC + k, SUB), :] == seg, x, 0.0)
                total = total + weight_ref[k : k + 1, col] * x
            act_ref[pl.ds(r0, SUB), col] = low(total * sigmoid(total))
        return carry

    lax.fori_loop(0, CW // 128, tile, 0)


def front_state(seg_ref, raw_ref, bias_ref, rate_ref, act_ref, dt_ref, cum_ref, end_ref, pass_ref):
    chunks = raw_ref.shape[0] // SUB
    spread = spreader()
    lower = jnp.where(iota((SUB, SUB), 0) >= iota((SUB, SUB), 1), 1.0, 0.0)
    end_ref[...] = jnp.zeros_like(end_ref)
    gain = jnp.ones((1, 128), jnp.float32)
    for c in range(chunks):
        rows = pl.ds(c * SUB, SUB)
        dt = softplus(raw_ref[rows, :] + bias_ref[...])
        cum = exact(lower, -dt * jnp.exp(rate_ref[...]))
        dt_ref[rows, :] = dt
        cum_ref[rows, :] = cum
        seg = seg_ref[pl.ds(c * SUB + 8, SUB), :]
        before = seg_ref[pl.ds(c * SUB + 7, 1), :]
        last = seg[SUB - 1 :, :]
        end = cum[SUB - 1 :, :]
        weight = jnp.where(seg == last, jnp.exp(end - cum), 0.0) * dt
        passing = jnp.where(last == before, jnp.exp(end), 0.0)
        gain = gain * passing
        values = act_ref[rows, 0:DI].astype(jnp.float32)
        fresh = dot_tn(act_ref[rows, DI : DI + NS], low(widen(weight, spread) * values))
        end_ref[...] = widen_row(passing, spread) * end_ref[...] + fresh
    pass_ref[...] = widen_row(gain, spread)


def mid_kernel(act_ref, dt_ref, cum_ref, seg_ref, segrow_ref, state_ref, z_ref, gain_ref, skip_ref,
               y_ref, gated_ref, kept_ref, carry_ref, first, until):
    spread = spreader()
    if first == 0:
        carry_ref[...] = state_ref[...]
    half = lane_halves(SUB)

    def chunk(c, nothing):
        r0 = pl.multiple_of(c * SUB, SUB)
        rows = pl.ds(r0, SUB)
        dt, cum = dt_ref[rows, :], cum_ref[rows, :]
        cum_t = cum.T
        seg = seg_ref[pl.ds(pl.multiple_of(r0 + 8, 8), SUB), :]
        before = seg_ref[pl.ds(pl.multiple_of(r0, 8), 8), :][7:8]
        last, end = seg[SUB - 1 :, :], cum[SUB - 1 :, :]
        keys, reads = act_ref[rows, DI : DI + NS], act_ref[rows, DI + NS : CW]
        affinity = dot_nt(reads, keys)
        allowed = (iota((SUB, SUB), 0) >= iota((SUB, SUB), 1)) & (seg == segrow_ref[0:1, rows])
        state = low(carry_ref[...])
        kept_ref[pl.ds(c, 1)] = state[None]
        entry = widen(jnp.where(seg == before, jnp.exp(cum), 0.0), spread)
        y_ref[rows, :] = dot_nn(reads, state) * entry
        values = act_ref[rows, 0:DI].astype(jnp.float32)
        scaled = values * widen(dt, spread)
        weight = jnp.where(seg == last, jnp.exp(end - cum), 0.0)
        passing = jnp.where(last == before, jnp.exp(end), 0.0)
        fresh = dot_tn(keys, low(widen(weight, spread) * scaled))
        carry_ref[...] = widen_row(passing, spread) * carry_ref[...] + fresh
        for pair in range(MH // 2):
            cols = slice(pair * 128, pair * 128 + 128)
            parts = []
            for h in (2 * pair, 2 * pair + 1):
                gap = jnp.where(allowed, cum[:, h : h + 1] - cum_t[h : h + 1, :], -1e30)
                parts.append(low(jnp.exp(gap) * affinity))
            v = scaled[:, cols]
            right = jnp.concatenate([low(jnp.where(half, v, 0.0)), low(jnp.where(half, 0.0, v))], 0)
            y_ref[rows, cols] = y_ref[rows, cols] + dot_nn(jnp.concatenate(parts, 1), right)
        z = z_ref[rows, :]
        g = (y_ref[rows, :] + skip_ref[...] * values) * (z * sigmoid(z))
        scale = lax.rsqrt(jnp.mean(g * g, axis=1, keepdims=True) + epsilon)
        gated_ref[rows, :] = low(g * scale * gain_ref[...])
        return nothing

    lax.fori_loop(first, until, chunk, 0)


def gate_back_kernel(grad_ref, y_ref, act_ref, z_ref, dt_ref, cum_ref, seg_ref, gain_ref, skip_ref,
                     ygrad_ref, zgrad_ref, gain_grad_ref, state_grad_ref, first, until):
    chunks = act_ref.shape[0] // SUB
    spread = spreader()
    if first == 0:
        gain_grad_ref[...] = jnp.zeros_like(gain_grad_ref)
        state_grad_ref[...] = jnp.zeros_like(state_grad_ref)

    def chunk(i, nothing):
        c = chunks - 1 - i
        r0 = pl.multiple_of(c * SUB, SUB)
        rows = pl.ds(r0, SUB)
        values = act_ref[rows, 0:DI].astype(jnp.float32)
        z = z_ref[rows, :]
        sig = sigmoid(z)
        silu = z * sig
        u = y_ref[rows, :] + skip_ref[...] * values
        g = u * silu
        grad = grad_ref[rows, :].astype(jnp.float32)
        scale = lax.rsqrt(jnp.mean(g * g, axis=1, keepdims=True) + epsilon)
        unit = g * scale
        gain_grad_ref[...] += jnp.sum(grad * unit, axis=0, keepdims=True)
        h = grad * gain_ref[...]
        dg = scale * (h - unit * jnp.mean(h * unit, axis=1, keepdims=True))
        dy = dg * silu
        ygrad_ref[rows, :] = dy
        zgrad_ref[rows, :] = low(dg * u * (sig * (1.0 + z * (1.0 - sig))))
        cum = cum_ref[rows, :]
        seg = seg_ref[pl.ds(pl.multiple_of(r0 + 8, 8), SUB), :]
        before = seg_ref[pl.ds(pl.multiple_of(r0, 8), 8), :][7:8]
        last, end = seg[SUB - 1 :, :], cum[SUB - 1 :, :]
        entry = widen(jnp.where(seg == before, jnp.exp(cum), 0.0), spread)
        passing = jnp.where(last == before, jnp.exp(end), 0.0)
        fresh = dot_tn(act_ref[rows, DI + NS : CW], low(entry * dy))
        state_grad_ref[...] = widen_row(passing, spread) * state_grad_ref[...] + fresh
        return nothing

    lax.fori_loop(first, until, chunk, 0)


def back_states(act_ref, dt_ref, cum_ref, seg_ref, segrow_ref, raw_ref, bias_ref, rate_ref, kept_ref,
                y_ref, ygrad_ref, skip_ref, raw_grad_ref, rate_grad_ref, bias_grad_ref, skip_grad_ref,
                value_grad_ref, pair_grad_ref, carry_ref, first, until):
    chunks = act_ref.shape[0] // SUB
    spread = spreader()
    half = lane_halves(SUB)
    upper = jnp.where(iota((SUB, SUB), 1) >= iota((SUB, SUB), 0), 1.0, 0.0)
    rate = jnp.exp(rate_ref[...])
    if first == 0:
        rate_grad_ref[...] = jnp.zeros_like(rate_grad_ref)
        bias_grad_ref[...] = jnp.zeros_like(bias_grad_ref)
        skip_grad_ref[...] = jnp.zeros_like(skip_grad_ref)

    def chunk(i, nothing):
        c = chunks - 1 - i
        r0 = pl.multiple_of(c * SUB, SUB)
        rows = pl.ds(r0, SUB)
        dt, cum = dt_ref[rows, :], cum_ref[rows, :]
        cum_t = cum.T
        seg = seg_ref[pl.ds(pl.multiple_of(r0 + 8, 8), SUB), :]
        before = seg_ref[pl.ds(pl.multiple_of(r0, 8), 8), :][7:8]
        last, end = seg[SUB - 1 :, :], cum[SUB - 1 :, :]
        keys, reads = act_ref[rows, DI : DI + NS], act_ref[rows, DI + NS : CW]
        affinity = dot_nt(keys, reads)
        allowed = (iota((SUB, SUB), 1) >= iota((SUB, SUB), 0)) & (seg == segrow_ref[0:1, rows])
        values = act_ref[rows, 0:DI].astype(jnp.float32)
        wide_dt = widen(dt, spread)
        scaled = values * wide_dt
        scaled_low = low(scaled)
        dy = ygrad_ref[rows, :]
        dy_low = low(dy)
        state, carry = kept_ref[pl.ds(c, 1)][0], carry_ref[...]
        carry_low = low(carry)
        wide_weight = widen(jnp.where(seg == last, jnp.exp(end - cum), 0.0), spread)
        wide_entry = widen(jnp.where(seg == before, jnp.exp(cum), 0.0), spread)
        wide_pass = widen_row(jnp.where(last == before, jnp.exp(end), 0.0), spread)
        from_state = dot_nn(keys, carry_low) * wide_weight
        mixed_grad = jnp.zeros((SUB, SUB), jnp.float32)
        for pair in range(MH // 2):
            cols = slice(pair * 128, pair * 128 + 128)
            v, d = scaled[:, cols], dy[:, cols]
            left = jnp.concatenate([low(jnp.where(half, v, 0.0)), low(jnp.where(half, 0.0, v))], 0)
            right = jnp.concatenate([low(jnp.where(half, d, 0.0)), low(jnp.where(half, 0.0, d))], 0)
            weight_grad = dot_nt(left, dy_low[:, cols])
            parts = []
            for n, h in enumerate((2 * pair, 2 * pair + 1)):
                gap = jnp.where(allowed, cum_t[h : h + 1, :] - cum[:, h : h + 1], -1e30)
                decay = jnp.exp(gap)
                parts.append(low(decay * affinity))
                mixed_grad = mixed_grad + decay * weight_grad[n * SUB : (n + 1) * SUB]
            value_grad_ref[rows, cols] = dot_nn(jnp.concatenate(parts, 1), right)
        x = value_grad_ref[rows, 0:DI] + from_state
        value_grad_ref[rows, 0:DI] = wide_dt * x + skip_ref[...] * dy
        mixed_low = low(mixed_grad)
        pair_grad_ref[rows, 0:NS] = dot_nn(mixed_low, reads) + dot_nt(
            low(wide_weight * scaled), carry_low
        )
        entered = low(wide_entry * dy)
        pair_grad_ref[rows, NS:] = dot_tn(mixed_low, keys) + dot_nt(entered, state)
        scaled_exact = scaled_low.astype(jnp.float32)
        direct = head_sums(values * x, spread)
        given = head_sums(scaled_exact * x, spread)
        taken = head_sums(dy_low.astype(jnp.float32) * y_ref[rows, :], spread)
        tail = jnp.sum(scaled_exact * from_state, axis=0, keepdims=True) + jnp.sum(
            wide_pass * carry * state.astype(jnp.float32), axis=0, keepdims=True
        )
        tail = head_sums(jnp.broadcast_to(tail, (8, DI)), spread)[0:1]
        decay_grad = exact(upper, taken - given) + tail
        rate_grad_ref[...] += jnp.sum(decay_grad * (-dt * rate), axis=0, keepdims=True)
        dt_grad = direct - decay_grad * rate
        raw_grad = dt_grad * sigmoid(raw_ref[rows, :] + bias_ref[...])
        raw_grad_ref[rows, :] = low(jnp.where(iota((SUB, 128), 1) < MH, raw_grad, 0.0))
        bias_grad_ref[...] += jnp.sum(raw_grad, axis=0, keepdims=True)
        skip_sum = jnp.sum(dy * values, axis=0, keepdims=True)
        skip_grad_ref[...] += head_sums(jnp.broadcast_to(skip_sum, (8, DI)), spread)[0:1]
        carry_ref[...] = wide_pass * carry + dot_tn(reads, entered)
        return nothing

    lax.fori_loop(first, until, chunk, 0)


def back_conv(conv_hbm, conv_ref, conv_sem, seg_ref, weight_ref, cbias_ref, act_grad_ref, shift,
              conv_grad_ref, edge_ref, tail_ref, weight_grad_ref, cbias_grad_ref, pre_ref, first, until):
    rows_total = act_grad_ref.shape[0]
    chunks = rows_total // SUB
    pre_ref[0:8, :] = jnp.zeros((8, 128), jnp.float32)
    pre_ref[rows_total + 8 : rows_total + 16, :] = jnp.zeros((8, 128), jnp.float32)

    def fetch(j, slot):
        return pltpu.make_async_copy(
            conv_hbm.at[:, pl.ds(pl.multiple_of(j * 128, 128), 128)], conv_ref.at[slot], conv_sem.at[slot]
        )

    fetch(first, first % 2).start()

    def tile(j, carry):
        slot = j % 2

        @pl.when(j + 1 < until)
        def _():
            fetch(j + 1, 1 - slot).start()

        fetch(j, slot).wait()
        col = pl.ds(pl.multiple_of(j * 128, 128), 128)
        sums = [jnp.zeros((1, 128), jnp.float32) for _ in range(KC + 1)]
        for c in range(chunks):
            r0 = c * SUB
            seg = seg_ref[pl.ds(r0 + 8, SUB), :]
            total = jnp.broadcast_to(cbias_ref[0:1, col], (SUB, 128))
            taps = []
            for k in range(KC):
                x = rounded_to(conv_ref[slot, pl.ds(r0 + 9 - KC + k, SUB), :])
                if k < KC - 1:
                    x = jnp.where(seg_ref[pl.ds(r0 + 9 - KC + k, SUB), :] == seg, x, 0.0)
                taps.append(x)
                total = total + weight_ref[k : k + 1, col] * x
            sig = sigmoid(total)
            act_col = pl.ds(pl.multiple_of((j - shift) * 128, 128), 128)
            pre = act_grad_ref[pl.ds(r0, SUB), act_col] * (sig * (1.0 + total * (1.0 - sig)))
            pre_ref[pl.ds(r0 + 8, SUB), :] = pre
            for k in range(KC):
                sums[k] = sums[k] + jnp.sum(pre * taps[k], axis=0, keepdims=True)
            sums[KC] = sums[KC] + jnp.sum(pre, axis=0, keepdims=True)
        for k in range(KC):
            weight_grad_ref[k : k + 1, col] = sums[k]
        cbias_grad_ref[0:1, col] = sums[KC]

        def spread_back(r0, size):
            seg = seg_ref[pl.ds(r0, size), :]
            total = jnp.zeros((size, 128), jnp.float32)
            for back in range(KC):
                x = pre_ref[pl.ds(r0 + back, size), :]
                if back:
                    x = jnp.where(seg_ref[pl.ds(r0 + back, size), :] == seg, x, 0.0)
                total = total + weight_ref[KC - 1 - back : KC - back, col] * x
            return total

        edge_ref[:, col] = spread_back(0, 8)
        for c in range(chunks):
            total = spread_back(c * SUB + 8, SUB)
            conv_grad_ref[pl.ds(c * SUB, SUB), act_col] = low(total)
        tail_ref[:, col] = total[SUB - 16 :]
        return carry

    lax.fori_loop(first, until, tile, 0)


def partner(values):
    lane = iota(values.shape, 1)
    half = HEAD_WIDTH // 2
    return jnp.where(
        lane % HEAD_WIDTH < half, pltpu.roll(values, 128 - half, 1), pltpu.roll(values, half, 1)
    )


def rotate_kernel(qkv_ref, cos_ref, sin_ref, query_ref, kv_ref):
    cos, sin = cos_ref[...], sin_ref[...]
    for g in range(5):
        x = qkv_ref[:, g * 128 : g * 128 + 128]
        x = low(x * cos + partner(x) * sin)
        if g < 4:
            query_ref[:, g * 128 : g * 128 + 128] = x * jnp.bfloat16(HEAD_WIDTH**-0.5)
        else:
            kv_ref[:, 0:128] = x
    kv_ref[:, 128:256] = low(qkv_ref[:, 640:768])


def lane_variants(block, out_ref):
    other = pltpu.roll(block, 64, 1)
    half = iota(block.shape, 1) < HEAD_WIDTH
    out_ref[0] = low(jnp.where(half, block, 0.0))
    out_ref[1] = low(jnp.where(half, 0.0, other))
    out_ref[2] = low(jnp.where(half, other, 0.0))
    out_ref[3] = low(jnp.where(half, 0.0, block))


def attend_bias(b, own, rows, segcol_ref, segrow_ref, bias_ref):
    seg = segcol_ref[pl.ds(pl.multiple_of(b * rows, rows), rows), :].astype(jnp.float32)
    seg = jnp.concatenate([seg] * (rows // 128), 1)
    causal = (iota((rows, rows), 0) - iota((rows, rows), 1)) <= jnp.where(b < own, rows, 0)
    bias_ref[...] = jnp.where(causal & (seg == segrow_ref[...]), 0.0, -1e30)


def attend_start(top_ref, sum_ref, out_t_ref):
    top_ref[...] = jnp.full_like(top_ref, -1e30)
    sum_ref[...] = jnp.zeros_like(sum_ref)
    out_t_ref[...] = jnp.zeros_like(out_t_ref)


def attend_block(b, own, query_ref, kv_ref, segcol_ref, segrow_ref, out_t_ref, bias_ref, keys_ref,
                 values_t_ref, top_ref, sum_ref):
    rows = query_ref.shape[0]
    at = pl.ds(pl.multiple_of(b * rows, rows), rows)
    attend_bias(b, own, rows, segcol_ref, segrow_ref, bias_ref)
    lane_variants(kv_ref[at, 0:128].astype(jnp.float32), keys_ref)
    values_t_ref[...] = low(kv_ref[at, 128:256].astype(jnp.float32).T)

    def pair(g, nothing):
        kv = g // 2
        query = query_ref[:, pl.ds(pl.multiple_of(g * 128, 128), 128)]
        for side in range(2):
            h = g * 2 + side
            row = pl.ds(pl.multiple_of(h * 8, 8), 8)
            scores = dot_nt(keys_ref[kv * 2 + side], query)
            scores = scores + bias_ref[...]
            old = top_ref[row, :][0:1]
            top = jnp.maximum(old, jnp.max(scores, axis=0, keepdims=True))
            p = jnp.exp(scores - top)
            fade = jnp.exp(old - top)
            total = sum_ref[row, :][0:1] * fade + jnp.sum(p, 0, keepdims=True)
            top_ref[row, :] = jnp.broadcast_to(top, (8, rows))
            sum_ref[row, :] = jnp.broadcast_to(total, (8, rows))
            at_h = pl.ds(pl.multiple_of(h * 64, 64), 64)
            values_t = values_t_ref[pl.ds(pl.multiple_of(kv * 64, 64), 64), :]
            out_t_ref[at_h, :] = out_t_ref[at_h, :] * fade + dot_nn(values_t, low(p))
        return nothing

    lax.fori_loop(0, QUERY_HEADS // 2, pair, 0)


def attend_finish(out_ref, out_t_ref, total_ref, top_ref, sum_ref):
    for h in range(QUERY_HEADS):
        at_h = slice(h * 64, h * 64 + 64)
        row = slice(h * 8, h * 8 + 8)
        total_ref[row, :] = top_ref[row, :] + jnp.log(sum_ref[row, :])
        out_t_ref[at_h, :] = out_t_ref[at_h, :] / sum_ref[h * 8 : h * 8 + 1, :]
    out_ref[...] = low(out_t_ref[...].T)


def attend_back_start(query_ref, grad_ref, out_t_ref, spread_ref):
    rows = query_ref.shape[0]
    grad_t = grad_ref[...].astype(jnp.float32).T
    product = grad_t * out_t_ref[...]
    for h in range(QUERY_HEADS):
        total = jnp.sum(product[h * 64 : h * 64 + 64, :], 0, keepdims=True)
        spread_ref[h * 8 : h * 8 + 8, :] = jnp.broadcast_to(total, (8, rows))
    out_t_ref[...] = jnp.zeros_like(out_t_ref)


def attend_back_block(b, own, query_ref, kv_ref, segcol_ref, segrow_ref, grad_ref, total_ref, kv_grad_ref,
                      bias_ref, keys_ref, values_ref, keys_t_ref, dkeys_ref, dvalues_ref, spread_ref, dq_ref):
    rows = query_ref.shape[0]
    at = pl.ds(pl.multiple_of(b * rows, rows), rows)
    attend_bias(b, own, rows, segcol_ref, segrow_ref, bias_ref)
    keys = kv_ref[at, 0:128].astype(jnp.float32)
    lane_variants(keys, keys_ref)
    lane_variants(kv_ref[at, 128:256].astype(jnp.float32), values_ref)
    keys_t_ref[...] = low(keys.T)
    dkeys_ref[...] = jnp.zeros_like(dkeys_ref)
    dvalues_ref[...] = jnp.zeros_like(dvalues_ref)

    lower_half = iota((rows, 128), 1) < HEAD_WIDTH

    def side_of(values, side):
        values = values.astype(jnp.float32)
        return low(jnp.where(lower_half, 0.0, values) if side else jnp.where(lower_half, values, 0.0))

    def pair(g, nothing):
        kv = g // 2
        lanes = pl.ds(pl.multiple_of(g * 128, 128), 128)
        for side in range(2):
            h = g * 2 + side
            row = pl.ds(pl.multiple_of(h * 8, 8), 8)
            scores = dot_nt(keys_ref[kv * 2 + side], query_ref[:, lanes]) + bias_ref[...]
            p = jnp.exp(scores - total_ref[row, :][0:1])
            dp = dot_nt(values_ref[kv * 2 + side], grad_ref[:, lanes])
            ds = low(p * (dp - spread_ref[row, :][0:1]))
            dkeys_ref[kv] = dkeys_ref[kv] + dot_nn(ds, side_of(query_ref[:, lanes], side))
            dvalues_ref[kv] = dvalues_ref[kv] + dot_nn(low(p), side_of(grad_ref[:, lanes], side))
            at_h = pl.ds(pl.multiple_of(h * 64, 64), 64)
            keys_t = keys_t_ref[pl.ds(pl.multiple_of(kv * 64, 64), 64), :]
            dq_ref[at_h, :] = dq_ref[at_h, :] + dot_nn(keys_t, ds)
        return nothing

    lax.fori_loop(0, QUERY_HEADS // 2, pair, 0)
    half = lower_half
    for src, lanes in ((dkeys_ref, slice(0, 128)), (dvalues_ref, slice(128, 256))):
        first, second = src[0], src[1]
        kv_grad_ref[at, lanes] = low(
            jnp.where(half, first + pltpu.roll(first, 64, 1), second + pltpu.roll(second, 64, 1))
        )


def attend_back_finish(dq_ref, cos_ref, sin_ref, qkv_grad_ref):
    dq = dq_ref[...].T * (HEAD_WIDTH**-0.5)
    cos, sin = cos_ref[...], sin_ref[...]
    for g in range(4):
        x = dq[:, g * 128 : g * 128 + 128]
        qkv_grad_ref[:, g * 128 : g * 128 + 128] = low(x * cos + partner(x * sin))


vmem = pl.BlockSpec(memory_space=pltpu.VMEM)
smem = pl.BlockSpec(memory_space=pltpu.SMEM)


def call(kernel, outs, args, scratch=(), first=vmem, flops=10**9):
    return pl.pallas_call(
        kernel,
        out_shape=[jax.ShapeDtypeStruct(shape, kind) for shape, kind in outs],
        in_specs=[first] + [vmem] * (len(args) - 1),
        out_specs=[vmem] * len(outs),
        scratch_shapes=[pltpu.VMEM(shape, kind) for shape, kind in scratch],
        compiler_params=pltpu.CompilerParams(vmem_limit_bytes=56 * 2**20),
        cost_estimate=pl.CostEstimate(flops=flops, bytes_accessed=10**7, transcendentals=10**6),
    )(*args)


MESH = pl.DeviceIdType.MESH


def position_bits(count):
    index = lax.axis_index("fsdp")
    return [(index // (1 << b)) % 2 for b in reversed(range(count))]


def across(bits, axis):
    count = len(bits)
    index = lax.axis_index("fsdp")
    step = 1 << (count - 1 - axis)
    return (index + step * (1 - 2 * bits[axis]), lax.axis_index("seq"))


def along(by):
    return (lax.axis_index("fsdp"), lax.axis_index("seq") + by)


class Item:
    def __init__(self, number, weight, start, size, order):
        self.number, self.weight, self.start, self.size, self.order = number, weight, start, size, order


def plan_items(shapes, parts, bit_count):
    items = []
    for w, ((rows, _), count) in enumerate(zip(shapes, parts)):
        for p in range(count):
            turn = p % max(bit_count - 1, 1)
            ici = list(range(bit_count - 1))
            order = [bit_count - 1] + ici[turn:] + ici[:turn]
            items.append(Item(len(items), w, p * (rows // count), rows // count, order))
            items[-1].slots = max(1, count // 2)
            items[-1].part = p
    return items


def own_shape(bit_count, shape, parts):
    return (*(2,) * (bit_count - 1), shape[0] // parts * max(1, parts // 2), shape[1])


class Reducer:
    def __init__(self, bit_count, depth, items, whole, own, landed, zin, zmid, out, send, recv, own_sem):
        self.bit_count, self.depth, self.items = bit_count, depth, items
        self.whole, self.own, self.landed = whole, own, landed
        self.zin, self.zmid, self.out = zin, zmid, out
        self.send, self.recv, self.own_sem = send, recv, own_sem
        self.bits = position_bits(bit_count)
        self.place = lax.axis_index("seq")

    def rows(self, item):
        return pl.ds(item.start, item.size)

    def left(self, item, stage):
        return sorted(item.order[stage:])

    def pick(self, item, stage, mine):
        axis = item.order[stage]
        at = self.left(item, stage).index(axis)
        bit = self.bits[axis] if mine else 1 - self.bits[axis]
        lead = [slice(None)] * (self.bit_count - stage)
        lead[at] = bit
        return (*lead, self.rows(item))

    def source(self, item, stage):
        if stage == 0:
            return self.whole[item.weight]
        return self.landed[stage - 1][item.weight]

    def copy(self, item, stage):
        lead = (slice(None),) * (self.bit_count - stage - 1)
        return pltpu.make_async_remote_copy(
            self.source(item, stage).at[self.pick(item, stage, False)],
            self.landed[stage][item.weight].at[(*lead, self.rows(item))],
            self.send.at[item.number, stage],
            self.recv.at[item.number, stage],
            device_id=across(self.bits, item.order[stage]),
            device_id_type=MESH,
        )

    def own_copy(self, item):
        lead = (slice(None),) * (self.bit_count - 1)
        return pltpu.make_async_copy(
            self.whole[item.weight].at[self.pick(item, 0, True)],
            self.own[item.weight].at[(*lead, pl.ds(self.own_start(item), item.size))],
            self.own_sem.at[item.number],
        )

    def own_start(self, item):
        return item.part % item.slots * item.size

    def begin(self, item):
        self.copy(item, 0).start()
        if item.part < item.slots:
            self.own_copy(item).start()

    def add(self, dst, dst_lead, other, other_lead, item, shift=0):
        group = 16

        def step(i, nothing):
            at = pl.ds(pl.multiple_of(item.start + i * group, group), group)
            at_other = pl.ds(pl.multiple_of(item.start + shift + i * group, group), group)
            dst[(*dst_lead, at)] = low(
                dst[(*dst_lead, at)].astype(f32) + other[(*other_lead, at_other)].astype(f32)
            )
            return nothing

        lax.fori_loop(0, item.size // group, step, 0)

    def advance(self, item, stage):
        self.copy(item, stage).wait_recv()
        landed = self.landed[stage][item.weight]
        kept = self.bit_count - stage - 1
        places = [[(i >> (kept - 1 - b)) & 1 for b in range(kept)] for i in range(1 << kept)]
        if stage == 0:
            self.own_copy(item).wait()
            for lead in places:
                self.add(landed, lead, self.own[item.weight], lead, item, self.own_start(item) - item.start)
            for other in self.items:
                if other.weight == item.weight and other.part == item.part + item.slots:
                    self.own_copy(other).start()
        else:
            source = self.source(item, stage)
            axis = item.order[stage]
            at = self.left(item, stage).index(axis)
            for lead in places:
                from_lead = [*lead[:at], self.bits[axis], *lead[at:]]
                self.add(landed, lead, source, from_lead, item)
        if stage + 1 < self.bit_count:
            self.copy(item, stage + 1).start()

    def z_copy(self, item, kind, by):
        w, rows = item.weight, self.rows(item)
        last = self.landed[self.bit_count - 1][w]
        src, dst = {
            "in": (last, self.zin[w]),
            "mid": (last, self.zmid[w]),
            "out": (self.zmid[w], self.zmid[w]),
        }[kind]
        slot = self.bit_count + {"in": 0, "mid": 1, "out": 2}[kind]
        return pltpu.make_async_remote_copy(
            src.at[rows],
            dst.at[rows],
            self.send.at[item.number, slot],
            self.recv.at[item.number, slot],
            device_id=along(by),
            device_id_type=MESH,
        )

    def sides(self):
        half = self.depth // 2
        outermost = (self.place == 0) | (self.place == self.depth - 1)
        middle = (self.place == half - 1) | (self.place == half)
        inward = 1 - 2 * (self.place // half)
        return outermost, middle, inward

    def z_first(self, item):
        outermost, middle, inward = self.sides()

        @pl.when(outermost & jnp.logical_not(middle))
        def _():
            self.z_copy(item, "in", inward).start()

    def z_second(self, item):
        outermost, middle, inward = self.sides()

        @pl.when(jnp.logical_not(outermost))
        def _():
            self.z_copy(item, "in", -inward).wait_recv()
            self.add(self.landed[self.bit_count - 1][item.weight], (), self.zin[item.weight], (), item)

            @pl.when(jnp.logical_not(middle))
            def _():
                self.z_copy(item, "in", inward).start()

        @pl.when(middle)
        def _():
            self.z_copy(item, "mid", inward).start()

    def z_third(self, item):
        outermost, middle, inward = self.sides()

        @pl.when(middle)
        def _():
            self.z_copy(item, "mid", inward).wait_recv()
            self.add(self.zmid[item.weight], (), self.landed[self.bit_count - 1][item.weight], (), item)

            @pl.when(jnp.logical_not(outermost))
            def _():
                self.z_copy(item, "out", -inward).start()

    def z_fourth(self, item):
        outermost, middle, inward = self.sides()

        @pl.when(jnp.logical_not(middle))
        def _():
            self.z_copy(item, "out", inward).wait_recv()

            @pl.when(jnp.logical_not(outermost))
            def _():
                self.z_copy(item, "out", -inward).start()

        self.out_copy(item).start()

    def out_copy(self, item):
        rows = self.rows(item)
        return pltpu.make_async_copy(
            self.zmid[item.weight].at[rows], self.out[item.weight].at[rows], self.own_sem.at[item.number]
        )

    def pump(self, count):
        for _ in range(min(count, len(self.todo))):
            self.todo.pop(0)()

    def finish(self, item):
        outermost, middle, inward = self.sides()
        self.out_copy(item).wait()
        for stage in range(self.bit_count):
            self.copy(item, stage).wait_send()

        @pl.when(jnp.logical_not(middle))
        def _():
            self.z_copy(item, "in", inward).wait_send()

        @pl.when(middle)
        def _():
            self.z_copy(item, "mid", inward).wait_send()

        @pl.when(jnp.logical_not(outermost))
        def _():
            self.z_copy(item, "out", -inward).wait_send()

    def actions(self, lag, z_lag):
        steps = []
        for i, item in enumerate(self.items):
            for stage in range(self.bit_count):
                steps.append((i + lag * stage, stage, lambda item=item, s=stage: self.advance(item, s)))
            t = i + lag * (self.bit_count - 1)
            for n, run in enumerate((self.z_first, self.z_second, self.z_third, self.z_fourth)):
                steps.append((t + n * z_lag, self.bit_count + n, lambda item=item, run=run: run(item)))
        self.todo = [action for _, _, action in sorted(steps, key=lambda s: s[:2])]


def enter(bit_count, depth):
    bits = position_bits(bit_count)
    place = lax.axis_index("seq")
    barrier = pltpu.get_barrier_semaphore()
    for axis in range(bit_count):
        pl.semaphore_signal(barrier, inc=1, device_id=across(bits, axis), device_id_type=MESH)

    @pl.when(place > 0)
    def _():
        pl.semaphore_signal(barrier, inc=1, device_id=along(-1), device_id_type=MESH)

    @pl.when(place < depth - 1)
    def _():
        pl.semaphore_signal(barrier, inc=1, device_id=along(1), device_id_type=MESH)

    ends = jnp.where(place == 0, 1, 0) + jnp.where(place == depth - 1, 1, 0)
    pl.semaphore_wait(barrier, bit_count + 2 - ends)


def small_sum(bit_count, depth, src, buf, out, send, recv):
    bits = position_bits(bit_count)
    place = lax.axis_index("seq")
    half = depth // 2
    outermost = (place == 0) | (place == depth - 1)
    middle = (place == half - 1) | (place == half)
    inward = 1 - 2 * (place // half)

    def flip(stage):
        return pltpu.make_async_remote_copy(
            (src if stage == 0 else out.at[stage - 1]),
            buf.at[stage],
            send.at[stage],
            recv.at[stage],
            device_id=across(bits, bit_count - 1 - stage),
            device_id_type=MESH,
        )

    def z_copy(kind, by):
        n = bit_count + kind
        return pltpu.make_async_remote_copy(
            out.at[(bit_count - 1, bit_count, bit_count + 1)[kind]],
            (buf.at[bit_count], buf.at[bit_count + 1], out.at[bit_count + 1])[kind],
            send.at[n],
            recv.at[n],
            device_id=along(by),
            device_id_type=MESH,
        )

    def flip_done(stage):
        flip(stage).wait_recv()
        mine = src[...] if stage == 0 else out[stage - 1]
        out[stage] = mine + buf[stage]
        if stage + 1 < bit_count:
            flip(stage + 1).start()

    def z_in():
        @pl.when(jnp.logical_not(middle))
        def _():
            @pl.when(jnp.logical_not(outermost))
            def _():
                z_copy(0, -inward).wait_recv()
                out[bit_count - 1] = out[bit_count - 1] + buf[bit_count]

            z_copy(0, inward).start()

        @pl.when(middle)
        def _():
            out[bit_count] = out[bit_count - 1]

            @pl.when(jnp.logical_not(outermost))
            def _():
                z_copy(0, -inward).wait_recv()
                out[bit_count] = out[bit_count] + buf[bit_count]

            z_copy(1, inward).start()

    def z_mid():
        @pl.when(middle)
        def _():
            z_copy(1, inward).wait_recv()
            out[bit_count + 1] = out[bit_count] + buf[bit_count + 1]

    def z_out():
        @pl.when(jnp.logical_not(middle))
        def _():
            z_copy(2, inward).wait_recv()

        @pl.when(jnp.logical_not(outermost))
        def _():
            z_copy(2, -inward).start()

    def finish():
        for stage in range(bit_count):
            flip(stage).wait_send()

        @pl.when(jnp.logical_not(middle))
        def _():
            z_copy(0, inward).wait_send()

        @pl.when(middle)
        def _():
            z_copy(1, inward).wait_send()

        @pl.when(jnp.logical_not(outermost))
        def _():
            z_copy(2, -inward).wait_send()

    begin = lambda: flip(0).start()
    steps = [lambda s=s: flip_done(s) for s in range(bit_count)] + [z_in, z_mid, z_out]
    return begin, steps, finish


def bit_length(count):
    return count.bit_length() - 1


def reduce_all(gradients, small, parts):
    fsdp, depth = lax.axis_size("fsdp"), lax.axis_size("seq")
    bit_count = bit_length(fsdp)
    shapes = [(g.shape[0] // fsdp, g.shape[1]) for g in gradients]
    items = plan_items(shapes, parts, bit_count)
    count = len(shapes)

    def kernel(*refs):
        at = 0

        def take(n):
            nonlocal at
            at += n
            return refs[at - n : at]

        whole, (small_ref,) = take(count), take(1)
        out, (small_out,) = take(count), take(1)
        own = take(count)
        landed = [take(count) for _ in range(bit_count)]
        zin, zmid = take(count), take(count)
        (small_buf, small_work) = take(2)
        send, recv, own_sem, small_send, small_recv = take(5)
        enter(bit_count, depth)
        work = Reducer(bit_count, depth, items, whole, own, landed, zin, zmid, out, send, recv, own_sem)
        begin, steps, finish = small_sum(
            bit_count, depth, small_ref, small_buf, small_work, small_send, small_recv
        )
        begin()
        for item in items:
            work.begin(item)
        work.actions(2, 2)
        while work.todo:
            work.pump(2)
            if steps:
                steps.pop(0)()
        for step in steps:
            step()
        small_out[...] = small_work[bit_count + 1]
        for item in items:
            work.finish(item)
        finish()

    two = (2,) * bit_count
    stacks = [[pltpu.VMEM((*two[: bit_count - 1 - s], *shape), bf16) for shape in shapes] for s in range(bit_count)]
    flat = [pltpu.VMEM(shape, bf16) for shape in shapes]
    rooms = [pltpu.VMEM(own_shape(bit_count, shape, n), bf16) for shape, n in zip(shapes, parts)]
    scratch = [*rooms, *[b for stage in stacks for b in stage], *flat, *flat]
    scratch += [pltpu.VMEM((bit_count + 2, *small.shape), f32)] * 2
    scratch += [
        pltpu.SemaphoreType.DMA((len(items), bit_count + 3)),
        pltpu.SemaphoreType.DMA((len(items), bit_count + 3)),
        pltpu.SemaphoreType.DMA((len(items),)),
        pltpu.SemaphoreType.DMA((bit_count + 3,)),
        pltpu.SemaphoreType.DMA((bit_count + 3,)),
    ]
    return pl.pallas_call(
        kernel,
        out_shape=[jax.ShapeDtypeStruct(shape, bf16) for shape in shapes]
        + [jax.ShapeDtypeStruct(small.shape, f32)],
        in_specs=[pl.BlockSpec(memory_space=pl.ANY)] * count + [vmem],
        out_specs=[pl.BlockSpec(memory_space=pl.ANY)] * count + [vmem],
        scratch_shapes=scratch,
        compiler_params=pltpu.CompilerParams(
            collective_id=0, has_side_effects=True, vmem_limit_bytes=60 * 2**20
        ),
    )(*[g.reshape(*two, *shape) for g, shape in zip(gradients, shapes)], small)


class Gatherer:
    def __init__(self, bit_count, items, shards, whole, loads, load_sem, cast_to, own_sem, send, recv):
        self.bit_count, self.items = bit_count, items
        self.shards, self.whole, self.loads, self.load_sem = shards, whole, loads, load_sem
        self.cast_to, self.own_sem, self.send, self.recv = cast_to, own_sem, send, recv
        self.bits = position_bits(bit_count)
        self.index = lax.axis_index("fsdp")
        self.ready = set()
        self.todo = []
        self.done = set()

    def block(self, axes):
        at = self.index
        for axis in axes:
            at = at + (1 << (self.bit_count - 1 - axis)) * (1 - 2 * self.bits[axis])
        return at

    def subsets(self, order):
        sets = [()]
        for axis in order:
            sets = sets + [(*s, axis) for s in sets]
        return sets

    def rows(self, item, axes):
        shard_rows = self.cast_to[item.weight].shape[0]
        return pl.ds(pl.multiple_of(self.block(axes) * shard_rows + item.start, 16), item.size)

    def copy(self, item, stage, number, axes):
        whole = self.whole[item.weight]
        at = self.rows(item, axes)
        src = self.cast_to[item.weight].at[pl.ds(item.start, item.size)] if not axes else whole.at[at]
        slot = (1 << stage) - 1 + number
        return pltpu.make_async_remote_copy(
            src,
            whole.at[at],
            self.send.at[item.number, slot],
            self.recv.at[item.number, slot],
            device_id=across(self.bits, item.order[stage]),
            device_id_type=MESH,
        )

    def landed(self, item, stage, number, axes):
        whole = self.whole[item.weight]
        at = self.rows(item, (*axes, item.order[stage]))
        slot = (1 << stage) - 1 + number
        return pltpu.make_async_remote_copy(
            whole.at[at],
            whole.at[at],
            self.send.at[item.number, slot],
            self.recv.at[item.number, slot],
            device_id=across(self.bits, item.order[stage]),
            device_id_type=MESH,
        )

    def load(self, weight):
        return pltpu.make_async_copy(self.shards[weight], self.loads[weight], self.load_sem.at[weight])

    def own(self, weight):
        rows = self.cast_to[weight].shape[0]
        return pltpu.make_async_copy(
            self.cast_to[weight],
            self.whole[weight].at[pl.ds(pl.multiple_of(self.index * rows, 16), rows)],
            self.own_sem.at[weight],
        )

    def begin(self, item):
        w = item.weight
        if w not in self.ready:
            self.ready.add(w)
            self.load(w).wait()
            group = 16

            def step(i, nothing):
                at = pl.ds(pl.multiple_of(i * group, group), group)
                self.cast_to[w][at] = low(self.loads[w][at])
                return nothing

            lax.fori_loop(0, self.cast_to[w].shape[0] // group, step, 0)
            self.own(w).start()
        for stage in range(self.bit_count):
            self.copy(item, stage, 0, ()).start()

    def advance(self, item, stage):
        before = self.subsets(item.order[:stage])
        for number, axes in enumerate(before):
            self.landed(item, stage, number, axes).wait_recv()
        for later in range(stage + 1, self.bit_count):
            sets = self.subsets(item.order[:later])
            for number, axes in enumerate(before):
                mine = (*axes, item.order[stage])
                self.copy(item, later, sets.index(mine), mine).start()
        if stage == self.bit_count - 1:
            self.done.add(item.number)

    def plan(self, lag):
        steps = []
        for i, item in enumerate(self.items):
            steps.append((i, 0, lambda item=item: self.begin(item)))
            for stage in range(self.bit_count):
                steps.append((i + lag * (stage + 1), stage + 1, lambda item=item, s=stage: self.advance(item, s)))
        self.todo = [action for _, _, action in sorted(steps, key=lambda s: s[:2])]

    def pump(self, count):
        for _ in range(min(count, len(self.todo))):
            self.todo.pop(0)()

    def until(self, weight):
        numbers = {item.number for item in self.items if item.weight == weight}
        while not numbers <= self.done:
            self.todo.pop(0)()
        self.own(weight).wait()

    def finish(self):
        for item in self.items:
            for stage in range(self.bit_count):
                for number, axes in enumerate(self.subsets(item.order[:stage])):
                    self.copy(item, stage, number, axes).wait_send()


def multiply(out_ref, out_rows, left, right_ref, first, width, tile):
    def step(j, nothing):
        at = pl.ds(pl.multiple_of(j * tile, tile), tile)
        from_at = pl.ds(pl.multiple_of(first + j * tile, 128), tile)
        out_ref[out_rows, at] = dot_nn(left[...], right_ref[:, from_at])
        return nothing

    lax.fori_loop(0, width // tile, step, 0)


def forward_part(tokens, seg_rows, norm_gain, cosine, signed, bias_row, rate_row, conv_weight,
                 conv_bias, mixer_gain, skip_row, shards, parts):
    fsdp, depth = lax.axis_size("fsdp"), lax.axis_size("seq")
    bit_count = bit_length(fsdp)
    shapes = [s.shape for s in shards]
    items = plan_items(shapes, parts, bit_count)
    for item in items:
        item.order = item.order[1:] + item.order[:1]
    count = tokens.shape[0]
    weights = len(shards)
    pieces = 2
    kept_shape = (count // SUB, NS, DI)
    results = dict(
        normed=((count, 1024), bf16),
        conv=((count + EDGE, CW), f32),
        raw=((count, 128), f32),
        z=((count, DI), f32),
        act=((count, CW), bf16),
        dt=((count, 128), f32),
        cum=((count, 128), f32),
        passing=((1, DI), f32),
        query=((count, 512), bf16),
        kv=((depth * count, 256), bf16),
        attended=((count, 512), bf16),
        attended_t=((512, count), f32),
        log_total=((QUERY_HEADS * 8, count), f32),
        y=((count, DI), f32),
        gated=((count, DI), bf16),
        kept=(kept_shape, bf16),
        seg_wide=((count + 2 * EDGE, 128), f32),
        seg_col=((depth * count, 128), bf16),
    )
    names = list(results)
    local = dict(
        normed_edge=((16, 1024), bf16),
        edge=((16, 1024), bf16),
        seg_all=((depth * 8, count), f32),
        qkv=((count, 768), f32),
        end=((NS, DI), f32),
        state=((NS, DI), f32),
        carry=((NS, DI), f32),
        state_send=((NS, DI), bf16),
        state_recv=((NS, DI), bf16),
        bias=((count, count), f32),
        keys=((4, count, 128), bf16),
        values_t=((128, count), bf16),
        top=((QUERY_HEADS * 8, count), f32),
        total=((QUERY_HEADS * 8, count), f32),
    )
    in_vmem = (0, 1)

    def kernel(*refs):
        at = 0

        def take(n):
            nonlocal at
            at += n
            return refs[at - n : at]

        (tokens_ref, segrow_ref, gain_ref, cos_ref, sin_ref, bias_ref, rate_ref, weight_ref, cbias_ref,
         mixer_gain_ref, skip_ref) = take(11)
        shard_refs = take(weights)
        out = dict(zip(names, take(len(names))))
        whole_out = take(weights)
        v = dict(zip(names, take(len(names))))
        v.update(zip(local, take(len(local))))
        loads, cast_to = take(weights), take(weights)
        whole_vmem = take(len(in_vmem))
        send, recv, load_sem, own_sem, save_sem, z_send, z_recv = take(7)
        place = lax.axis_index("seq")
        whole = [whole_vmem[in_vmem.index(w)] if w in in_vmem else whole_out[w] for w in range(weights)]
        gather = Gatherer(bit_count, items, shard_refs, whole, loads, load_sem, cast_to, own_sem, send, recv)
        for w in range(weights):
            gather.load(w).start()
        enter(bit_count, depth)
        gather.plan(2)
        saved = []

        def save(src, dst):
            copy = pltpu.make_async_copy(src, dst, save_sem.at[len(saved)])
            copy.start()
            saved.append(copy)

        def keep(*which):
            for name in which:
                save(v[name], out[name])

        def to_next(src, dst, slot):
            return pltpu.make_async_remote_copy(
                src, dst, z_send.at[slot], z_recv.at[slot], device_id=along(1), device_id_type=MESH
            )

        started = []

        def send_on(condition, src, dst, slot):
            @pl.when(condition)
            def _():
                to_next(src, dst, slot).start()

            started.append((condition, src, dst, slot))

        def ring(ref, rows, hop, slot):
            b = place - hop + 1
            part = ref.at[pl.ds(pl.multiple_of(jnp.maximum(b, 0) * rows, 8), rows)]
            send_on((b >= 0) & (place < depth - 1), part, part, slot)

        def ring_wait(ref, rows, hop, slot):
            b = place - hop
            part = ref.at[pl.ds(pl.multiple_of(jnp.maximum(b, 0) * rows, 8), rows)]

            @pl.when(b >= 0)
            def _():
                to_next(part, part, slot).wait_recv()

        tail = tokens_ref.at[pl.ds(count - 16, 16)]
        gather.pump(2)
        send_on(place < depth - 1, tail, v["edge"], 0)
        v["seg_all"][pl.ds(pl.multiple_of(place * 8, 8), 8)] = jnp.broadcast_to(segrow_ref[...], (8, count))
        ring(v["seg_all"], 8, 1, 1)

        def normalise(src, dst, rows, group):
            def step(i, nothing):
                at = pl.ds(pl.multiple_of(i * group, group), group)
                x = src[at].astype(f32)
                scale = lax.rsqrt(jnp.mean(x * x, axis=1, keepdims=True) + epsilon)
                dst[at] = low(x * scale * gain_ref[...])
                return nothing

            lax.fori_loop(0, rows // group, step, 0)

        normalise(tokens_ref, v["normed"], count, 64)
        gather.pump(1)

        @pl.when(place == 0)
        def _():
            v["edge"][...] = jnp.zeros((16, 1024), bf16)

        @pl.when(place > 0)
        def _():
            to_next(tail, v["edge"], 0).wait_recv()

        normalise(v["edge"], v["normed_edge"], 16, 16)
        gather.pump(1)
        for hop in range(1, depth):
            ring_wait(v["seg_all"], 8, hop, hop)
            if hop < depth - 1:
                ring(v["seg_all"], 8, hop + 1, hop + 1)

        def column(row):
            return low(jnp.broadcast_to(row, (128, count)).T)

        for b in range(depth):

            @pl.when(b <= place)
            def _(b=b):
                v["seg_col"][b * count : (b + 1) * count, :] = column(v["seg_all"][b * 8 : b * 8 + 1, :])

            @pl.when(b > place)
            def _(b=b):
                v["seg_col"][b * count : (b + 1) * count, :] = jnp.full((count, 128), -2.0, bf16)

        own_rows = pl.ds(pl.multiple_of(place * count, 8), count)
        v["seg_wide"][EDGE : EDGE + count, :] = v["seg_col"][own_rows, :].astype(f32)
        v["seg_wide"][EDGE + count :, :] = jnp.full((EDGE, 128), -2.0, f32)
        before = pl.ds(pl.multiple_of(jnp.maximum(place * count - 16, 0), 16), 16)
        v["seg_wide"][0:EDGE, :] = jnp.where(place == 0, -1.0, v["seg_col"][before, :].astype(f32)[16 - EDGE :])
        v["raw"][...] = jnp.zeros((count, 128), f32)
        gather.until(0)
        save(whole[0], whole_out[0])
        multiply(v["conv"], pl.ds(EDGE, count), v["normed"], whole[0], DI, CW, 256)
        v["conv"][0:EDGE, :] = dot_nn(v["normed_edge"][...], whole[0][:, DI : DI + CW])[EDGE:]
        v["raw"][:, 0:MH] = dot_nn(v["normed"][...], whole[0][:, DI + CW : DI + CW + MH])
        gather.pump(4)
        front_conv(v["conv"], v["seg_wide"], weight_ref, cbias_ref, v["act"])
        gather.pump(4)
        front_state(v["seg_wide"], v["raw"], bias_ref, rate_ref, v["act"], v["dt"], v["cum"], v["end"], v["passing"])
        keep("normed", "conv", "raw", "act", "dt", "cum", "passing", "seg_wide", "seg_col")
        width = DI // pieces
        state_slot, kv_slot = depth, depth + pieces

        def chain(j):
            for p in range(pieces):
                cols = pl.ds(p * width, width)

                @pl.when(place == j)
                def _():
                    if j == 0:
                        v["state"][:, cols] = jnp.zeros((NS, width), f32)
                    else:
                        to_next(
                            v["state_send"].at[:, cols], v["state_recv"].at[:, cols], state_slot + p
                        ).wait_recv()
                        v["state"][:, cols] = v["state_recv"][:, cols].astype(f32)
                    if j < depth - 1:
                        v["state_send"][:, cols] = low(
                            v["passing"][:, cols] * v["state"][:, cols] + v["end"][:, cols]
                        )
                        to_next(
                            v["state_send"].at[:, cols], v["state_recv"].at[:, cols], state_slot + p
                        ).start()

        chain(0)
        gather.until(1)
        save(whole[1], whole_out[1])
        multiply(v["qkv"], slice(None), v["normed"], whole[1], 0, 768, 256)
        rotate_kernel(v["qkv"], cos_ref, sin_ref, v["query"], v["kv"].at[own_rows])
        ring(v["kv"], count, 1, kv_slot + 1)
        keep("query")
        gather.pump(4)
        multiply(v["z"], slice(None), v["normed"], whole[0], 0, DI, 256)
        keep("z")
        gather.pump(4)
        chain(1)
        attend_start(v["top"], v["total"], v["attended_t"])

        def attend(b):
            attend_block(b, place, v["query"], v["kv"], v["seg_col"], segrow_ref, v["attended_t"], v["bias"],
                         v["keys"], v["values_t"], v["top"], v["total"])

        attend(place)
        gather.pump(4)
        for hop in range(1, depth):
            ring_wait(v["kv"], count, hop, kv_slot + hop)
            if hop < depth - 1:
                ring(v["kv"], count, hop + 1, kv_slot + hop + 1)

            @pl.when(place >= hop)
            def _(hop=hop):
                attend(place - hop)

            gather.pump(4)
            if hop < depth - 1:
                chain(hop + 1)

        attend_finish(v["attended"], v["attended_t"], v["log_total"], v["top"], v["total"])
        keep("attended", "attended_t", "log_total", "kv")
        for first in range(0, count // SUB, 2):
            gather.pump(4)
            mid_kernel(v["act"], v["dt"], v["cum"], v["seg_wide"], segrow_ref, v["state"], v["z"], mixer_gain_ref,
                       skip_ref, v["y"], v["gated"], v["kept"], v["carry"], first, first + 2)
        keep("y", "gated", "kept")
        for w in range(2, weights):
            gather.until(w)
        gather.finish()
        for condition, src, dst, slot in started:

            @pl.when(condition)
            def _(src=src, dst=dst, slot=slot):
                to_next(src, dst, slot).wait_send()

        @pl.when(place < depth - 1)
        def _():
            for p in range(pieces):
                cols = pl.ds(p * width, width)
                to_next(v["state_send"].at[:, cols], v["state_recv"].at[:, cols], state_slot + p).wait_send()

        for copy in saved:
            copy.wait()

    wholes = [((fsdp * rows, cols), bf16) for rows, cols in shapes]
    scratch = [pltpu.VMEM(*results[n]) for n in names] + [pltpu.VMEM(*a) for a in local.values()]
    scratch += [pltpu.VMEM(shape, f32) for shape in shapes] + [pltpu.VMEM(shape, bf16) for shape in shapes]
    scratch += [pltpu.VMEM(*wholes[w]) for w in in_vmem]
    slots = (1 << bit_count) - 1
    z_slots = depth + pieces + depth
    scratch += [
        pltpu.SemaphoreType.DMA((len(items), slots)),
        pltpu.SemaphoreType.DMA((len(items), slots)),
        pltpu.SemaphoreType.DMA((weights,)),
        pltpu.SemaphoreType.DMA((weights,)),
        pltpu.SemaphoreType.DMA((len(names) + 2,)),
        pltpu.SemaphoreType.DMA((z_slots,)),
        pltpu.SemaphoreType.DMA((z_slots,)),
    ]
    hbm = pl.BlockSpec(memory_space=pl.ANY)
    made = pl.pallas_call(
        kernel,
        out_shape=[jax.ShapeDtypeStruct(*a) for a in list(results.values()) + wholes],
        in_specs=[vmem] * 11 + [hbm] * weights,
        out_specs=[hbm] * (len(names) + weights),
        scratch_shapes=scratch,
        compiler_params=pltpu.CompilerParams(
            collective_id=1, has_side_effects=True, vmem_limit_bytes=62 * 2**20
        ),
    )(tokens, seg_rows, norm_gain, cosine, signed, bias_row, rate_row, conv_weight, conv_bias, mixer_gain,
      skip_row, *shards)
    return dict(zip(names, made)), made[len(names) :]


def backward_part(v, gated_grad, attended_grad, cosine, signed, seg_row, bias_row, rate_row, conv_weight,
                  conv_bias, mixer_gain, skip_row, gradients, parts):
    fsdp, depth = lax.axis_size("fsdp"), lax.axis_size("seq")
    bit_count = bit_length(fsdp)
    shapes = [(g.shape[0] // fsdp, g.shape[1]) for g in gradients]
    items = plan_items(shapes, parts, bit_count)
    weights = len(shapes)
    count = gated_grad.shape[0]
    pieces = 2
    loaded = dict(
        grad=gated_grad, y=v["y"], act=v["act"], z=v["z"], dt=v["dt"], cum=v["cum"], seg_wide=v["seg_wide"],
        out_grad=attended_grad, query=v["query"], out_t=v["attended_t"], kv=v["kv"], seg_col=v["seg_col"],
        log_total=v["log_total"], cos=cosine, sin=signed, raw=v["raw"], kept=v["kept"],
    )
    rows_in = (seg_row, bias_row, rate_row, conv_weight, conv_bias, mixer_gain, skip_row, v["passing"])
    results = dict(
        raw_grad=((count, 128), bf16),
        qkv_grad=((count, 768), bf16),
    )
    names, loads = list(results), list(loaded)
    rows_out = [((1, DI), f32), ((KC, CW), f32), ((1, CW), f32), ((1, 128), f32), ((1, 128), f32), ((1, 128), f32)]
    local = dict(
        ygrad=((count, DI), f32),
        state_grad=((NS, DI), f32),
        later=((NS, DI), f32),
        state_send=((NS, DI), bf16),
        state_recv=((NS, DI), bf16),
        bias=((count, count), f32),
        keys=((4, count, 128), bf16),
        values=((4, count, 128), bf16),
        keys_t=((128, count), bf16),
        dkeys=((2, count, 128), f32),
        dvalues=((2, count, 128), f32),
        spread=((QUERY_HEADS * 8, count), f32),
        kv_grad=((depth * count, 256), bf16),
        kv_recv=(((depth - 1) * count, 256), bf16),
        pair_grad=((count, 2 * NS), f32),
        pair_conv_grad=((count, 2 * NS), bf16),
        conv=((2, count + EDGE, 128), f32),
        pre=((count + 2 * EDGE, 128), f32),
        edge=((EDGE, CW), f32),
        edge_recv=((EDGE, CW), f32),
        tail=((16, CW), f32),
    )

    def kernel(*refs):
        at = 0

        def take(n):
            nonlocal at
            at += n
            return refs[at - n : at]

        (segrow_ref, bias_ref, rate_ref, weight_ref, cbias_ref, gain_ref, skip_ref, passing_ref) = take(len(rows_in))
        inputs = dict(zip(loads, take(len(loads))))
        (conv_hbm,) = take(1)
        whole = take(weights)
        out = dict(zip(names, take(len(names))))
        conv_grad_out, zgrad_out = take(2)
        gain_grad, weight_grad, cbias_grad, rate_grad, bias_grad, skip_grad = take(6)
        sums = take(weights)
        b = dict(zip(names, take(len(names))))
        b.update(zip(loads, take(len(loads))))
        b.update(zip(local, take(len(local))))
        own = take(weights)
        landed = [take(weights) for _ in range(bit_count)]
        zin, zmid = take(weights), take(weights)
        send, recv, own_sem, load_sem, save_sem, conv_sem, z_send, z_recv = take(8)
        place = lax.axis_index("seq")

        def load(name):
            return pltpu.make_async_copy(inputs[name], b[name], load_sem.at[loads.index(name)])

        def need(*which):
            for name in which:
                load(name).wait()

        for name in loads:
            load(name).start()
        enter(bit_count, depth)
        work = Reducer(bit_count, depth, items, whole, own, landed, zin, zmid, sums, send, recv, own_sem)
        for item in items:
            work.begin(item)
        work.actions(2, 2)
        saved, numbers = [], iter(range(len(names) + 3))

        def save(src, dst):
            copy = pltpu.make_async_copy(src, dst, save_sem.at[next(numbers)])
            copy.start()
            saved.append(copy)

        def to(by, src, dst, slot):
            return pltpu.make_async_remote_copy(
                src, dst, z_send.at[slot], z_recv.at[slot], device_id=along(by), device_id_type=MESH
            )

        need("grad", "y", "act", "z", "dt", "cum", "seg_wide")
        for first in range(0, count // SUB, 2):
            gate_back_kernel(b["grad"], b["y"], b["act"], b["z"], b["dt"], b["cum"], b["seg_wide"], gain_ref,
                             skip_ref, b["ygrad"], b["grad"], gain_grad, b["state_grad"], first, first + 2)
            work.pump(4)
        save(b["grad"], zgrad_out)
        width = DI // pieces

        def chain(j):
            for p in range(pieces):
                cols = pl.ds(p * width, width)

                @pl.when(place == j)
                def _():
                    copy = to(-1, b["state_send"].at[:, cols], b["state_recv"].at[:, cols], p)
                    if j == depth - 1:
                        b["later"][:, cols] = jnp.zeros((NS, width), f32)
                    else:
                        copy.wait_recv()
                        b["later"][:, cols] = b["state_recv"][:, cols].astype(f32)
                    if j > 0:
                        b["state_send"][:, cols] = low(
                            passing_ref[:, cols] * b["later"][:, cols] + b["state_grad"][:, cols]
                        )
                        copy.start()

        def kv_hop(i):
            part = pl.ds(i * count, count)
            copy = to(-1, b["kv_grad"].at[part], b["kv_recv"].at[part], pieces + i)

            @pl.when((place >= i) & (place < depth - 1))
            def _():
                copy.wait_recv()

                def step(n, nothing):
                    at = pl.ds(pl.multiple_of(i * count + n * 64, 64), 64)
                    b["kv_grad"][at] = low(b["kv_grad"][at].astype(f32) + b["kv_recv"][at].astype(f32))
                    return nothing

                lax.fori_loop(0, count // 64, step, 0)

            @pl.when(place > i)
            def _():
                copy.start()

        chain(depth - 1)
        need("out_grad", "query", "out_t", "kv", "seg_col", "log_total", "cos", "sin")
        attend_back_start(b["query"], b["out_grad"], b["out_t"], b["spread"])
        for i in range(depth):

            @pl.when(i <= place)
            def _(i=i):
                attend_back_block(i, place, b["query"], b["kv"], b["seg_col"], segrow_ref, b["out_grad"],
                                  b["log_total"], b["kv_grad"], b["bias"], b["keys"], b["values"], b["keys_t"],
                                  b["dkeys"], b["dvalues"], b["spread"], b["out_t"])

            work.pump(5)
            if i < depth - 1:
                chain(depth - 2 - i)
            if i > 0:
                kv_hop(i - 1)
        attend_back_finish(b["out_t"], b["cos"], b["sin"], b["qkv_grad"])
        need("raw", "kept")
        for first in range(0, count // SUB, 2):
            back_states(b["act"], b["dt"], b["cum"], b["seg_wide"], segrow_ref, b["raw"], bias_ref, rate_ref,
                        b["kept"], b["y"], b["ygrad"], skip_ref, b["raw_grad"], rate_grad, bias_grad, skip_grad,
                        b["z"], b["pair_grad"], b["later"], first, first + 2)
            work.pump(5)
        save(b["raw_grad"], out["raw_grad"])
        own_rows = pl.ds(pl.multiple_of(place * count, 8), count)
        x = b["kv_grad"][own_rows, 0:128].astype(f32)
        b["qkv_grad"][:, 512:640] = low(x * b["cos"][...] + partner(x * b["sin"][...]))
        b["qkv_grad"][:, 640:768] = b["kv_grad"][own_rows, 128:256]
        save(b["qkv_grad"], out["qkv_grad"])
        saved.pop(0).wait()
        tiles, value_tiles = CW // 128, DI // 128
        for first, until in ((0, value_tiles // 2), (value_tiles // 2, value_tiles), (value_tiles, tiles)):
            source, dst, shift = b["z"], b["grad"], 0
            if until > value_tiles:
                source, dst, shift = b["pair_grad"], b["pair_conv_grad"], value_tiles
            back_conv(conv_hbm, b["conv"], conv_sem, b["seg_wide"], weight_ref, cbias_ref, source, shift,
                      dst, b["edge"], b["tail"], weight_grad, cbias_grad, b["pre"], first, until)
            work.pump(5)
        edge = to(-1, b["edge"], b["edge_recv"], pieces + depth)

        @pl.when(place > 0)
        def _():
            edge.start()

        work.pump(len(work.todo))

        @pl.when(place < depth - 1)
        def _():
            edge.wait_recv()
            b["tail"][16 - EDGE :, :] = b["tail"][16 - EDGE :, :] + b["edge_recv"][...]
            b["grad"][count - 16 :, :] = low(b["tail"][:, :DI])
            b["pair_conv_grad"][count - 16 :, :] = low(b["tail"][:, DI:])

        save(b["grad"], conv_grad_out.at[:, :DI])
        save(b["pair_conv_grad"], conv_grad_out.at[:, DI:])
        for item in items:
            work.finish(item)

        @pl.when(place > 0)
        def _():
            edge.wait_send()
            for p in range(pieces):
                cols = pl.ds(p * width, width)
                to(-1, b["state_send"].at[:, cols], b["state_recv"].at[:, cols], p).wait_send()

        for i in range(depth - 1):

            @pl.when(place > i)
            def _(i=i):
                part = pl.ds(i * count, count)
                to(-1, b["kv_grad"].at[part], b["kv_recv"].at[part], pieces + i).wait_send()

        for copy in saved:
            copy.wait()

    two = (2,) * bit_count
    hbm = pl.BlockSpec(memory_space=pl.ANY)
    scratch = [pltpu.VMEM(*results[n]) for n in names]
    scratch += [pltpu.VMEM(x.shape, x.dtype) for x in loaded.values()]
    scratch += [pltpu.VMEM(*a) for a in local.values()]
    stacks = [[pltpu.VMEM((*two[: bit_count - 1 - s], *shape), bf16) for shape in shapes] for s in range(bit_count)]
    flat = [pltpu.VMEM(shape, bf16) for shape in shapes]
    rooms = [pltpu.VMEM(own_shape(bit_count, shape, n), bf16) for shape, n in zip(shapes, parts)]
    scratch += [*rooms, *[x for stage in stacks for x in stage], *flat, *flat]
    slots = pieces + depth + 1
    scratch += [
        pltpu.SemaphoreType.DMA((len(items), bit_count + 3)),
        pltpu.SemaphoreType.DMA((len(items), bit_count + 3)),
        pltpu.SemaphoreType.DMA((len(items),)),
        pltpu.SemaphoreType.DMA((len(loads),)),
        pltpu.SemaphoreType.DMA((len(names) + 3,)),
        pltpu.SemaphoreType.DMA((2,)),
        pltpu.SemaphoreType.DMA((slots,)),
        pltpu.SemaphoreType.DMA((slots,)),
    ]
    outs = [*results.values(), ((count, CW), bf16), ((count, DI), bf16), *rows_out, *[(shape, bf16) for shape in shapes]]
    made = pl.pallas_call(
        kernel,
        out_shape=[jax.ShapeDtypeStruct(*a) for a in outs],
        in_specs=[vmem] * len(rows_in) + [hbm] * (len(loads) + 1 + weights),
        out_specs=[hbm] * (len(names) + 2) + [vmem] * len(rows_out) + [hbm] * weights,
        scratch_shapes=scratch,
        compiler_params=pltpu.CompilerParams(
            collective_id=2, has_side_effects=True, vmem_limit_bytes=63 * 2**20
        ),
    )(*rows_in, *loaded.values(), v["conv"], *[g.reshape(*two, *shape) for g, shape in zip(gradients, shapes)])
    n = len(names) + 2
    return made[:n], made[n : n + len(rows_out)], made[n + len(rows_out) :]


def shifted(array, axis, by):
    devices = lax.axis_size(axis)
    pairs = [(i, i + by) for i in range(devices) if 0 <= i + by < devices]
    return lax.ppermute(array, axis, pairs)


def contract(left, right):
    return dot_tn(left, right)


def rms_scale(values, gain_vec):
    return (
        values * lax.rsqrt(jnp.mean(values * values, axis=-1, keepdims=True) + epsilon) * gain_vec
    )


def reduced(gradient):
    return low(gradient)


def padded(vector):
    return jnp.pad(vector, (0, 128 - vector.shape[0]))[None]


def on_device(
    tokens,
    cotangent,
    segment_ids,
    norm_gain,
    ffn_gain,
    mixer_gain,
    conv_weight,
    conv_bias,
    decay_log,
    step_bias,
    skip_gain,
    in_proj,
    mixer_out,
    qkv_proj,
    attn_proj,
    gate_up,
    down_proj,
):
    place, devices = lax.axis_index("seq"), lax.axis_size("seq")
    count = tokens.shape[1]
    position = place * count + jnp.arange(count, dtype=jnp.int32)
    half = HEAD_WIDTH // 2
    lane = jnp.arange(128, dtype=jnp.int32)
    exponent = (lane % half).astype(f32) * (2.0 / HEAD_WIDTH)
    frequencies = jnp.power(rope_base, -exponent)
    angles = position.astype(f32)[:, None] * frequencies[None, :]
    cosine = jnp.cos(angles)
    signed = jnp.sin(angles) * jnp.where(lane % HEAD_WIDTH < half, -1.0, 1.0)[None]
    seg_row = segment_ids.astype(f32)
    bias_row, rate_row = padded(step_bias), padded(decay_log)
    skip_row = jnp.repeat(skip_gain, MP)[None]
    own = place.astype(jnp.int32)[None]
    v, (in_full, qkv_full, mix_full, attn_full, gate_full, down_full) = forward_part(
        tokens[0], seg_row, norm_gain[None], cosine, signed, bias_row, rate_row, conv_weight, conv_bias[None],
        mixer_gain[None], skip_row, (in_proj, qkv_proj, mixer_out, attn_proj, gate_up, down_proj),
        (4, 2, 2, 2, 4, 4),
    )
    normed, attended, gated, mixer_y, act, dt, cum = (
        v[n] for n in ("normed", "attended", "gated", "y", "act", "dt", "cum")
    )
    gate_z, seg_wide, seg_col, kept, kv_all, query = (
        v[n] for n in ("z", "seg_wide", "seg_col", "kept", "kv", "query")
    )
    attended_t, log_total, conv_ext, step_raw = (v[n] for n in ("attended_t", "log_total", "conv", "raw"))
    length = kv_all.shape[0]
    token_rows = tokens[0].astype(f32)
    _, norm_pull = jax.vjp(rms_scale, token_rows, norm_gain)
    hidden = token_rows + (dot_nn(attended, attn_full) + dot_nn(gated, mix_full))
    ffn_in32, ffn_pull = jax.vjp(rms_scale, hidden, ffn_gain)
    ffn_in = low(ffn_in32)
    gates = dot_nn(ffn_in, gate_full)

    def swiglu(values):
        return jax.nn.silu(values[:, :FF]) * values[:, FF:]

    act32, act_pull = jax.vjp(swiglu, gates)
    inner = low(act32)
    result = hidden + dot_nn(inner, down_full)
    back_rows = cotangent[0]
    down_piece = reduced(contract(inner, back_rows))
    (gates_grad,) = act_pull(dot_nt(back_rows, down_full))
    gates_grad = low(gates_grad)
    gate_piece = reduced(contract(ffn_in, gates_grad))
    hidden_extra, ffn_gain_grad = ffn_pull(dot_nt(gates_grad, gate_full))
    hidden_grad = back_rows.astype(f32) + hidden_extra
    branch = low(hidden_grad)
    attn_piece = reduced(contract(attended, branch))
    attended_grad = low(dot_nt(branch, attn_full))
    mixer_piece = reduced(contract(gated, branch))
    gated_grad = low(dot_nt(branch, mix_full))

    (raw_grad, qkv_grad, conv_grad, gate_z_grad), small_rows, early = backward_part(
        v, gated_grad, attended_grad, cosine, signed, seg_row, bias_row, rate_row, conv_weight, conv_bias[None],
        mixer_gain[None], skip_row, (down_piece, gate_piece, mixer_piece, attn_piece), (4, 4, 2, 2),
    )
    mixer_gain_grad, conv_weight_grad, conv_bias_grad, rate_grad, bias_grad, skip_grad = small_rows
    qkv_piece = reduced(contract(normed, qkv_grad))
    normed_grad = dot_nt(qkv_grad, qkv_full)
    mixed_grad = jnp.concatenate([gate_z_grad, conv_grad, raw_grad[:, :MH]], axis=1)
    in_piece = reduced(contract(normed, mixed_grad))
    normed_grad = normed_grad + dot_nt(mixed_grad, in_full)
    rows_extra, norm_gain_grad = norm_pull(normed_grad)
    input_grad = hidden_grad + rows_extra
    rows = (
        norm_gain_grad,
        ffn_gain_grad,
        mixer_gain_grad,
        conv_weight_grad,
        conv_bias_grad,
        rate_grad,
        bias_grad,
        skip_grad,
    )
    flat = jnp.concatenate([row.reshape(-1) for row in rows])
    flat = jnp.pad(flat, (0, 16384 - flat.shape[0])).reshape(16, 1024)
    in_sum, qkv_sum, flat = reduce_all((in_piece, qkv_piece), flat, (4, 2))
    down_sum, gate_sum, mixer_sum, attn_sum = early
    shards = [x.astype(f32) for x in (in_sum, mixer_sum, qkv_sum, attn_sum, gate_sum, down_sum)]
    flat, small, at = flat.reshape(-1), [], 0
    for row, keep in zip(rows, (None, None, None, None, None, MH, MH, MH)):
        part = flat[at : at + row.size].reshape(row.shape)
        at += row.size
        part = part[:, :keep] if keep else part
        small.append(part if part.shape[0] == KC else part.reshape(-1))
    return (low(result)[None], input_grad[None], *small, *shards)


def solution(mesh):
    rows, whole, split_rows = P("fsdp", "seq", None), P(), P("fsdp", None)
    return jax.shard_map(
        on_device,
        mesh=mesh,
        in_specs=(rows, rows, P("fsdp", "seq"), *[whole] * 8, *[split_rows] * 6),
        out_specs=(rows, rows, *[whole] * 8, *[split_rows] * 6),
        check_vma=False,
    )
```

```python
import jax
import jax.numpy as jnp
from jax import lax
from jax.experimental import pallas as pl
from jax.experimental.pallas import tpu as pltpu
from jax.sharding import PartitionSpec as P

FF = 2048
QUERY_HEADS = 8
KEY_VALUE_HEADS = 2
HEAD_WIDTH = 64
MH = 24
MP = 64
NS = 128
KC = 4
SUB = 128
DI = 1536
CW = 1792
EDGE = 8

epsilon = 1e-05
rope_base = 100000000000.0
highest = lax.Precision.HIGHEST
f32 = jnp.float32
bf16 = jnp.bfloat16


def dot_nn(left, right):
    return jnp.dot(left, right, preferred_element_type=jnp.float32)


def dot_nt(left, right):
    return lax.dot_general(
        left, right, (((1,), (1,)), ((), ())), preferred_element_type=jnp.float32
    )


def dot_tn(left, right):
    return lax.dot_general(
        left, right, (((0,), (0,)), ((), ())), preferred_element_type=jnp.float32
    )


def exact(left, right):
    return jnp.dot(left, right, precision=highest, preferred_element_type=jnp.float32)


def low(values):
    return values.astype(jnp.bfloat16)


def split(values):
    top = low(values)
    return top, low(values - top.astype(jnp.float32))


def iota(shape, axis):
    return lax.broadcasted_iota(jnp.int32, shape, axis)


def spreader():
    return low(jnp.where(iota((128, DI), 1) // MP == iota((128, DI), 0), 1.0, 0.0))


def widen(values, spread):
    top, rest = split(values)
    return dot_nn(top, spread) + dot_nn(rest, spread)


def widen_row(row, spread):
    return widen(jnp.broadcast_to(row, (8, 128)), spread)[0:1]


def head_sums(values, spread):
    top, rest = split(values)
    return dot_nt(top, spread) + dot_nt(rest, spread)


def softplus(values):
    return jnp.maximum(values, 0.0) + jnp.log1p(jnp.exp(-jnp.abs(values)))


def sigmoid(values):
    return 1.0 / (1.0 + jnp.exp(-values))


def lane_halves(rows):
    lane = iota((rows, 128), 1)
    return lane < MP


def rounded_to(values):
    return low(values).astype(jnp.float32)


def front_conv(conv_ref, seg_ref, weight_ref, cbias_ref, act_ref):
    chunks = act_ref.shape[0] // SUB

    def tile(j, carry):
        col = pl.ds(pl.multiple_of(j * 128, 128), 128)
        for c in range(chunks):
            r0 = c * SUB
            seg = seg_ref[pl.ds(r0 + 8, SUB), :]
            total = jnp.broadcast_to(cbias_ref[0:1, col], (SUB, 128))
            for k in range(KC):
                x = rounded_to(conv_ref[pl.ds(r0 + 9 - KC + k, SUB), col])
                if k < KC - 1:
                    x = jnp.where(seg_ref[pl.ds(r0 + 9 - KC + k, SUB), :] == seg, x, 0.0)
                total = total + weight_ref[k : k + 1, col] * x
            act_ref[pl.ds(r0, SUB), col] = low(total * sigmoid(total))
        return carry

    lax.fori_loop(0, CW // 128, tile, 0)


def front_state(seg_ref, raw_ref, bias_ref, rate_ref, act_ref, dt_ref, cum_ref, end_ref, pass_ref):
    chunks = raw_ref.shape[0] // SUB
    spread = spreader()
    lower = jnp.where(iota((SUB, SUB), 0) >= iota((SUB, SUB), 1), 1.0, 0.0)
    end_ref[...] = jnp.zeros_like(end_ref)
    gain = jnp.ones((1, 128), jnp.float32)
    for c in range(chunks):
        rows = pl.ds(c * SUB, SUB)
        dt = softplus(raw_ref[rows, :] + bias_ref[...])
        cum = exact(lower, -dt * jnp.exp(rate_ref[...]))
        dt_ref[rows, :] = dt
        cum_ref[rows, :] = cum
        seg = seg_ref[pl.ds(c * SUB + 8, SUB), :]
        before = seg_ref[pl.ds(c * SUB + 7, 1), :]
        last = seg[SUB - 1 :, :]
        end = cum[SUB - 1 :, :]
        weight = jnp.where(seg == last, jnp.exp(end - cum), 0.0) * dt
        passing = jnp.where(last == before, jnp.exp(end), 0.0)
        gain = gain * passing
        values = act_ref[rows, 0:DI].astype(jnp.float32)
        fresh = dot_tn(act_ref[rows, DI : DI + NS], low(widen(weight, spread) * values))
        end_ref[...] = widen_row(passing, spread) * end_ref[...] + fresh
    pass_ref[...] = widen_row(gain, spread)


def mid_kernel(act_ref, dt_ref, cum_ref, seg_ref, segrow_ref, state_ref, z_ref, gain_ref, skip_ref,
               y_ref, gated_ref, kept_ref, carry_ref, first, until):
    spread = spreader()
    if first == 0:
        carry_ref[...] = state_ref[...]
    half = lane_halves(SUB)

    def chunk(c, nothing):
        r0 = pl.multiple_of(c * SUB, SUB)
        rows = pl.ds(r0, SUB)
        dt, cum = dt_ref[rows, :], cum_ref[rows, :]
        cum_t = cum.T
        seg = seg_ref[pl.ds(pl.multiple_of(r0 + 8, 8), SUB), :]
        before = seg_ref[pl.ds(pl.multiple_of(r0, 8), 8), :][7:8]
        last, end = seg[SUB - 1 :, :], cum[SUB - 1 :, :]
        keys, reads = act_ref[rows, DI : DI + NS], act_ref[rows, DI + NS : CW]
        affinity = dot_nt(reads, keys)
        allowed = (iota((SUB, SUB), 0) >= iota((SUB, SUB), 1)) & (seg == segrow_ref[0:1, rows])
        state = low(carry_ref[...])
        kept_ref[pl.ds(c, 1)] = state[None]
        entry = widen(jnp.where(seg == before, jnp.exp(cum), 0.0), spread)
        y_ref[rows, :] = dot_nn(reads, state) * entry
        values = act_ref[rows, 0:DI].astype(jnp.float32)
        scaled = values * widen(dt, spread)
        weight = jnp.where(seg == last, jnp.exp(end - cum), 0.0)
        passing = jnp.where(last == before, jnp.exp(end), 0.0)
        fresh = dot_tn(keys, low(widen(weight, spread) * scaled))
        carry_ref[...] = widen_row(passing, spread) * carry_ref[...] + fresh
        for pair in range(MH // 2):
            cols = slice(pair * 128, pair * 128 + 128)
            parts = []
            for h in (2 * pair, 2 * pair + 1):
                gap = jnp.where(allowed, cum[:, h : h + 1] - cum_t[h : h + 1, :], -1e30)
                parts.append(low(jnp.exp(gap) * affinity))
            v = scaled[:, cols]
            right = jnp.concatenate([low(jnp.where(half, v, 0.0)), low(jnp.where(half, 0.0, v))], 0)
            y_ref[rows, cols] = y_ref[rows, cols] + dot_nn(jnp.concatenate(parts, 1), right)
        z = z_ref[rows, :]
        g = (y_ref[rows, :] + skip_ref[...] * values) * (z * sigmoid(z))
        scale = lax.rsqrt(jnp.mean(g * g, axis=1, keepdims=True) + epsilon)
        gated_ref[rows, :] = low(g * scale * gain_ref[...])
        return nothing

    lax.fori_loop(first, until, chunk, 0)


def gate_back_kernel(grad_ref, y_ref, act_ref, z_ref, dt_ref, cum_ref, seg_ref, gain_ref, skip_ref,
                     ygrad_ref, zgrad_ref, gain_grad_ref, state_grad_ref, first, until):
    chunks = act_ref.shape[0] // SUB
    spread = spreader()
    if first == 0:
        gain_grad_ref[...] = jnp.zeros_like(gain_grad_ref)
        state_grad_ref[...] = jnp.zeros_like(state_grad_ref)

    def chunk(i, nothing):
        c = chunks - 1 - i
        r0 = pl.multiple_of(c * SUB, SUB)
        rows = pl.ds(r0, SUB)
        values = act_ref[rows, 0:DI].astype(jnp.float32)
        z = z_ref[rows, :]
        sig = sigmoid(z)
        silu = z * sig
        u = y_ref[rows, :] + skip_ref[...] * values
        g = u * silu
        grad = grad_ref[rows, :].astype(jnp.float32)
        scale = lax.rsqrt(jnp.mean(g * g, axis=1, keepdims=True) + epsilon)
        unit = g * scale
        gain_grad_ref[...] += jnp.sum(grad * unit, axis=0, keepdims=True)
        h = grad * gain_ref[...]
        dg = scale * (h - unit * jnp.mean(h * unit, axis=1, keepdims=True))
        dy = dg * silu
        ygrad_ref[rows, :] = dy
        zgrad_ref[rows, :] = low(dg * u * (sig * (1.0 + z * (1.0 - sig))))
        cum = cum_ref[rows, :]
        seg = seg_ref[pl.ds(pl.multiple_of(r0 + 8, 8), SUB), :]
        before = seg_ref[pl.ds(pl.multiple_of(r0, 8), 8), :][7:8]
        last, end = seg[SUB - 1 :, :], cum[SUB - 1 :, :]
        entry = widen(jnp.where(seg == before, jnp.exp(cum), 0.0), spread)
        passing = jnp.where(last == before, jnp.exp(end), 0.0)
        fresh = dot_tn(act_ref[rows, DI + NS : CW], low(entry * dy))
        state_grad_ref[...] = widen_row(passing, spread) * state_grad_ref[...] + fresh
        return nothing

    lax.fori_loop(first, until, chunk, 0)


def back_states(act_ref, dt_ref, cum_ref, seg_ref, segrow_ref, raw_ref, bias_ref, rate_ref, kept_ref,
                y_ref, ygrad_ref, skip_ref, raw_grad_ref, rate_grad_ref, bias_grad_ref, skip_grad_ref,
                value_grad_ref, pair_grad_ref, carry_ref, first, until):
    chunks = act_ref.shape[0] // SUB
    spread = spreader()
    half = lane_halves(SUB)
    upper = jnp.where(iota((SUB, SUB), 1) >= iota((SUB, SUB), 0), 1.0, 0.0)
    rate = jnp.exp(rate_ref[...])
    if first == 0:
        rate_grad_ref[...] = jnp.zeros_like(rate_grad_ref)
        bias_grad_ref[...] = jnp.zeros_like(bias_grad_ref)
        skip_grad_ref[...] = jnp.zeros_like(skip_grad_ref)

    def chunk(i, nothing):
        c = chunks - 1 - i
        r0 = pl.multiple_of(c * SUB, SUB)
        rows = pl.ds(r0, SUB)
        dt, cum = dt_ref[rows, :], cum_ref[rows, :]
        cum_t = cum.T
        seg = seg_ref[pl.ds(pl.multiple_of(r0 + 8, 8), SUB), :]
        before = seg_ref[pl.ds(pl.multiple_of(r0, 8), 8), :][7:8]
        last, end = seg[SUB - 1 :, :], cum[SUB - 1 :, :]
        keys, reads = act_ref[rows, DI : DI + NS], act_ref[rows, DI + NS : CW]
        affinity = dot_nt(keys, reads)
        allowed = (iota((SUB, SUB), 1) >= iota((SUB, SUB), 0)) & (seg == segrow_ref[0:1, rows])
        values = act_ref[rows, 0:DI].astype(jnp.float32)
        wide_dt = widen(dt, spread)
        scaled = values * wide_dt
        scaled_low = low(scaled)
        dy = ygrad_ref[rows, :]
        dy_low = low(dy)
        state, carry = kept_ref[pl.ds(c, 1)][0], carry_ref[...]
        carry_low = low(carry)
        wide_weight = widen(jnp.where(seg == last, jnp.exp(end - cum), 0.0), spread)
        wide_entry = widen(jnp.where(seg == before, jnp.exp(cum), 0.0), spread)
        wide_pass = widen_row(jnp.where(last == before, jnp.exp(end), 0.0), spread)
        from_state = dot_nn(keys, carry_low) * wide_weight
        mixed_grad = jnp.zeros((SUB, SUB), jnp.float32)
        for pair in range(MH // 2):
            cols = slice(pair * 128, pair * 128 + 128)
            v, d = scaled[:, cols], dy[:, cols]
            left = jnp.concatenate([low(jnp.where(half, v, 0.0)), low(jnp.where(half, 0.0, v))], 0)
            right = jnp.concatenate([low(jnp.where(half, d, 0.0)), low(jnp.where(half, 0.0, d))], 0)
            weight_grad = dot_nt(left, dy_low[:, cols])
            parts = []
            for n, h in enumerate((2 * pair, 2 * pair + 1)):
                gap = jnp.where(allowed, cum_t[h : h + 1, :] - cum[:, h : h + 1], -1e30)
                decay = jnp.exp(gap)
                parts.append(low(decay * affinity))
                mixed_grad = mixed_grad + decay * weight_grad[n * SUB : (n + 1) * SUB]
            value_grad_ref[rows, cols] = dot_nn(jnp.concatenate(parts, 1), right)
        x = value_grad_ref[rows, 0:DI] + from_state
        value_grad_ref[rows, 0:DI] = wide_dt * x + skip_ref[...] * dy
        mixed_low = low(mixed_grad)
        pair_grad_ref[rows, 0:NS] = dot_nn(mixed_low, reads) + dot_nt(
            low(wide_weight * scaled), carry_low
        )
        entered = low(wide_entry * dy)
        pair_grad_ref[rows, NS:] = dot_tn(mixed_low, keys) + dot_nt(entered, state)
        scaled_exact = scaled_low.astype(jnp.float32)
        direct = head_sums(values * x, spread)
        given = head_sums(scaled_exact * x, spread)
        taken = head_sums(dy_low.astype(jnp.float32) * y_ref[rows, :], spread)
        tail = jnp.sum(scaled_exact * from_state, axis=0, keepdims=True) + jnp.sum(
            wide_pass * carry * state.astype(jnp.float32), axis=0, keepdims=True
        )
        tail = head_sums(jnp.broadcast_to(tail, (8, DI)), spread)[0:1]
        decay_grad = exact(upper, taken - given) + tail
        rate_grad_ref[...] += jnp.sum(decay_grad * (-dt * rate), axis=0, keepdims=True)
        dt_grad = direct - decay_grad * rate
        raw_grad = dt_grad * sigmoid(raw_ref[rows, :] + bias_ref[...])
        raw_grad_ref[rows, :] = low(jnp.where(iota((SUB, 128), 1) < MH, raw_grad, 0.0))
        bias_grad_ref[...] += jnp.sum(raw_grad, axis=0, keepdims=True)
        skip_sum = jnp.sum(dy * values, axis=0, keepdims=True)
        skip_grad_ref[...] += head_sums(jnp.broadcast_to(skip_sum, (8, DI)), spread)[0:1]
        carry_ref[...] = wide_pass * carry + dot_tn(reads, entered)
        return nothing

    lax.fori_loop(first, until, chunk, 0)


def back_conv(conv_hbm, conv_ref, conv_sem, seg_ref, weight_ref, cbias_ref, act_grad_ref, shift,
              conv_grad_ref, edge_ref, tail_ref, weight_grad_ref, cbias_grad_ref, pre_ref, first, until):
    rows_total = act_grad_ref.shape[0]
    chunks = rows_total // SUB
    pre_ref[0:8, :] = jnp.zeros((8, 128), jnp.float32)
    pre_ref[rows_total + 8 : rows_total + 16, :] = jnp.zeros((8, 128), jnp.float32)

    def fetch(j, slot):
        return pltpu.make_async_copy(
            conv_hbm.at[:, pl.ds(pl.multiple_of(j * 128, 128), 128)], conv_ref.at[slot], conv_sem.at[slot]
        )

    fetch(first, first % 2).start()

    def tile(j, carry):
        slot = j % 2

        @pl.when(j + 1 < until)
        def _():
            fetch(j + 1, 1 - slot).start()

        fetch(j, slot).wait()
        col = pl.ds(pl.multiple_of(j * 128, 128), 128)
        sums = [jnp.zeros((1, 128), jnp.float32) for _ in range(KC + 1)]
        for c in range(chunks):
            r0 = c * SUB
            seg = seg_ref[pl.ds(r0 + 8, SUB), :]
            total = jnp.broadcast_to(cbias_ref[0:1, col], (SUB, 128))
            taps = []
            for k in range(KC):
                x = rounded_to(conv_ref[slot, pl.ds(r0 + 9 - KC + k, SUB), :])
                if k < KC - 1:
                    x = jnp.where(seg_ref[pl.ds(r0 + 9 - KC + k, SUB), :] == seg, x, 0.0)
                taps.append(x)
                total = total + weight_ref[k : k + 1, col] * x
            sig = sigmoid(total)
            act_col = pl.ds(pl.multiple_of((j - shift) * 128, 128), 128)
            pre = act_grad_ref[pl.ds(r0, SUB), act_col] * (sig * (1.0 + total * (1.0 - sig)))
            pre_ref[pl.ds(r0 + 8, SUB), :] = pre
            for k in range(KC):
                sums[k] = sums[k] + jnp.sum(pre * taps[k], axis=0, keepdims=True)
            sums[KC] = sums[KC] + jnp.sum(pre, axis=0, keepdims=True)
        for k in range(KC):
            weight_grad_ref[k : k + 1, col] = sums[k]
        cbias_grad_ref[0:1, col] = sums[KC]

        def spread_back(r0, size):
            seg = seg_ref[pl.ds(r0, size), :]
            total = jnp.zeros((size, 128), jnp.float32)
            for back in range(KC):
                x = pre_ref[pl.ds(r0 + back, size), :]
                if back:
                    x = jnp.where(seg_ref[pl.ds(r0 + back, size), :] == seg, x, 0.0)
                total = total + weight_ref[KC - 1 - back : KC - back, col] * x
            return total

        edge_ref[:, col] = spread_back(0, 8)
        for c in range(chunks):
            total = spread_back(c * SUB + 8, SUB)
            conv_grad_ref[pl.ds(c * SUB, SUB), act_col] = low(total)
        tail_ref[:, col] = total[SUB - 16 :]
        return carry

    lax.fori_loop(first, until, tile, 0)


def partner(values):
    lane = iota(values.shape, 1)
    half = HEAD_WIDTH // 2
    return jnp.where(
        lane % HEAD_WIDTH < half, pltpu.roll(values, 128 - half, 1), pltpu.roll(values, half, 1)
    )


def rotate_kernel(qkv_ref, cos_ref, sin_ref, query_ref, kv_ref):
    cos, sin = cos_ref[...], sin_ref[...]
    for g in range(5):
        x = qkv_ref[:, g * 128 : g * 128 + 128]
        x = low(x * cos + partner(x) * sin)
        if g < 4:
            query_ref[:, g * 128 : g * 128 + 128] = x * jnp.bfloat16(HEAD_WIDTH**-0.5)
        else:
            kv_ref[:, 0:128] = x
    kv_ref[:, 128:256] = low(qkv_ref[:, 640:768])


def lane_variants(block, out_ref):
    other = pltpu.roll(block, 64, 1)
    half = iota(block.shape, 1) < HEAD_WIDTH
    out_ref[0] = low(jnp.where(half, block, 0.0))
    out_ref[1] = low(jnp.where(half, 0.0, other))
    out_ref[2] = low(jnp.where(half, other, 0.0))
    out_ref[3] = low(jnp.where(half, 0.0, block))


def seg_column(row):
    return jnp.broadcast_to(row, (128, row.shape[1])).T


def attend_bias(b, own, rows, segall_ref, segrow_ref, bias_ref):
    seg = seg_column(segall_ref[pl.ds(pl.multiple_of(b * 8, 8), 8), :][0:1])
    seg = jnp.concatenate([seg] * (rows // 128), 1)
    causal = (iota((rows, rows), 0) - iota((rows, rows), 1)) <= jnp.where(b < own, rows, 0)
    bias_ref[...] = jnp.where(causal & (seg == segrow_ref[...]), 0.0, -1e30)


def attend_start(top_ref, sum_ref, out_t_ref):
    top_ref[...] = jnp.full_like(top_ref, -1e30)
    sum_ref[...] = jnp.zeros_like(sum_ref)
    out_t_ref[...] = jnp.zeros_like(out_t_ref)


def attend_block(b, own, query_ref, kv_ref, segall_ref, segrow_ref, out_t_ref, bias_ref, keys_ref,
                 values_t_ref, top_ref, sum_ref):
    rows = query_ref.shape[0]
    at = pl.ds(pl.multiple_of(b * rows, rows), rows)
    attend_bias(b, own, rows, segall_ref, segrow_ref, bias_ref)
    lane_variants(kv_ref[at, 0:128].astype(jnp.float32), keys_ref)
    values_t_ref[...] = low(kv_ref[at, 128:256].astype(jnp.float32).T)

    def pair(g, nothing):
        kv = g // 2
        query = query_ref[:, pl.ds(pl.multiple_of(g * 128, 128), 128)]
        for side in range(2):
            h = g * 2 + side
            row = pl.ds(pl.multiple_of(h * 8, 8), 8)
            scores = dot_nt(keys_ref[kv * 2 + side], query)
            scores = scores + bias_ref[...]
            old = top_ref[row, :][0:1]
            top = jnp.maximum(old, jnp.max(scores, axis=0, keepdims=True))
            p = jnp.exp(scores - top)
            fade = jnp.exp(old - top)
            total = sum_ref[row, :][0:1] * fade + jnp.sum(p, 0, keepdims=True)
            top_ref[row, :] = jnp.broadcast_to(top, (8, rows))
            sum_ref[row, :] = jnp.broadcast_to(total, (8, rows))
            at_h = pl.ds(pl.multiple_of(h * 64, 64), 64)
            values_t = values_t_ref[pl.ds(pl.multiple_of(kv * 64, 64), 64), :]
            out_t_ref[at_h, :] = out_t_ref[at_h, :] * fade + dot_nn(values_t, low(p))
        return nothing

    lax.fori_loop(0, QUERY_HEADS // 2, pair, 0)


def attend_finish(out_ref, out_t_ref, total_ref, top_ref, sum_ref):
    for h in range(QUERY_HEADS):
        at_h = slice(h * 64, h * 64 + 64)
        row = slice(h * 8, h * 8 + 8)
        total_ref[row, :] = top_ref[row, :] + jnp.log(sum_ref[row, :])
        out_t_ref[at_h, :] = out_t_ref[at_h, :] / sum_ref[h * 8 : h * 8 + 1, :]
    out_ref[...] = low(out_t_ref[...].T)


def attend_back_start(query_ref, grad_ref, out_t_ref, spread_ref):
    rows = query_ref.shape[0]
    grad_t = grad_ref[...].astype(jnp.float32).T
    product = grad_t * out_t_ref[...]
    for h in range(QUERY_HEADS):
        total = jnp.sum(product[h * 64 : h * 64 + 64, :], 0, keepdims=True)
        spread_ref[h * 8 : h * 8 + 8, :] = jnp.broadcast_to(total, (8, rows))
    out_t_ref[...] = jnp.zeros_like(out_t_ref)


def attend_back_block(b, own, query_ref, kv_ref, segall_ref, segrow_ref, grad_ref, total_ref, kv_grad_ref,
                      bias_ref, keys_ref, values_ref, keys_t_ref, dkeys_ref, dvalues_ref, spread_ref, dq_ref,
                      first, until):
    rows = query_ref.shape[0]
    at = pl.ds(pl.multiple_of(b * rows, rows), rows)
    if first == 0:
        attend_bias(b, own, rows, segall_ref, segrow_ref, bias_ref)
        keys = kv_ref[at, 0:128].astype(jnp.float32)
        lane_variants(keys, keys_ref)
        lane_variants(kv_ref[at, 128:256].astype(jnp.float32), values_ref)
        keys_t_ref[...] = low(keys.T)
        dkeys_ref[...] = jnp.zeros_like(dkeys_ref)
        dvalues_ref[...] = jnp.zeros_like(dvalues_ref)

    lower_half = iota((rows, 128), 1) < HEAD_WIDTH

    def side_of(values, side):
        values = values.astype(jnp.float32)
        return low(jnp.where(lower_half, 0.0, values) if side else jnp.where(lower_half, values, 0.0))

    def pair(g, nothing):
        kv = g // 2
        lanes = pl.ds(pl.multiple_of(g * 128, 128), 128)
        for side in range(2):
            h = g * 2 + side
            row = pl.ds(pl.multiple_of(h * 8, 8), 8)
            scores = dot_nt(keys_ref[kv * 2 + side], query_ref[:, lanes]) + bias_ref[...]
            p = jnp.exp(scores - total_ref[row, :][0:1])
            dp = dot_nt(values_ref[kv * 2 + side], grad_ref[:, lanes])
            ds = low(p * (dp - spread_ref[row, :][0:1]))
            dkeys_ref[kv] = dkeys_ref[kv] + dot_nn(ds, side_of(query_ref[:, lanes], side))
            dvalues_ref[kv] = dvalues_ref[kv] + dot_nn(low(p), side_of(grad_ref[:, lanes], side))
            at_h = pl.ds(pl.multiple_of(h * 64, 64), 64)
            keys_t = keys_t_ref[pl.ds(pl.multiple_of(kv * 64, 64), 64), :]
            dq_ref[at_h, :] = dq_ref[at_h, :] + dot_nn(keys_t, ds)
        return nothing

    lax.fori_loop(first, until, pair, 0)
    if until < QUERY_HEADS // 2:
        return
    half = lower_half
    for src, lanes in ((dkeys_ref, slice(0, 128)), (dvalues_ref, slice(128, 256))):
        first, second = src[0], src[1]
        kv_grad_ref[at, lanes] = low(
            jnp.where(half, first + pltpu.roll(first, 64, 1), second + pltpu.roll(second, 64, 1))
        )


def attend_back_finish(dq_ref, cos_ref, sin_ref, qkv_grad_ref):
    dq = dq_ref[...].T * (HEAD_WIDTH**-0.5)
    cos, sin = cos_ref[...], sin_ref[...]
    for g in range(4):
        x = dq[:, g * 128 : g * 128 + 128]
        qkv_grad_ref[:, g * 128 : g * 128 + 128] = low(x * cos + partner(x * sin))


vmem = pl.BlockSpec(memory_space=pltpu.VMEM)
smem = pl.BlockSpec(memory_space=pltpu.SMEM)


def call(kernel, outs, args, scratch=(), first=vmem, flops=10**9):
    return pl.pallas_call(
        kernel,
        out_shape=[jax.ShapeDtypeStruct(shape, kind) for shape, kind in outs],
        in_specs=[first] + [vmem] * (len(args) - 1),
        out_specs=[vmem] * len(outs),
        scratch_shapes=[pltpu.VMEM(shape, kind) for shape, kind in scratch],
        compiler_params=pltpu.CompilerParams(vmem_limit_bytes=56 * 2**20),
        cost_estimate=pl.CostEstimate(flops=flops, bytes_accessed=10**7, transcendentals=10**6),
    )(*args)


MESH = pl.DeviceIdType.MESH


def position_bits(count):
    index = lax.axis_index("fsdp")
    return [(index // (1 << b)) % 2 for b in reversed(range(count))]


def across(bits, axis):
    count = len(bits)
    index = lax.axis_index("fsdp")
    step = 1 << (count - 1 - axis)
    return (index + step * (1 - 2 * bits[axis]), lax.axis_index("seq"))


def along(by):
    return (lax.axis_index("fsdp"), lax.axis_index("seq") + by)


class Item:
    def __init__(self, number, weight, start, size, order):
        self.number, self.weight, self.start, self.size, self.order = number, weight, start, size, order


def fit(shapes, wanted):
    return [max(d for d in range(1, n + 1) if rows // 16 % d == 0) for (rows, _), n in zip(shapes, wanted)]


def plan_items(shapes, parts, bit_count):
    items = []
    for w, ((rows, _), count) in enumerate(zip(shapes, parts)):
        for p in range(count):
            turn = p % max(bit_count - 1, 1)
            ici = list(range(bit_count - 1))
            order = [bit_count - 1] + ici[turn:] + ici[:turn]
            items.append(Item(len(items), w, p * (rows // count), rows // count, order))
            items[-1].slots = max(1, count // 2)
            items[-1].part = p
    return items


def own_shape(bit_count, shape, parts):
    return (*(2,) * (bit_count - 1), shape[0] // parts * max(1, parts // 2), shape[1])


class Reducer:
    def __init__(self, bit_count, depth, items, whole, own, landed, zin, zmid, out, send, recv, own_sem):
        self.bit_count, self.depth, self.items = bit_count, depth, items
        self.whole, self.own, self.landed = whole, own, landed
        self.zin, self.zmid, self.out = zin, zmid, out
        self.send, self.recv, self.own_sem = send, recv, own_sem
        self.bits = position_bits(bit_count)
        self.place = lax.axis_index("seq")

    def rows(self, item):
        return pl.ds(item.start, item.size)

    def left(self, item, stage):
        return sorted(item.order[stage:])

    def pick(self, item, stage, mine):
        axis = item.order[stage]
        at = self.left(item, stage).index(axis)
        bit = self.bits[axis] if mine else 1 - self.bits[axis]
        lead = [slice(None)] * (self.bit_count - stage)
        lead[at] = bit
        return (*lead, self.rows(item))

    def source(self, item, stage):
        if stage == 0:
            return self.whole[item.weight]
        return self.landed[stage - 1][item.weight]

    def copy(self, item, stage):
        lead = (slice(None),) * (self.bit_count - stage - 1)
        return pltpu.make_async_remote_copy(
            self.source(item, stage).at[self.pick(item, stage, False)],
            self.landed[stage][item.weight].at[(*lead, self.rows(item))],
            self.send.at[item.number, stage],
            self.recv.at[item.number, stage],
            device_id=across(self.bits, item.order[stage]),
            device_id_type=MESH,
        )

    def own_copy(self, item):
        lead = (slice(None),) * (self.bit_count - 1)
        return pltpu.make_async_copy(
            self.whole[item.weight].at[self.pick(item, 0, True)],
            self.own[item.weight].at[(*lead, pl.ds(self.own_start(item), item.size))],
            self.own_sem.at[item.number],
        )

    def own_start(self, item):
        return item.part % item.slots * item.size

    def begin(self, item):
        self.copy(item, 0).start()
        if item.part < item.slots:
            self.own_copy(item).start()

    def add(self, dst, dst_lead, other, other_lead, item, shift=0):
        group = 16

        def step(i, nothing):
            at = pl.ds(pl.multiple_of(item.start + i * group, group), group)
            at_other = pl.ds(pl.multiple_of(item.start + shift + i * group, group), group)
            dst[(*dst_lead, at)] = low(
                dst[(*dst_lead, at)].astype(f32) + other[(*other_lead, at_other)].astype(f32)
            )
            return nothing

        lax.fori_loop(0, item.size // group, step, 0)

    def advance(self, item, stage):
        self.copy(item, stage).wait_recv()
        landed = self.landed[stage][item.weight]
        kept = self.bit_count - stage - 1
        places = [[(i >> (kept - 1 - b)) & 1 for b in range(kept)] for i in range(1 << kept)]
        if stage == 0:
            self.own_copy(item).wait()
            for lead in places:
                self.add(landed, lead, self.own[item.weight], lead, item, self.own_start(item) - item.start)
            for other in self.items:
                if other.weight == item.weight and other.part == item.part + item.slots:
                    self.own_copy(other).start()
        else:
            source = self.source(item, stage)
            axis = item.order[stage]
            at = self.left(item, stage).index(axis)
            for lead in places:
                from_lead = [*lead[:at], self.bits[axis], *lead[at:]]
                self.add(landed, lead, source, from_lead, item)
        if stage + 1 < self.bit_count:
            self.copy(item, stage + 1).start()

    def z_copy(self, item, kind, by):
        w, rows = item.weight, self.rows(item)
        last = self.landed[self.bit_count - 1][w]
        src, dst = {
            "in": (last, self.zin[w]),
            "mid": (last, self.zmid[w]),
            "out": (self.zmid[w], self.zmid[w]),
        }[kind]
        slot = self.bit_count + {"in": 0, "mid": 1, "out": 2}[kind]
        return pltpu.make_async_remote_copy(
            src.at[rows],
            dst.at[rows],
            self.send.at[item.number, slot],
            self.recv.at[item.number, slot],
            device_id=along(by),
            device_id_type=MESH,
        )

    def sides(self):
        half = self.depth // 2
        outermost = (self.place == 0) | (self.place == self.depth - 1)
        middle = (self.place == half - 1) | (self.place == half)
        inward = 1 - 2 * (self.place // half)
        return outermost, middle, inward

    def z_first(self, item):
        outermost, middle, inward = self.sides()

        @pl.when(outermost & jnp.logical_not(middle))
        def _():
            self.z_copy(item, "in", inward).start()

    def z_second(self, item):
        outermost, middle, inward = self.sides()

        @pl.when(jnp.logical_not(outermost))
        def _():
            self.z_copy(item, "in", -inward).wait_recv()
            self.add(self.landed[self.bit_count - 1][item.weight], (), self.zin[item.weight], (), item)

            @pl.when(jnp.logical_not(middle))
            def _():
                self.z_copy(item, "in", inward).start()

        @pl.when(middle)
        def _():
            self.z_copy(item, "mid", inward).start()

    def z_third(self, item):
        outermost, middle, inward = self.sides()

        @pl.when(middle)
        def _():
            self.z_copy(item, "mid", inward).wait_recv()
            self.add(self.zmid[item.weight], (), self.landed[self.bit_count - 1][item.weight], (), item)

            @pl.when(jnp.logical_not(outermost))
            def _():
                self.z_copy(item, "out", -inward).start()

    def z_fourth(self, item):
        outermost, middle, inward = self.sides()

        @pl.when(jnp.logical_not(middle))
        def _():
            self.z_copy(item, "out", inward).wait_recv()

            @pl.when(jnp.logical_not(outermost))
            def _():
                self.z_copy(item, "out", -inward).start()

        self.out_copy(item).start()

    def out_copy(self, item):
        rows = self.rows(item)
        return pltpu.make_async_copy(
            self.zmid[item.weight].at[rows], self.out[item.weight].at[rows], self.own_sem.at[item.number]
        )

    def pump(self, count):
        while count and self.todo and (self.todo[0][0] is None or self.todo[0][0] in self.have):
            self.todo.pop(0)[1]()
            count -= 1

    def finish(self, item):
        outermost, middle, inward = self.sides()
        self.out_copy(item).wait()
        for stage in range(self.bit_count):
            self.copy(item, stage).wait_send()

        @pl.when(jnp.logical_not(middle))
        def _():
            self.z_copy(item, "in", inward).wait_send()

        @pl.when(middle)
        def _():
            self.z_copy(item, "mid", inward).wait_send()

        @pl.when(jnp.logical_not(outermost))
        def _():
            self.z_copy(item, "out", -inward).wait_send()

    def actions(self, lag, z_lag, late=(), reused=(), ready_sem=None):
        last_use = max(
            [i + lag * (self.bit_count - 1) + 3 * z_lag for i, item in enumerate(self.items) if item.weight in reused],
            default=0,
        )
        first_late = min([i for i, item in enumerate(self.items) if item.weight in late], default=0)
        gap = max(0, last_use + 2 - first_late)
        steps = []
        for i, item in enumerate(self.items):
            if item.weight in late:
                if i == first_late:
                    steps.append((i + gap - 1, -2, item.weight, lambda: self.hand_over(reused, ready_sem)))
                i += gap
                steps.append((i - 1, -1, item.weight, lambda item=item: self.begin(item)))
            for stage in range(self.bit_count):
                steps.append((i + lag * stage, stage, None, lambda item=item, s=stage: self.advance(item, s)))
            t = i + lag * (self.bit_count - 1)
            for n, run in enumerate((self.z_first, self.z_second, self.z_third, self.z_fourth)):
                steps.append((t + n * z_lag, self.bit_count + n, None, lambda item=item, run=run: run(item)))
        self.todo = [step[2:] for step in sorted(steps, key=lambda s: s[:2])]
        self.have = set()

    def hand_over(self, weights, ready_sem):
        for item in self.items:
            if item.weight in weights:
                self.finish(item)
        meet(self.bits, self.place, self.depth, ready_sem)


def meet(bits, place, depth, semaphore):
    for axis in range(len(bits)):
        pl.semaphore_signal(semaphore, inc=1, device_id=across(bits, axis), device_id_type=MESH)

    @pl.when(place > 0)
    def _():
        pl.semaphore_signal(semaphore, inc=1, device_id=along(-1), device_id_type=MESH)

    @pl.when(place < depth - 1)
    def _():
        pl.semaphore_signal(semaphore, inc=1, device_id=along(1), device_id_type=MESH)

    ends = jnp.where(place == 0, 1, 0) + jnp.where(place == depth - 1, 1, 0)
    pl.semaphore_wait(semaphore, len(bits) + 2 - ends)


def enter(bit_count, depth):
    meet(position_bits(bit_count), lax.axis_index("seq"), depth, pltpu.get_barrier_semaphore())


def small_sum(bit_count, depth, src, buf, out, send, recv):
    bits = position_bits(bit_count)
    place = lax.axis_index("seq")
    half = depth // 2
    outermost = (place == 0) | (place == depth - 1)
    middle = (place == half - 1) | (place == half)
    inward = 1 - 2 * (place // half)

    def flip(stage):
        return pltpu.make_async_remote_copy(
            (src if stage == 0 else out.at[stage - 1]),
            buf.at[stage],
            send.at[stage],
            recv.at[stage],
            device_id=across(bits, bit_count - 1 - stage),
            device_id_type=MESH,
        )

    def z_copy(kind, by):
        n = bit_count + kind
        return pltpu.make_async_remote_copy(
            out.at[(bit_count - 1, bit_count, bit_count + 1)[kind]],
            (buf.at[bit_count], buf.at[bit_count + 1], out.at[bit_count + 1])[kind],
            send.at[n],
            recv.at[n],
            device_id=along(by),
            device_id_type=MESH,
        )

    def flip_done(stage):
        flip(stage).wait_recv()
        mine = src[...] if stage == 0 else out[stage - 1]
        out[stage] = mine + buf[stage]
        if stage + 1 < bit_count:
            flip(stage + 1).start()

    def z_in():
        @pl.when(jnp.logical_not(middle))
        def _():
            @pl.when(jnp.logical_not(outermost))
            def _():
                z_copy(0, -inward).wait_recv()
                out[bit_count - 1] = out[bit_count - 1] + buf[bit_count]

            z_copy(0, inward).start()

        @pl.when(middle)
        def _():
            out[bit_count] = out[bit_count - 1]

            @pl.when(jnp.logical_not(outermost))
            def _():
                z_copy(0, -inward).wait_recv()
                out[bit_count] = out[bit_count] + buf[bit_count]

            z_copy(1, inward).start()

    def z_mid():
        @pl.when(middle)
        def _():
            z_copy(1, inward).wait_recv()
            out[bit_count + 1] = out[bit_count] + buf[bit_count + 1]

    def z_out():
        @pl.when(jnp.logical_not(middle))
        def _():
            z_copy(2, inward).wait_recv()

        @pl.when(jnp.logical_not(outermost))
        def _():
            z_copy(2, -inward).start()

    def finish():
        for stage in range(bit_count):
            flip(stage).wait_send()

        @pl.when(jnp.logical_not(middle))
        def _():
            z_copy(0, inward).wait_send()

        @pl.when(middle)
        def _():
            z_copy(1, inward).wait_send()

        @pl.when(jnp.logical_not(outermost))
        def _():
            z_copy(2, -inward).wait_send()

    begin = lambda: flip(0).start()
    steps = [lambda s=s: flip_done(s) for s in range(bit_count)] + [z_in, z_mid, z_out]
    return begin, steps, finish


def bit_length(count):
    return count.bit_length() - 1


class Gatherer:
    def __init__(self, bit_count, items, shards, whole, loads, load_sem, cast_to, own_sem, send, recv):
        self.bit_count, self.items = bit_count, items
        self.shards, self.whole, self.loads, self.load_sem = shards, whole, loads, load_sem
        self.cast_to, self.own_sem, self.send, self.recv = cast_to, own_sem, send, recv
        self.bits = position_bits(bit_count)
        self.index = lax.axis_index("fsdp")
        self.ready = set()
        self.todo = []
        self.done = set()

    def block(self, axes):
        at = self.index
        for axis in axes:
            at = at + (1 << (self.bit_count - 1 - axis)) * (1 - 2 * self.bits[axis])
        return at

    def subsets(self, order):
        sets = [()]
        for axis in order:
            sets = sets + [(*s, axis) for s in sets]
        return sets

    def rows(self, item, axes):
        shard_rows = self.cast_to[item.weight].shape[0]
        return pl.ds(pl.multiple_of(self.block(axes) * shard_rows + item.start, 16), item.size)

    def copy(self, item, stage, number, axes):
        whole = self.whole[item.weight]
        at = self.rows(item, axes)
        src = self.cast_to[item.weight].at[pl.ds(item.start, item.size)] if not axes else whole.at[at]
        slot = (1 << stage) - 1 + number
        return pltpu.make_async_remote_copy(
            src,
            whole.at[at],
            self.send.at[item.number, slot],
            self.recv.at[item.number, slot],
            device_id=across(self.bits, item.order[stage]),
            device_id_type=MESH,
        )

    def landed(self, item, stage, number, axes):
        whole = self.whole[item.weight]
        at = self.rows(item, (*axes, item.order[stage]))
        slot = (1 << stage) - 1 + number
        return pltpu.make_async_remote_copy(
            whole.at[at],
            whole.at[at],
            self.send.at[item.number, slot],
            self.recv.at[item.number, slot],
            device_id=across(self.bits, item.order[stage]),
            device_id_type=MESH,
        )

    def load(self, weight):
        return pltpu.make_async_copy(self.shards[weight], self.loads[weight], self.load_sem.at[weight])

    def own(self, weight):
        rows = self.cast_to[weight].shape[0]
        return pltpu.make_async_copy(
            self.cast_to[weight],
            self.whole[weight].at[pl.ds(pl.multiple_of(self.index * rows, 16), rows)],
            self.own_sem.at[weight],
        )

    def begin(self, item):
        w = item.weight
        if w not in self.ready:
            self.ready.add(w)
            self.load(w).wait()
            group = 16

            def step(i, nothing):
                at = pl.ds(pl.multiple_of(i * group, group), group)
                self.cast_to[w][at] = low(self.loads[w][at])
                return nothing

            lax.fori_loop(0, self.cast_to[w].shape[0] // group, step, 0)
            self.own(w).start()
        for stage in range(self.bit_count):
            self.copy(item, stage, 0, ()).start()

    def advance(self, item, stage):
        before = self.subsets(item.order[:stage])
        for number, axes in enumerate(before):
            self.landed(item, stage, number, axes).wait_recv()
        for later in range(stage + 1, self.bit_count):
            sets = self.subsets(item.order[:later])
            for number, axes in enumerate(before):
                mine = (*axes, item.order[stage])
                self.copy(item, later, sets.index(mine), mine).start()
        if stage == self.bit_count - 1:
            self.done.add(item.number)

    def plan(self, lag):
        steps = []
        for i, item in enumerate(self.items):
            steps.append((i, 0, lambda item=item: self.begin(item)))
            for stage in range(self.bit_count):
                steps.append((i + lag * (stage + 1), stage + 1, lambda item=item, s=stage: self.advance(item, s)))
        self.todo = [action for _, _, action in sorted(steps, key=lambda s: s[:2])]

    def pump(self, count):
        for _ in range(min(count, len(self.todo))):
            self.todo.pop(0)()

    def until(self, weight):
        numbers = {item.number for item in self.items if item.weight == weight}
        while not numbers <= self.done:
            self.todo.pop(0)()
        self.own(weight).wait()

    def finish(self):
        for item in self.items:
            for stage in range(self.bit_count):
                for number, axes in enumerate(self.subsets(item.order[:stage])):
                    self.copy(item, stage, number, axes).wait_send()


def multiply(out_ref, out_rows, left, right_ref, first, width, tile):
    def step(j, nothing):
        at = pl.ds(pl.multiple_of(j * tile, tile), tile)
        from_at = pl.ds(pl.multiple_of(first + j * tile, 128), tile)
        out_ref[out_rows, at] = dot_nn(left[...], right_ref[:, from_at])
        return nothing

    lax.fori_loop(0, width // tile, step, 0)


def forward_part(tokens, seg_rows, norm_gain, cosine, signed, bias_row, rate_row, conv_weight,
                 conv_bias, mixer_gain, skip_row, shards, parts):
    fsdp, depth = lax.axis_size("fsdp"), lax.axis_size("seq")
    bit_count = bit_length(fsdp)
    shapes = [s.shape for s in shards]
    items = plan_items(shapes, fit(shapes, parts), bit_count)
    for item in items:
        item.order = item.order[1:] + item.order[:1]
    count = tokens.shape[0]
    weights = len(shards)
    pieces = 2
    kept_shape = (count // SUB, NS, DI)
    results = dict(
        normed=((count, 1024), bf16),
        conv=((count + EDGE, CW), f32),
        raw=((count, 128), f32),
        raw_w=((1024, 128), bf16),
        z=((count, DI), f32),
        act=((count, CW), bf16),
        dt=((count, 128), f32),
        cum=((count, 128), f32),
        passing=((1, DI), f32),
        query=((count, 512), bf16),
        kv=((depth * count, 256), bf16),
        attended=((count, 512), bf16),
        attended_t=((512, count), f32),
        log_total=((QUERY_HEADS * 8, count), f32),
        y=((count, DI), f32),
        gated=((count, DI), bf16),
        kept=(kept_shape, bf16),
        seg_wide=((count + 2 * EDGE, 128), f32),
        seg_all=((depth * 8, count), f32),
    )
    names = list(results)
    local = dict(
        normed_edge=((16, 1024), bf16),
        edge=((16, 1024), bf16),
        qkv=((count, 768), f32),
        end=((NS, DI), f32),
        state=((NS, DI), f32),
        carry=((NS, DI), f32),
        state_send=((NS, DI), bf16),
        state_recv=((NS, DI), bf16),
        bias=((count, count), f32),
        keys=((4, count, 128), bf16),
        values_t=((128, count), bf16),
        top=((QUERY_HEADS * 8, count), f32),
        total=((QUERY_HEADS * 8, count), f32),
    )
    in_vmem = (0, 1)

    def kernel(*refs):
        at = 0

        def take(n):
            nonlocal at
            at += n
            return refs[at - n : at]

        (tokens_ref, segrow_ref, gain_ref, cos_ref, sin_ref, bias_ref, rate_ref, weight_ref, cbias_ref,
         mixer_gain_ref, skip_ref) = take(11)
        shard_refs = take(weights)
        out = dict(zip(names, take(len(names))))
        whole_out = take(weights)
        v = dict(zip(names, take(len(names))))
        v.update(zip(local, take(len(local))))
        loads, cast_to = take(weights), take(weights)
        whole_vmem = take(len(in_vmem))
        send, recv, load_sem, own_sem, save_sem, z_send, z_recv = take(7)
        place = lax.axis_index("seq")
        whole = [whole_vmem[in_vmem.index(w)] if w in in_vmem else whole_out[w] for w in range(weights)]
        gather = Gatherer(bit_count, items, shard_refs, whole, loads, load_sem, cast_to, own_sem, send, recv)
        for w in range(weights):
            gather.load(w).start()
        enter(bit_count, depth)
        gather.plan(2)
        saved = []

        def save(src, dst):
            copy = pltpu.make_async_copy(src, dst, save_sem.at[len(saved)])
            copy.start()
            saved.append(copy)

        def keep(*which):
            for name in which:
                save(v[name], out[name])

        def to_next(src, dst, slot):
            return pltpu.make_async_remote_copy(
                src, dst, z_send.at[slot], z_recv.at[slot], device_id=along(1), device_id_type=MESH
            )

        started = []

        def send_on(condition, src, dst, slot):
            @pl.when(condition)
            def _():
                to_next(src, dst, slot).start()

            started.append((condition, src, dst, slot))

        def ring(ref, rows, hop, slot):
            b = place - hop + 1
            part = ref.at[pl.ds(pl.multiple_of(jnp.maximum(b, 0) * rows, 8), rows)]
            send_on((b >= 0) & (place < depth - 1), part, part, slot)

        def ring_wait(ref, rows, hop, slot):
            b = place - hop
            part = ref.at[pl.ds(pl.multiple_of(jnp.maximum(b, 0) * rows, 8), rows)]

            @pl.when(b >= 0)
            def _():
                to_next(part, part, slot).wait_recv()

        tail = tokens_ref.at[pl.ds(count - 16, 16)]
        gather.pump(2)
        send_on(place < depth - 1, tail, v["edge"], 0)
        v["seg_all"][pl.ds(pl.multiple_of(place * 8, 8), 8)] = jnp.broadcast_to(segrow_ref[...], (8, count))
        ring(v["seg_all"], 8, 1, 1)

        def normalise(src, dst, rows, group):
            def step(i, nothing):
                at = pl.ds(pl.multiple_of(i * group, group), group)
                x = src[at].astype(f32)
                scale = lax.rsqrt(jnp.mean(x * x, axis=1, keepdims=True) + epsilon)
                dst[at] = low(x * scale * gain_ref[...])
                return nothing

            lax.fori_loop(0, rows // group, step, 0)

        normalise(tokens_ref, v["normed"], count, 64)
        gather.pump(1)

        @pl.when(place == 0)
        def _():
            v["edge"][...] = jnp.zeros((16, 1024), bf16)

        @pl.when(place > 0)
        def _():
            to_next(tail, v["edge"], 0).wait_recv()

        normalise(v["edge"], v["normed_edge"], 16, 16)
        gather.pump(1)
        for hop in range(1, depth):
            ring_wait(v["seg_all"], 8, hop, hop)
            if hop < depth - 1:
                ring(v["seg_all"], 8, hop + 1, hop + 1)

        before = v["seg_all"][pl.ds(pl.multiple_of(jnp.maximum(place - 1, 0) * 8, 8), 8)][0:1]
        v["seg_wide"][0:EDGE, :] = jnp.where(place == 0, -1.0, seg_column(before)[count - EDGE :])
        v["seg_wide"][EDGE : EDGE + count, :] = seg_column(segrow_ref[...])
        v["seg_wide"][EDGE + count :, :] = jnp.full((EDGE, 128), -2.0, f32)
        own_rows = pl.ds(pl.multiple_of(place * count, 8), count)
        v["raw_w"][...] = jnp.zeros((1024, 128), bf16)
        gather.until(0)
        save(whole[0], whole_out[0])
        multiply(v["conv"], pl.ds(EDGE, count), v["normed"], whole[0], DI, CW, 256)
        v["conv"][0:EDGE, :] = dot_nn(v["normed_edge"][...], whole[0][:, DI : DI + CW])[EDGE:]
        v["raw_w"][:, 0:MH] = whole[0][:, DI + CW : DI + CW + MH]
        v["raw"][...] = dot_nn(v["normed"][...], v["raw_w"][...])
        gather.pump(4)
        front_conv(v["conv"], v["seg_wide"], weight_ref, cbias_ref, v["act"])
        gather.pump(4)
        front_state(v["seg_wide"], v["raw"], bias_ref, rate_ref, v["act"], v["dt"], v["cum"], v["end"], v["passing"])
        keep("normed", "conv", "raw", "raw_w", "act", "dt", "cum", "passing", "seg_wide", "seg_all")
        width = DI // pieces
        state_slot, kv_slot = depth, depth + pieces

        def chain(j):
            for p in range(pieces):
                cols = pl.ds(p * width, width)

                @pl.when(place == j)
                def _():
                    if j == 0:
                        v["state"][:, cols] = jnp.zeros((NS, width), f32)
                    else:
                        to_next(
                            v["state_send"].at[:, cols], v["state_recv"].at[:, cols], state_slot + p
                        ).wait_recv()
                        v["state"][:, cols] = v["state_recv"][:, cols].astype(f32)
                    if j < depth - 1:
                        v["state_send"][:, cols] = low(
                            v["passing"][:, cols] * v["state"][:, cols] + v["end"][:, cols]
                        )
                        to_next(
                            v["state_send"].at[:, cols], v["state_recv"].at[:, cols], state_slot + p
                        ).start()

        chain(0)
        gather.until(1)
        save(whole[1], whole_out[1])
        multiply(v["qkv"], slice(None), v["normed"], whole[1], 0, 768, 256)
        rotate_kernel(v["qkv"], cos_ref, sin_ref, v["query"], v["kv"].at[own_rows])
        ring(v["kv"], count, 1, kv_slot + 1)
        keep("query")
        gather.pump(4)
        multiply(v["z"], slice(None), v["normed"], whole[0], 0, DI, 256)
        keep("z")
        gather.pump(4)
        chain(1)
        attend_start(v["top"], v["total"], v["attended_t"])

        def attend(b):
            attend_block(b, place, v["query"], v["kv"], v["seg_all"], segrow_ref, v["attended_t"], v["bias"],
                         v["keys"], v["values_t"], v["top"], v["total"])

        attend(place)
        gather.pump(4)
        for hop in range(1, depth):
            ring_wait(v["kv"], count, hop, kv_slot + hop)
            if hop < depth - 1:
                ring(v["kv"], count, hop + 1, kv_slot + hop + 1)

            @pl.when(place >= hop)
            def _(hop=hop):
                attend(place - hop)

            gather.pump(4)
            if hop < depth - 1:
                chain(hop + 1)

        attend_finish(v["attended"], v["attended_t"], v["log_total"], v["top"], v["total"])
        keep("attended", "attended_t", "log_total", "kv")
        for first in range(0, count // SUB, 2):
            gather.pump(4)
            mid_kernel(v["act"], v["dt"], v["cum"], v["seg_wide"], segrow_ref, v["state"], v["z"], mixer_gain_ref,
                       skip_ref, v["y"], v["gated"], v["kept"], v["carry"], first, first + 2)
        keep("y", "gated", "kept")
        for w in range(2, weights):
            gather.until(w)
        gather.finish()
        for condition, src, dst, slot in started:

            @pl.when(condition)
            def _(src=src, dst=dst, slot=slot):
                to_next(src, dst, slot).wait_send()

        @pl.when(place < depth - 1)
        def _():
            for p in range(pieces):
                cols = pl.ds(p * width, width)
                to_next(v["state_send"].at[:, cols], v["state_recv"].at[:, cols], state_slot + p).wait_send()

        for copy in saved:
            copy.wait()

    wholes = [((fsdp * rows, cols), bf16) for rows, cols in shapes]
    scratch = [pltpu.VMEM(*results[n]) for n in names] + [pltpu.VMEM(*a) for a in local.values()]
    scratch += [pltpu.VMEM(shape, f32) for shape in shapes] + [pltpu.VMEM(shape, bf16) for shape in shapes]
    scratch += [pltpu.VMEM(*wholes[w]) for w in in_vmem]
    slots = (1 << bit_count) - 1
    z_slots = depth + pieces + depth
    scratch += [
        pltpu.SemaphoreType.DMA((len(items), slots)),
        pltpu.SemaphoreType.DMA((len(items), slots)),
        pltpu.SemaphoreType.DMA((weights,)),
        pltpu.SemaphoreType.DMA((weights,)),
        pltpu.SemaphoreType.DMA((len(names) + 2,)),
        pltpu.SemaphoreType.DMA((z_slots,)),
        pltpu.SemaphoreType.DMA((z_slots,)),
    ]
    hbm = pl.BlockSpec(memory_space=pl.ANY)
    made = pl.pallas_call(
        kernel,
        out_shape=[jax.ShapeDtypeStruct(*a) for a in list(results.values()) + wholes],
        in_specs=[vmem] * 11 + [hbm] * weights,
        out_specs=[hbm] * (len(names) + weights),
        scratch_shapes=scratch,
        compiler_params=pltpu.CompilerParams(
            collective_id=1, has_side_effects=True, vmem_limit_bytes=62 * 2**20
        ),
    )(tokens, seg_rows, norm_gain, cosine, signed, bias_row, rate_row, conv_weight, conv_bias, mixer_gain,
      skip_row, *shards)
    return dict(zip(names, made)), made[len(names) :]


PA, PB, PC, PD, PE = 3, 4, 6, 6, 2


def backward_part(v, gated_grad, attended_grad, cosine, signed, seg_row, bias_row, rate_row, conv_weight,
                  conv_bias, mixer_gain, skip_row, norm_gain, ffn_gain_grad, tokens, hidden_grad, in_full, qkv_full,
                  gradients):
    fsdp, depth = lax.axis_size("fsdp"), lax.axis_size("seq")
    bit_count = bit_length(fsdp)
    made_here = len(gradients)
    model = in_full.shape[0]
    shapes = [(g.shape[0] // fsdp, g.shape[1]) for g in gradients]
    shapes += [(model // fsdp, width) for width in (DI, 768, CW, 128)]
    parts = fit(shapes, (8, 4, 4, 2, 4, 2, 4, 1))
    items = plan_items(shapes, parts, bit_count)
    weights = len(shapes)
    gate_w, down_w, in_z, qkv_w, conv_w, raw_w = 0, 1, made_here, made_here + 1, made_here + 2, made_here + 3
    hosts = {in_z: (gate_w, 0), conv_w: (gate_w, DI), qkv_w: (gate_w, DI + CW), raw_w: (down_w, 0)}
    count = gated_grad.shape[0]
    pieces = 2
    loaded = dict(
        grad=gated_grad, y=v["y"], act=v["act"], z=v["z"], dt=v["dt"], cum=v["cum"], seg_wide=v["seg_wide"],
        out_grad=attended_grad, query=v["query"], out_t=v["attended_t"], kv=v["kv"], seg_all=v["seg_all"],
        log_total=v["log_total"], cos=cosine, sin=signed, raw=v["raw"], kept=v["kept"],
    )
    rows_in = (seg_row, bias_row, rate_row, conv_weight, conv_bias, mixer_gain, skip_row, v["passing"], norm_gain,
               ffn_gain_grad)
    later_in = (v["conv"], v["normed"], tokens, hidden_grad, in_full, qkv_full, v["raw_w"])
    results = dict(
        raw_grad=((count, 128), bf16),
        qkv_grad=((count, 768), bf16),
    )
    names, loads = list(results), list(loaded)
    rows_out = [((1, model), f32)] * 2
    rows_out += [((1, DI), f32), ((KC, CW), f32), ((1, CW), f32), ((1, 128), f32), ((1, 128), f32), ((1, 128), f32)]
    groups = sum(shape[0] * shape[1] // 128 for shape, _ in rows_out)
    small_shape = (-(-groups // 8) * 8, 128)
    local = dict(
        ygrad=((count, DI), f32),
        state_grad=((NS, DI), f32),
        later=((NS, DI), f32),
        state_send=((NS, DI), bf16),
        state_recv=((NS, DI), bf16),
        bias=((count, count), f32),
        keys=((4, count, 128), bf16),
        values=((4, count, 128), bf16),
        keys_t=((128, count), bf16),
        dkeys=((2, count, 128), f32),
        dvalues=((2, count, 128), f32),
        spread=((QUERY_HEADS * 8, count), f32),
        kv_grad=((depth * count, 256), bf16),
        kv_recv=(((depth - 1) * count, 256), bf16),
        pair_grad=((count, 2 * NS), f32),
        pair_conv_grad=((count, 2 * NS), bf16),
        conv=((2, count + EDGE, 128), f32),
        pre=((count + 2 * EDGE, 128), f32),
        edge=((EDGE, CW), f32),
        edge_recv=((EDGE, CW), f32),
        tail=((16, CW), f32),
    )

    def kernel(*refs):
        at = 0

        def take(n):
            nonlocal at
            at += n
            return refs[at - n : at]

        (segrow_ref, bias_ref, rate_ref, weight_ref, cbias_ref, gain_ref, skip_ref, passing_ref,
         norm_gain_ref, ffn_gain_grad_ref) = take(len(rows_in))
        inputs = dict(zip(loads, take(len(loads))))
        conv_hbm, normed_hbm, tokens_hbm, hidden_hbm, in_hbm, qkv_hbm, raw_w_hbm = take(len(later_in))
        whole = take(made_here)
        (input_grad_out,) = take(1)
        small_out = take(len(rows_out))
        sums = take(weights)
        whole = [*whole, *take(weights - made_here)]
        b = dict(zip(names, take(len(names))))
        b.update(zip(loads, take(len(loads))))
        b.update(zip(local, take(len(local))))
        norm_gain_grad, gain_grad, weight_grad, cbias_grad, rate_grad, bias_grad, skip_grad = take(7)

        def with_views(arrays, lead):
            views = []
            for w in range(made_here, weights):
                host, column = hosts[w]
                cols = pl.ds(column, shapes[w][1])
                views.append(arrays[host].at[(slice(None),) * (lead + 1) + (cols,)])
            return [*arrays, *views]

        own = with_views(take(made_here), bit_count - 1)
        landed = [with_views(take(made_here), bit_count - 1 - s) for s in range(bit_count)]
        zin, zmid = with_views(take(made_here), 0), with_views(take(made_here), 0)
        small_src, small_buf, small_work = take(3)
        (send, recv, own_sem, load_sem, save_sem, conv_sem, z_send, z_recv, small_send, small_recv, tile_sem, grad_sem,
         late_sem, ready_sem) = take(14)
        place = lax.axis_index("seq")

        def load(name):
            return pltpu.make_async_copy(inputs[name], b[name], load_sem.at[loads.index(name)])

        def need(*which):
            for name in which:
                load(name).wait()

        for name in loads:
            load(name).start()
        enter(bit_count, depth)
        work = Reducer(bit_count, depth, items, whole, own, landed, zin, zmid, sums, send, recv, own_sem)
        work.actions(2, 2, tuple(range(made_here, weights)), (gate_w, down_w), ready_sem)
        for item in items:
            if item.weight < made_here:
                work.begin(item)

        def to(by, src, dst, slot):
            return pltpu.make_async_remote_copy(
                src, dst, z_send.at[slot], z_recv.at[slot], device_id=along(by), device_id_type=MESH
            )

        need("grad", "y", "act", "z", "dt", "cum", "seg_wide")
        for first in range(count // SUB):
            gate_back_kernel(b["grad"], b["y"], b["act"], b["z"], b["dt"], b["cum"], b["seg_wide"], gain_ref,
                             skip_ref, b["ygrad"], b["grad"], gain_grad, b["state_grad"], first, first + 1)
            work.pump(PA)
        width = DI // pieces

        def chain(j):
            for p in range(pieces):
                cols = pl.ds(p * width, width)

                @pl.when(place == j)
                def _():
                    copy = to(-1, b["state_send"].at[:, cols], b["state_recv"].at[:, cols], p)
                    if j == depth - 1:
                        b["later"][:, cols] = jnp.zeros((NS, width), f32)
                    else:
                        copy.wait_recv()
                        b["later"][:, cols] = b["state_recv"][:, cols].astype(f32)
                    if j > 0:
                        b["state_send"][:, cols] = low(
                            passing_ref[:, cols] * b["later"][:, cols] + b["state_grad"][:, cols]
                        )
                        copy.start()

        def kv_hop(i):
            part = pl.ds(i * count, count)
            copy = to(-1, b["kv_grad"].at[part], b["kv_recv"].at[part], pieces + i)

            @pl.when((place >= i) & (place < depth - 1))
            def _():
                copy.wait_recv()

                def step(n, nothing):
                    at = pl.ds(pl.multiple_of(i * count + n * 64, 64), 64)
                    b["kv_grad"][at] = low(b["kv_grad"][at].astype(f32) + b["kv_recv"][at].astype(f32))
                    return nothing

                lax.fori_loop(0, count // 64, step, 0)

            @pl.when(place > i)
            def _():
                copy.start()

        chain(depth - 1)
        need("out_grad", "query", "out_t", "kv", "seg_all", "log_total", "cos", "sin")
        attend_back_start(b["query"], b["out_grad"], b["out_t"], b["spread"])
        for i in range(depth):

            for first in (0, 2):

                @pl.when(i <= place)
                def _(i=i, first=first):
                    attend_back_block(i, place, b["query"], b["kv"], b["seg_all"], segrow_ref, b["out_grad"],
                                      b["log_total"], b["kv_grad"], b["bias"], b["keys"], b["values"], b["keys_t"],
                                      b["dkeys"], b["dvalues"], b["spread"], b["out_t"], first, first + 2)

                work.pump(PB)
            if i < depth - 1:
                chain(depth - 2 - i)
            if i > 0:
                kv_hop(i - 1)
        attend_back_finish(b["out_t"], b["cos"], b["sin"], b["qkv_grad"])
        need("raw", "kept")
        for first in range(count // SUB):
            back_states(b["act"], b["dt"], b["cum"], b["seg_wide"], segrow_ref, b["raw"], bias_ref, rate_ref,
                        b["kept"], b["y"], b["ygrad"], skip_ref, b["raw_grad"], rate_grad, bias_grad, skip_grad,
                        b["z"], b["pair_grad"], b["later"], first, first + 1)
            work.pump(PC)
        normed, total = b["act"].at[:, :model], b["y"].at[:, :model]
        half = model // 2

        def late(src, dst, n):
            copy = pltpu.make_async_copy(src, dst, late_sem.at[n])
            copy.start()
            return copy

        normed_copy = late(normed_hbm, normed, 0)
        late_copies = [
            late(hidden_hbm, b["ygrad"].at[:, :model], 1),
            late(tokens_hbm.at[:, :half], b["query"], 2),
            late(tokens_hbm.at[:, half:], b["out_grad"], 3),
        ]
        shard = model // fsdp
        flying = {}

        def weight_gradient(w, rights):
            steps = [(group, right, column, c) for group in range(2) for right, column in rights
                     for c in range(0, right.shape[1], 768)]
            for n, (group, right, column, c) in enumerate(steps):
                slot, width = n % 2, min(768, right.shape[1] - c)
                for copy in flying.pop(slot, ()):
                    copy.wait()
                value = low(dot_tn(normed[:, group * half : group * half + half], right[:, c : c + width]))
                copies = []
                for m in range(half // shard):
                    owner, row = group * (half // shard) + m, m * shard
                    lead = tuple((owner >> (bit_count - 1 - i)) & 1 for i in range(bit_count))
                    room = b["kept"].at[row // 128, pl.ds(row % 128, shard), pl.ds(slot * 768, width)]
                    room[...] = value[row : row + shard]
                    copies.append(
                        pltpu.make_async_copy(
                            room, whole[w].at[(*lead, slice(None), pl.ds(column + c, width))], grad_sem.at[slot, m]
                        )
                    )
                    copies[-1].start()
                flying[slot] = copies
                work.pump(3)
            for slot in list(flying):
                for copy in flying.pop(slot):
                    copy.wait()
            work.have.add(w)

        def fetch(k, source, column, width):
            slot, room = k % 2, (b["keys"], b["values"])[k % 2]
            copies = []
            for c in range(width // 128):
                for r in range(2):
                    copies.append(
                        pltpu.make_async_copy(
                            source.at[pl.ds(r * half, half), pl.ds(column + c * 128, 128)],
                            room.at[c * 2 + r],
                            tile_sem.at[slot, c * 2 + r],
                        )
                    )
            return copies

        def input_gradient(pairs, first):
            plans = [fetch(k, source, column, left.shape[1]) for k, (left, source, column) in enumerate(pairs)]
            for copy in plans[0]:
                copy.start()
            for k, (left, source, column) in enumerate(pairs):
                if k + 1 < len(pairs):
                    for copy in plans[k + 1]:
                        copy.start()
                for copy in plans[k]:
                    copy.wait()
                room, tiles = (b["keys"], b["values"])[k % 2], left.shape[1] // 128
                for r in range(2):
                    right = room[r] if tiles == 1 else jnp.concatenate([room[r], room[2 + r]], 1)
                    cols = slice(r * half, r * half + half)
                    value = dot_nt(left[...], right)
                    total[:, cols] = value if first and k == 0 else total[:, cols] + value
                work.pump(PE)

        def columns(ref, j):
            return ref.at[:, j * 256 : j * 256 + 256]

        own_rows = pl.ds(pl.multiple_of(place * count, 8), count)
        x = b["kv_grad"][own_rows, 0:128].astype(f32)
        b["qkv_grad"][:, 512:640] = low(x * b["cos"][...] + partner(x * b["sin"][...]))
        b["qkv_grad"][:, 640:768] = b["kv_grad"][own_rows, 128:256]
        normed_copy.wait()
        weight_gradient(in_z, [(b["grad"], 0)])
        work.pump(4)
        weight_gradient(qkv_w, [(b["qkv_grad"], 0)])
        work.pump(4)
        input_gradient([(columns(b["grad"], j), in_hbm, j * 256) for j in range(DI // 256)], True)
        tiles, value_tiles = CW // 128, DI // 128
        for first, until in ((0, value_tiles // 2), (value_tiles // 2, value_tiles), (value_tiles, tiles)):
            source, dst, shift = b["z"], b["grad"], 0
            if until > value_tiles:
                source, dst, shift = b["pair_grad"], b["pair_conv_grad"], value_tiles
            back_conv(conv_hbm, b["conv"], conv_sem, b["seg_wide"], weight_ref, cbias_ref, source, shift,
                      dst, b["edge"], b["tail"], weight_grad, cbias_grad, b["pre"], first, until)
            work.pump(PD)
        edge = to(-1, b["edge"], b["edge_recv"], pieces + depth)

        @pl.when(place > 0)
        def _():
            edge.start()

        input_gradient([(columns(b["qkv_grad"], j), qkv_hbm, j * 256) for j in range(3)], False)

        @pl.when(place < depth - 1)
        def _():
            edge.wait_recv()
            b["tail"][16 - EDGE :, :] = b["tail"][16 - EDGE :, :] + b["edge_recv"][...]
            b["grad"][count - 16 :, :] = low(b["tail"][:, :DI])
            b["pair_conv_grad"][count - 16 :, :] = low(b["tail"][:, DI:])

        weight_gradient(conv_w, [(b["grad"], 0), (b["pair_conv_grad"], DI)])
        weight_gradient(raw_w, [(b["raw_grad"], 0)])
        work.pump(12)
        input_gradient(
            [(columns(b["grad"], j), in_hbm, DI + j * 256) for j in range(DI // 256)]
            + [(b["pair_conv_grad"], in_hbm, 2 * DI), (b["raw_grad"], raw_w_hbm, 0)],
            False,
        )
        for copy in late_copies:
            copy.wait()
        norm_gain_grad[...] = jnp.zeros_like(norm_gain_grad)
        group = 32

        def norm_back(i, nothing):
            at = pl.ds(pl.multiple_of(i * group, group), group)
            x = jnp.concatenate([b["query"][at, :].astype(f32), b["out_grad"][at, :].astype(f32)], 1)
            unit = x * lax.rsqrt(jnp.mean(x * x, axis=1, keepdims=True) + epsilon)
            scale = lax.rsqrt(jnp.mean(x * x, axis=1, keepdims=True) + epsilon)
            grad = total[at, :]
            norm_gain_grad[...] += jnp.sum(grad * unit, axis=0, keepdims=True)
            h = grad * norm_gain_ref[...]
            total[at, :] = b["ygrad"][at, :model] + scale * (h - unit * jnp.mean(h * unit, axis=1, keepdims=True))
            return nothing

        lax.fori_loop(0, count // group, norm_back, 0)
        save = pltpu.make_async_copy(total, input_grad_out, save_sem.at[0])
        save.start()
        small_rows = (norm_gain_grad, ffn_gain_grad_ref, gain_grad, weight_grad, cbias_grad, rate_grad, bias_grad,
                      skip_grad)
        places = [(r, i, g) for r, ref in enumerate(small_rows) for i in range(ref.shape[0])
                  for g in range(ref.shape[1] // 128)]
        small_src[...] = jnp.zeros(small_shape, f32)
        for n, (r, i, g) in enumerate(places):
            small_src[n : n + 1, :] = small_rows[r][i : i + 1, g * 128 : g * 128 + 128]
        begin, steps, small_finish = small_sum(
            bit_count, depth, small_src, small_buf, small_work, small_send, small_recv
        )
        begin()
        while work.todo or steps:
            work.pump(6)
            if steps:
                steps.pop(0)()
        for n, (r, i, g) in enumerate(places):
            small_out[r][i : i + 1, g * 128 : g * 128 + 128] = small_work[bit_count + 1, n : n + 1, :]
        small_finish()
        for item in items:
            if item.weight not in (gate_w, down_w):
                work.finish(item)

        @pl.when(place > 0)
        def _():
            edge.wait_send()
            for p in range(pieces):
                cols = pl.ds(p * width, width)
                to(-1, b["state_send"].at[:, cols], b["state_recv"].at[:, cols], p).wait_send()

        for i in range(depth - 1):

            @pl.when(place > i)
            def _(i=i):
                part = pl.ds(i * count, count)
                to(-1, b["kv_grad"].at[part], b["kv_recv"].at[part], pieces + i).wait_send()

        save.wait()

    two = (2,) * bit_count
    hbm = pl.BlockSpec(memory_space=pl.ANY)
    scratch = [pltpu.VMEM(*results[n]) for n in names]
    scratch += [pltpu.VMEM(x.shape, x.dtype) for x in loaded.values()]
    scratch += [pltpu.VMEM(*a) for a in local.values()]
    mine = shapes[:made_here]
    scratch += [pltpu.VMEM(*rows_out[0])] + [pltpu.VMEM(*a) for a in rows_out[2:]]
    stacks = [[pltpu.VMEM((*two[: bit_count - 1 - s], *shape), bf16) for shape in mine] for s in range(bit_count)]
    flat = [pltpu.VMEM(shape, bf16) for shape in mine]
    rooms = [pltpu.VMEM(own_shape(bit_count, shape, n), bf16) for shape, n in zip(mine, parts)]
    scratch += [*rooms, *[x for stage in stacks for x in stage], *flat, *flat]
    scratch += [pltpu.VMEM(small_shape, f32)] + [pltpu.VMEM((bit_count + 2, *small_shape), f32)] * 2
    slots = pieces + depth + 1
    dma = pltpu.SemaphoreType.DMA
    scratch += [
        dma((len(items), bit_count + 3)), dma((len(items), bit_count + 3)), dma((len(items),)), dma((len(loads),)),
        dma((1,)), dma((2,)), dma((slots,)), dma((slots,)), dma((bit_count + 3,)), dma((bit_count + 3,)), dma((2, 4)),
        dma((2, fsdp)), dma((4,)), pltpu.SemaphoreType.REGULAR,
    ]
    outs = [((count, model), f32), *rows_out, *[(shape, bf16) for shape in shapes]]
    outs += [((*two, *shape), bf16) for shape in shapes[made_here:]]
    made = pl.pallas_call(
        kernel,
        out_shape=[jax.ShapeDtypeStruct(*a) for a in outs],
        in_specs=[vmem] * len(rows_in) + [hbm] * (len(loads) + len(later_in) + made_here),
        out_specs=[hbm] + [vmem] * len(rows_out) + [hbm] * (2 * weights - made_here),
        scratch_shapes=scratch,
        compiler_params=pltpu.CompilerParams(
            collective_id=2, has_side_effects=True, vmem_limit_bytes=63 * 2**20
        ),
    )(
        *rows_in, *loaded.values(), *later_in,
        *[g.reshape(*two, *shape) for g, shape in zip(gradients, shapes)],
    )
    n = 1 + len(rows_out)
    return made[0], made[1:n], made[n : n + weights]


def shifted(array, axis, by):
    devices = lax.axis_size(axis)
    pairs = [(i, i + by) for i in range(devices) if 0 <= i + by < devices]
    return lax.ppermute(array, axis, pairs)


def contract(left, right):
    return dot_tn(left, right)


def rms_scale(values, gain_vec):
    return (
        values * lax.rsqrt(jnp.mean(values * values, axis=-1, keepdims=True) + epsilon) * gain_vec
    )


def reduced(gradient):
    return low(gradient)


def padded(vector):
    return jnp.pad(vector, (0, 128 - vector.shape[0]))[None]


def on_device(
    tokens,
    cotangent,
    segment_ids,
    norm_gain,
    ffn_gain,
    mixer_gain,
    conv_weight,
    conv_bias,
    decay_log,
    step_bias,
    skip_gain,
    in_proj,
    mixer_out,
    qkv_proj,
    attn_proj,
    gate_up,
    down_proj,
):
    place, devices = lax.axis_index("seq"), lax.axis_size("seq")
    count = tokens.shape[1]
    position = place * count + jnp.arange(count, dtype=jnp.int32)
    half = HEAD_WIDTH // 2
    lane = jnp.arange(128, dtype=jnp.int32)
    exponent = (lane % half).astype(f32) * (2.0 / HEAD_WIDTH)
    frequencies = jnp.power(rope_base, -exponent)
    angles = position.astype(f32)[:, None] * frequencies[None, :]
    cosine = jnp.cos(angles)
    signed = jnp.sin(angles) * jnp.where(lane % HEAD_WIDTH < half, -1.0, 1.0)[None]
    seg_row = segment_ids.astype(f32)
    bias_row, rate_row = padded(step_bias), padded(decay_log)
    skip_row = jnp.repeat(skip_gain, MP)[None]
    v, (in_full, qkv_full, mix_full, attn_full, gate_full, down_full) = forward_part(
        tokens[0], seg_row, norm_gain[None], cosine, signed, bias_row, rate_row, conv_weight, conv_bias[None],
        mixer_gain[None], skip_row, (in_proj, qkv_proj, mixer_out, attn_proj, gate_up, down_proj),
        (4, 2, 2, 2, 4, 4),
    )
    attended, gated = v["attended"], v["gated"]
    token_rows = tokens[0].astype(f32)
    hidden = token_rows + (dot_nn(attended, attn_full) + dot_nn(gated, mix_full))
    ffn_in32, ffn_pull = jax.vjp(rms_scale, hidden, ffn_gain)
    ffn_in = low(ffn_in32)
    gates = dot_nn(ffn_in, gate_full)

    def swiglu(values):
        return jax.nn.silu(values[:, :FF]) * values[:, FF:]

    act32, act_pull = jax.vjp(swiglu, gates)
    inner = low(act32)
    result = hidden + dot_nn(inner, down_full)
    back_rows = cotangent[0]
    down_piece = reduced(contract(inner, back_rows))
    (gates_grad,) = act_pull(dot_nt(back_rows, down_full))
    gates_grad = low(gates_grad)
    gate_piece = reduced(contract(ffn_in, gates_grad))
    hidden_extra, ffn_gain_grad = ffn_pull(dot_nt(gates_grad, gate_full))
    hidden_grad = back_rows.astype(f32) + hidden_extra
    branch = low(hidden_grad)
    attn_piece = reduced(contract(attended, branch))
    attended_grad = low(dot_nt(branch, attn_full))
    mixer_piece = reduced(contract(gated, branch))
    gated_grad = low(dot_nt(branch, mix_full))

    input_grad, small_rows, sums = backward_part(
        v, gated_grad, attended_grad, cosine, signed, seg_row, bias_row, rate_row, conv_weight, conv_bias[None],
        mixer_gain[None], skip_row, norm_gain[None], ffn_gain_grad[None], tokens[0], hidden_grad, in_full, qkv_full,
        (gate_piece, down_piece, mixer_piece, attn_piece),
    )
    gate_sum, down_sum, mixer_sum, attn_sum, z_sum, qkv_sum, conv_sum, raw_sum = sums
    in_sum = jnp.concatenate([z_sum, conv_sum, raw_sum[:, :MH]], axis=1)
    shards = [x.astype(f32) for x in (in_sum, mixer_sum, qkv_sum, attn_sum, gate_sum, down_sum)]
    small = [row if row.shape[0] == KC else row[0] for row in small_rows]
    small = [row[:MH] if row.shape[0] == 128 else row for row in small]
    return (low(result)[None], input_grad[None], *small, *shards)


def solution(mesh):
    rows, whole, split_rows = P("fsdp", "seq", None), P(), P("fsdp", None)
    return jax.shard_map(
        on_device,
        mesh=mesh,
        in_specs=(rows, rows, P("fsdp", "seq"), *[whole] * 8, *[split_rows] * 6),
        out_specs=(rows, rows, *[whole] * 8, *[split_rows] * 6),
        check_vma=False,
    )
```

```python
import jax
import jax.numpy as jnp
from jax import lax
from jax.experimental import pallas as pl
from jax.experimental.pallas import tpu as pltpu
from jax.sharding import PartitionSpec as P

FF = 2048
QUERY_HEADS = 8
KEY_VALUE_HEADS = 2
HEAD_WIDTH = 64
MH = 24
MP = 64
NS = 128
KC = 4
SUB = 128
DI = 1536
CW = 1792
EDGE = 8

epsilon = 1e-05
rope_base = 100000000000.0
highest = lax.Precision.HIGHEST
f32 = jnp.float32
bf16 = jnp.bfloat16


def dot_nn(left, right):
    return jnp.dot(left, right, preferred_element_type=jnp.float32)


def dot_nt(left, right):
    return lax.dot_general(
        left, right, (((1,), (1,)), ((), ())), preferred_element_type=jnp.float32
    )


def dot_tn(left, right):
    return lax.dot_general(
        left, right, (((0,), (0,)), ((), ())), preferred_element_type=jnp.float32
    )


def exact(left, right):
    return jnp.dot(left, right, precision=highest, preferred_element_type=jnp.float32)


def low(values):
    return values.astype(jnp.bfloat16)


def split(values):
    top = low(values)
    return top, low(values - top.astype(jnp.float32))


def iota(shape, axis):
    return lax.broadcasted_iota(jnp.int32, shape, axis)


def spreader():
    return low(jnp.where(iota((128, DI), 1) // MP == iota((128, DI), 0), 1.0, 0.0))


def widen(values, spread):
    top, rest = split(values)
    return dot_nn(top, spread) + dot_nn(rest, spread)


def widen_row(row, spread):
    return widen(jnp.broadcast_to(row, (8, 128)), spread)[0:1]


def head_sums(values, spread):
    top, rest = split(values)
    return dot_nt(top, spread) + dot_nt(rest, spread)


def softplus(values):
    return jnp.maximum(values, 0.0) + jnp.log1p(jnp.exp(-jnp.abs(values)))


def sigmoid(values):
    return 1.0 / (1.0 + jnp.exp(-values))


def lane_halves(rows):
    lane = iota((rows, 128), 1)
    return lane < MP


def rounded_to(values):
    return low(values).astype(jnp.float32)


def front_conv(conv_ref, seg_ref, weight_ref, cbias_ref, act_ref):
    chunks = act_ref.shape[0] // SUB

    def tile(j, carry):
        col = pl.ds(pl.multiple_of(j * 128, 128), 128)
        for c in range(chunks):
            r0 = c * SUB
            seg = seg_ref[pl.ds(r0 + 8, SUB), :]
            total = jnp.broadcast_to(cbias_ref[0:1, col], (SUB, 128))
            for k in range(KC):
                x = rounded_to(conv_ref[pl.ds(r0 + 9 - KC + k, SUB), col])
                if k < KC - 1:
                    x = jnp.where(seg_ref[pl.ds(r0 + 9 - KC + k, SUB), :] == seg, x, 0.0)
                total = total + weight_ref[k : k + 1, col] * x
            act_ref[pl.ds(r0, SUB), col] = low(total * sigmoid(total))
        return carry

    lax.fori_loop(0, CW // 128, tile, 0)


def front_state(seg_ref, raw_ref, bias_ref, rate_ref, act_ref, dt_ref, cum_ref, end_ref, pass_ref):
    chunks = raw_ref.shape[0] // SUB
    spread = spreader()
    lower = jnp.where(iota((SUB, SUB), 0) >= iota((SUB, SUB), 1), 1.0, 0.0)
    end_ref[...] = jnp.zeros_like(end_ref)
    gain = jnp.ones((1, 128), jnp.float32)
    for c in range(chunks):
        rows = pl.ds(c * SUB, SUB)
        dt = softplus(raw_ref[rows, :] + bias_ref[...])
        cum = exact(lower, -dt * jnp.exp(rate_ref[...]))
        dt_ref[rows, :] = dt
        cum_ref[rows, :] = cum
        seg = seg_ref[pl.ds(c * SUB + 8, SUB), :]
        before = seg_ref[pl.ds(c * SUB + 7, 1), :]
        last = seg[SUB - 1 :, :]
        end = cum[SUB - 1 :, :]
        weight = jnp.where(seg == last, jnp.exp(end - cum), 0.0) * dt
        passing = jnp.where(last == before, jnp.exp(end), 0.0)
        gain = gain * passing
        values = act_ref[rows, 0:DI].astype(jnp.float32)
        fresh = dot_tn(act_ref[rows, DI : DI + NS], low(widen(weight, spread) * values))
        end_ref[...] = widen_row(passing, spread) * end_ref[...] + fresh
    pass_ref[...] = widen_row(gain, spread)


def mid_kernel(act_ref, dt_ref, cum_ref, seg_ref, segrow_ref, state_ref, z_ref, gain_ref, skip_ref,
               y_ref, gated_ref, kept_ref, carry_ref, first, until):
    spread = spreader()
    if first == 0:
        carry_ref[...] = state_ref[...]
    half = lane_halves(SUB)

    def chunk(c, nothing):
        r0 = pl.multiple_of(c * SUB, SUB)
        rows = pl.ds(r0, SUB)
        dt, cum = dt_ref[rows, :], cum_ref[rows, :]
        cum_t = cum.T
        seg = seg_ref[pl.ds(pl.multiple_of(r0 + 8, 8), SUB), :]
        before = seg_ref[pl.ds(pl.multiple_of(r0, 8), 8), :][7:8]
        last, end = seg[SUB - 1 :, :], cum[SUB - 1 :, :]
        keys, reads = act_ref[rows, DI : DI + NS], act_ref[rows, DI + NS : CW]
        affinity = dot_nt(reads, keys)
        allowed = (iota((SUB, SUB), 0) >= iota((SUB, SUB), 1)) & (seg == segrow_ref[0:1, rows])
        state = low(carry_ref[...])
        kept_ref[pl.ds(c, 1)] = state[None]
        entry = widen(jnp.where(seg == before, jnp.exp(cum), 0.0), spread)
        y_ref[rows, :] = dot_nn(reads, state) * entry
        values = act_ref[rows, 0:DI].astype(jnp.float32)
        scaled = values * widen(dt, spread)
        weight = jnp.where(seg == last, jnp.exp(end - cum), 0.0)
        passing = jnp.where(last == before, jnp.exp(end), 0.0)
        fresh = dot_tn(keys, low(widen(weight, spread) * scaled))
        carry_ref[...] = widen_row(passing, spread) * carry_ref[...] + fresh
        for pair in range(MH // 2):
            cols = slice(pair * 128, pair * 128 + 128)
            parts = []
            for h in (2 * pair, 2 * pair + 1):
                gap = jnp.where(allowed, cum[:, h : h + 1] - cum_t[h : h + 1, :], -1e30)
                parts.append(low(jnp.exp(gap) * affinity))
            v = scaled[:, cols]
            right = jnp.concatenate([low(jnp.where(half, v, 0.0)), low(jnp.where(half, 0.0, v))], 0)
            y_ref[rows, cols] = y_ref[rows, cols] + dot_nn(jnp.concatenate(parts, 1), right)
        z = z_ref[rows, :]
        g = (y_ref[rows, :] + skip_ref[...] * values) * (z * sigmoid(z))
        scale = lax.rsqrt(jnp.mean(g * g, axis=1, keepdims=True) + epsilon)
        gated_ref[rows, :] = low(g * scale * gain_ref[...])
        return nothing

    lax.fori_loop(first, until, chunk, 0)


def gate_back_kernel(grad_ref, y_ref, act_ref, z_ref, dt_ref, cum_ref, seg_ref, gain_ref, skip_ref,
                     ygrad_ref, zgrad_ref, gain_grad_ref, state_grad_ref, first, until):
    chunks = act_ref.shape[0] // SUB
    spread = spreader()
    if first == 0:
        gain_grad_ref[...] = jnp.zeros_like(gain_grad_ref)
        state_grad_ref[...] = jnp.zeros_like(state_grad_ref)

    def chunk(i, nothing):
        c = chunks - 1 - i
        r0 = pl.multiple_of(c * SUB, SUB)
        rows = pl.ds(r0, SUB)
        values = act_ref[rows, 0:DI].astype(jnp.float32)
        z = z_ref[rows, :]
        sig = sigmoid(z)
        silu = z * sig
        u = y_ref[rows, :] + skip_ref[...] * values
        g = u * silu
        grad = grad_ref[rows, :].astype(jnp.float32)
        scale = lax.rsqrt(jnp.mean(g * g, axis=1, keepdims=True) + epsilon)
        unit = g * scale
        gain_grad_ref[...] += jnp.sum(grad * unit, axis=0, keepdims=True)
        h = grad * gain_ref[...]
        dg = scale * (h - unit * jnp.mean(h * unit, axis=1, keepdims=True))
        dy = dg * silu
        ygrad_ref[rows, :] = dy
        zgrad_ref[rows, :] = low(dg * u * (sig * (1.0 + z * (1.0 - sig))))
        cum = cum_ref[rows, :]
        seg = seg_ref[pl.ds(pl.multiple_of(r0 + 8, 8), SUB), :]
        before = seg_ref[pl.ds(pl.multiple_of(r0, 8), 8), :][7:8]
        last, end = seg[SUB - 1 :, :], cum[SUB - 1 :, :]
        entry = widen(jnp.where(seg == before, jnp.exp(cum), 0.0), spread)
        passing = jnp.where(last == before, jnp.exp(end), 0.0)
        fresh = dot_tn(act_ref[rows, DI + NS : CW], low(entry * dy))
        state_grad_ref[...] = widen_row(passing, spread) * state_grad_ref[...] + fresh
        return nothing

    lax.fori_loop(first, until, chunk, 0)


def back_states(act_ref, dt_ref, cum_ref, seg_ref, segrow_ref, raw_ref, bias_ref, rate_ref, kept_ref,
                y_ref, ygrad_ref, skip_ref, raw_grad_ref, rate_grad_ref, bias_grad_ref, skip_grad_ref,
                value_grad_ref, pair_grad_ref, carry_ref, first, until):
    chunks = act_ref.shape[0] // SUB
    spread = spreader()
    half = lane_halves(SUB)
    upper = jnp.where(iota((SUB, SUB), 1) >= iota((SUB, SUB), 0), 1.0, 0.0)
    rate = jnp.exp(rate_ref[...])
    if first == 0:
        rate_grad_ref[...] = jnp.zeros_like(rate_grad_ref)
        bias_grad_ref[...] = jnp.zeros_like(bias_grad_ref)
        skip_grad_ref[...] = jnp.zeros_like(skip_grad_ref)

    def chunk(i, nothing):
        c = chunks - 1 - i
        r0 = pl.multiple_of(c * SUB, SUB)
        rows = pl.ds(r0, SUB)
        dt, cum = dt_ref[rows, :], cum_ref[rows, :]
        cum_t = cum.T
        seg = seg_ref[pl.ds(pl.multiple_of(r0 + 8, 8), SUB), :]
        before = seg_ref[pl.ds(pl.multiple_of(r0, 8), 8), :][7:8]
        last, end = seg[SUB - 1 :, :], cum[SUB - 1 :, :]
        keys, reads = act_ref[rows, DI : DI + NS], act_ref[rows, DI + NS : CW]
        affinity = dot_nt(keys, reads)
        allowed = (iota((SUB, SUB), 1) >= iota((SUB, SUB), 0)) & (seg == segrow_ref[0:1, rows])
        values = act_ref[rows, 0:DI].astype(jnp.float32)
        wide_dt = widen(dt, spread)
        scaled = values * wide_dt
        scaled_low = low(scaled)
        dy = ygrad_ref[rows, :]
        dy_low = low(dy)
        state, carry = kept_ref[pl.ds(c, 1)][0], carry_ref[...]
        carry_low = low(carry)
        wide_weight = widen(jnp.where(seg == last, jnp.exp(end - cum), 0.0), spread)
        wide_entry = widen(jnp.where(seg == before, jnp.exp(cum), 0.0), spread)
        wide_pass = widen_row(jnp.where(last == before, jnp.exp(end), 0.0), spread)
        from_state = dot_nn(keys, carry_low) * wide_weight
        mixed_grad = jnp.zeros((SUB, SUB), jnp.float32)
        for pair in range(MH // 2):
            cols = slice(pair * 128, pair * 128 + 128)
            v, d = scaled[:, cols], dy[:, cols]
            left = jnp.concatenate([low(jnp.where(half, v, 0.0)), low(jnp.where(half, 0.0, v))], 0)
            right = jnp.concatenate([low(jnp.where(half, d, 0.0)), low(jnp.where(half, 0.0, d))], 0)
            weight_grad = dot_nt(left, dy_low[:, cols])
            parts = []
            for n, h in enumerate((2 * pair, 2 * pair + 1)):
                gap = jnp.where(allowed, cum_t[h : h + 1, :] - cum[:, h : h + 1], -1e30)
                decay = jnp.exp(gap)
                parts.append(low(decay * affinity))
                mixed_grad = mixed_grad + decay * weight_grad[n * SUB : (n + 1) * SUB]
            value_grad_ref[rows, cols] = dot_nn(jnp.concatenate(parts, 1), right)
        x = value_grad_ref[rows, 0:DI] + from_state
        value_grad_ref[rows, 0:DI] = wide_dt * x + skip_ref[...] * dy
        mixed_low = low(mixed_grad)
        pair_grad_ref[rows, 0:NS] = dot_nn(mixed_low, reads) + dot_nt(
            low(wide_weight * scaled), carry_low
        )
        entered = low(wide_entry * dy)
        pair_grad_ref[rows, NS:] = dot_tn(mixed_low, keys) + dot_nt(entered, state)
        scaled_exact = scaled_low.astype(jnp.float32)
        direct = head_sums(values * x, spread)
        given = head_sums(scaled_exact * x, spread)
        taken = head_sums(dy_low.astype(jnp.float32) * y_ref[rows, :], spread)
        tail = jnp.sum(scaled_exact * from_state, axis=0, keepdims=True) + jnp.sum(
            wide_pass * carry * state.astype(jnp.float32), axis=0, keepdims=True
        )
        tail = head_sums(jnp.broadcast_to(tail, (8, DI)), spread)[0:1]
        decay_grad = exact(upper, taken - given) + tail
        rate_grad_ref[...] += jnp.sum(decay_grad * (-dt * rate), axis=0, keepdims=True)
        dt_grad = direct - decay_grad * rate
        raw_grad = dt_grad * sigmoid(raw_ref[rows, :] + bias_ref[...])
        raw_grad_ref[rows, :] = low(jnp.where(iota((SUB, 128), 1) < MH, raw_grad, 0.0))
        bias_grad_ref[...] += jnp.sum(raw_grad, axis=0, keepdims=True)
        skip_sum = jnp.sum(dy * values, axis=0, keepdims=True)
        skip_grad_ref[...] += head_sums(jnp.broadcast_to(skip_sum, (8, DI)), spread)[0:1]
        carry_ref[...] = wide_pass * carry + dot_tn(reads, entered)
        return nothing

    lax.fori_loop(first, until, chunk, 0)


def back_conv(conv_hbm, conv_ref, conv_sem, seg_ref, weight_ref, cbias_ref, act_grad_ref, shift,
              conv_grad_ref, edge_ref, tail_ref, weight_grad_ref, cbias_grad_ref, pre_ref, first, until):
    rows_total = act_grad_ref.shape[0]
    chunks = rows_total // SUB
    pre_ref[0:8, :] = jnp.zeros((8, 128), jnp.float32)
    pre_ref[rows_total + 8 : rows_total + 16, :] = jnp.zeros((8, 128), jnp.float32)

    def fetch(j, slot):
        return pltpu.make_async_copy(
            conv_hbm.at[:, pl.ds(pl.multiple_of(j * 128, 128), 128)], conv_ref.at[slot], conv_sem.at[slot]
        )

    fetch(first, first % 2).start()

    def tile(j, carry):
        slot = j % 2

        @pl.when(j + 1 < until)
        def _():
            fetch(j + 1, 1 - slot).start()

        fetch(j, slot).wait()
        col = pl.ds(pl.multiple_of(j * 128, 128), 128)
        sums = [jnp.zeros((1, 128), jnp.float32) for _ in range(KC + 1)]
        for c in range(chunks):
            r0 = c * SUB
            seg = seg_ref[pl.ds(r0 + 8, SUB), :]
            total = jnp.broadcast_to(cbias_ref[0:1, col], (SUB, 128))
            taps = []
            for k in range(KC):
                x = rounded_to(conv_ref[slot, pl.ds(r0 + 9 - KC + k, SUB), :])
                if k < KC - 1:
                    x = jnp.where(seg_ref[pl.ds(r0 + 9 - KC + k, SUB), :] == seg, x, 0.0)
                taps.append(x)
                total = total + weight_ref[k : k + 1, col] * x
            sig = sigmoid(total)
            act_col = pl.ds(pl.multiple_of((j - shift) * 128, 128), 128)
            pre = act_grad_ref[pl.ds(r0, SUB), act_col] * (sig * (1.0 + total * (1.0 - sig)))
            pre_ref[pl.ds(r0 + 8, SUB), :] = pre
            for k in range(KC):
                sums[k] = sums[k] + jnp.sum(pre * taps[k], axis=0, keepdims=True)
            sums[KC] = sums[KC] + jnp.sum(pre, axis=0, keepdims=True)
        for k in range(KC):
            weight_grad_ref[k : k + 1, col] = sums[k]
        cbias_grad_ref[0:1, col] = sums[KC]

        def spread_back(r0, size):
            seg = seg_ref[pl.ds(r0, size), :]
            total = jnp.zeros((size, 128), jnp.float32)
            for back in range(KC):
                x = pre_ref[pl.ds(r0 + back, size), :]
                if back:
                    x = jnp.where(seg_ref[pl.ds(r0 + back, size), :] == seg, x, 0.0)
                total = total + weight_ref[KC - 1 - back : KC - back, col] * x
            return total

        edge_ref[:, col] = spread_back(0, 8)
        for c in range(chunks):
            total = spread_back(c * SUB + 8, SUB)
            conv_grad_ref[pl.ds(c * SUB, SUB), act_col] = low(total)
        tail_ref[:, col] = total[SUB - 16 :]
        return carry

    lax.fori_loop(first, until, tile, 0)


def partner(values):
    lane = iota(values.shape, 1)
    half = HEAD_WIDTH // 2
    return jnp.where(
        lane % HEAD_WIDTH < half, pltpu.roll(values, 128 - half, 1), pltpu.roll(values, half, 1)
    )


def rotate_kernel(qkv_ref, cos_ref, sin_ref, query_ref, kv_ref):
    cos, sin = cos_ref[...], sin_ref[...]
    for g in range(5):
        x = qkv_ref[:, g * 128 : g * 128 + 128]
        x = low(x * cos + partner(x) * sin)
        if g < 4:
            query_ref[:, g * 128 : g * 128 + 128] = x * jnp.bfloat16(HEAD_WIDTH**-0.5)
        else:
            kv_ref[:, 0:128] = x
    kv_ref[:, 128:256] = low(qkv_ref[:, 640:768])


def lane_variants(block, out_ref):
    other = pltpu.roll(block, 64, 1)
    half = iota(block.shape, 1) < HEAD_WIDTH
    out_ref[0] = low(jnp.where(half, block, 0.0))
    out_ref[1] = low(jnp.where(half, 0.0, other))
    out_ref[2] = low(jnp.where(half, other, 0.0))
    out_ref[3] = low(jnp.where(half, 0.0, block))


def seg_column(row):
    return jnp.broadcast_to(row, (128, row.shape[1])).T


def attend_bias(b, own, rows, segall_ref, segrow_ref, bias_ref):
    seg = seg_column(segall_ref[pl.ds(pl.multiple_of(b * 8, 8), 8), :][0:1])
    seg = jnp.concatenate([seg] * (rows // 128), 1)
    causal = (iota((rows, rows), 0) - iota((rows, rows), 1)) <= jnp.where(b < own, rows, 0)
    bias_ref[...] = jnp.where(causal & (seg == segrow_ref[...]), 0.0, -1e30)


def attend_start(top_ref, sum_ref, out_t_ref):
    top_ref[...] = jnp.full_like(top_ref, -1e30)
    sum_ref[...] = jnp.zeros_like(sum_ref)
    out_t_ref[...] = jnp.zeros_like(out_t_ref)


def attend_block(b, own, query_ref, kv_ref, segall_ref, segrow_ref, out_t_ref, bias_ref, keys_ref,
                 values_t_ref, top_ref, sum_ref):
    rows = query_ref.shape[0]
    at = pl.ds(pl.multiple_of(b * rows, rows), rows)
    attend_bias(b, own, rows, segall_ref, segrow_ref, bias_ref)
    lane_variants(kv_ref[at, 0:128].astype(jnp.float32), keys_ref)
    values_t_ref[...] = low(kv_ref[at, 128:256].astype(jnp.float32).T)

    def pair(g, nothing):
        kv = g // 2
        query = query_ref[:, pl.ds(pl.multiple_of(g * 128, 128), 128)]
        for side in range(2):
            h = g * 2 + side
            row = pl.ds(pl.multiple_of(h * 8, 8), 8)
            scores = dot_nt(keys_ref[kv * 2 + side], query)
            scores = scores + bias_ref[...]
            old = top_ref[row, :][0:1]
            top = jnp.maximum(old, jnp.max(scores, axis=0, keepdims=True))
            p = jnp.exp(scores - top)
            fade = jnp.exp(old - top)
            total = sum_ref[row, :][0:1] * fade + jnp.sum(p, 0, keepdims=True)
            top_ref[row, :] = jnp.broadcast_to(top, (8, rows))
            sum_ref[row, :] = jnp.broadcast_to(total, (8, rows))
            at_h = pl.ds(pl.multiple_of(h * 64, 64), 64)
            values_t = values_t_ref[pl.ds(pl.multiple_of(kv * 64, 64), 64), :]
            out_t_ref[at_h, :] = out_t_ref[at_h, :] * fade + dot_nn(values_t, low(p))
        return nothing

    lax.fori_loop(0, QUERY_HEADS // 2, pair, 0)


def attend_finish(out_ref, out_t_ref, total_ref, top_ref, sum_ref):
    for h in range(QUERY_HEADS):
        at_h = slice(h * 64, h * 64 + 64)
        row = slice(h * 8, h * 8 + 8)
        total_ref[row, :] = top_ref[row, :] + jnp.log(sum_ref[row, :])
        out_t_ref[at_h, :] = out_t_ref[at_h, :] / sum_ref[h * 8 : h * 8 + 1, :]
    out_ref[...] = low(out_t_ref[...].T)


def attend_back_start(query_ref, grad_ref, out_t_ref, spread_ref):
    rows = query_ref.shape[0]
    grad_t = grad_ref[...].astype(jnp.float32).T
    product = grad_t * out_t_ref[...]
    for h in range(QUERY_HEADS):
        total = jnp.sum(product[h * 64 : h * 64 + 64, :], 0, keepdims=True)
        spread_ref[h * 8 : h * 8 + 8, :] = jnp.broadcast_to(total, (8, rows))
    out_t_ref[...] = jnp.zeros_like(out_t_ref)


def attend_back_block(b, own, query_ref, kv_ref, segall_ref, segrow_ref, grad_ref, total_ref, kv_grad_ref,
                      bias_ref, keys_ref, values_ref, keys_t_ref, dkeys_ref, dvalues_ref, spread_ref, dq_ref,
                      first, until):
    rows = query_ref.shape[0]
    at = pl.ds(pl.multiple_of(b * rows, rows), rows)
    if first == 0:
        attend_bias(b, own, rows, segall_ref, segrow_ref, bias_ref)
        keys = kv_ref[at, 0:128].astype(jnp.float32)
        lane_variants(keys, keys_ref)
        lane_variants(kv_ref[at, 128:256].astype(jnp.float32), values_ref)
        keys_t_ref[...] = low(keys.T)
        dkeys_ref[...] = jnp.zeros_like(dkeys_ref)
        dvalues_ref[...] = jnp.zeros_like(dvalues_ref)

    lower_half = iota((rows, 128), 1) < HEAD_WIDTH

    def side_of(values, side):
        values = values.astype(jnp.float32)
        return low(jnp.where(lower_half, 0.0, values) if side else jnp.where(lower_half, values, 0.0))

    def pair(g, nothing):
        kv = g // 2
        lanes = pl.ds(pl.multiple_of(g * 128, 128), 128)
        for side in range(2):
            h = g * 2 + side
            row = pl.ds(pl.multiple_of(h * 8, 8), 8)
            scores = dot_nt(keys_ref[kv * 2 + side], query_ref[:, lanes]) + bias_ref[...]
            p = jnp.exp(scores - total_ref[row, :][0:1])
            dp = dot_nt(values_ref[kv * 2 + side], grad_ref[:, lanes])
            ds = low(p * (dp - spread_ref[row, :][0:1]))
            dkeys_ref[kv] = dkeys_ref[kv] + dot_nn(ds, side_of(query_ref[:, lanes], side))
            dvalues_ref[kv] = dvalues_ref[kv] + dot_nn(low(p), side_of(grad_ref[:, lanes], side))
            at_h = pl.ds(pl.multiple_of(h * 64, 64), 64)
            keys_t = keys_t_ref[pl.ds(pl.multiple_of(kv * 64, 64), 64), :]
            dq_ref[at_h, :] = dq_ref[at_h, :] + dot_nn(keys_t, ds)
        return nothing

    lax.fori_loop(first, until, pair, 0)
    if until < QUERY_HEADS // 2:
        return
    half = lower_half
    for src, lanes in ((dkeys_ref, slice(0, 128)), (dvalues_ref, slice(128, 256))):
        first, second = src[0], src[1]
        kv_grad_ref[at, lanes] = low(
            jnp.where(half, first + pltpu.roll(first, 64, 1), second + pltpu.roll(second, 64, 1))
        )


def attend_back_finish(dq_ref, cos_ref, sin_ref, qkv_grad_ref):
    dq = dq_ref[...].T * (HEAD_WIDTH**-0.5)
    cos, sin = cos_ref[...], sin_ref[...]
    for g in range(4):
        x = dq[:, g * 128 : g * 128 + 128]
        qkv_grad_ref[:, g * 128 : g * 128 + 128] = low(x * cos + partner(x * sin))


vmem = pl.BlockSpec(memory_space=pltpu.VMEM)
smem = pl.BlockSpec(memory_space=pltpu.SMEM)


def call(kernel, outs, args, scratch=(), first=vmem, flops=10**9):
    return pl.pallas_call(
        kernel,
        out_shape=[jax.ShapeDtypeStruct(shape, kind) for shape, kind in outs],
        in_specs=[first] + [vmem] * (len(args) - 1),
        out_specs=[vmem] * len(outs),
        scratch_shapes=[pltpu.VMEM(shape, kind) for shape, kind in scratch],
        compiler_params=pltpu.CompilerParams(vmem_limit_bytes=56 * 2**20),
        cost_estimate=pl.CostEstimate(flops=flops, bytes_accessed=10**7, transcendentals=10**6),
    )(*args)


MESH = pl.DeviceIdType.MESH


def position_bits(count):
    index = lax.axis_index("fsdp")
    return [(index // (1 << b)) % 2 for b in reversed(range(count))]


def across(bits, axis):
    count = len(bits)
    index = lax.axis_index("fsdp")
    step = 1 << (count - 1 - axis)
    return (index + step * (1 - 2 * bits[axis]), lax.axis_index("seq"))


def along(by):
    return (lax.axis_index("fsdp"), lax.axis_index("seq") + by)


class Item:
    def __init__(self, number, weight, start, size, order):
        self.number, self.weight, self.start, self.size, self.order = number, weight, start, size, order


def fit(shapes, wanted):
    return [max(d for d in range(1, n + 1) if rows // 16 % d == 0) for (rows, _), n in zip(shapes, wanted)]


def plan_items(shapes, parts, bit_count):
    items = []
    for w, ((rows, _), count) in enumerate(zip(shapes, parts)):
        for p in range(count):
            turn = p % max(bit_count - 1, 1)
            ici = list(range(bit_count - 1))
            order = [bit_count - 1] + ici[turn:] + ici[:turn]
            items.append(Item(len(items), w, p * (rows // count), rows // count, order))
            items[-1].slots = max(1, count // 2)
            items[-1].part = p
    return items


def own_shape(bit_count, shape, parts):
    return (*(2,) * (bit_count - 1), shape[0] // parts * max(1, parts // 2), shape[1])


class Reducer:
    def __init__(self, bit_count, depth, items, whole, own, landed, zin, zmid, out, send, recv, own_sem):
        self.bit_count, self.depth, self.items = bit_count, depth, items
        self.whole, self.own, self.landed = whole, own, landed
        self.zin, self.zmid, self.out = zin, zmid, out
        self.send, self.recv, self.own_sem = send, recv, own_sem
        self.bits = position_bits(bit_count)
        self.place = lax.axis_index("seq")

    def rows(self, item):
        return pl.ds(item.start, item.size)

    def left(self, item, stage):
        return sorted(item.order[stage:])

    def pick(self, item, stage, mine):
        axis = item.order[stage]
        at = self.left(item, stage).index(axis)
        bit = self.bits[axis] if mine else 1 - self.bits[axis]
        lead = [slice(None)] * (self.bit_count - stage)
        lead[at] = bit
        return (*lead, self.rows(item))

    def source(self, item, stage):
        if stage == 0:
            return self.whole[item.weight]
        return self.landed[stage - 1][item.weight]

    def copy(self, item, stage):
        lead = (slice(None),) * (self.bit_count - stage - 1)
        return pltpu.make_async_remote_copy(
            self.source(item, stage).at[self.pick(item, stage, False)],
            self.landed[stage][item.weight].at[(*lead, self.rows(item))],
            self.send.at[item.number, stage],
            self.recv.at[item.number, stage],
            device_id=across(self.bits, item.order[stage]),
            device_id_type=MESH,
        )

    def own_copy(self, item):
        lead = (slice(None),) * (self.bit_count - 1)
        return pltpu.make_async_copy(
            self.whole[item.weight].at[self.pick(item, 0, True)],
            self.own[item.weight].at[(*lead, pl.ds(self.own_start(item), item.size))],
            self.own_sem.at[item.number],
        )

    def own_start(self, item):
        return item.part % item.slots * item.size

    def begin(self, item):
        self.copy(item, 0).start()
        if item.part < item.slots:
            self.own_copy(item).start()

    def add(self, dst, dst_lead, other, other_lead, item, shift=0):
        width = self.out[item.weight].shape[1]
        group = max(g for g in (16, 32, 64) if item.size % g == 0 and (g == 16 or g * width <= 65536))

        def step(i, nothing):
            at = pl.ds(pl.multiple_of(item.start + i * group, 16), group)
            at_other = pl.ds(pl.multiple_of(item.start + shift + i * group, 16), group)
            dst[(*dst_lead, at)] = dst[(*dst_lead, at)] + other[(*other_lead, at_other)]
            return nothing

        lax.fori_loop(0, item.size // group, step, 0)

    def advance(self, item, stage):
        self.copy(item, stage).wait_recv()
        landed = self.landed[stage][item.weight]
        kept = self.bit_count - stage - 1
        places = [[(i >> (kept - 1 - b)) & 1 for b in range(kept)] for i in range(1 << kept)]
        if stage == 0:
            self.own_copy(item).wait()
            for lead in places:
                self.add(landed, lead, self.own[item.weight], lead, item, self.own_start(item) - item.start)
            for other in self.items:
                if other.weight == item.weight and other.part == item.part + item.slots:
                    self.own_copy(other).start()
        else:
            source = self.source(item, stage)
            axis = item.order[stage]
            at = self.left(item, stage).index(axis)
            for lead in places:
                from_lead = [*lead[:at], self.bits[axis], *lead[at:]]
                self.add(landed, lead, source, from_lead, item)
        if stage + 1 < self.bit_count:
            self.copy(item, stage + 1).start()

    def z_copy(self, item, kind, by):
        w, rows = item.weight, self.rows(item)
        last = self.landed[self.bit_count - 1][w]
        src, dst = {
            "in": (last, self.zin[w]),
            "mid": (last, self.zmid[w]),
            "out": (self.zmid[w], self.zmid[w]),
        }[kind]
        slot = self.bit_count + {"in": 0, "mid": 1, "out": 2}[kind]
        return pltpu.make_async_remote_copy(
            src.at[rows],
            dst.at[rows],
            self.send.at[item.number, slot],
            self.recv.at[item.number, slot],
            device_id=along(by),
            device_id_type=MESH,
        )

    def sides(self):
        half = self.depth // 2
        outermost = (self.place == 0) | (self.place == self.depth - 1)
        middle = (self.place == half - 1) | (self.place == half)
        inward = 1 - 2 * (self.place // half)
        return outermost, middle, inward

    def z_first(self, item):
        outermost, middle, inward = self.sides()

        @pl.when(outermost & jnp.logical_not(middle))
        def _():
            self.z_copy(item, "in", inward).start()

    def z_second(self, item):
        outermost, middle, inward = self.sides()

        @pl.when(jnp.logical_not(outermost))
        def _():
            self.z_copy(item, "in", -inward).wait_recv()
            self.add(self.landed[self.bit_count - 1][item.weight], (), self.zin[item.weight], (), item)

            @pl.when(jnp.logical_not(middle))
            def _():
                self.z_copy(item, "in", inward).start()

        @pl.when(middle)
        def _():
            self.z_copy(item, "mid", inward).start()

    def z_third(self, item):
        outermost, middle, inward = self.sides()

        @pl.when(middle)
        def _():
            self.z_copy(item, "mid", inward).wait_recv()
            self.add(self.zmid[item.weight], (), self.landed[self.bit_count - 1][item.weight], (), item)

            @pl.when(jnp.logical_not(outermost))
            def _():
                self.z_copy(item, "out", -inward).start()

    def z_fourth(self, item):
        outermost, middle, inward = self.sides()

        @pl.when(jnp.logical_not(middle))
        def _():
            self.z_copy(item, "out", inward).wait_recv()

            @pl.when(jnp.logical_not(outermost))
            def _():
                self.z_copy(item, "out", -inward).start()

        self.out_copy(item).start()

    def out_copy(self, item):
        rows = self.rows(item)
        return pltpu.make_async_copy(
            self.zmid[item.weight].at[rows], self.out[item.weight].at[rows], self.own_sem.at[item.number]
        )

    def pump(self, count):
        while count and self.todo and (self.todo[0][0] is None or self.todo[0][0] in self.have):
            self.todo.pop(0)[1]()
            count -= 1

    def finish(self, item):
        outermost, middle, inward = self.sides()
        self.out_copy(item).wait()
        for stage in range(self.bit_count):
            self.copy(item, stage).wait_send()

        @pl.when(jnp.logical_not(middle))
        def _():
            self.z_copy(item, "in", inward).wait_send()

        @pl.when(middle)
        def _():
            self.z_copy(item, "mid", inward).wait_send()

        @pl.when(jnp.logical_not(outermost))
        def _():
            self.z_copy(item, "out", -inward).wait_send()

    def actions(self, lag, z_lag, late=(), reused=(), ready_sem=None):
        last_use = max(
            [i + lag * (self.bit_count - 1) + 3 * z_lag for i, item in enumerate(self.items) if item.weight in reused],
            default=0,
        )
        first_late = min([i for i, item in enumerate(self.items) if item.weight in late], default=0)
        gap = max(0, last_use + 2 - first_late)
        steps = []
        for i, item in enumerate(self.items):
            if item.weight in late:
                if i == first_late:
                    steps.append((i + gap - 1, -2, item.weight, lambda: self.hand_over(reused, ready_sem)))
                i += gap
                steps.append((i - 1, -1, item.weight, lambda item=item: self.begin(item)))
            for stage in range(self.bit_count):
                steps.append((i + lag * stage, stage, None, lambda item=item, s=stage: self.advance(item, s)))
            t = i + lag * (self.bit_count - 1)
            for n, run in enumerate((self.z_first, self.z_second, self.z_third, self.z_fourth)):
                steps.append((t + n * z_lag, self.bit_count + n, None, lambda item=item, run=run: run(item)))
        self.todo = [step[2:] for step in sorted(steps, key=lambda s: s[:2])]
        self.have = set()

    def hand_over(self, weights, ready_sem):
        for item in self.items:
            if item.weight in weights:
                self.finish(item)
        meet(self.bits, self.place, self.depth, ready_sem)


def meet(bits, place, depth, semaphore):
    for axis in range(len(bits)):
        pl.semaphore_signal(semaphore, inc=1, device_id=across(bits, axis), device_id_type=MESH)

    @pl.when(place > 0)
    def _():
        pl.semaphore_signal(semaphore, inc=1, device_id=along(-1), device_id_type=MESH)

    @pl.when(place < depth - 1)
    def _():
        pl.semaphore_signal(semaphore, inc=1, device_id=along(1), device_id_type=MESH)

    ends = jnp.where(place == 0, 1, 0) + jnp.where(place == depth - 1, 1, 0)
    pl.semaphore_wait(semaphore, len(bits) + 2 - ends)


def enter(bit_count, depth):
    meet(position_bits(bit_count), lax.axis_index("seq"), depth, pltpu.get_barrier_semaphore())


def small_sum(bit_count, depth, src, buf, out, send, recv):
    bits = position_bits(bit_count)
    place = lax.axis_index("seq")
    half = depth // 2
    outermost = (place == 0) | (place == depth - 1)
    middle = (place == half - 1) | (place == half)
    inward = 1 - 2 * (place // half)

    def flip(stage):
        return pltpu.make_async_remote_copy(
            (src if stage == 0 else out.at[stage - 1]),
            buf.at[stage],
            send.at[stage],
            recv.at[stage],
            device_id=across(bits, bit_count - 1 - stage),
            device_id_type=MESH,
        )

    def z_copy(kind, by):
        n = bit_count + kind
        return pltpu.make_async_remote_copy(
            out.at[(bit_count - 1, bit_count, bit_count + 1)[kind]],
            (buf.at[bit_count], buf.at[bit_count + 1], out.at[bit_count + 1])[kind],
            send.at[n],
            recv.at[n],
            device_id=along(by),
            device_id_type=MESH,
        )

    def flip_done(stage):
        flip(stage).wait_recv()
        mine = src[...] if stage == 0 else out[stage - 1]
        out[stage] = mine + buf[stage]
        if stage + 1 < bit_count:
            flip(stage + 1).start()

    def z_in():
        @pl.when(jnp.logical_not(middle))
        def _():
            @pl.when(jnp.logical_not(outermost))
            def _():
                z_copy(0, -inward).wait_recv()
                out[bit_count - 1] = out[bit_count - 1] + buf[bit_count]

            z_copy(0, inward).start()

        @pl.when(middle)
        def _():
            out[bit_count] = out[bit_count - 1]

            @pl.when(jnp.logical_not(outermost))
            def _():
                z_copy(0, -inward).wait_recv()
                out[bit_count] = out[bit_count] + buf[bit_count]

            z_copy(1, inward).start()

    def z_mid():
        @pl.when(middle)
        def _():
            z_copy(1, inward).wait_recv()
            out[bit_count + 1] = out[bit_count] + buf[bit_count + 1]

    def z_out():
        @pl.when(jnp.logical_not(middle))
        def _():
            z_copy(2, inward).wait_recv()

        @pl.when(jnp.logical_not(outermost))
        def _():
            z_copy(2, -inward).start()

    def finish():
        for stage in range(bit_count):
            flip(stage).wait_send()

        @pl.when(jnp.logical_not(middle))
        def _():
            z_copy(0, inward).wait_send()

        @pl.when(middle)
        def _():
            z_copy(1, inward).wait_send()

        @pl.when(jnp.logical_not(outermost))
        def _():
            z_copy(2, -inward).wait_send()

    begin = lambda: flip(0).start()
    steps = [lambda s=s: flip_done(s) for s in range(bit_count)] + [z_in, z_mid, z_out]
    return begin, steps, finish


def bit_length(count):
    return count.bit_length() - 1


class Gatherer:
    def __init__(self, bit_count, items, shards, whole, loads, load_sem, cast_to, own_sem, send, recv):
        self.bit_count, self.items = bit_count, items
        self.shards, self.whole, self.loads, self.load_sem = shards, whole, loads, load_sem
        self.cast_to, self.own_sem, self.send, self.recv = cast_to, own_sem, send, recv
        self.bits = position_bits(bit_count)
        self.index = lax.axis_index("fsdp")
        self.ready = set()
        self.todo = []
        self.done = set()

    def block(self, axes):
        at = self.index
        for axis in axes:
            at = at + (1 << (self.bit_count - 1 - axis)) * (1 - 2 * self.bits[axis])
        return at

    def subsets(self, order):
        sets = [()]
        for axis in order:
            sets = sets + [(*s, axis) for s in sets]
        return sets

    def rows(self, item, axes):
        shard_rows = self.cast_to[item.weight].shape[0]
        return pl.ds(pl.multiple_of(self.block(axes) * shard_rows + item.start, 16), item.size)

    def copy(self, item, stage, number, axes):
        whole = self.whole[item.weight]
        at = self.rows(item, axes)
        src = self.cast_to[item.weight].at[pl.ds(item.start, item.size)] if not axes else whole.at[at]
        slot = (1 << stage) - 1 + number
        return pltpu.make_async_remote_copy(
            src,
            whole.at[at],
            self.send.at[item.number, slot],
            self.recv.at[item.number, slot],
            device_id=across(self.bits, item.order[stage]),
            device_id_type=MESH,
        )

    def landed(self, item, stage, number, axes):
        whole = self.whole[item.weight]
        at = self.rows(item, (*axes, item.order[stage]))
        slot = (1 << stage) - 1 + number
        return pltpu.make_async_remote_copy(
            whole.at[at],
            whole.at[at],
            self.send.at[item.number, slot],
            self.recv.at[item.number, slot],
            device_id=across(self.bits, item.order[stage]),
            device_id_type=MESH,
        )

    def load(self, weight):
        return pltpu.make_async_copy(self.shards[weight], self.loads[weight], self.load_sem.at[weight])

    def own(self, weight):
        rows = self.cast_to[weight].shape[0]
        return pltpu.make_async_copy(
            self.cast_to[weight],
            self.whole[weight].at[pl.ds(pl.multiple_of(self.index * rows, 16), rows)],
            self.own_sem.at[weight],
        )

    def begin(self, item):
        w = item.weight
        if w not in self.ready:
            self.ready.add(w)
            self.load(w).wait()
            group = 16

            def step(i, nothing):
                at = pl.ds(pl.multiple_of(i * group, group), group)
                self.cast_to[w][at] = low(self.loads[w][at])
                return nothing

            lax.fori_loop(0, self.cast_to[w].shape[0] // group, step, 0)
            self.own(w).start()
        for stage in range(self.bit_count):
            self.copy(item, stage, 0, ()).start()

    def advance(self, item, stage):
        before = self.subsets(item.order[:stage])
        for number, axes in enumerate(before):
            self.landed(item, stage, number, axes).wait_recv()
        for later in range(stage + 1, self.bit_count):
            sets = self.subsets(item.order[:later])
            for number, axes in enumerate(before):
                mine = (*axes, item.order[stage])
                self.copy(item, later, sets.index(mine), mine).start()
        if stage == self.bit_count - 1:
            self.done.add(item.number)

    def plan(self, lag):
        steps = []
        for i, item in enumerate(self.items):
            steps.append((i, 0, lambda item=item: self.begin(item)))
            for stage in range(self.bit_count):
                steps.append((i + lag * (stage + 1), stage + 1, lambda item=item, s=stage: self.advance(item, s)))
        self.todo = [action for _, _, action in sorted(steps, key=lambda s: s[:2])]

    def pump(self, count):
        for _ in range(min(count, len(self.todo))):
            self.todo.pop(0)()

    def until(self, weight):
        numbers = {item.number for item in self.items if item.weight == weight}
        while not numbers <= self.done:
            self.todo.pop(0)()
        self.own(weight).wait()

    def finish(self):
        for item in self.items:
            for stage in range(self.bit_count):
                for number, axes in enumerate(self.subsets(item.order[:stage])):
                    self.copy(item, stage, number, axes).wait_send()


def multiply(out_ref, out_rows, left, right_ref, first, width, tile):
    def step(j, nothing):
        at = pl.ds(pl.multiple_of(j * tile, tile), tile)
        from_at = pl.ds(pl.multiple_of(first + j * tile, 128), tile)
        out_ref[out_rows, at] = dot_nn(left[...], right_ref[:, from_at])
        return nothing

    lax.fori_loop(0, width // tile, step, 0)


def forward_part(tokens, seg_rows, norm_gain, cosine, signed, bias_row, rate_row, conv_weight,
                 conv_bias, mixer_gain, skip_row, shards, parts):
    fsdp, depth = lax.axis_size("fsdp"), lax.axis_size("seq")
    bit_count = bit_length(fsdp)
    shapes = [s.shape for s in shards]
    items = plan_items(shapes, fit(shapes, parts), bit_count)
    for item in items:
        item.order = item.order[1:] + item.order[:1]
    count = tokens.shape[0]
    weights = len(shards)
    pieces = 2
    kept_shape = (count // SUB, NS, DI)
    results = dict(
        normed=((count, 1024), bf16),
        conv=((count + EDGE, CW), f32),
        raw=((count, 128), f32),
        raw_w=((1024, 128), bf16),
        z=((count, DI), f32),
        act=((count, CW), bf16),
        dt=((count, 128), f32),
        cum=((count, 128), f32),
        passing=((1, DI), f32),
        query=((count, 512), bf16),
        kv=((depth * count, 256), bf16),
        attended=((count, 512), bf16),
        attended_t=((512, count), f32),
        log_total=((QUERY_HEADS * 8, count), f32),
        y=((count, DI), f32),
        gated=((count, DI), bf16),
        kept=(kept_shape, bf16),
        seg_wide=((count + 2 * EDGE, 128), f32),
        seg_all=((depth * 8, count), f32),
    )
    names = list(results)
    local = dict(
        normed_edge=((16, 1024), bf16),
        edge=((16, 1024), bf16),
        qkv=((count, 768), f32),
        end=((NS, DI), f32),
        state=((NS, DI), f32),
        carry=((NS, DI), f32),
        state_send=((NS, DI), bf16),
        state_recv=((NS, DI), bf16),
        bias=((count, count), f32),
        keys=((4, count, 128), bf16),
        values_t=((128, count), bf16),
        top=((QUERY_HEADS * 8, count), f32),
        total=((QUERY_HEADS * 8, count), f32),
    )
    in_vmem = (0, 1)

    def kernel(*refs):
        at = 0

        def take(n):
            nonlocal at
            at += n
            return refs[at - n : at]

        (tokens_ref, segrow_ref, gain_ref, cos_ref, sin_ref, bias_ref, rate_ref, weight_ref, cbias_ref,
         mixer_gain_ref, skip_ref) = take(11)
        shard_refs = take(weights)
        out = dict(zip(names, take(len(names))))
        whole_out = take(weights)
        v = dict(zip(names, take(len(names))))
        v.update(zip(local, take(len(local))))
        loads, cast_to = take(weights), take(weights)
        whole_vmem = take(len(in_vmem))
        send, recv, load_sem, own_sem, save_sem, z_send, z_recv = take(7)
        place = lax.axis_index("seq")
        whole = [whole_vmem[in_vmem.index(w)] if w in in_vmem else whole_out[w] for w in range(weights)]
        gather = Gatherer(bit_count, items, shard_refs, whole, loads, load_sem, cast_to, own_sem, send, recv)
        for w in range(weights):
            gather.load(w).start()
        enter(bit_count, depth)
        gather.plan(2)
        saved = []

        def save(src, dst):
            copy = pltpu.make_async_copy(src, dst, save_sem.at[len(saved)])
            copy.start()
            saved.append(copy)

        def keep(*which):
            for name in which:
                save(v[name], out[name])

        def to_next(src, dst, slot):
            return pltpu.make_async_remote_copy(
                src, dst, z_send.at[slot], z_recv.at[slot], device_id=along(1), device_id_type=MESH
            )

        started = []

        def send_on(condition, src, dst, slot):
            @pl.when(condition)
            def _():
                to_next(src, dst, slot).start()

            started.append((condition, src, dst, slot))

        def ring(ref, rows, hop, slot):
            b = place - hop + 1
            part = ref.at[pl.ds(pl.multiple_of(jnp.maximum(b, 0) * rows, 8), rows)]
            send_on((b >= 0) & (place < depth - 1), part, part, slot)

        def ring_wait(ref, rows, hop, slot):
            b = place - hop
            part = ref.at[pl.ds(pl.multiple_of(jnp.maximum(b, 0) * rows, 8), rows)]

            @pl.when(b >= 0)
            def _():
                to_next(part, part, slot).wait_recv()

        tail = tokens_ref.at[pl.ds(count - 16, 16)]
        gather.pump(2)
        send_on(place < depth - 1, tail, v["edge"], 0)
        v["seg_all"][pl.ds(pl.multiple_of(place * 8, 8), 8)] = jnp.broadcast_to(segrow_ref[...], (8, count))
        ring(v["seg_all"], 8, 1, 1)

        def normalise(src, dst, rows, group):
            def step(i, nothing):
                at = pl.ds(pl.multiple_of(i * group, group), group)
                x = src[at].astype(f32)
                scale = lax.rsqrt(jnp.mean(x * x, axis=1, keepdims=True) + epsilon)
                dst[at] = low(x * scale * gain_ref[...])
                return nothing

            lax.fori_loop(0, rows // group, step, 0)

        normalise(tokens_ref, v["normed"], count, 64)
        gather.pump(1)

        @pl.when(place == 0)
        def _():
            v["edge"][...] = jnp.zeros((16, 1024), bf16)

        @pl.when(place > 0)
        def _():
            to_next(tail, v["edge"], 0).wait_recv()

        normalise(v["edge"], v["normed_edge"], 16, 16)
        gather.pump(1)
        for hop in range(1, depth):
            ring_wait(v["seg_all"], 8, hop, hop)
            if hop < depth - 1:
                ring(v["seg_all"], 8, hop + 1, hop + 1)

        before = v["seg_all"][pl.ds(pl.multiple_of(jnp.maximum(place - 1, 0) * 8, 8), 8)][0:1]
        v["seg_wide"][0:EDGE, :] = jnp.where(place == 0, -1.0, seg_column(before)[count - EDGE :])
        v["seg_wide"][EDGE : EDGE + count, :] = seg_column(segrow_ref[...])
        v["seg_wide"][EDGE + count :, :] = jnp.full((EDGE, 128), -2.0, f32)
        own_rows = pl.ds(pl.multiple_of(place * count, 8), count)
        v["raw_w"][...] = jnp.zeros((1024, 128), bf16)
        gather.until(0)
        save(whole[0], whole_out[0])
        multiply(v["conv"], pl.ds(EDGE, count), v["normed"], whole[0], DI, CW, 256)
        v["conv"][0:EDGE, :] = dot_nn(v["normed_edge"][...], whole[0][:, DI : DI + CW])[EDGE:]
        v["raw_w"][:, 0:MH] = whole[0][:, DI + CW : DI + CW + MH]
        v["raw"][...] = dot_nn(v["normed"][...], v["raw_w"][...])
        gather.pump(4)
        front_conv(v["conv"], v["seg_wide"], weight_ref, cbias_ref, v["act"])
        gather.pump(4)
        front_state(v["seg_wide"], v["raw"], bias_ref, rate_ref, v["act"], v["dt"], v["cum"], v["end"], v["passing"])
        keep("normed", "conv", "raw", "raw_w", "act", "dt", "cum", "passing", "seg_wide", "seg_all")
        width = DI // pieces
        state_slot, kv_slot = depth, depth + pieces

        def chain(j):
            for p in range(pieces):
                cols = pl.ds(p * width, width)

                @pl.when(place == j)
                def _():
                    if j == 0:
                        v["state"][:, cols] = jnp.zeros((NS, width), f32)
                    else:
                        to_next(
                            v["state_send"].at[:, cols], v["state_recv"].at[:, cols], state_slot + p
                        ).wait_recv()
                        v["state"][:, cols] = v["state_recv"][:, cols].astype(f32)
                    if j < depth - 1:
                        v["state_send"][:, cols] = low(
                            v["passing"][:, cols] * v["state"][:, cols] + v["end"][:, cols]
                        )
                        to_next(
                            v["state_send"].at[:, cols], v["state_recv"].at[:, cols], state_slot + p
                        ).start()

        chain(0)
        gather.until(1)
        save(whole[1], whole_out[1])
        multiply(v["qkv"], slice(None), v["normed"], whole[1], 0, 768, 256)
        rotate_kernel(v["qkv"], cos_ref, sin_ref, v["query"], v["kv"].at[own_rows])
        ring(v["kv"], count, 1, kv_slot + 1)
        keep("query")
        gather.pump(4)
        multiply(v["z"], slice(None), v["normed"], whole[0], 0, DI, 256)
        keep("z")
        gather.pump(4)
        chain(1)
        attend_start(v["top"], v["total"], v["attended_t"])

        def attend(b):
            attend_block(b, place, v["query"], v["kv"], v["seg_all"], segrow_ref, v["attended_t"], v["bias"],
                         v["keys"], v["values_t"], v["top"], v["total"])

        attend(place)
        gather.pump(4)
        for hop in range(1, depth):
            ring_wait(v["kv"], count, hop, kv_slot + hop)
            if hop < depth - 1:
                ring(v["kv"], count, hop + 1, kv_slot + hop + 1)

            @pl.when(place >= hop)
            def _(hop=hop):
                attend(place - hop)

            gather.pump(4)
            if hop < depth - 1:
                chain(hop + 1)

        attend_finish(v["attended"], v["attended_t"], v["log_total"], v["top"], v["total"])
        keep("attended", "attended_t", "log_total", "kv")
        for first in range(0, count // SUB, 2):
            gather.pump(4)
            mid_kernel(v["act"], v["dt"], v["cum"], v["seg_wide"], segrow_ref, v["state"], v["z"], mixer_gain_ref,
                       skip_ref, v["y"], v["gated"], v["kept"], v["carry"], first, first + 2)
        keep("y", "gated", "kept")
        for w in range(2, weights):
            gather.until(w)
        gather.finish()
        for condition, src, dst, slot in started:

            @pl.when(condition)
            def _(src=src, dst=dst, slot=slot):
                to_next(src, dst, slot).wait_send()

        @pl.when(place < depth - 1)
        def _():
            for p in range(pieces):
                cols = pl.ds(p * width, width)
                to_next(v["state_send"].at[:, cols], v["state_recv"].at[:, cols], state_slot + p).wait_send()

        for copy in saved:
            copy.wait()

    wholes = [((fsdp * rows, cols), bf16) for rows, cols in shapes]
    scratch = [pltpu.VMEM(*results[n]) for n in names] + [pltpu.VMEM(*a) for a in local.values()]
    scratch += [pltpu.VMEM(shape, f32) for shape in shapes] + [pltpu.VMEM(shape, bf16) for shape in shapes]
    scratch += [pltpu.VMEM(*wholes[w]) for w in in_vmem]
    slots = (1 << bit_count) - 1
    z_slots = depth + pieces + depth
    scratch += [
        pltpu.SemaphoreType.DMA((len(items), slots)),
        pltpu.SemaphoreType.DMA((len(items), slots)),
        pltpu.SemaphoreType.DMA((weights,)),
        pltpu.SemaphoreType.DMA((weights,)),
        pltpu.SemaphoreType.DMA((len(names) + 2,)),
        pltpu.SemaphoreType.DMA((z_slots,)),
        pltpu.SemaphoreType.DMA((z_slots,)),
    ]
    hbm = pl.BlockSpec(memory_space=pl.ANY)
    made = pl.pallas_call(
        kernel,
        out_shape=[jax.ShapeDtypeStruct(*a) for a in list(results.values()) + wholes],
        in_specs=[vmem] * 11 + [hbm] * weights,
        out_specs=[hbm] * (len(names) + weights),
        scratch_shapes=scratch,
        compiler_params=pltpu.CompilerParams(
            collective_id=1, has_side_effects=True, vmem_limit_bytes=62 * 2**20
        ),
    )(tokens, seg_rows, norm_gain, cosine, signed, bias_row, rate_row, conv_weight, conv_bias, mixer_gain,
      skip_row, *shards)
    return dict(zip(names, made)), made[len(names) :]


PA, PB, PC, PD, PE = 3, 4, 6, 6, 2


def backward_part(v, gated_grad, attended_grad, cosine, signed, seg_row, bias_row, rate_row, conv_weight,
                  conv_bias, mixer_gain, skip_row, norm_gain, ffn_gain_grad, tokens, hidden_grad, in_full, qkv_full,
                  gradients):
    fsdp, depth = lax.axis_size("fsdp"), lax.axis_size("seq")
    bit_count = bit_length(fsdp)
    made_here = len(gradients)
    model = in_full.shape[0]
    shapes = [(g.shape[0] // fsdp, g.shape[1]) for g in gradients]
    shapes += [(model // fsdp, width) for width in (DI, 768, CW, 128)]
    parts = fit(shapes, (8, 4, 4, 2, 4, 2, 4, 1))
    items = plan_items(shapes, parts, bit_count)
    weights = len(shapes)
    gate_w, down_w, in_z, qkv_w, conv_w, raw_w = 0, 1, made_here, made_here + 1, made_here + 2, made_here + 3
    hosts = {in_z: (gate_w, 0), conv_w: (gate_w, DI), qkv_w: (gate_w, DI + CW), raw_w: (down_w, 0)}
    count = gated_grad.shape[0]
    pieces = 2
    loaded = dict(
        grad=gated_grad, y=v["y"], act=v["act"], z=v["z"], dt=v["dt"], cum=v["cum"], seg_wide=v["seg_wide"],
        out_grad=attended_grad, query=v["query"], out_t=v["attended_t"], kv=v["kv"], seg_all=v["seg_all"],
        log_total=v["log_total"], cos=cosine, sin=signed, raw=v["raw"], kept=v["kept"],
    )
    rows_in = (seg_row, bias_row, rate_row, conv_weight, conv_bias, mixer_gain, skip_row, v["passing"], norm_gain,
               ffn_gain_grad)
    later_in = (v["conv"], v["normed"], tokens, hidden_grad, in_full, qkv_full, v["raw_w"])
    results = dict(
        raw_grad=((count, 128), bf16),
        qkv_grad=((count, 768), bf16),
    )
    names, loads = list(results), list(loaded)
    rows_out = [((1, model), f32)] * 2
    rows_out += [((1, DI), f32), ((KC, CW), f32), ((1, CW), f32), ((1, 128), f32), ((1, 128), f32), ((1, 128), f32)]
    groups = sum(shape[0] * shape[1] // 128 for shape, _ in rows_out)
    small_shape = (-(-groups // 8) * 8, 128)
    local = dict(
        ygrad=((count, DI), f32),
        state_grad=((NS, DI), f32),
        later=((NS, DI), f32),
        state_send=((NS, DI), bf16),
        state_recv=((NS, DI), bf16),
        bias=((count, count), f32),
        keys=((4, count, 128), bf16),
        values=((4, count, 128), bf16),
        keys_t=((128, count), bf16),
        dkeys=((2, count, 128), f32),
        dvalues=((2, count, 128), f32),
        spread=((QUERY_HEADS * 8, count), f32),
        kv_grad=((depth * count, 256), bf16),
        kv_recv=(((depth - 1) * count, 256), bf16),
        pair_grad=((count, 2 * NS), f32),
        pair_conv_grad=((count, 2 * NS), bf16),
        conv=((2, count + EDGE, 128), f32),
        pre=((count + 2 * EDGE, 128), f32),
        edge=((EDGE, CW), f32),
        edge_recv=((EDGE, CW), f32),
        tail=((16, CW), f32),
    )

    def kernel(*refs):
        at = 0

        def take(n):
            nonlocal at
            at += n
            return refs[at - n : at]

        (segrow_ref, bias_ref, rate_ref, weight_ref, cbias_ref, gain_ref, skip_ref, passing_ref,
         norm_gain_ref, ffn_gain_grad_ref) = take(len(rows_in))
        inputs = dict(zip(loads, take(len(loads))))
        conv_hbm, normed_hbm, tokens_hbm, hidden_hbm, in_hbm, qkv_hbm, raw_w_hbm = take(len(later_in))
        whole = take(made_here)
        (input_grad_out,) = take(1)
        small_out = take(len(rows_out))
        sums = take(weights)
        whole = [*whole, *take(weights - made_here)]
        b = dict(zip(names, take(len(names))))
        b.update(zip(loads, take(len(loads))))
        b.update(zip(local, take(len(local))))
        norm_gain_grad, gain_grad, weight_grad, cbias_grad, rate_grad, bias_grad, skip_grad = take(7)

        def with_views(arrays, lead):
            views = []
            for w in range(made_here, weights):
                host, column = hosts[w]
                cols = pl.ds(column, shapes[w][1])
                views.append(arrays[host].at[(slice(None),) * (lead + 1) + (cols,)])
            return [*arrays, *views]

        own = with_views(take(made_here), bit_count - 1)
        landed = [with_views(take(made_here), bit_count - 1 - s) for s in range(bit_count)]
        zin, zmid = with_views(take(made_here), 0), with_views(take(made_here), 0)
        small_src, small_buf, small_work = take(3)
        (send, recv, own_sem, load_sem, save_sem, conv_sem, z_send, z_recv, small_send, small_recv, tile_sem, grad_sem,
         late_sem, ready_sem) = take(14)
        place = lax.axis_index("seq")

        def load(name):
            return pltpu.make_async_copy(inputs[name], b[name], load_sem.at[loads.index(name)])

        def need(*which):
            for name in which:
                load(name).wait()

        for name in loads:
            load(name).start()
        enter(bit_count, depth)
        work = Reducer(bit_count, depth, items, whole, own, landed, zin, zmid, sums, send, recv, own_sem)
        work.actions(2, 2, tuple(range(made_here, weights)), (gate_w, down_w), ready_sem)
        for item in items:
            if item.weight < made_here:
                work.begin(item)

        def to(by, src, dst, slot):
            return pltpu.make_async_remote_copy(
                src, dst, z_send.at[slot], z_recv.at[slot], device_id=along(by), device_id_type=MESH
            )

        need("grad", "y", "act", "z", "dt", "cum", "seg_wide")
        for first in range(count // SUB):
            gate_back_kernel(b["grad"], b["y"], b["act"], b["z"], b["dt"], b["cum"], b["seg_wide"], gain_ref,
                             skip_ref, b["ygrad"], b["grad"], gain_grad, b["state_grad"], first, first + 1)
            work.pump(PA)
        width = DI // pieces

        def chain(j):
            for p in range(pieces):
                cols = pl.ds(p * width, width)

                @pl.when(place == j)
                def _():
                    copy = to(-1, b["state_send"].at[:, cols], b["state_recv"].at[:, cols], p)
                    if j == depth - 1:
                        b["later"][:, cols] = jnp.zeros((NS, width), f32)
                    else:
                        copy.wait_recv()
                        b["later"][:, cols] = b["state_recv"][:, cols].astype(f32)
                    if j > 0:
                        b["state_send"][:, cols] = low(
                            passing_ref[:, cols] * b["later"][:, cols] + b["state_grad"][:, cols]
                        )
                        copy.start()

        def kv_hop(i):
            part = pl.ds(i * count, count)
            copy = to(-1, b["kv_grad"].at[part], b["kv_recv"].at[part], pieces + i)

            @pl.when((place >= i) & (place < depth - 1))
            def _():
                copy.wait_recv()

                def step(n, nothing):
                    at = pl.ds(pl.multiple_of(i * count + n * 64, 64), 64)
                    b["kv_grad"][at] = b["kv_grad"][at] + b["kv_recv"][at]
                    return nothing

                lax.fori_loop(0, count // 64, step, 0)

            @pl.when(place > i)
            def _():
                copy.start()

        chain(depth - 1)
        need("out_grad", "query", "out_t", "kv", "seg_all", "log_total", "cos", "sin")
        attend_back_start(b["query"], b["out_grad"], b["out_t"], b["spread"])
        for i in range(depth):

            for first in (0, 2):

                @pl.when(i <= place)
                def _(i=i, first=first):
                    attend_back_block(i, place, b["query"], b["kv"], b["seg_all"], segrow_ref, b["out_grad"],
                                      b["log_total"], b["kv_grad"], b["bias"], b["keys"], b["values"], b["keys_t"],
                                      b["dkeys"], b["dvalues"], b["spread"], b["out_t"], first, first + 2)

                work.pump(PB)
            if i < depth - 1:
                chain(depth - 2 - i)
            if i > 0:
                kv_hop(i - 1)
        attend_back_finish(b["out_t"], b["cos"], b["sin"], b["qkv_grad"])
        need("raw", "kept")
        for first in range(count // SUB):
            back_states(b["act"], b["dt"], b["cum"], b["seg_wide"], segrow_ref, b["raw"], bias_ref, rate_ref,
                        b["kept"], b["y"], b["ygrad"], skip_ref, b["raw_grad"], rate_grad, bias_grad, skip_grad,
                        b["z"], b["pair_grad"], b["later"], first, first + 1)
            work.pump(PC)
        normed, total = b["act"].at[:, :model], b["y"].at[:, :model]
        half = model // 2

        def late(src, dst, n):
            copy = pltpu.make_async_copy(src, dst, late_sem.at[n])
            copy.start()
            return copy

        normed_copy = late(normed_hbm, normed, 0)
        late_copies = [
            late(hidden_hbm, b["ygrad"].at[:, :model], 1),
            late(tokens_hbm.at[:, :half], b["query"], 2),
            late(tokens_hbm.at[:, half:], b["out_grad"], 3),
        ]
        shard = model // fsdp
        flying = {}

        def weight_gradient(w, rights):
            steps = [(group, right, column, c) for group in range(2) for right, column in rights
                     for c in range(0, right.shape[1], 768)]
            for n, (group, right, column, c) in enumerate(steps):
                slot, width = n % 2, min(768, right.shape[1] - c)
                for copy in flying.pop(slot, ()):
                    copy.wait()
                value = low(dot_tn(normed[:, group * half : group * half + half], right[:, c : c + width]))
                copies = []
                for m in range(half // shard):
                    owner, row = group * (half // shard) + m, m * shard
                    lead = tuple((owner >> (bit_count - 1 - i)) & 1 for i in range(bit_count))
                    room = b["kept"].at[row // 128, pl.ds(row % 128, shard), pl.ds(slot * 768, width)]
                    room[...] = value[row : row + shard]
                    copies.append(
                        pltpu.make_async_copy(
                            room, whole[w].at[(*lead, slice(None), pl.ds(column + c, width))], grad_sem.at[slot, m]
                        )
                    )
                    copies[-1].start()
                flying[slot] = copies
                work.pump(3)
            for slot in list(flying):
                for copy in flying.pop(slot):
                    copy.wait()
            work.have.add(w)

        def fetch(k, source, column, width):
            slot, room = k % 2, (b["keys"], b["values"])[k % 2]
            copies = []
            for c in range(width // 128):
                for r in range(2):
                    copies.append(
                        pltpu.make_async_copy(
                            source.at[pl.ds(r * half, half), pl.ds(column + c * 128, 128)],
                            room.at[c * 2 + r],
                            tile_sem.at[slot, c * 2 + r],
                        )
                    )
            return copies

        def input_gradient(pairs, first):
            plans = [fetch(k, source, column, left.shape[1]) for k, (left, source, column) in enumerate(pairs)]
            for copy in plans[0]:
                copy.start()
            for k, (left, source, column) in enumerate(pairs):
                if k + 1 < len(pairs):
                    for copy in plans[k + 1]:
                        copy.start()
                for copy in plans[k]:
                    copy.wait()
                room, tiles = (b["keys"], b["values"])[k % 2], left.shape[1] // 128
                for r in range(2):
                    right = room[r] if tiles == 1 else jnp.concatenate([room[r], room[2 + r]], 1)
                    cols = slice(r * half, r * half + half)
                    value = dot_nt(left[...], right)
                    total[:, cols] = value if first and k == 0 else total[:, cols] + value
                work.pump(PE)

        def columns(ref, j):
            return ref.at[:, j * 256 : j * 256 + 256]

        own_rows = pl.ds(pl.multiple_of(place * count, 8), count)
        x = b["kv_grad"][own_rows, 0:128].astype(f32)
        b["qkv_grad"][:, 512:640] = low(x * b["cos"][...] + partner(x * b["sin"][...]))
        b["qkv_grad"][:, 640:768] = b["kv_grad"][own_rows, 128:256]
        normed_copy.wait()
        weight_gradient(in_z, [(b["grad"], 0)])
        work.pump(4)
        weight_gradient(qkv_w, [(b["qkv_grad"], 0)])
        work.pump(4)
        input_gradient([(columns(b["grad"], j), in_hbm, j * 256) for j in range(DI // 256)], True)
        tiles, value_tiles = CW // 128, DI // 128
        for first, until in ((0, value_tiles // 2), (value_tiles // 2, value_tiles), (value_tiles, tiles)):
            source, dst, shift = b["z"], b["grad"], 0
            if until > value_tiles:
                source, dst, shift = b["pair_grad"], b["pair_conv_grad"], value_tiles
            back_conv(conv_hbm, b["conv"], conv_sem, b["seg_wide"], weight_ref, cbias_ref, source, shift,
                      dst, b["edge"], b["tail"], weight_grad, cbias_grad, b["pre"], first, until)
            work.pump(PD)
        edge = to(-1, b["edge"], b["edge_recv"], pieces + depth)

        @pl.when(place > 0)
        def _():
            edge.start()

        input_gradient([(columns(b["qkv_grad"], j), qkv_hbm, j * 256) for j in range(3)], False)

        @pl.when(place < depth - 1)
        def _():
            edge.wait_recv()
            b["tail"][16 - EDGE :, :] = b["tail"][16 - EDGE :, :] + b["edge_recv"][...]
            b["grad"][count - 16 :, :] = low(b["tail"][:, :DI])
            b["pair_conv_grad"][count - 16 :, :] = low(b["tail"][:, DI:])

        weight_gradient(conv_w, [(b["grad"], 0), (b["pair_conv_grad"], DI)])
        weight_gradient(raw_w, [(b["raw_grad"], 0)])
        work.pump(12)
        input_gradient(
            [(columns(b["grad"], j), in_hbm, DI + j * 256) for j in range(DI // 256)]
            + [(b["pair_conv_grad"], in_hbm, 2 * DI), (b["raw_grad"], raw_w_hbm, 0)],
            False,
        )
        for copy in late_copies:
            copy.wait()
        norm_gain_grad[...] = jnp.zeros_like(norm_gain_grad)
        group = 32

        def norm_back(i, nothing):
            at = pl.ds(pl.multiple_of(i * group, group), group)
            x = jnp.concatenate([b["query"][at, :].astype(f32), b["out_grad"][at, :].astype(f32)], 1)
            unit = x * lax.rsqrt(jnp.mean(x * x, axis=1, keepdims=True) + epsilon)
            scale = lax.rsqrt(jnp.mean(x * x, axis=1, keepdims=True) + epsilon)
            grad = total[at, :]
            norm_gain_grad[...] += jnp.sum(grad * unit, axis=0, keepdims=True)
            h = grad * norm_gain_ref[...]
            total[at, :] = b["ygrad"][at, :model] + scale * (h - unit * jnp.mean(h * unit, axis=1, keepdims=True))
            return nothing

        lax.fori_loop(0, count // group, norm_back, 0)
        save = pltpu.make_async_copy(total, input_grad_out, save_sem.at[0])
        save.start()
        small_rows = (norm_gain_grad, ffn_gain_grad_ref, gain_grad, weight_grad, cbias_grad, rate_grad, bias_grad,
                      skip_grad)
        places = [(r, i, g) for r, ref in enumerate(small_rows) for i in range(ref.shape[0])
                  for g in range(ref.shape[1] // 128)]
        small_src[...] = jnp.zeros(small_shape, f32)
        for n, (r, i, g) in enumerate(places):
            small_src[n : n + 1, :] = small_rows[r][i : i + 1, g * 128 : g * 128 + 128]
        begin, steps, small_finish = small_sum(
            bit_count, depth, small_src, small_buf, small_work, small_send, small_recv
        )
        begin()
        while work.todo or steps:
            work.pump(6)
            if steps:
                steps.pop(0)()
        for n, (r, i, g) in enumerate(places):
            small_out[r][i : i + 1, g * 128 : g * 128 + 128] = small_work[bit_count + 1, n : n + 1, :]
        small_finish()
        for item in items:
            if item.weight not in (gate_w, down_w):
                work.finish(item)

        @pl.when(place > 0)
        def _():
            edge.wait_send()
            for p in range(pieces):
                cols = pl.ds(p * width, width)
                to(-1, b["state_send"].at[:, cols], b["state_recv"].at[:, cols], p).wait_send()

        for i in range(depth - 1):

            @pl.when(place > i)
            def _(i=i):
                part = pl.ds(i * count, count)
                to(-1, b["kv_grad"].at[part], b["kv_recv"].at[part], pieces + i).wait_send()

        save.wait()

    two = (2,) * bit_count
    hbm = pl.BlockSpec(memory_space=pl.ANY)
    scratch = [pltpu.VMEM(*results[n]) for n in names]
    scratch += [pltpu.VMEM(x.shape, x.dtype) for x in loaded.values()]
    scratch += [pltpu.VMEM(*a) for a in local.values()]
    mine = shapes[:made_here]
    scratch += [pltpu.VMEM(*rows_out[0])] + [pltpu.VMEM(*a) for a in rows_out[2:]]
    stacks = [[pltpu.VMEM((*two[: bit_count - 1 - s], *shape), bf16) for shape in mine] for s in range(bit_count)]
    flat = [pltpu.VMEM(shape, bf16) for shape in mine]
    rooms = [pltpu.VMEM(own_shape(bit_count, shape, n), bf16) for shape, n in zip(mine, parts)]
    scratch += [*rooms, *[x for stage in stacks for x in stage], *flat, *flat]
    scratch += [pltpu.VMEM(small_shape, f32)] + [pltpu.VMEM((bit_count + 2, *small_shape), f32)] * 2
    slots = pieces + depth + 1
    dma = pltpu.SemaphoreType.DMA
    scratch += [
        dma((len(items), bit_count + 3)), dma((len(items), bit_count + 3)), dma((len(items),)), dma((len(loads),)),
        dma((1,)), dma((2,)), dma((slots,)), dma((slots,)), dma((bit_count + 3,)), dma((bit_count + 3,)), dma((2, 4)),
        dma((2, fsdp)), dma((4,)), pltpu.SemaphoreType.REGULAR,
    ]
    outs = [((count, model), f32), *rows_out, *[(shape, bf16) for shape in shapes]]
    outs += [((*two, *shape), bf16) for shape in shapes[made_here:]]
    made = pl.pallas_call(
        kernel,
        out_shape=[jax.ShapeDtypeStruct(*a) for a in outs],
        in_specs=[vmem] * len(rows_in) + [hbm] * (len(loads) + len(later_in) + made_here),
        out_specs=[hbm] + [vmem] * len(rows_out) + [hbm] * (2 * weights - made_here),
        scratch_shapes=scratch,
        compiler_params=pltpu.CompilerParams(
            collective_id=2, has_side_effects=True, vmem_limit_bytes=63 * 2**20
        ),
    )(
        *rows_in, *loaded.values(), *later_in,
        *[g.reshape(*two, *shape) for g, shape in zip(gradients, shapes)],
    )
    n = 1 + len(rows_out)
    return made[0], made[1:n], made[n : n + weights]


def shifted(array, axis, by):
    devices = lax.axis_size(axis)
    pairs = [(i, i + by) for i in range(devices) if 0 <= i + by < devices]
    return lax.ppermute(array, axis, pairs)


def contract(left, right):
    return dot_tn(left, right)


def rms_scale(values, gain_vec):
    return (
        values * lax.rsqrt(jnp.mean(values * values, axis=-1, keepdims=True) + epsilon) * gain_vec
    )


def reduced(gradient):
    return low(gradient)


def padded(vector):
    return jnp.pad(vector, (0, 128 - vector.shape[0]))[None]


def on_device(
    tokens,
    cotangent,
    segment_ids,
    norm_gain,
    ffn_gain,
    mixer_gain,
    conv_weight,
    conv_bias,
    decay_log,
    step_bias,
    skip_gain,
    in_proj,
    mixer_out,
    qkv_proj,
    attn_proj,
    gate_up,
    down_proj,
):
    place, devices = lax.axis_index("seq"), lax.axis_size("seq")
    count = tokens.shape[1]
    position = place * count + jnp.arange(count, dtype=jnp.int32)
    half = HEAD_WIDTH // 2
    lane = jnp.arange(128, dtype=jnp.int32)
    exponent = (lane % half).astype(f32) * (2.0 / HEAD_WIDTH)
    frequencies = jnp.power(rope_base, -exponent)
    angles = position.astype(f32)[:, None] * frequencies[None, :]
    cosine = jnp.cos(angles)
    signed = jnp.sin(angles) * jnp.where(lane % HEAD_WIDTH < half, -1.0, 1.0)[None]
    seg_row = segment_ids.astype(f32)
    bias_row, rate_row = padded(step_bias), padded(decay_log)
    skip_row = jnp.repeat(skip_gain, MP)[None]
    v, (in_full, qkv_full, mix_full, attn_full, gate_full, down_full) = forward_part(
        tokens[0], seg_row, norm_gain[None], cosine, signed, bias_row, rate_row, conv_weight, conv_bias[None],
        mixer_gain[None], skip_row, (in_proj, qkv_proj, mixer_out, attn_proj, gate_up, down_proj),
        (4, 2, 2, 2, 4, 4),
    )
    attended, gated = v["attended"], v["gated"]
    token_rows = tokens[0].astype(f32)
    hidden = token_rows + (dot_nn(attended, attn_full) + dot_nn(gated, mix_full))
    ffn_in32, ffn_pull = jax.vjp(rms_scale, hidden, ffn_gain)
    ffn_in = lax.optimization_barrier(low(ffn_in32))
    gates = lax.optimization_barrier(dot_nn(ffn_in, gate_full))

    gate, up = gates[:, :FF], gates[:, FF:]
    sig = jax.nn.sigmoid(gate)
    inner = lax.optimization_barrier(low(gate * sig * up))
    result = hidden + dot_nn(inner, down_full)
    back_rows = cotangent[0]
    down_piece = reduced(contract(inner, back_rows))
    act_grad = lax.optimization_barrier(dot_nt(back_rows, down_full))
    gates_grad = lax.optimization_barrier(
        jnp.concatenate(
            [low(act_grad * up * (sig * (1.0 + gate * (1.0 - sig)))), low(act_grad * (gate * sig))], axis=1
        )
    )
    gate_piece = reduced(contract(ffn_in, gates_grad))
    hidden_extra, ffn_gain_grad = ffn_pull(dot_nt(gates_grad, gate_full))
    hidden_grad = back_rows.astype(f32) + hidden_extra
    branch = lax.optimization_barrier(low(hidden_grad))
    attn_piece = reduced(contract(attended, branch))
    attended_grad = low(dot_nt(branch, attn_full))
    mixer_piece = reduced(contract(gated, branch))
    gated_grad = low(dot_nt(branch, mix_full))

    input_grad, small_rows, sums = backward_part(
        v, gated_grad, attended_grad, cosine, signed, seg_row, bias_row, rate_row, conv_weight, conv_bias[None],
        mixer_gain[None], skip_row, norm_gain[None], ffn_gain_grad[None], tokens[0], hidden_grad, in_full, qkv_full,
        (gate_piece, down_piece, mixer_piece, attn_piece),
    )
    gate_sum, down_sum, mixer_sum, attn_sum, z_sum, qkv_sum, conv_sum, raw_sum = sums
    in_sum = jnp.concatenate([z_sum, conv_sum, raw_sum[:, :MH]], axis=1)
    shards = [x.astype(f32) for x in (in_sum, mixer_sum, qkv_sum, attn_sum, gate_sum, down_sum)]
    small = [row if row.shape[0] == KC else row[0] for row in small_rows]
    small = [row[:MH] if row.shape[0] == 128 else row for row in small]
    return (low(result)[None], input_grad[None], *small, *shards)


def solution(mesh):
    rows, whole, split_rows = P("fsdp", "seq", None), P(), P("fsdp", None)
    return jax.shard_map(
        on_device,
        mesh=mesh,
        in_specs=(rows, rows, P("fsdp", "seq"), *[whole] * 8, *[split_rows] * 6),
        out_specs=(rows, rows, *[whole] * 8, *[split_rows] * 6),
        check_vma=False,
    )
```

```python
import jax
import jax.numpy as jnp
from jax import lax
from jax.experimental import pallas as pl
from jax.experimental.pallas import tpu as pltpu
from jax.sharding import PartitionSpec as P

FF = 2048
QUERY_HEADS = 8
KEY_VALUE_HEADS = 2
HEAD_WIDTH = 64
MH = 24
MP = 64
NS = 128
KC = 4
SUB = 128
DI = 1536
CW = 1792
EDGE = 8

epsilon = 1e-05
rope_base = 100000000000.0
highest = lax.Precision.HIGHEST
f32 = jnp.float32
bf16 = jnp.bfloat16


def dot_nn(left, right):
    return jnp.dot(left, right, preferred_element_type=jnp.float32)


def dot_nt(left, right):
    return lax.dot_general(
        left, right, (((1,), (1,)), ((), ())), preferred_element_type=jnp.float32
    )


def dot_tn(left, right):
    return lax.dot_general(
        left, right, (((0,), (0,)), ((), ())), preferred_element_type=jnp.float32
    )


def exact(left, right):
    return jnp.dot(left, right, precision=highest, preferred_element_type=jnp.float32)


def low(values):
    return values.astype(jnp.bfloat16)


def split(values):
    top = low(values)
    return top, low(values - top.astype(jnp.float32))


def iota(shape, axis):
    return lax.broadcasted_iota(jnp.int32, shape, axis)


def spreader():
    return low(jnp.where(iota((128, DI), 1) // MP == iota((128, DI), 0), 1.0, 0.0))


def widen(values, spread):
    top, rest = split(values)
    return dot_nn(top, spread) + dot_nn(rest, spread)


def widen_row(row, spread):
    return widen(jnp.broadcast_to(row, (8, 128)), spread)[0:1]


def head_sums(values, spread):
    top, rest = split(values)
    return dot_nt(top, spread) + dot_nt(rest, spread)


def softplus(values):
    return jnp.maximum(values, 0.0) + jnp.log1p(jnp.exp(-jnp.abs(values)))


def sigmoid(values):
    return 1.0 / (1.0 + jnp.exp(-values))


def lane_halves(rows):
    lane = iota((rows, 128), 1)
    return lane < MP


def rounded_to(values):
    return low(values).astype(jnp.float32)


def front_conv(conv_ref, seg_ref, weight_ref, cbias_ref, act_ref):
    chunks = act_ref.shape[0] // SUB

    def tile(j, carry):
        col = pl.ds(pl.multiple_of(j * 128, 128), 128)
        for c in range(chunks):
            r0 = c * SUB
            seg = seg_ref[pl.ds(r0 + 8, SUB), :]
            total = jnp.broadcast_to(cbias_ref[0:1, col], (SUB, 128))
            for k in range(KC):
                x = rounded_to(conv_ref[pl.ds(r0 + 9 - KC + k, SUB), col])
                if k < KC - 1:
                    x = jnp.where(seg_ref[pl.ds(r0 + 9 - KC + k, SUB), :] == seg, x, 0.0)
                total = total + weight_ref[k : k + 1, col] * x
            act_ref[pl.ds(r0, SUB), col] = low(total * sigmoid(total))
        return carry

    lax.fori_loop(0, CW // 128, tile, 0)


def front_state(seg_ref, raw_ref, bias_ref, rate_ref, act_ref, dt_ref, cum_ref, end_ref, pass_ref):
    chunks = raw_ref.shape[0] // SUB
    spread = spreader()
    lower = jnp.where(iota((SUB, SUB), 0) >= iota((SUB, SUB), 1), 1.0, 0.0)
    end_ref[...] = jnp.zeros_like(end_ref)
    gain = jnp.ones((1, 128), jnp.float32)
    for c in range(chunks):
        rows = pl.ds(c * SUB, SUB)
        dt = softplus(raw_ref[rows, :] + bias_ref[...])
        cum = exact(lower, -dt * jnp.exp(rate_ref[...]))
        dt_ref[rows, :] = dt
        cum_ref[rows, :] = cum
        seg = seg_ref[pl.ds(c * SUB + 8, SUB), :]
        before = seg_ref[pl.ds(c * SUB + 7, 1), :]
        last = seg[SUB - 1 :, :]
        end = cum[SUB - 1 :, :]
        weight = jnp.where(seg == last, jnp.exp(end - cum), 0.0) * dt
        passing = jnp.where(last == before, jnp.exp(end), 0.0)
        gain = gain * passing
        values = act_ref[rows, 0:DI].astype(jnp.float32)
        fresh = dot_tn(act_ref[rows, DI : DI + NS], low(widen(weight, spread) * values))
        end_ref[...] = widen_row(passing, spread) * end_ref[...] + fresh
    pass_ref[...] = widen_row(gain, spread)


def mid_kernel(act_ref, dt_ref, cum_ref, seg_ref, segrow_ref, state_ref, z_ref, gain_ref, skip_ref,
               y_ref, gated_ref, kept_ref, carry_ref, first, until):
    spread = spreader()
    if first == 0:
        carry_ref[...] = state_ref[...]
    half = lane_halves(SUB)

    def chunk(c, nothing):
        r0 = pl.multiple_of(c * SUB, SUB)
        rows = pl.ds(r0, SUB)
        dt, cum = dt_ref[rows, :], cum_ref[rows, :]
        cum_t = cum.T
        seg = seg_ref[pl.ds(pl.multiple_of(r0 + 8, 8), SUB), :]
        before = seg_ref[pl.ds(pl.multiple_of(r0, 8), 8), :][7:8]
        last, end = seg[SUB - 1 :, :], cum[SUB - 1 :, :]
        keys, reads = act_ref[rows, DI : DI + NS], act_ref[rows, DI + NS : CW]
        affinity = dot_nt(reads, keys)
        allowed = (iota((SUB, SUB), 0) >= iota((SUB, SUB), 1)) & (seg == segrow_ref[0:1, rows])
        state = low(carry_ref[...])
        kept_ref[pl.ds(c, 1)] = state[None]
        entry = widen(jnp.where(seg == before, jnp.exp(cum), 0.0), spread)
        y_ref[rows, :] = dot_nn(reads, state) * entry
        values = act_ref[rows, 0:DI].astype(jnp.float32)
        scaled = values * widen(dt, spread)
        weight = jnp.where(seg == last, jnp.exp(end - cum), 0.0)
        passing = jnp.where(last == before, jnp.exp(end), 0.0)
        fresh = dot_tn(keys, low(widen(weight, spread) * scaled))
        carry_ref[...] = widen_row(passing, spread) * carry_ref[...] + fresh
        for pair in range(MH // 2):
            cols = slice(pair * 128, pair * 128 + 128)
            parts = []
            for h in (2 * pair, 2 * pair + 1):
                gap = jnp.where(allowed, cum[:, h : h + 1] - cum_t[h : h + 1, :], -1e30)
                parts.append(low(jnp.exp(gap) * affinity))
            v = scaled[:, cols]
            right = jnp.concatenate([low(jnp.where(half, v, 0.0)), low(jnp.where(half, 0.0, v))], 0)
            y_ref[rows, cols] = y_ref[rows, cols] + dot_nn(jnp.concatenate(parts, 1), right)
        z = z_ref[rows, :]
        g = (y_ref[rows, :] + skip_ref[...] * values) * (z * sigmoid(z))
        scale = lax.rsqrt(jnp.mean(g * g, axis=1, keepdims=True) + epsilon)
        gated_ref[rows, :] = low(g * scale * gain_ref[...])
        return nothing

    lax.fori_loop(first, until, chunk, 0)


def gate_back_kernel(grad_ref, y_ref, act_ref, z_ref, dt_ref, cum_ref, seg_ref, gain_ref, skip_ref,
                     ygrad_ref, zgrad_ref, gain_grad_ref, state_grad_ref, first, until):
    chunks = act_ref.shape[0] // SUB
    spread = spreader()
    if first == 0:
        gain_grad_ref[...] = jnp.zeros_like(gain_grad_ref)
        state_grad_ref[...] = jnp.zeros_like(state_grad_ref)

    def chunk(i, nothing):
        c = chunks - 1 - i
        r0 = pl.multiple_of(c * SUB, SUB)
        rows = pl.ds(r0, SUB)
        values = act_ref[rows, 0:DI].astype(jnp.float32)
        z = z_ref[rows, :]
        sig = sigmoid(z)
        silu = z * sig
        u = y_ref[rows, :] + skip_ref[...] * values
        g = u * silu
        grad = grad_ref[rows, :].astype(jnp.float32)
        scale = lax.rsqrt(jnp.mean(g * g, axis=1, keepdims=True) + epsilon)
        unit = g * scale
        gain_grad_ref[...] += jnp.sum(grad * unit, axis=0, keepdims=True)
        h = grad * gain_ref[...]
        dg = scale * (h - unit * jnp.mean(h * unit, axis=1, keepdims=True))
        dy = dg * silu
        ygrad_ref[rows, :] = dy
        zgrad_ref[rows, :] = low(dg * u * (sig * (1.0 + z * (1.0 - sig))))
        cum = cum_ref[rows, :]
        seg = seg_ref[pl.ds(pl.multiple_of(r0 + 8, 8), SUB), :]
        before = seg_ref[pl.ds(pl.multiple_of(r0, 8), 8), :][7:8]
        last, end = seg[SUB - 1 :, :], cum[SUB - 1 :, :]
        entry = widen(jnp.where(seg == before, jnp.exp(cum), 0.0), spread)
        passing = jnp.where(last == before, jnp.exp(end), 0.0)
        fresh = dot_tn(act_ref[rows, DI + NS : CW], low(entry * dy))
        state_grad_ref[...] = widen_row(passing, spread) * state_grad_ref[...] + fresh
        return nothing

    lax.fori_loop(first, until, chunk, 0)


def back_states(act_ref, dt_ref, cum_ref, seg_ref, segrow_ref, raw_ref, bias_ref, rate_ref, kept_ref,
                y_ref, ygrad_ref, skip_ref, raw_grad_ref, rate_grad_ref, bias_grad_ref, skip_grad_ref,
                value_grad_ref, pair_grad_ref, carry_ref, first, until):
    chunks = act_ref.shape[0] // SUB
    spread = spreader()
    half = lane_halves(SUB)
    upper = jnp.where(iota((SUB, SUB), 1) >= iota((SUB, SUB), 0), 1.0, 0.0)
    rate = jnp.exp(rate_ref[...])
    if first == 0:
        rate_grad_ref[...] = jnp.zeros_like(rate_grad_ref)
        bias_grad_ref[...] = jnp.zeros_like(bias_grad_ref)
        skip_grad_ref[...] = jnp.zeros_like(skip_grad_ref)

    def chunk(i, nothing):
        c = chunks - 1 - i
        r0 = pl.multiple_of(c * SUB, SUB)
        rows = pl.ds(r0, SUB)
        dt, cum = dt_ref[rows, :], cum_ref[rows, :]
        cum_t = cum.T
        seg = seg_ref[pl.ds(pl.multiple_of(r0 + 8, 8), SUB), :]
        before = seg_ref[pl.ds(pl.multiple_of(r0, 8), 8), :][7:8]
        last, end = seg[SUB - 1 :, :], cum[SUB - 1 :, :]
        keys, reads = act_ref[rows, DI : DI + NS], act_ref[rows, DI + NS : CW]
        affinity = dot_nt(keys, reads)
        allowed = (iota((SUB, SUB), 1) >= iota((SUB, SUB), 0)) & (seg == segrow_ref[0:1, rows])
        values = act_ref[rows, 0:DI].astype(jnp.float32)
        wide_dt = widen(dt, spread)
        scaled = values * wide_dt
        scaled_low = low(scaled)
        dy = ygrad_ref[rows, :]
        dy_low = low(dy)
        state, carry = kept_ref[pl.ds(c, 1)][0], carry_ref[...]
        carry_low = low(carry)
        wide_weight = widen(jnp.where(seg == last, jnp.exp(end - cum), 0.0), spread)
        wide_entry = widen(jnp.where(seg == before, jnp.exp(cum), 0.0), spread)
        wide_pass = widen_row(jnp.where(last == before, jnp.exp(end), 0.0), spread)
        from_state = dot_nn(keys, carry_low) * wide_weight
        mixed_grad = jnp.zeros((SUB, SUB), jnp.float32)
        for pair in range(MH // 2):
            cols = slice(pair * 128, pair * 128 + 128)
            v, d = scaled[:, cols], dy[:, cols]
            left = jnp.concatenate([low(jnp.where(half, v, 0.0)), low(jnp.where(half, 0.0, v))], 0)
            right = jnp.concatenate([low(jnp.where(half, d, 0.0)), low(jnp.where(half, 0.0, d))], 0)
            weight_grad = dot_nt(left, dy_low[:, cols])
            parts = []
            for n, h in enumerate((2 * pair, 2 * pair + 1)):
                gap = jnp.where(allowed, cum_t[h : h + 1, :] - cum[:, h : h + 1], -1e30)
                decay = jnp.exp(gap)
                parts.append(low(decay * affinity))
                mixed_grad = mixed_grad + decay * weight_grad[n * SUB : (n + 1) * SUB]
            value_grad_ref[rows, cols] = dot_nn(jnp.concatenate(parts, 1), right)
        x = value_grad_ref[rows, 0:DI] + from_state
        value_grad_ref[rows, 0:DI] = wide_dt * x + skip_ref[...] * dy
        mixed_low = low(mixed_grad)
        pair_grad_ref[rows, 0:NS] = dot_nn(mixed_low, reads) + dot_nt(
            low(wide_weight * scaled), carry_low
        )
        entered = low(wide_entry * dy)
        pair_grad_ref[rows, NS:] = dot_tn(mixed_low, keys) + dot_nt(entered, state)
        scaled_exact = scaled_low.astype(jnp.float32)
        direct = head_sums(values * x, spread)
        given = head_sums(scaled_exact * x, spread)
        taken = head_sums(dy_low.astype(jnp.float32) * y_ref[rows, :], spread)
        tail = jnp.sum(scaled_exact * from_state, axis=0, keepdims=True) + jnp.sum(
            wide_pass * carry * state.astype(jnp.float32), axis=0, keepdims=True
        )
        tail = head_sums(jnp.broadcast_to(tail, (8, DI)), spread)[0:1]
        decay_grad = exact(upper, taken - given) + tail
        rate_grad_ref[...] += jnp.sum(decay_grad * (-dt * rate), axis=0, keepdims=True)
        dt_grad = direct - decay_grad * rate
        raw_grad = dt_grad * sigmoid(raw_ref[rows, :] + bias_ref[...])
        raw_grad_ref[rows, :] = low(jnp.where(iota((SUB, 128), 1) < MH, raw_grad, 0.0))
        bias_grad_ref[...] += jnp.sum(raw_grad, axis=0, keepdims=True)
        skip_sum = jnp.sum(dy * values, axis=0, keepdims=True)
        skip_grad_ref[...] += head_sums(jnp.broadcast_to(skip_sum, (8, DI)), spread)[0:1]
        carry_ref[...] = wide_pass * carry + dot_tn(reads, entered)
        return nothing

    lax.fori_loop(first, until, chunk, 0)


def back_conv(conv_hbm, conv_ref, conv_sem, seg_ref, weight_ref, cbias_ref, act_grad_ref, shift,
              conv_grad_ref, edge_ref, tail_ref, weight_grad_ref, cbias_grad_ref, pre_ref, first, until):
    rows_total = act_grad_ref.shape[0]
    chunks = rows_total // SUB
    pre_ref[0:8, :] = jnp.zeros((8, 128), jnp.float32)
    pre_ref[rows_total + 8 : rows_total + 16, :] = jnp.zeros((8, 128), jnp.float32)

    def fetch(j, slot):
        return pltpu.make_async_copy(
            conv_hbm.at[:, pl.ds(pl.multiple_of(j * 128, 128), 128)], conv_ref.at[slot], conv_sem.at[slot]
        )

    fetch(first, first % 2).start()

    def tile(j, carry):
        slot = j % 2

        @pl.when(j + 1 < until)
        def _():
            fetch(j + 1, 1 - slot).start()

        fetch(j, slot).wait()
        col = pl.ds(pl.multiple_of(j * 128, 128), 128)
        sums = [jnp.zeros((1, 128), jnp.float32) for _ in range(KC + 1)]
        for c in range(chunks):
            r0 = c * SUB
            seg = seg_ref[pl.ds(r0 + 8, SUB), :]
            total = jnp.broadcast_to(cbias_ref[0:1, col], (SUB, 128))
            taps = []
            for k in range(KC):
                x = rounded_to(conv_ref[slot, pl.ds(r0 + 9 - KC + k, SUB), :])
                if k < KC - 1:
                    x = jnp.where(seg_ref[pl.ds(r0 + 9 - KC + k, SUB), :] == seg, x, 0.0)
                taps.append(x)
                total = total + weight_ref[k : k + 1, col] * x
            sig = sigmoid(total)
            act_col = pl.ds(pl.multiple_of((j - shift) * 128, 128), 128)
            pre = act_grad_ref[pl.ds(r0, SUB), act_col] * (sig * (1.0 + total * (1.0 - sig)))
            pre_ref[pl.ds(r0 + 8, SUB), :] = pre
            for k in range(KC):
                sums[k] = sums[k] + jnp.sum(pre * taps[k], axis=0, keepdims=True)
            sums[KC] = sums[KC] + jnp.sum(pre, axis=0, keepdims=True)
        for k in range(KC):
            weight_grad_ref[k : k + 1, col] = sums[k]
        cbias_grad_ref[0:1, col] = sums[KC]

        def spread_back(r0, size):
            seg = seg_ref[pl.ds(r0, size), :]
            total = jnp.zeros((size, 128), jnp.float32)
            for back in range(KC):
                x = pre_ref[pl.ds(r0 + back, size), :]
                if back:
                    x = jnp.where(seg_ref[pl.ds(r0 + back, size), :] == seg, x, 0.0)
                total = total + weight_ref[KC - 1 - back : KC - back, col] * x
            return total

        edge_ref[:, col] = spread_back(0, 8)
        for c in range(chunks):
            total = spread_back(c * SUB + 8, SUB)
            conv_grad_ref[pl.ds(c * SUB, SUB), act_col] = low(total)
        tail_ref[:, col] = total[SUB - 16 :]
        return carry

    lax.fori_loop(first, until, tile, 0)


def partner(values):
    lane = iota(values.shape, 1)
    half = HEAD_WIDTH // 2
    return jnp.where(
        lane % HEAD_WIDTH < half, pltpu.roll(values, 128 - half, 1), pltpu.roll(values, half, 1)
    )


def rotate_kernel(qkv_ref, cos_ref, sin_ref, query_ref, kv_ref):
    cos, sin = cos_ref[...], sin_ref[...]
    for g in range(5):
        x = qkv_ref[:, g * 128 : g * 128 + 128]
        x = low(x * cos + partner(x) * sin)
        if g < 4:
            query_ref[:, g * 128 : g * 128 + 128] = x * jnp.bfloat16(HEAD_WIDTH**-0.5)
        else:
            kv_ref[:, 0:128] = x
    kv_ref[:, 128:256] = low(qkv_ref[:, 640:768])


def lane_variants(block, out_ref):
    other = pltpu.roll(block, 64, 1)
    half = iota(block.shape, 1) < HEAD_WIDTH
    out_ref[0] = low(jnp.where(half, block, 0.0))
    out_ref[1] = low(jnp.where(half, 0.0, other))
    out_ref[2] = low(jnp.where(half, other, 0.0))
    out_ref[3] = low(jnp.where(half, 0.0, block))


def seg_column(row):
    return jnp.broadcast_to(row, (128, row.shape[1])).T


def attend_bias(b, own, rows, segall_ref, segrow_ref, bias_ref):
    seg = seg_column(segall_ref[pl.ds(pl.multiple_of(b * 8, 8), 8), :][0:1])
    seg = jnp.concatenate([seg] * (rows // 128), 1)
    causal = (iota((rows, rows), 0) - iota((rows, rows), 1)) <= jnp.where(b < own, rows, 0)
    bias_ref[...] = jnp.where(causal & (seg == segrow_ref[...]), 0.0, -1e30)


def attend_start(top_ref, sum_ref, out_t_ref):
    top_ref[...] = jnp.full_like(top_ref, -1e30)
    sum_ref[...] = jnp.zeros_like(sum_ref)
    out_t_ref[...] = jnp.zeros_like(out_t_ref)


def attend_block(b, own, query_ref, kv_ref, segall_ref, segrow_ref, out_t_ref, bias_ref, keys_ref,
                 values_t_ref, top_ref, sum_ref):
    rows = query_ref.shape[0]
    at = pl.ds(pl.multiple_of(b * rows, rows), rows)
    attend_bias(b, own, rows, segall_ref, segrow_ref, bias_ref)
    lane_variants(kv_ref[at, 0:128].astype(jnp.float32), keys_ref)
    values_t_ref[...] = low(kv_ref[at, 128:256].astype(jnp.float32).T)

    def pair(g, nothing):
        kv = g // 2
        query = query_ref[:, pl.ds(pl.multiple_of(g * 128, 128), 128)]
        for side in range(2):
            h = g * 2 + side
            row = pl.ds(pl.multiple_of(h * 8, 8), 8)
            scores = dot_nt(keys_ref[kv * 2 + side], query)
            scores = scores + bias_ref[...]
            old = top_ref[row, :][0:1]
            top = jnp.maximum(old, jnp.max(scores, axis=0, keepdims=True))
            p = jnp.exp(scores - top)
            fade = jnp.exp(old - top)
            total = sum_ref[row, :][0:1] * fade + jnp.sum(p, 0, keepdims=True)
            top_ref[row, :] = jnp.broadcast_to(top, (8, rows))
            sum_ref[row, :] = jnp.broadcast_to(total, (8, rows))
            at_h = pl.ds(pl.multiple_of(h * 64, 64), 64)
            values_t = values_t_ref[pl.ds(pl.multiple_of(kv * 64, 64), 64), :]
            out_t_ref[at_h, :] = out_t_ref[at_h, :] * fade + dot_nn(values_t, low(p))
        return nothing

    lax.fori_loop(0, QUERY_HEADS // 2, pair, 0)


def attend_finish(out_ref, out_t_ref, total_ref, top_ref, sum_ref):
    for h in range(QUERY_HEADS):
        at_h = slice(h * 64, h * 64 + 64)
        row = slice(h * 8, h * 8 + 8)
        total_ref[row, :] = top_ref[row, :] + jnp.log(sum_ref[row, :])
        out_t_ref[at_h, :] = out_t_ref[at_h, :] / sum_ref[h * 8 : h * 8 + 1, :]
    out_ref[...] = low(out_t_ref[...].T)


def attend_back_start(query_ref, grad_ref, out_t_ref, spread_ref):
    rows = query_ref.shape[0]
    grad_t = grad_ref[...].astype(jnp.float32).T
    product = grad_t * out_t_ref[...]
    for h in range(QUERY_HEADS):
        total = jnp.sum(product[h * 64 : h * 64 + 64, :], 0, keepdims=True)
        spread_ref[h * 8 : h * 8 + 8, :] = jnp.broadcast_to(total, (8, rows))
    out_t_ref[...] = jnp.zeros_like(out_t_ref)


def attend_back_block(b, own, query_ref, kv_ref, segall_ref, segrow_ref, grad_ref, total_ref, kv_grad_ref,
                      bias_ref, keys_ref, values_ref, keys_t_ref, dkeys_ref, dvalues_ref, spread_ref, dq_ref,
                      first, until):
    rows = query_ref.shape[0]
    at = pl.ds(pl.multiple_of(b * rows, rows), rows)
    if first == 0:
        attend_bias(b, own, rows, segall_ref, segrow_ref, bias_ref)
        keys = kv_ref[at, 0:128].astype(jnp.float32)
        lane_variants(keys, keys_ref)
        lane_variants(kv_ref[at, 128:256].astype(jnp.float32), values_ref)
        keys_t_ref[...] = low(keys.T)
        dkeys_ref[...] = jnp.zeros_like(dkeys_ref)
        dvalues_ref[...] = jnp.zeros_like(dvalues_ref)

    lower_half = iota((rows, 128), 1) < HEAD_WIDTH

    def side_of(values, side):
        values = values.astype(jnp.float32)
        return low(jnp.where(lower_half, 0.0, values) if side else jnp.where(lower_half, values, 0.0))

    def pair(g, nothing):
        kv = g // 2
        lanes = pl.ds(pl.multiple_of(g * 128, 128), 128)
        for side in range(2):
            h = g * 2 + side
            row = pl.ds(pl.multiple_of(h * 8, 8), 8)
            scores = dot_nt(keys_ref[kv * 2 + side], query_ref[:, lanes]) + bias_ref[...]
            p = jnp.exp(scores - total_ref[row, :][0:1])
            dp = dot_nt(values_ref[kv * 2 + side], grad_ref[:, lanes])
            ds = low(p * (dp - spread_ref[row, :][0:1]))
            dkeys_ref[kv] = dkeys_ref[kv] + dot_nn(ds, side_of(query_ref[:, lanes], side))
            dvalues_ref[kv] = dvalues_ref[kv] + dot_nn(low(p), side_of(grad_ref[:, lanes], side))
            at_h = pl.ds(pl.multiple_of(h * 64, 64), 64)
            keys_t = keys_t_ref[pl.ds(pl.multiple_of(kv * 64, 64), 64), :]
            dq_ref[at_h, :] = dq_ref[at_h, :] + dot_nn(keys_t, ds)
        return nothing

    lax.fori_loop(first, until, pair, 0)
    if until < QUERY_HEADS // 2:
        return
    half = lower_half
    for src, lanes in ((dkeys_ref, slice(0, 128)), (dvalues_ref, slice(128, 256))):
        first, second = src[0], src[1]
        kv_grad_ref[at, lanes] = low(
            jnp.where(half, first + pltpu.roll(first, 64, 1), second + pltpu.roll(second, 64, 1))
        )


def attend_back_finish(dq_ref, cos_ref, sin_ref, qkv_grad_ref):
    dq = dq_ref[...].T * (HEAD_WIDTH**-0.5)
    cos, sin = cos_ref[...], sin_ref[...]
    for g in range(4):
        x = dq[:, g * 128 : g * 128 + 128]
        qkv_grad_ref[:, g * 128 : g * 128 + 128] = low(x * cos + partner(x * sin))


vmem = pl.BlockSpec(memory_space=pltpu.VMEM)
smem = pl.BlockSpec(memory_space=pltpu.SMEM)


def call(kernel, outs, args, scratch=(), first=vmem, flops=10**9):
    return pl.pallas_call(
        kernel,
        out_shape=[jax.ShapeDtypeStruct(shape, kind) for shape, kind in outs],
        in_specs=[first] + [vmem] * (len(args) - 1),
        out_specs=[vmem] * len(outs),
        scratch_shapes=[pltpu.VMEM(shape, kind) for shape, kind in scratch],
        compiler_params=pltpu.CompilerParams(vmem_limit_bytes=56 * 2**20),
        cost_estimate=pl.CostEstimate(flops=flops, bytes_accessed=10**7, transcendentals=10**6),
    )(*args)


MESH = pl.DeviceIdType.MESH


def position_bits(count):
    index = lax.axis_index("fsdp")
    return [(index // (1 << b)) % 2 for b in reversed(range(count))]


def across(bits, axis):
    count = len(bits)
    index = lax.axis_index("fsdp")
    step = 1 << (count - 1 - axis)
    return (index + step * (1 - 2 * bits[axis]), lax.axis_index("seq"))


def along(by):
    return (lax.axis_index("fsdp"), lax.axis_index("seq") + by)


class Item:
    def __init__(self, number, weight, start, size, order):
        self.number, self.weight, self.start, self.size, self.order = number, weight, start, size, order


def fit(shapes, wanted):
    return [max(d for d in range(1, n + 1) if rows // 16 % d == 0) for (rows, _), n in zip(shapes, wanted)]


def plan_items(shapes, parts, bit_count):
    items = []
    for w, ((rows, _), count) in enumerate(zip(shapes, parts)):
        for p in range(count):
            turn = p % max(bit_count - 1, 1)
            ici = list(range(bit_count - 1))
            order = [bit_count - 1] + ici[turn:] + ici[:turn]
            items.append(Item(len(items), w, p * (rows // count), rows // count, order))
            items[-1].slots = max(1, count // 2)
            items[-1].part = p
    return items


def own_shape(bit_count, shape, parts):
    return (*(2,) * (bit_count - 1), shape[0] // parts * max(1, parts // 2), shape[1])


class Reducer:
    def __init__(self, bit_count, depth, items, whole, own, landed, zin, zmid, out, send, recv, own_sem):
        self.bit_count, self.depth, self.items = bit_count, depth, items
        self.whole, self.own, self.landed = whole, own, landed
        self.zin, self.zmid, self.out = zin, zmid, out
        self.send, self.recv, self.own_sem = send, recv, own_sem
        self.bits = position_bits(bit_count)
        self.place = lax.axis_index("seq")

    def rows(self, item):
        return pl.ds(item.start, item.size)

    def left(self, item, stage):
        return sorted(item.order[stage:])

    def pick(self, item, stage, mine):
        axis = item.order[stage]
        at = self.left(item, stage).index(axis)
        bit = self.bits[axis] if mine else 1 - self.bits[axis]
        lead = [slice(None)] * (self.bit_count - stage)
        lead[at] = bit
        return (*lead, self.rows(item))

    def source(self, item, stage):
        if stage == 0:
            return self.whole[item.weight]
        return self.landed[stage - 1][item.weight]

    def copy(self, item, stage):
        lead = (slice(None),) * (self.bit_count - stage - 1)
        return pltpu.make_async_remote_copy(
            self.source(item, stage).at[self.pick(item, stage, False)],
            self.landed[stage][item.weight].at[(*lead, self.rows(item))],
            self.send.at[item.number, stage],
            self.recv.at[item.number, stage],
            device_id=across(self.bits, item.order[stage]),
            device_id_type=MESH,
        )

    def own_copy(self, item):
        lead = (slice(None),) * (self.bit_count - 1)
        return pltpu.make_async_copy(
            self.whole[item.weight].at[self.pick(item, 0, True)],
            self.own[item.weight].at[(*lead, pl.ds(self.own_start(item), item.size))],
            self.own_sem.at[item.number],
        )

    def own_start(self, item):
        return item.part % item.slots * item.size

    def begin(self, item):
        self.copy(item, 0).start()
        if item.part < item.slots:
            self.own_copy(item).start()

    def add(self, dst, dst_lead, other, other_lead, item, shift=0):
        width = self.out[item.weight].shape[1]
        group = max(g for g in (16, 32, 64) if item.size % g == 0 and (g == 16 or g * width <= 65536))

        def step(i, nothing):
            at = pl.ds(pl.multiple_of(item.start + i * group, 16), group)
            at_other = pl.ds(pl.multiple_of(item.start + shift + i * group, 16), group)
            dst[(*dst_lead, at)] = dst[(*dst_lead, at)] + other[(*other_lead, at_other)]
            return nothing

        lax.fori_loop(0, item.size // group, step, 0)

    def advance(self, item, stage):
        self.copy(item, stage).wait_recv()
        landed = self.landed[stage][item.weight]
        kept = self.bit_count - stage - 1
        places = [[(i >> (kept - 1 - b)) & 1 for b in range(kept)] for i in range(1 << kept)]
        if stage == 0:
            self.own_copy(item).wait()
            for lead in places:
                self.add(landed, lead, self.own[item.weight], lead, item, self.own_start(item) - item.start)
            for other in self.items:
                if other.weight == item.weight and other.part == item.part + item.slots:
                    self.own_copy(other).start()
        else:
            source = self.source(item, stage)
            axis = item.order[stage]
            at = self.left(item, stage).index(axis)
            for lead in places:
                from_lead = [*lead[:at], self.bits[axis], *lead[at:]]
                self.add(landed, lead, source, from_lead, item)
        if stage + 1 < self.bit_count:
            self.copy(item, stage + 1).start()

    def z_copy(self, item, kind, by):
        w, rows = item.weight, self.rows(item)
        last = self.landed[self.bit_count - 1][w]
        src, dst = {
            "in": (last, self.zin[w]),
            "mid": (last, self.zmid[w]),
            "out": (self.zmid[w], self.zmid[w]),
        }[kind]
        slot = self.bit_count + {"in": 0, "mid": 1, "out": 2}[kind]
        return pltpu.make_async_remote_copy(
            src.at[rows],
            dst.at[rows],
            self.send.at[item.number, slot],
            self.recv.at[item.number, slot],
            device_id=along(by),
            device_id_type=MESH,
        )

    def sides(self):
        half = self.depth // 2
        outermost = (self.place == 0) | (self.place == self.depth - 1)
        middle = (self.place == half - 1) | (self.place == half)
        inward = 1 - 2 * (self.place // half)
        return outermost, middle, inward

    def z_first(self, item):
        outermost, middle, inward = self.sides()

        @pl.when(outermost & jnp.logical_not(middle))
        def _():
            self.z_copy(item, "in", inward).start()

    def z_second(self, item):
        outermost, middle, inward = self.sides()

        @pl.when(jnp.logical_not(outermost))
        def _():
            self.z_copy(item, "in", -inward).wait_recv()
            self.add(self.landed[self.bit_count - 1][item.weight], (), self.zin[item.weight], (), item)

            @pl.when(jnp.logical_not(middle))
            def _():
                self.z_copy(item, "in", inward).start()

        @pl.when(middle)
        def _():
            self.z_copy(item, "mid", inward).start()

    def z_third(self, item):
        outermost, middle, inward = self.sides()

        @pl.when(middle)
        def _():
            self.z_copy(item, "mid", inward).wait_recv()
            self.add(self.zmid[item.weight], (), self.landed[self.bit_count - 1][item.weight], (), item)

            @pl.when(jnp.logical_not(outermost))
            def _():
                self.z_copy(item, "out", -inward).start()

    def z_fourth(self, item):
        outermost, middle, inward = self.sides()

        @pl.when(jnp.logical_not(middle))
        def _():
            self.z_copy(item, "out", inward).wait_recv()

            @pl.when(jnp.logical_not(outermost))
            def _():
                self.z_copy(item, "out", -inward).start()

        self.out_copy(item).start()

    def out_copy(self, item):
        rows = self.rows(item)
        return pltpu.make_async_copy(
            self.zmid[item.weight].at[rows], self.out[item.weight].at[rows], self.own_sem.at[item.number]
        )

    def pump(self, count):
        while count and self.todo and (self.todo[0][0] is None or self.todo[0][0] in self.have):
            self.todo.pop(0)[1]()
            count -= 1

    def finish(self, item):
        outermost, middle, inward = self.sides()
        self.out_copy(item).wait()
        for stage in range(self.bit_count):
            self.copy(item, stage).wait_send()

        @pl.when(jnp.logical_not(middle))
        def _():
            self.z_copy(item, "in", inward).wait_send()

        @pl.when(middle)
        def _():
            self.z_copy(item, "mid", inward).wait_send()

        @pl.when(jnp.logical_not(outermost))
        def _():
            self.z_copy(item, "out", -inward).wait_send()

    def actions(self, lag, z_lag, late=(), reused=(), ready_sem=None):
        last_use = max(
            [i + lag * (self.bit_count - 1) + 3 * z_lag for i, item in enumerate(self.items) if item.weight in reused],
            default=0,
        )
        first_late = min([i for i, item in enumerate(self.items) if item.weight in late], default=0)
        gap = max(0, last_use + 2 - first_late)
        steps = []
        for i, item in enumerate(self.items):
            if item.weight in late:
                if i == first_late:
                    steps.append((i + gap - 1, -2, item.weight, lambda: self.hand_over(reused, ready_sem)))
                i += gap
                steps.append((i - 1, -1, item.weight, lambda item=item: self.begin(item)))
            for stage in range(self.bit_count):
                steps.append((i + lag * stage, stage, None, lambda item=item, s=stage: self.advance(item, s)))
            t = i + lag * (self.bit_count - 1)
            for n, run in enumerate((self.z_first, self.z_second, self.z_third, self.z_fourth)):
                steps.append((t + n * z_lag, self.bit_count + n, None, lambda item=item, run=run: run(item)))
        self.todo = [step[2:] for step in sorted(steps, key=lambda s: s[:2])]
        self.have = set()

    def hand_over(self, weights, ready_sem):
        for item in self.items:
            if item.weight in weights:
                self.finish(item)
        meet(self.bits, self.place, self.depth, ready_sem)


def meet(bits, place, depth, semaphore):
    for axis in range(len(bits)):
        pl.semaphore_signal(semaphore, inc=1, device_id=across(bits, axis), device_id_type=MESH)

    @pl.when(place > 0)
    def _():
        pl.semaphore_signal(semaphore, inc=1, device_id=along(-1), device_id_type=MESH)

    @pl.when(place < depth - 1)
    def _():
        pl.semaphore_signal(semaphore, inc=1, device_id=along(1), device_id_type=MESH)

    ends = jnp.where(place == 0, 1, 0) + jnp.where(place == depth - 1, 1, 0)
    pl.semaphore_wait(semaphore, len(bits) + 2 - ends)


def enter(bit_count, depth):
    meet(position_bits(bit_count), lax.axis_index("seq"), depth, pltpu.get_barrier_semaphore())


def small_sum(bit_count, depth, src, buf, out, send, recv):
    bits = position_bits(bit_count)
    place = lax.axis_index("seq")
    half = depth // 2
    outermost = (place == 0) | (place == depth - 1)
    middle = (place == half - 1) | (place == half)
    inward = 1 - 2 * (place // half)

    def flip(stage):
        return pltpu.make_async_remote_copy(
            (src if stage == 0 else out.at[stage - 1]),
            buf.at[stage],
            send.at[stage],
            recv.at[stage],
            device_id=across(bits, bit_count - 1 - stage),
            device_id_type=MESH,
        )

    def z_copy(kind, by):
        n = bit_count + kind
        return pltpu.make_async_remote_copy(
            out.at[(bit_count - 1, bit_count, bit_count + 1)[kind]],
            (buf.at[bit_count], buf.at[bit_count + 1], out.at[bit_count + 1])[kind],
            send.at[n],
            recv.at[n],
            device_id=along(by),
            device_id_type=MESH,
        )

    def flip_done(stage):
        flip(stage).wait_recv()
        mine = src[...] if stage == 0 else out[stage - 1]
        out[stage] = mine + buf[stage]
        if stage + 1 < bit_count:
            flip(stage + 1).start()

    def z_in():
        @pl.when(jnp.logical_not(middle))
        def _():
            @pl.when(jnp.logical_not(outermost))
            def _():
                z_copy(0, -inward).wait_recv()
                out[bit_count - 1] = out[bit_count - 1] + buf[bit_count]

            z_copy(0, inward).start()

        @pl.when(middle)
        def _():
            out[bit_count] = out[bit_count - 1]

            @pl.when(jnp.logical_not(outermost))
            def _():
                z_copy(0, -inward).wait_recv()
                out[bit_count] = out[bit_count] + buf[bit_count]

            z_copy(1, inward).start()

    def z_mid():
        @pl.when(middle)
        def _():
            z_copy(1, inward).wait_recv()
            out[bit_count + 1] = out[bit_count] + buf[bit_count + 1]

    def z_out():
        @pl.when(jnp.logical_not(middle))
        def _():
            z_copy(2, inward).wait_recv()

        @pl.when(jnp.logical_not(outermost))
        def _():
            z_copy(2, -inward).start()

    def finish():
        for stage in range(bit_count):
            flip(stage).wait_send()

        @pl.when(jnp.logical_not(middle))
        def _():
            z_copy(0, inward).wait_send()

        @pl.when(middle)
        def _():
            z_copy(1, inward).wait_send()

        @pl.when(jnp.logical_not(outermost))
        def _():
            z_copy(2, -inward).wait_send()

    begin = lambda: flip(0).start()
    steps = [lambda s=s: flip_done(s) for s in range(bit_count)] + [z_in, z_mid, z_out]
    return begin, steps, finish


def bit_length(count):
    return count.bit_length() - 1


class Gatherer:
    def __init__(self, bit_count, items, shards, whole, loads, load_sem, cast_to, own_sem, send, recv):
        self.bit_count, self.items = bit_count, items
        self.shards, self.whole, self.loads, self.load_sem = shards, whole, loads, load_sem
        self.cast_to, self.own_sem, self.send, self.recv = cast_to, own_sem, send, recv
        self.bits = position_bits(bit_count)
        self.index = lax.axis_index("fsdp")
        self.ready = set()
        self.todo = []
        self.done = set()

    def block(self, axes):
        at = self.index
        for axis in axes:
            at = at + (1 << (self.bit_count - 1 - axis)) * (1 - 2 * self.bits[axis])
        return at

    def subsets(self, order):
        sets = [()]
        for axis in order:
            sets = sets + [(*s, axis) for s in sets]
        return sets

    def rows(self, item, axes):
        shard_rows = self.cast_to[item.weight].shape[0]
        return pl.ds(pl.multiple_of(self.block(axes) * shard_rows + item.start, 16), item.size)

    def copy(self, item, stage, number, axes):
        whole = self.whole[item.weight]
        at = self.rows(item, axes)
        src = self.cast_to[item.weight].at[pl.ds(item.start, item.size)] if not axes else whole.at[at]
        slot = (1 << stage) - 1 + number
        return pltpu.make_async_remote_copy(
            src,
            whole.at[at],
            self.send.at[item.number, slot],
            self.recv.at[item.number, slot],
            device_id=across(self.bits, item.order[stage]),
            device_id_type=MESH,
        )

    def landed(self, item, stage, number, axes):
        whole = self.whole[item.weight]
        at = self.rows(item, (*axes, item.order[stage]))
        slot = (1 << stage) - 1 + number
        return pltpu.make_async_remote_copy(
            whole.at[at],
            whole.at[at],
            self.send.at[item.number, slot],
            self.recv.at[item.number, slot],
            device_id=across(self.bits, item.order[stage]),
            device_id_type=MESH,
        )

    def load(self, weight):
        return pltpu.make_async_copy(self.shards[weight], self.loads[weight], self.load_sem.at[weight])

    def own(self, weight):
        rows = self.cast_to[weight].shape[0]
        return pltpu.make_async_copy(
            self.cast_to[weight],
            self.whole[weight].at[pl.ds(pl.multiple_of(self.index * rows, 16), rows)],
            self.own_sem.at[weight],
        )

    def begin(self, item):
        w = item.weight
        if w not in self.ready:
            self.ready.add(w)
            self.load(w).wait()
            group = 16

            def step(i, nothing):
                at = pl.ds(pl.multiple_of(i * group, group), group)
                self.cast_to[w][at] = low(self.loads[w][at])
                return nothing

            lax.fori_loop(0, self.cast_to[w].shape[0] // group, step, 0)
            self.own(w).start()
        for stage in range(self.bit_count):
            self.copy(item, stage, 0, ()).start()

    def advance(self, item, stage):
        before = self.subsets(item.order[:stage])
        for number, axes in enumerate(before):
            self.landed(item, stage, number, axes).wait_recv()
        for later in range(stage + 1, self.bit_count):
            sets = self.subsets(item.order[:later])
            for number, axes in enumerate(before):
                mine = (*axes, item.order[stage])
                self.copy(item, later, sets.index(mine), mine).start()
        if stage == self.bit_count - 1:
            self.done.add(item.number)

    def plan(self, lag):
        steps = []
        for i, item in enumerate(self.items):
            steps.append((i, 0, lambda item=item: self.begin(item)))
            for stage in range(self.bit_count):
                steps.append((i + lag * (stage + 1), stage + 1, lambda item=item, s=stage: self.advance(item, s)))
        self.todo = [action for _, _, action in sorted(steps, key=lambda s: s[:2])]

    def pump(self, count):
        for _ in range(min(count, len(self.todo))):
            self.todo.pop(0)()

    def until(self, weight):
        numbers = {item.number for item in self.items if item.weight == weight}
        while not numbers <= self.done:
            self.todo.pop(0)()
        self.own(weight).wait()

    def finish(self):
        for item in self.items:
            for stage in range(self.bit_count):
                for number, axes in enumerate(self.subsets(item.order[:stage])):
                    self.copy(item, stage, number, axes).wait_send()


def multiply(out_ref, out_rows, left, right_ref, first, width, tile):
    def step(j, nothing):
        at = pl.ds(pl.multiple_of(j * tile, tile), tile)
        from_at = pl.ds(pl.multiple_of(first + j * tile, 128), tile)
        out_ref[out_rows, at] = dot_nn(left[...], right_ref[:, from_at])
        return nothing

    lax.fori_loop(0, width // tile, step, 0)


def forward_part(tokens, seg_rows, norm_gain, cosine, signed, bias_row, rate_row, conv_weight,
                 conv_bias, mixer_gain, skip_row, shards, parts):
    fsdp, depth = lax.axis_size("fsdp"), lax.axis_size("seq")
    bit_count = bit_length(fsdp)
    shapes = [s.shape for s in shards]
    items = plan_items(shapes, fit(shapes, parts), bit_count)
    for item in items:
        item.order = item.order[1:] + item.order[:1]
    count = tokens.shape[0]
    weights = len(shards)
    pieces = 2
    kept_shape = (count // SUB, NS, DI)
    results = dict(
        normed=((count, 1024), bf16),
        conv=((count + EDGE, CW), f32),
        raw=((count, 128), f32),
        raw_w=((1024, 128), bf16),
        z=((count, DI), f32),
        act=((count, CW), bf16),
        dt=((count, 128), f32),
        cum=((count, 128), f32),
        passing=((1, DI), f32),
        query=((count, 512), bf16),
        kv=((depth * count, 256), bf16),
        attended=((count, 512), bf16),
        attended_t=((512, count), f32),
        log_total=((QUERY_HEADS * 8, count), f32),
        y=((count, DI), f32),
        gated=((count, DI), bf16),
        kept=(kept_shape, bf16),
        seg_wide=((count + 2 * EDGE, 128), f32),
        seg_all=((depth * 8, count), f32),
    )
    names = list(results)
    local = dict(
        normed_edge=((16, 1024), bf16),
        edge=((16, 1024), bf16),
        qkv=((count, 768), f32),
        end=((NS, DI), f32),
        state=((NS, DI), f32),
        carry=((NS, DI), f32),
        state_send=((NS, DI), bf16),
        state_recv=((NS, DI), bf16),
        bias=((count, count), f32),
        keys=((4, count, 128), bf16),
        values_t=((128, count), bf16),
        top=((QUERY_HEADS * 8, count), f32),
        total=((QUERY_HEADS * 8, count), f32),
    )
    in_vmem = (0, 1)

    def kernel(*refs):
        at = 0

        def take(n):
            nonlocal at
            at += n
            return refs[at - n : at]

        (tokens_ref, segrow_ref, gain_ref, cos_ref, sin_ref, bias_ref, rate_ref, weight_ref, cbias_ref,
         mixer_gain_ref, skip_ref) = take(11)
        shard_refs = take(weights)
        out = dict(zip(names, take(len(names))))
        whole_out = take(weights)
        v = dict(zip(names, take(len(names))))
        v.update(zip(local, take(len(local))))
        loads, cast_to = take(weights), take(weights)
        whole_vmem = take(len(in_vmem))
        send, recv, load_sem, own_sem, save_sem, z_send, z_recv = take(7)
        place = lax.axis_index("seq")
        whole = [whole_vmem[in_vmem.index(w)] if w in in_vmem else whole_out[w] for w in range(weights)]
        gather = Gatherer(bit_count, items, shard_refs, whole, loads, load_sem, cast_to, own_sem, send, recv)
        for w in range(weights):
            gather.load(w).start()
        enter(bit_count, depth)
        gather.plan(2)
        saved = []

        def save(src, dst):
            copy = pltpu.make_async_copy(src, dst, save_sem.at[len(saved)])
            copy.start()
            saved.append(copy)

        def keep(*which):
            for name in which:
                save(v[name], out[name])

        def to_next(src, dst, slot):
            return pltpu.make_async_remote_copy(
                src, dst, z_send.at[slot], z_recv.at[slot], device_id=along(1), device_id_type=MESH
            )

        started = []

        def send_on(condition, src, dst, slot):
            @pl.when(condition)
            def _():
                to_next(src, dst, slot).start()

            started.append((condition, src, dst, slot))

        def ring(ref, rows, hop, slot):
            b = place - hop + 1
            part = ref.at[pl.ds(pl.multiple_of(jnp.maximum(b, 0) * rows, 8), rows)]
            send_on((b >= 0) & (place < depth - 1), part, part, slot)

        def ring_wait(ref, rows, hop, slot):
            b = place - hop
            part = ref.at[pl.ds(pl.multiple_of(jnp.maximum(b, 0) * rows, 8), rows)]

            @pl.when(b >= 0)
            def _():
                to_next(part, part, slot).wait_recv()

        tail = tokens_ref.at[pl.ds(count - 16, 16)]
        gather.pump(2)
        send_on(place < depth - 1, tail, v["edge"], 0)
        v["seg_all"][pl.ds(pl.multiple_of(place * 8, 8), 8)] = jnp.broadcast_to(segrow_ref[...], (8, count))
        ring(v["seg_all"], 8, 1, 1)

        def normalise(src, dst, rows, group):
            def step(i, nothing):
                at = pl.ds(pl.multiple_of(i * group, group), group)
                x = src[at].astype(f32)
                scale = lax.rsqrt(jnp.mean(x * x, axis=1, keepdims=True) + epsilon)
                dst[at] = low(x * scale * gain_ref[...])
                return nothing

            lax.fori_loop(0, rows // group, step, 0)

        normalise(tokens_ref, v["normed"], count, 64)
        gather.pump(1)

        @pl.when(place == 0)
        def _():
            v["edge"][...] = jnp.zeros((16, 1024), bf16)

        @pl.when(place > 0)
        def _():
            to_next(tail, v["edge"], 0).wait_recv()

        normalise(v["edge"], v["normed_edge"], 16, 16)
        gather.pump(1)
        for hop in range(1, depth):
            ring_wait(v["seg_all"], 8, hop, hop)
            if hop < depth - 1:
                ring(v["seg_all"], 8, hop + 1, hop + 1)

        before = v["seg_all"][pl.ds(pl.multiple_of(jnp.maximum(place - 1, 0) * 8, 8), 8)][0:1]
        v["seg_wide"][0:EDGE, :] = jnp.where(place == 0, -1.0, seg_column(before)[count - EDGE :])
        v["seg_wide"][EDGE : EDGE + count, :] = seg_column(segrow_ref[...])
        v["seg_wide"][EDGE + count :, :] = jnp.full((EDGE, 128), -2.0, f32)
        own_rows = pl.ds(pl.multiple_of(place * count, 8), count)
        v["raw_w"][...] = jnp.zeros((1024, 128), bf16)
        gather.until(0)
        save(whole[0], whole_out[0])
        multiply(v["conv"], pl.ds(EDGE, count), v["normed"], whole[0], DI, CW, 256)
        v["conv"][0:EDGE, :] = dot_nn(v["normed_edge"][...], whole[0][:, DI : DI + CW])[EDGE:]
        v["raw_w"][:, 0:MH] = whole[0][:, DI + CW : DI + CW + MH]
        v["raw"][...] = dot_nn(v["normed"][...], v["raw_w"][...])
        gather.pump(4)
        front_conv(v["conv"], v["seg_wide"], weight_ref, cbias_ref, v["act"])
        gather.pump(4)
        front_state(v["seg_wide"], v["raw"], bias_ref, rate_ref, v["act"], v["dt"], v["cum"], v["end"], v["passing"])
        keep("normed", "conv", "raw", "raw_w", "act", "dt", "cum", "passing", "seg_wide", "seg_all")
        width = DI // pieces
        state_slot, kv_slot = depth, depth + pieces

        def chain(j):
            for p in range(pieces):
                cols = pl.ds(p * width, width)

                @pl.when(place == j)
                def _():
                    if j == 0:
                        v["state"][:, cols] = jnp.zeros((NS, width), f32)
                    else:
                        to_next(
                            v["state_send"].at[:, cols], v["state_recv"].at[:, cols], state_slot + p
                        ).wait_recv()
                        v["state"][:, cols] = v["state_recv"][:, cols].astype(f32)
                    if j < depth - 1:
                        v["state_send"][:, cols] = low(
                            v["passing"][:, cols] * v["state"][:, cols] + v["end"][:, cols]
                        )
                        to_next(
                            v["state_send"].at[:, cols], v["state_recv"].at[:, cols], state_slot + p
                        ).start()

        chain(0)
        gather.until(1)
        save(whole[1], whole_out[1])
        multiply(v["qkv"], slice(None), v["normed"], whole[1], 0, 768, 256)
        rotate_kernel(v["qkv"], cos_ref, sin_ref, v["query"], v["kv"].at[own_rows])
        ring(v["kv"], count, 1, kv_slot + 1)
        keep("query")
        gather.pump(4)
        multiply(v["z"], slice(None), v["normed"], whole[0], 0, DI, 256)
        keep("z")
        gather.pump(4)
        chain(1)
        attend_start(v["top"], v["total"], v["attended_t"])

        def attend(b):
            attend_block(b, place, v["query"], v["kv"], v["seg_all"], segrow_ref, v["attended_t"], v["bias"],
                         v["keys"], v["values_t"], v["top"], v["total"])

        attend(place)
        gather.pump(4)
        for hop in range(1, depth):
            ring_wait(v["kv"], count, hop, kv_slot + hop)
            if hop < depth - 1:
                ring(v["kv"], count, hop + 1, kv_slot + hop + 1)

            @pl.when(place >= hop)
            def _(hop=hop):
                attend(place - hop)

            gather.pump(4)
            if hop < depth - 1:
                chain(hop + 1)

        attend_finish(v["attended"], v["attended_t"], v["log_total"], v["top"], v["total"])
        keep("attended", "attended_t", "log_total", "kv")
        for first in range(0, count // SUB, 2):
            gather.pump(4)
            mid_kernel(v["act"], v["dt"], v["cum"], v["seg_wide"], segrow_ref, v["state"], v["z"], mixer_gain_ref,
                       skip_ref, v["y"], v["gated"], v["kept"], v["carry"], first, first + 2)
        keep("y", "gated", "kept")
        for w in range(2, weights):
            gather.until(w)
        gather.finish()
        for condition, src, dst, slot in started:

            @pl.when(condition)
            def _(src=src, dst=dst, slot=slot):
                to_next(src, dst, slot).wait_send()

        @pl.when(place < depth - 1)
        def _():
            for p in range(pieces):
                cols = pl.ds(p * width, width)
                to_next(v["state_send"].at[:, cols], v["state_recv"].at[:, cols], state_slot + p).wait_send()

        for copy in saved:
            copy.wait()

    wholes = [((fsdp * rows, cols), bf16) for rows, cols in shapes]
    scratch = [pltpu.VMEM(*results[n]) for n in names] + [pltpu.VMEM(*a) for a in local.values()]
    scratch += [pltpu.VMEM(shape, f32) for shape in shapes] + [pltpu.VMEM(shape, bf16) for shape in shapes]
    scratch += [pltpu.VMEM(*wholes[w]) for w in in_vmem]
    slots = (1 << bit_count) - 1
    z_slots = depth + pieces + depth
    scratch += [
        pltpu.SemaphoreType.DMA((len(items), slots)),
        pltpu.SemaphoreType.DMA((len(items), slots)),
        pltpu.SemaphoreType.DMA((weights,)),
        pltpu.SemaphoreType.DMA((weights,)),
        pltpu.SemaphoreType.DMA((len(names) + 2,)),
        pltpu.SemaphoreType.DMA((z_slots,)),
        pltpu.SemaphoreType.DMA((z_slots,)),
    ]
    hbm = pl.BlockSpec(memory_space=pl.ANY)
    made = pl.pallas_call(
        kernel,
        out_shape=[jax.ShapeDtypeStruct(*a) for a in list(results.values()) + wholes],
        in_specs=[vmem] * 11 + [hbm] * weights,
        out_specs=[hbm] * (len(names) + weights),
        scratch_shapes=scratch,
        compiler_params=pltpu.CompilerParams(
            collective_id=1, has_side_effects=True, vmem_limit_bytes=62 * 2**20
        ),
    )(tokens, seg_rows, norm_gain, cosine, signed, bias_row, rate_row, conv_weight, conv_bias, mixer_gain,
      skip_row, *shards)
    return dict(zip(names, made)), made[len(names) :]


PA, PB, PC, PD, PE = 2, 3, 4, 5, 1


def backward_part(v, gated_grad, attended_grad, cosine, signed, seg_row, bias_row, rate_row, conv_weight,
                  conv_bias, mixer_gain, skip_row, norm_gain, ffn_gain_grad, tokens, hidden_grad, in_full, qkv_full,
                  gradients):
    fsdp, depth = lax.axis_size("fsdp"), lax.axis_size("seq")
    bit_count = bit_length(fsdp)
    made_here = len(gradients)
    model = in_full.shape[0]
    shapes = [(g.shape[0] // fsdp, g.shape[1]) for g in gradients]
    shapes += [(model // fsdp, width) for width in (DI, 768, CW, 128)]
    parts = fit(shapes, (8, 4, 4, 2, 4, 2, 4, 1))
    items = plan_items(shapes, parts, bit_count)
    weights = len(shapes)
    gate_w, down_w, in_z, qkv_w, conv_w, raw_w = 0, 1, made_here, made_here + 1, made_here + 2, made_here + 3
    hosts = {in_z: (gate_w, 0), conv_w: (gate_w, DI), qkv_w: (gate_w, DI + CW), raw_w: (down_w, 0)}
    count = gated_grad.shape[0]
    pieces = 2
    loaded = dict(
        grad=gated_grad, y=v["y"], act=v["act"], z=v["z"], dt=v["dt"], cum=v["cum"], seg_wide=v["seg_wide"],
        out_grad=attended_grad, query=v["query"], out_t=v["attended_t"], kv=v["kv"], seg_all=v["seg_all"],
        log_total=v["log_total"], cos=cosine, sin=signed, raw=v["raw"], kept=v["kept"],
    )
    rows_in = (seg_row, bias_row, rate_row, conv_weight, conv_bias, mixer_gain, skip_row, v["passing"], norm_gain,
               ffn_gain_grad)
    later_in = (v["conv"], v["normed"], tokens, hidden_grad, in_full, qkv_full, v["raw_w"])
    results = dict(
        raw_grad=((count, 128), bf16),
        qkv_grad=((count, 768), bf16),
    )
    names, loads = list(results), list(loaded)
    rows_out = [((1, model), f32)] * 2
    rows_out += [((1, DI), f32), ((KC, CW), f32), ((1, CW), f32), ((1, 128), f32), ((1, 128), f32), ((1, 128), f32)]
    groups = sum(shape[0] * shape[1] // 128 for shape, _ in rows_out)
    small_shape = (-(-groups // 8) * 8, 128)
    local = dict(
        ygrad=((count, DI), f32),
        state_grad=((NS, DI), f32),
        later=((NS, DI), f32),
        state_send=((NS, DI), bf16),
        state_recv=((NS, DI), bf16),
        bias=((count, count), f32),
        keys=((4, count, 128), bf16),
        values=((4, count, 128), bf16),
        keys_t=((128, count), bf16),
        dkeys=((2, count, 128), f32),
        dvalues=((2, count, 128), f32),
        spread=((QUERY_HEADS * 8, count), f32),
        kv_grad=((depth * count, 256), bf16),
        kv_recv=(((depth - 1) * count, 256), bf16),
        pair_grad=((count, 2 * NS), f32),
        pair_conv_grad=((count, 2 * NS), bf16),
        conv=((2, count + EDGE, 128), f32),
        pre=((count + 2 * EDGE, 128), f32),
        edge=((EDGE, CW), f32),
        edge_recv=((EDGE, CW), f32),
        tail=((16, CW), f32),
    )

    def kernel(*refs):
        at = 0

        def take(n):
            nonlocal at
            at += n
            return refs[at - n : at]

        (segrow_ref, bias_ref, rate_ref, weight_ref, cbias_ref, gain_ref, skip_ref, passing_ref,
         norm_gain_ref, ffn_gain_grad_ref) = take(len(rows_in))
        inputs = dict(zip(loads, take(len(loads))))
        conv_hbm, normed_hbm, tokens_hbm, hidden_hbm, in_hbm, qkv_hbm, raw_w_hbm = take(len(later_in))
        whole = take(made_here)
        (input_grad_out,) = take(1)
        small_out = take(len(rows_out))
        sums = take(weights)
        whole = [*whole, *take(weights - made_here)]
        b = dict(zip(names, take(len(names))))
        b.update(zip(loads, take(len(loads))))
        b.update(zip(local, take(len(local))))
        norm_gain_grad, gain_grad, weight_grad, cbias_grad, rate_grad, bias_grad, skip_grad = take(7)

        def with_views(arrays, lead):
            views = []
            for w in range(made_here, weights):
                host, column = hosts[w]
                cols = pl.ds(column, shapes[w][1])
                views.append(arrays[host].at[(slice(None),) * (lead + 1) + (cols,)])
            return [*arrays, *views]

        own = with_views(take(made_here), bit_count - 1)
        landed = [with_views(take(made_here), bit_count - 1 - s) for s in range(bit_count)]
        zin, zmid = with_views(take(made_here), 0), with_views(take(made_here), 0)
        small_src, small_buf, small_work = take(3)
        (send, recv, own_sem, load_sem, save_sem, conv_sem, z_send, z_recv, small_send, small_recv, tile_sem, grad_sem,
         late_sem, ready_sem) = take(14)
        place = lax.axis_index("seq")

        def load(name):
            return pltpu.make_async_copy(inputs[name], b[name], load_sem.at[loads.index(name)])

        def need(*which):
            for name in which:
                load(name).wait()

        for name in loads:
            load(name).start()
        enter(bit_count, depth)
        work = Reducer(bit_count, depth, items, whole, own, landed, zin, zmid, sums, send, recv, own_sem)
        work.actions(2, 2, tuple(range(made_here, weights)), (gate_w, down_w), ready_sem)
        for item in items:
            if item.weight < made_here:
                work.begin(item)

        def to(by, src, dst, slot):
            return pltpu.make_async_remote_copy(
                src, dst, z_send.at[slot], z_recv.at[slot], device_id=along(by), device_id_type=MESH
            )

        need("grad", "y", "act", "z", "dt", "cum", "seg_wide")
        for first in range(count // SUB):
            gate_back_kernel(b["grad"], b["y"], b["act"], b["z"], b["dt"], b["cum"], b["seg_wide"], gain_ref,
                             skip_ref, b["ygrad"], b["grad"], gain_grad, b["state_grad"], first, first + 1)
            work.pump(PA)
        width = DI // pieces

        def chain(j):
            for p in range(pieces):
                cols = pl.ds(p * width, width)

                @pl.when(place == j)
                def _():
                    copy = to(-1, b["state_send"].at[:, cols], b["state_recv"].at[:, cols], p)
                    if j == depth - 1:
                        b["later"][:, cols] = jnp.zeros((NS, width), f32)
                    else:
                        copy.wait_recv()
                        b["later"][:, cols] = b["state_recv"][:, cols].astype(f32)
                    if j > 0:
                        b["state_send"][:, cols] = low(
                            passing_ref[:, cols] * b["later"][:, cols] + b["state_grad"][:, cols]
                        )
                        copy.start()

        def kv_hop(i):
            part = pl.ds(i * count, count)
            copy = to(-1, b["kv_grad"].at[part], b["kv_recv"].at[part], pieces + i)

            @pl.when((place >= i) & (place < depth - 1))
            def _():
                copy.wait_recv()

                def step(n, nothing):
                    at = pl.ds(pl.multiple_of(i * count + n * 64, 64), 64)
                    b["kv_grad"][at] = b["kv_grad"][at] + b["kv_recv"][at]
                    return nothing

                lax.fori_loop(0, count // 64, step, 0)

            @pl.when(place > i)
            def _():
                copy.start()

        chain(depth - 1)
        need("out_grad", "query", "out_t", "kv", "seg_all", "log_total", "cos", "sin")
        attend_back_start(b["query"], b["out_grad"], b["out_t"], b["spread"])
        for i in range(depth):

            for first in (0, 2):

                @pl.when(i <= place)
                def _(i=i, first=first):
                    attend_back_block(i, place, b["query"], b["kv"], b["seg_all"], segrow_ref, b["out_grad"],
                                      b["log_total"], b["kv_grad"], b["bias"], b["keys"], b["values"], b["keys_t"],
                                      b["dkeys"], b["dvalues"], b["spread"], b["out_t"], first, first + 2)

                work.pump(PB)
            if i < depth - 1:
                chain(depth - 2 - i)
            if i > 0:
                kv_hop(i - 1)
        attend_back_finish(b["out_t"], b["cos"], b["sin"], b["qkv_grad"])
        need("raw", "kept")
        for first in range(count // SUB):
            back_states(b["act"], b["dt"], b["cum"], b["seg_wide"], segrow_ref, b["raw"], bias_ref, rate_ref,
                        b["kept"], b["y"], b["ygrad"], skip_ref, b["raw_grad"], rate_grad, bias_grad, skip_grad,
                        b["z"], b["pair_grad"], b["later"], first, first + 1)
            work.pump(PC)
        normed, total = b["act"].at[:, :model], b["y"].at[:, :model]
        half = model // 2

        def late(src, dst, n):
            copy = pltpu.make_async_copy(src, dst, late_sem.at[n])
            copy.start()
            return copy

        normed_copy = late(normed_hbm, normed, 0)
        late_copies = [
            late(hidden_hbm, b["ygrad"].at[:, :model], 1),
            late(tokens_hbm.at[:, :half], b["query"], 2),
            late(tokens_hbm.at[:, half:], b["out_grad"], 3),
        ]
        shard = model // fsdp
        flying = {}

        def weight_gradient(w, rights):
            steps = [(group, right, column, c) for group in range(2) for right, column in rights
                     for c in range(0, right.shape[1], 768)]
            for n, (group, right, column, c) in enumerate(steps):
                slot, width = n % 2, min(768, right.shape[1] - c)
                for copy in flying.pop(slot, ()):
                    copy.wait()
                value = low(dot_tn(normed[:, group * half : group * half + half], right[:, c : c + width]))
                copies = []
                for m in range(half // shard):
                    owner, row = group * (half // shard) + m, m * shard
                    lead = tuple((owner >> (bit_count - 1 - i)) & 1 for i in range(bit_count))
                    room = b["kept"].at[row // 128, pl.ds(row % 128, shard), pl.ds(slot * 768, width)]
                    room[...] = value[row : row + shard]
                    copies.append(
                        pltpu.make_async_copy(
                            room, whole[w].at[(*lead, slice(None), pl.ds(column + c, width))], grad_sem.at[slot, m]
                        )
                    )
                    copies[-1].start()
                flying[slot] = copies
                work.pump(3)
            for slot in list(flying):
                for copy in flying.pop(slot):
                    copy.wait()
            work.have.add(w)

        def fetch(k, source, column, width):
            slot, room = k % 2, (b["keys"], b["values"])[k % 2]
            copies = []
            for c in range(width // 128):
                for r in range(2):
                    copies.append(
                        pltpu.make_async_copy(
                            source.at[pl.ds(r * half, half), pl.ds(column + c * 128, 128)],
                            room.at[c * 2 + r],
                            tile_sem.at[slot, c * 2 + r],
                        )
                    )
            return copies

        def input_gradient(pairs, first):
            plans = [fetch(k, source, column, left.shape[1]) for k, (left, source, column) in enumerate(pairs)]
            for copy in plans[0]:
                copy.start()
            for k, (left, source, column) in enumerate(pairs):
                if k + 1 < len(pairs):
                    for copy in plans[k + 1]:
                        copy.start()
                for copy in plans[k]:
                    copy.wait()
                room, tiles = (b["keys"], b["values"])[k % 2], left.shape[1] // 128
                for r in range(2):
                    right = room[r] if tiles == 1 else jnp.concatenate([room[r], room[2 + r]], 1)
                    cols = slice(r * half, r * half + half)
                    value = dot_nt(left[...], right)
                    total[:, cols] = value if first and k == 0 else total[:, cols] + value
                work.pump(PE)

        def columns(ref, j):
            return ref.at[:, j * 256 : j * 256 + 256]

        own_rows = pl.ds(pl.multiple_of(place * count, 8), count)
        x = b["kv_grad"][own_rows, 0:128].astype(f32)
        b["qkv_grad"][:, 512:640] = low(x * b["cos"][...] + partner(x * b["sin"][...]))
        b["qkv_grad"][:, 640:768] = b["kv_grad"][own_rows, 128:256]
        normed_copy.wait()
        weight_gradient(in_z, [(b["grad"], 0)])
        work.pump(4)
        weight_gradient(qkv_w, [(b["qkv_grad"], 0)])
        work.pump(4)
        input_gradient([(columns(b["grad"], j), in_hbm, j * 256) for j in range(DI // 256)], True)
        tiles, value_tiles = CW // 128, DI // 128
        for first, until in ((0, value_tiles // 2), (value_tiles // 2, value_tiles), (value_tiles, tiles)):
            source, dst, shift = b["z"], b["grad"], 0
            if until > value_tiles:
                source, dst, shift = b["pair_grad"], b["pair_conv_grad"], value_tiles
            back_conv(conv_hbm, b["conv"], conv_sem, b["seg_wide"], weight_ref, cbias_ref, source, shift,
                      dst, b["edge"], b["tail"], weight_grad, cbias_grad, b["pre"], first, until)
            work.pump(PD)
        edge = to(-1, b["edge"], b["edge_recv"], pieces + depth)

        @pl.when(place > 0)
        def _():
            edge.start()

        input_gradient([(columns(b["qkv_grad"], j), qkv_hbm, j * 256) for j in range(3)], False)

        @pl.when(place < depth - 1)
        def _():
            edge.wait_recv()
            b["tail"][16 - EDGE :, :] = b["tail"][16 - EDGE :, :] + b["edge_recv"][...]
            b["grad"][count - 16 :, :] = low(b["tail"][:, :DI])
            b["pair_conv_grad"][count - 16 :, :] = low(b["tail"][:, DI:])

        weight_gradient(conv_w, [(b["grad"], 0), (b["pair_conv_grad"], DI)])
        weight_gradient(raw_w, [(b["raw_grad"], 0)])
        work.pump(4)
        input_gradient(
            [(columns(b["grad"], j), in_hbm, DI + j * 256) for j in range(DI // 256)]
            + [(b["pair_conv_grad"], in_hbm, 2 * DI), (b["raw_grad"], raw_w_hbm, 0)],
            False,
        )
        for copy in late_copies:
            copy.wait()
        norm_gain_grad[...] = jnp.zeros_like(norm_gain_grad)
        group = 32

        def norm_back(i, nothing):
            at = pl.ds(pl.multiple_of(i * group, group), group)
            x = jnp.concatenate([b["query"][at, :].astype(f32), b["out_grad"][at, :].astype(f32)], 1)
            unit = x * lax.rsqrt(jnp.mean(x * x, axis=1, keepdims=True) + epsilon)
            scale = lax.rsqrt(jnp.mean(x * x, axis=1, keepdims=True) + epsilon)
            grad = total[at, :]
            norm_gain_grad[...] += jnp.sum(grad * unit, axis=0, keepdims=True)
            h = grad * norm_gain_ref[...]
            total[at, :] = b["ygrad"][at, :model] + scale * (h - unit * jnp.mean(h * unit, axis=1, keepdims=True))
            return nothing

        lax.fori_loop(0, count // group, norm_back, 0)
        save = pltpu.make_async_copy(total, input_grad_out, save_sem.at[0])
        save.start()
        small_rows = (norm_gain_grad, ffn_gain_grad_ref, gain_grad, weight_grad, cbias_grad, rate_grad, bias_grad,
                      skip_grad)
        places = [(r, i, g) for r, ref in enumerate(small_rows) for i in range(ref.shape[0])
                  for g in range(ref.shape[1] // 128)]
        small_src[...] = jnp.zeros(small_shape, f32)
        for n, (r, i, g) in enumerate(places):
            small_src[n : n + 1, :] = small_rows[r][i : i + 1, g * 128 : g * 128 + 128]
        begin, steps, small_finish = small_sum(
            bit_count, depth, small_src, small_buf, small_work, small_send, small_recv
        )
        begin()
        while work.todo or steps:
            work.pump(3)
            if steps:
                steps.pop(0)()
        for n, (r, i, g) in enumerate(places):
            small_out[r][i : i + 1, g * 128 : g * 128 + 128] = small_work[bit_count + 1, n : n + 1, :]
        small_finish()
        for item in items:
            if item.weight not in (gate_w, down_w):
                work.finish(item)

        @pl.when(place > 0)
        def _():
            edge.wait_send()
            for p in range(pieces):
                cols = pl.ds(p * width, width)
                to(-1, b["state_send"].at[:, cols], b["state_recv"].at[:, cols], p).wait_send()

        for i in range(depth - 1):

            @pl.when(place > i)
            def _(i=i):
                part = pl.ds(i * count, count)
                to(-1, b["kv_grad"].at[part], b["kv_recv"].at[part], pieces + i).wait_send()

        save.wait()

    two = (2,) * bit_count
    hbm = pl.BlockSpec(memory_space=pl.ANY)
    scratch = [pltpu.VMEM(*results[n]) for n in names]
    scratch += [pltpu.VMEM(x.shape, x.dtype) for x in loaded.values()]
    scratch += [pltpu.VMEM(*a) for a in local.values()]
    mine = shapes[:made_here]
    scratch += [pltpu.VMEM(*rows_out[0])] + [pltpu.VMEM(*a) for a in rows_out[2:]]
    stacks = [[pltpu.VMEM((*two[: bit_count - 1 - s], *shape), bf16) for shape in mine] for s in range(bit_count)]
    flat = [pltpu.VMEM(shape, bf16) for shape in mine]
    rooms = [pltpu.VMEM(own_shape(bit_count, shape, n), bf16) for shape, n in zip(mine, parts)]
    scratch += [*rooms, *[x for stage in stacks for x in stage], *flat, *flat]
    scratch += [pltpu.VMEM(small_shape, f32)] + [pltpu.VMEM((bit_count + 2, *small_shape), f32)] * 2
    slots = pieces + depth + 1
    dma = pltpu.SemaphoreType.DMA
    scratch += [
        dma((len(items), bit_count + 3)), dma((len(items), bit_count + 3)), dma((len(items),)), dma((len(loads),)),
        dma((1,)), dma((2,)), dma((slots,)), dma((slots,)), dma((bit_count + 3,)), dma((bit_count + 3,)), dma((2, 4)),
        dma((2, fsdp)), dma((4,)), pltpu.SemaphoreType.REGULAR,
    ]
    outs = [((count, model), f32), *rows_out, *[(shape, bf16) for shape in shapes]]
    outs += [((*two, *shape), bf16) for shape in shapes[made_here:]]
    made = pl.pallas_call(
        kernel,
        out_shape=[jax.ShapeDtypeStruct(*a) for a in outs],
        in_specs=[vmem] * len(rows_in) + [hbm] * (len(loads) + len(later_in) + made_here),
        out_specs=[hbm] + [vmem] * len(rows_out) + [hbm] * (2 * weights - made_here),
        scratch_shapes=scratch,
        compiler_params=pltpu.CompilerParams(
            collective_id=2, has_side_effects=True, vmem_limit_bytes=63 * 2**20
        ),
    )(
        *rows_in, *loaded.values(), *later_in,
        *[g.reshape(*two, *shape) for g, shape in zip(gradients, shapes)],
    )
    n = 1 + len(rows_out)
    return made[0], made[1:n], made[n : n + weights]


def shifted(array, axis, by):
    devices = lax.axis_size(axis)
    pairs = [(i, i + by) for i in range(devices) if 0 <= i + by < devices]
    return lax.ppermute(array, axis, pairs)


def contract(left, right):
    return dot_tn(left, right)


def rms_scale(values, gain_vec):
    return (
        values * lax.rsqrt(jnp.mean(values * values, axis=-1, keepdims=True) + epsilon) * gain_vec
    )


def reduced(gradient):
    return low(gradient)


def padded(vector):
    return jnp.pad(vector, (0, 128 - vector.shape[0]))[None]


def on_device(
    tokens,
    cotangent,
    segment_ids,
    norm_gain,
    ffn_gain,
    mixer_gain,
    conv_weight,
    conv_bias,
    decay_log,
    step_bias,
    skip_gain,
    in_proj,
    mixer_out,
    qkv_proj,
    attn_proj,
    gate_up,
    down_proj,
):
    place, devices = lax.axis_index("seq"), lax.axis_size("seq")
    count = tokens.shape[1]
    position = place * count + jnp.arange(count, dtype=jnp.int32)
    half = HEAD_WIDTH // 2
    lane = jnp.arange(128, dtype=jnp.int32)
    exponent = (lane % half).astype(f32) * (2.0 / HEAD_WIDTH)
    frequencies = jnp.power(rope_base, -exponent)
    angles = position.astype(f32)[:, None] * frequencies[None, :]
    cosine = jnp.cos(angles)
    signed = jnp.sin(angles) * jnp.where(lane % HEAD_WIDTH < half, -1.0, 1.0)[None]
    seg_row = segment_ids.astype(f32)
    bias_row, rate_row = padded(step_bias), padded(decay_log)
    skip_row = jnp.repeat(skip_gain, MP)[None]
    v, (in_full, qkv_full, mix_full, attn_full, gate_full, down_full) = forward_part(
        tokens[0], seg_row, norm_gain[None], cosine, signed, bias_row, rate_row, conv_weight, conv_bias[None],
        mixer_gain[None], skip_row, (in_proj, qkv_proj, mixer_out, attn_proj, gate_up, down_proj),
        (4, 2, 2, 2, 4, 4),
    )
    attended, gated = v["attended"], v["gated"]
    token_rows = tokens[0].astype(f32)
    hidden = token_rows + (dot_nn(attended, attn_full) + dot_nn(gated, mix_full))
    ffn_in32, ffn_pull = jax.vjp(rms_scale, hidden, ffn_gain)
    ffn_in = lax.optimization_barrier(low(ffn_in32))
    gates = lax.optimization_barrier(dot_nn(ffn_in, gate_full))

    gate, up = gates[:, :FF], gates[:, FF:]
    sig = jax.nn.sigmoid(gate)
    inner = lax.optimization_barrier(low(gate * sig * up))
    result = hidden + dot_nn(inner, down_full)
    back_rows = cotangent[0]
    down_piece = reduced(contract(inner, back_rows))
    act_grad = lax.optimization_barrier(dot_nt(back_rows, down_full))
    gates_grad = lax.optimization_barrier(
        jnp.concatenate(
            [low(act_grad * up * (sig * (1.0 + gate * (1.0 - sig)))), low(act_grad * (gate * sig))], axis=1
        )
    )
    gate_piece = reduced(contract(ffn_in, gates_grad))
    hidden_extra, ffn_gain_grad = ffn_pull(dot_nt(gates_grad, gate_full))
    hidden_grad = back_rows.astype(f32) + hidden_extra
    branch = lax.optimization_barrier(low(hidden_grad))
    attn_piece = reduced(contract(attended, branch))
    attended_grad = low(dot_nt(branch, attn_full))
    mixer_piece = reduced(contract(gated, branch))
    gated_grad = low(dot_nt(branch, mix_full))

    input_grad, small_rows, sums = backward_part(
        v, gated_grad, attended_grad, cosine, signed, seg_row, bias_row, rate_row, conv_weight, conv_bias[None],
        mixer_gain[None], skip_row, norm_gain[None], ffn_gain_grad[None], tokens[0], hidden_grad, in_full, qkv_full,
        (gate_piece, down_piece, mixer_piece, attn_piece),
    )
    gate_sum, down_sum, mixer_sum, attn_sum, z_sum, qkv_sum, conv_sum, raw_sum = sums
    in_sum = jnp.concatenate([z_sum, conv_sum, raw_sum[:, :MH]], axis=1)
    shards = [x.astype(f32) for x in (in_sum, mixer_sum, qkv_sum, attn_sum, gate_sum, down_sum)]
    small = [row if row.shape[0] == KC else row[0] for row in small_rows]
    small = [row[:MH] if row.shape[0] == 128 else row for row in small]
    return (low(result)[None], input_grad[None], *small, *shards)


def solution(mesh):
    rows, whole, split_rows = P("fsdp", "seq", None), P(), P("fsdp", None)
    return jax.shard_map(
        on_device,
        mesh=mesh,
        in_specs=(rows, rows, P("fsdp", "seq"), *[whole] * 8, *[split_rows] * 6),
        out_specs=(rows, rows, *[whole] * 8, *[split_rows] * 6),
        check_vma=False,
    )
```
